32 devices in a mesh: tm: 4 (over y, x), space: 8 (over z, core).
Axes of the slice: x: 2, y: 2, z: 4, core: 2. Of those that a mesh axis runs over, the one named last changes fastest.
Arguments:
- wave_field: bfloat16 [8, 2048, 256], P('tm', 'space'), may hold values from -600 to 600
- cotangent: bfloat16 [8, 2048, 256], P('tm', 'space'), may hold values from -6 to 6
- block_lists: int32 [8, 16, 4], P('tm', 'space'), may hold values from 0 to 15, as said below
- project_weights: bfloat16 [2, 256, 768], replicated, may hold values from -2 to 2
- combine_weights: bfloat16 [2, 256, 256], replicated, may hold values from -0.375 to 0.375
Outputs:
- mixed_field: bfloat16 [8, 2048, 256], P('tm', 'space')
- field_grad: bfloat16 [8, 2048, 256], P('tm', 'space')
- project_grad: float32 [2, 256, 768], replicated
- combine_grad: float32 [2, 256, 256], replicated
The draws below stay inside these ranges and needn't reach their ends.
Inputs may be any that keep to these rules, and one draw needn't show every extreme that they name: `block_lists`: for frame f and block b, entry 0 is b itself, entry 1 is b - 2 or b + 2, and every entry lies within 2 blocks of b; entries may repeat.
All inputs are finite; a program needn't handle non-finite values.
Results may differ from the reference program's by a relative error of at most 0.012.
Values may be sent and summed in bfloat16 or wider, within the bound.
No kernel may reach another device: no remote copies, remote signals or barrier semaphores. Data moves between devices by JAX's collectives and lax.ppermute only.
A program may use at most 128 MiB of HBM per device.

```python
import math
import jax
import jax.numpy as jnp
from jax import lax

D = 256
HEADS = 8
BLOCK = 128
KB = 4
HREACH = 2
ROWS_DEV = 256
FRAMES = 8
TOKENS_F = 2048


def draw_wave_field(key, part):
    key_base = jax.random.fold_in(key, 0)
    full_shape = (FRAMES, TOKENS_F, D)
    drawn = jnp.clip(jax.random.normal(key_base, full_shape, jnp.float32), -4.0, 4.0)
    return drawn.astype(jnp.bfloat16)


def draw_project_weights(key, part):
    key_base = jax.random.fold_in(key, 0)
    drawn = jnp.clip(jax.random.normal(key_base, (2, D, 3 * D), jnp.float32), -4.0, 4.0) / math.sqrt(D)
    return drawn.astype(jnp.bfloat16)


def draw_block_lists(key, part):
    key_sign, key_rest = jax.random.split(key)
    total_blocks = TOKENS_F // BLOCK
    own_block = jnp.broadcast_to(jnp.arange(total_blocks, dtype=jnp.int32)[None, :, None], (FRAMES, total_blocks, 1))
    direction = jax.random.randint(key_sign, (FRAMES, total_blocks, 1), 0, 2).astype(jnp.int32) * 2 - 1
    far_block = own_block + direction * HREACH
    far_block = jnp.where((far_block < 0) | (far_block >= total_blocks), own_block - direction * HREACH, far_block)
    offsets = jax.random.randint(key_rest, (FRAMES, total_blocks, KB - 2), -HREACH, HREACH + 1).astype(jnp.int32)
    others = jnp.clip(own_block + offsets, 0, total_blocks - 1)
    return jnp.concatenate([own_block, far_block, others], axis=2).astype(jnp.int32)


def shard_levels(stream_key, shape, cuts, least, largest):
    def one(dim, blocks):
        heights = jax.random.uniform(jax.random.fold_in(jax.random.fold_in(stream_key, 6), dim), (blocks,), jnp.float32, least / len(cuts), largest / len(cuts))
        return jnp.repeat(jnp.exp(heights), shape[dim] // blocks).reshape((-1,) + (1,) * (len(shape) - dim - 1))

    level = one(*cuts[0])
    for cut in cuts[1:]:
        level = level * one(*cut)
    return level


def bell_draw(rng, shape, scale, reach, cuts=(), held_as=jnp.bfloat16):
    entries = scale * jax.random.normal(rng, shape, jnp.float32)
    if cuts:
        entries = entries * shard_levels(rng, shape, cuts, -0.22, 0.18)
    return jnp.clip(entries, -reach, reach).astype(held_as)


def setup_inputs(seed: int = 0) -> dict:
    seeds = jax.random.split(jax.random.key(seed), 6)
    return {
        "wave_field": draw_wave_field(jax.random.fold_in(seeds[5], 71), 0),
        "cotangent": bell_draw(seeds[1], (FRAMES, TOKENS_F, D), 1.0, 6.0, ((0, 4), (1, 8))),
        "block_lists": draw_block_lists(jax.random.fold_in(seeds[5], 71), 0),
        "project_weights": draw_project_weights(jax.random.fold_in(seeds[5], 71), 0),
        "combine_weights": bell_draw(seeds[4], (2, D, D), D ** -0.5, 0.375),
    }


epsilon = 1e-05

def layer_norm(tok_rows):
    widened = tok_rows.astype(jnp.float32)
    centered = widened - lax.optimization_barrier(jnp.mean(widened, axis=-1, keepdims=True))
    inverse = lax.rsqrt(lax.optimization_barrier(jnp.mean(centered * centered, axis=-1, keepdims=True)) + epsilon)
    return (centered * inverse, inverse)

def norm_backward(upstream, normed, inverse):
    mean_grad = lax.optimization_barrier(jnp.mean(upstream, axis=-1, keepdims=True))
    mean_cross = lax.optimization_barrier(jnp.mean(upstream * normed, axis=-1, keepdims=True))
    return inverse * (upstream - mean_grad - normed * mean_cross)

def matmul(left_op, right_op):
    return jnp.dot(left_op, right_op, preferred_element_type=jnp.float32)

def wide_dot(left_op, right_op):
    return jnp.dot(left_op.astype(jnp.float32), right_op.astype(jnp.float32), precision=lax.Precision.HIGHEST)

def to_wide(values_in):
    return values_in.astype(jnp.float32)

def rounded_wide(values_in):
    return to_wide(lax.optimization_barrier(values_in.astype(jnp.bfloat16)))

def softmax_rows(scores, reduce_axis):
    row_max = lax.optimization_barrier(jnp.max(scores, axis=reduce_axis, keepdims=True))
    exp_scores = jnp.exp(scores - row_max)
    return lax.optimization_barrier((exp_scores / lax.optimization_barrier(jnp.sum(exp_scores, axis=reduce_axis, keepdims=True))).astype(jnp.bfloat16))

def spatial_forward(tok_rows, key_lists, project, combine, score_scale):
    tokens, features = tok_rows.shape
    head_width = features // HEADS
    normed, inverse = layer_norm(tok_rows)
    normed_act = normed.astype(jnp.bfloat16)
    projected = matmul(normed_act, project).astype(jnp.bfloat16)
    blocks = projected.reshape(tokens // BLOCK, BLOCK, 3, HEADS, head_width)

    def one_block(element):
        query_block, key_list = element
        picked = blocks[key_list].reshape(KB * BLOCK, 3, HEADS, head_width)
        scores = jnp.einsum('qhe,khe->hqk', to_wide(query_block[:, 0]), to_wide(picked[:, 1])) * score_scale
        attn_probs = softmax_rows(scores, 2)
        return jnp.einsum('hqk,khe->qhe', to_wide(attn_probs), to_wide(picked[:, 2])).astype(jnp.bfloat16)
    attended = lax.map(one_block, (blocks, key_lists)).reshape(tokens, features)
    mixed = (to_wide(tok_rows) + matmul(attended, combine)).astype(jnp.bfloat16)
    return (mixed, attended, normed, inverse, normed_act, blocks)

def spatial_backward(tok_rows, key_lists, mixed_grad, project, combine, score_scale):
    tokens, features = tok_rows.shape
    head_width = features // HEADS
    block_count = tokens // BLOCK
    mixed, attended, normed, inverse, normed_act, blocks = spatial_forward(tok_rows, key_lists, project, combine, score_scale)
    outward = matmul(attended.T, mixed_grad)
    attn_grad = matmul(mixed_grad, combine.T).astype(jnp.bfloat16).reshape(block_count, BLOCK, HEADS, head_width)

    def one_block(element):
        query_block, key_list, block_grad = element
        picked = blocks[key_list].reshape(KB * BLOCK, 3, HEADS, head_width)
        queries = to_wide(query_block[:, 0])
        key_part = to_wide(picked[:, 1])
        value_part = to_wide(picked[:, 2])
        prob_wide = to_wide(softmax_rows(jnp.einsum('qhe,khe->hqk', queries, key_part) * score_scale, 2))
        grad_wide = to_wide(block_grad)
        grad_probs = jnp.einsum('qhe,khe->hqk', grad_wide, value_part)
        row_delta = lax.optimization_barrier(jnp.sum(prob_wide * grad_probs, axis=2, keepdims=True))
        grad_scores = rounded_wide(prob_wide * (grad_probs - row_delta) * score_scale)
        grad_query = jnp.einsum('hqk,khe->qhe', grad_scores, key_part).astype(jnp.bfloat16)
        grad_keys = jnp.einsum('hqk,qhe->khe', grad_scores, queries)
        grad_values = jnp.einsum('hqk,qhe->khe', prob_wide, grad_wide)
        key_tiles = jnp.stack([grad_keys, grad_values], axis=1).reshape(KB, BLOCK * 2 * features)
        return (grad_query, key_tiles)
    grad_query, key_tiles = lax.map(one_block, (blocks, key_lists, attn_grad))
    summed = jax.ops.segment_sum(key_tiles.reshape(block_count * KB, BLOCK * 2 * features), key_lists.reshape(-1).astype(jnp.int32), num_segments=block_count)
    pair_flat = summed.reshape(tokens, 2 * features)
    query_flat = grad_query.reshape(tokens, features)
    inward = jnp.concatenate([matmul(normed_act.T, query_flat), wide_dot(normed_act.T, pair_flat)], axis=1)
    act_grad = matmul(query_flat, project[:, :features].T) + wide_dot(pair_flat, project[:, features:].T)
    field_rows = (to_wide(mixed_grad) + norm_backward(act_grad, normed, inverse)).astype(jnp.bfloat16)
    return (field_rows, inward, outward)

def temporal_pair(tok_rows, cot_rows, project, combine, score_scale):
    frame_count, row_count, features = tok_rows.shape
    head_width = features // HEADS
    normed, inverse = layer_norm(tok_rows)
    normed_act = normed.astype(jnp.bfloat16).reshape(frame_count * row_count, features)
    projected = matmul(normed_act, project).astype(jnp.bfloat16).reshape(frame_count, row_count, 3, HEADS, head_width)
    queries = to_wide(projected[:, :, 0])
    key_part = to_wide(projected[:, :, 1])
    value_part = to_wide(projected[:, :, 2])
    prob_wide = to_wide(softmax_rows(jnp.einsum('frhe,grhe->hfgr', queries, key_part) * score_scale, 2))
    attended = jnp.einsum('hfgr,grhe->frhe', prob_wide, value_part).astype(jnp.bfloat16).reshape(frame_count * row_count, features)
    mixed = (to_wide(tok_rows) + matmul(attended, combine).reshape(frame_count, row_count, features)).astype(jnp.bfloat16)
    flat_cot = cot_rows.reshape(frame_count * row_count, features)
    outward = matmul(attended.T, flat_cot)
    attn_grad = rounded_wide(matmul(flat_cot, combine.T)).reshape(frame_count, row_count, HEADS, head_width)
    grad_probs = jnp.einsum('frhe,grhe->hfgr', attn_grad, value_part)
    row_delta = lax.optimization_barrier(jnp.sum(prob_wide * grad_probs, axis=2, keepdims=True))
    grad_scores = rounded_wide(prob_wide * (grad_probs - row_delta) * score_scale)
    grad_query = jnp.einsum('hfgr,grhe->frhe', grad_scores, key_part)
    grad_keys = jnp.einsum('hfgr,frhe->grhe', grad_scores, queries)
    grad_values = jnp.einsum('hfgr,frhe->grhe', prob_wide, attn_grad)
    project_rows = jnp.stack([grad_query, grad_keys, grad_values], axis=2).astype(jnp.bfloat16).reshape(frame_count * row_count, 3 * features)
    inward = matmul(normed_act.T, project_rows)
    act_grad = matmul(project_rows, project.T).reshape(frame_count, row_count, features)
    field_rows = (to_wide(cot_rows) + norm_backward(act_grad, normed, inverse)).astype(jnp.bfloat16)
    return (mixed, field_rows, inward, outward)

def reference(wave_field, cotangent, block_lists, project_weights, combine_weights):
    frame_count, tokens, features = wave_field.shape
    score_scale = 1.0 / math.sqrt(features // HEADS)

    def forward_frame(element):
        return spatial_forward(element[0], element[1], project_weights[0], combine_weights[0], score_scale)[0]
    mixed_space = lax.map(forward_frame, (wave_field, block_lists))
    pieces = tokens // ROWS_DEV
    space_pieces = mixed_space.reshape(frame_count, pieces, ROWS_DEV, features).transpose(1, 0, 2, 3)
    cot_pieces = cotangent.reshape(frame_count, pieces, ROWS_DEV, features).transpose(1, 0, 2, 3)

    def time_step(running, element):
        mixed, field_rows, inward, outward = temporal_pair(element[0], element[1], project_weights[1], combine_weights[1], score_scale)
        return ((running[0] + inward, running[1] + outward), (mixed, field_rows))
    zero_grads = (jnp.zeros((features, 3 * features), jnp.float32), jnp.zeros((features, features), jnp.float32))
    (time_inward, time_outward), (mixed_pieces, grad_pieces) = lax.scan(time_step, zero_grads, (space_pieces, cot_pieces))
    mixed_field = mixed_pieces.transpose(1, 0, 2, 3).reshape(frame_count, tokens, features)
    mixed_grad = grad_pieces.transpose(1, 0, 2, 3).reshape(frame_count, tokens, features)

    def space_step(running, element):
        field_rows, inward, outward = spatial_backward(element[0], element[1], element[2], project_weights[0], combine_weights[0], score_scale)
        return ((running[0] + inward, running[1] + outward), field_rows)
    (space_inward, space_outward), field_grad = lax.scan(space_step, zero_grads, (wave_field, block_lists, mixed_grad))
    factor = 1.0 / math.sqrt(frame_count * tokens)
    project_grad = jnp.stack([space_inward, time_inward]) * factor
    combine_grad = jnp.stack([space_outward, time_outward]) * factor
    return (mixed_field, field_grad, project_grad, combine_grad)
```

```python
import math

import jax
import jax.numpy as jnp
from jax import lax
from jax.experimental import pallas as pl
from jax.experimental.pallas import tpu as pltpu
from jax.sharding import PartitionSpec as P

HEADS = 8
BLOCK = 128
HREACH = 2
LANES = 128
GROUP_ROWS = 16
VMEM_BYTES = 48 * 1024 * 1024
BF16 = jnp.bfloat16
F32 = jnp.float32


epsilon = 1e-05


def dot_nn(left, right):
    return lax.dot_general(left, right, (((1,), (0,)), ((), ())), preferred_element_type=F32)


def dot_nt(left, right):
    return lax.dot_general(left, right, (((1,), (1,)), ((), ())), preferred_element_type=F32)


def dot_tn(left, right):
    return lax.dot_general(left, right, (((0,), (0,)), ((), ())), preferred_element_type=F32)


def layer_norm(rows):
    widened = rows.astype(F32)
    centered = widened - jnp.mean(widened, axis=-1, keepdims=True)
    inverse = lax.rsqrt(jnp.mean(centered * centered, axis=-1, keepdims=True) + epsilon)
    return (centered * inverse, inverse)


def norm_backward(upstream, normed, inverse):
    mean_grad = jnp.mean(upstream, axis=-1, keepdims=True)
    mean_cross = jnp.mean(upstream * normed, axis=-1, keepdims=True)
    return inverse * (upstream - mean_grad - normed * mean_cross)


def flip(matrix):
    return matrix.astype(F32).T.astype(BF16)


def pair_columns(rows_t, pair, width):
    count = rows_t.shape[1]
    base = (pair * 2 * width) // LANES * LANES
    parts = []
    for head in (2 * pair, 2 * pair + 1):
        start = head * width - base
        pieces = []
        if start:
            pieces.append(jnp.zeros((start, count), rows_t.dtype))
        pieces.append(rows_t[head * width : (head + 1) * width])
        if start + width < LANES:
            pieces.append(jnp.zeros((LANES - start - width, count), rows_t.dtype))
        parts.append(jnp.concatenate(pieces, axis=0))
    return jnp.concatenate(parts, axis=1)


def pair_group(matrix, pair, width):
    base = (pair * 2 * width) // LANES * LANES
    return matrix[:, base : base + LANES]


def pair_diagonal(product, width):
    count = product.shape[1] // 2
    return jnp.concatenate([product[:width, :count], product[width:, count:]], axis=0)


def head_rows(rows, width):
    column = lax.broadcasted_iota(jnp.int32, (1, rows.shape[1]), 1) // width
    return jnp.concatenate(
        [rows * (column == head).astype(F32).astype(BF16) for head in range(HEADS)], axis=0
    )


def head_spread(per_head, width):
    return jnp.concatenate(
        [
            jnp.broadcast_to(per_head[head : head + 1], (width, per_head.shape[1]))
            for head in range(HEADS)
        ],
        axis=0,
    )


def listed_blocks(lists_ref, frame, block):
    own = lists_ref[frame, block, 0]
    return [
        lists_ref[frame, block, entry] - own + (block + HREACH)
        for entry in range(lists_ref.shape[2])
    ]


def space_forward_kernel(
    lists_ref,
    left_ref,
    wave_ref,
    right_ref,
    project_ref,
    combine_ref,
    mixed_ref,
    act_ref,
    kv_ref,
    query_ref,
    probs_ref,
    inverse_sum_ref,
    attended_ref,
    values_t,
):
    frame = pl.program_id(0)
    row_count, features = wave_ref.shape[1:]
    width = features // HEADS
    block_count = row_count // BLOCK
    exponent_scale = math.log2(math.e) / math.sqrt(width)
    rows = jnp.concatenate([left_ref[0], wave_ref[0], right_ref[0]], axis=0)
    normed, _ = layer_norm(rows)
    act = normed.astype(BF16)
    act_ref[0] = act
    keys_values = dot_nn(act, project_ref[0, :, features:]).astype(BF16)
    kv_ref[0] = keys_values
    rim = left_ref.shape[1]
    queries = dot_nn(act[rim : rim + row_count], project_ref[0, :, :features]).astype(BF16)
    query_ref[0] = queries
    for place in range(block_count + 2 * HREACH):
        values_t[place] = flip(keys_values[place * BLOCK : (place + 1) * BLOCK, features:])
    for block in range(block_count):
        places = listed_blocks(lists_ref, frame, block)
        keys = jnp.concatenate(
            [kv_ref[0, pl.ds(place * BLOCK, BLOCK), :features] for place in places], axis=0
        )
        block_values_t = jnp.concatenate([values_t[place] for place in places], axis=1)
        query_t = flip(queries[block * BLOCK : (block + 1) * BLOCK])
        outs = []
        for pair in range(HEADS // 2):
            scores = dot_nn(pair_group(keys, pair, width), pair_columns(query_t, pair, width))
            top = jnp.max(scores, axis=0, keepdims=True)
            exp_scores = jnp.exp2((scores - top) * exponent_scale)
            inverse_sum = 1.0 / jnp.sum(exp_scores, axis=0, keepdims=True)
            probs = exp_scores.astype(BF16)
            probs_ref[0, block, :, pair * 2 * BLOCK : (pair + 1) * 2 * BLOCK] = probs
            inverse_sum_ref[0, block, 2 * pair : 2 * pair + 1] = inverse_sum[:, :BLOCK]
            inverse_sum_ref[0, block, 2 * pair + 1 : 2 * pair + 2] = inverse_sum[:, BLOCK:]
            out = dot_nn(block_values_t[pair * 2 * width : (pair + 1) * 2 * width], probs)
            outs.append(pair_diagonal(out * inverse_sum, width))
        attended_t = jnp.concatenate(outs, axis=0)
        attended_ref[0, block] = attended_t.astype(BF16)
        attended = attended_t.T.astype(BF16)
        mixed = (
            wave_ref[0, block * BLOCK : (block + 1) * BLOCK].astype(F32)
            + dot_nn(attended, combine_ref[0])
        ).astype(BF16)
        sent_rows = mixed_ref.shape[2]
        for part in range(max(1, BLOCK // sent_rows)):
            mixed_ref[(block * BLOCK) // sent_rows + part, 0] = mixed[
                part * sent_rows : (part + 1) * sent_rows
            ]


def time_kernel(
    scale,
    factor,
    history_ref,
    cot_ref,
    project_ref,
    combine_ref,
    both_ref,
    grads_ref,
    proj_s,
    dattn_s,
    attended_s,
    dproj_s,
):
    frames, row_count, features = history_ref.shape
    width = features // HEADS
    tokens = frames * row_count
    exponent_scale = scale * math.log2(math.e)
    rows = history_ref[...].reshape(tokens, features)
    normed, inverse = layer_norm(rows)
    act = normed.astype(BF16)
    proj_s[...] = dot_nn(act, project_ref[0]).astype(BF16).reshape(proj_s.shape)
    cot = cot_ref[...].reshape(tokens, features)
    dattn_s[...] = dot_nt(cot, combine_ref[0]).astype(BF16).reshape(dattn_s.shape)
    count = frames * GROUP_ROWS
    key_row = lax.broadcasted_iota(jnp.int32, (count, 2 * count), 0) % GROUP_ROWS
    query_row = lax.broadcasted_iota(jnp.int32, (count, 2 * count), 1) % GROUP_ROWS
    same_row = key_row == query_row
    for group in range(row_count // GROUP_ROWS):
        span = slice(group * GROUP_ROWS, (group + 1) * GROUP_ROWS)
        queries = proj_s[:, span, :features].reshape(count, features)
        keys = proj_s[:, span, features : 2 * features].reshape(count, features)
        values = proj_s[:, span, 2 * features :].reshape(count, features)
        dattn = dattn_s[:, span].reshape(count, features)
        query_t, keys_t, values_t, dattn_t = flip(queries), flip(keys), flip(values), flip(dattn)
        outs, probs_parts, dscore_parts, dquery_parts = [], [], [], []
        for pair in range(HEADS // 2):
            heads = slice(pair * 2 * width, (pair + 1) * 2 * width)
            scores = dot_nn(pair_group(keys, pair, width), pair_columns(query_t, pair, width))
            scores = jnp.where(same_row, scores, -3e38)
            top = jnp.max(scores, axis=0, keepdims=True)
            exp_scores = jnp.exp2((scores - top) * exponent_scale)
            probs = (exp_scores * (1.0 / jnp.sum(exp_scores, axis=0, keepdims=True))).astype(BF16)
            probs_wide = probs.astype(F32)
            outs.append(pair_diagonal(dot_nn(values_t[heads], probs), width))
            dprobs = dot_nn(pair_group(values, pair, width), pair_columns(dattn_t, pair, width))
            delta = jnp.sum(probs_wide * dprobs, axis=0, keepdims=True)
            dscores = (probs_wide * (dprobs - delta) * scale).astype(BF16)
            dquery_parts.append(pair_diagonal(dot_nn(keys_t[heads], dscores), width))
            probs_parts.append(probs)
            dscore_parts.append(dscores)
        attended_s[:, span] = (
            jnp.concatenate(outs, axis=0).T.astype(BF16).reshape(frames, GROUP_ROWS, features)
        )
        dquery = jnp.concatenate(dquery_parts, axis=0).T
        dkeys = dot_nn(jnp.concatenate(dscore_parts, axis=1), head_rows(queries, width))
        dvalues = dot_nn(jnp.concatenate(probs_parts, axis=1), head_rows(dattn, width))
        dproj = jnp.concatenate([dquery, dkeys, dvalues], axis=1).astype(BF16)
        dproj_s[:, span] = dproj.reshape(frames, GROUP_ROWS, 3 * features)
    attended = attended_s[...].reshape(tokens, features)
    mixed = (rows.astype(F32) + dot_nn(attended, combine_ref[0])).astype(BF16)
    both_ref[:, :, :features] = mixed.reshape(frames, row_count, features)
    dproj = dproj_s[...].reshape(tokens, 3 * features)
    dact = dot_nt(dproj, project_ref[0])
    mixed_grad = (cot.astype(F32) + norm_backward(dact, normed, inverse)).astype(BF16)
    both_ref[:, :, features:] = mixed_grad.reshape(frames, row_count, features)
    grads_ref[:, : 3 * features] = (dot_tn(act, dproj) * factor).astype(BF16)
    grads_ref[:, 3 * features :] = (dot_tn(attended, cot) * factor).astype(BF16)


def space_backward_kernel(
    scale,
    factor,
    lists_ref,
    mixed_in_ref,
    grad_in_ref,
    act_ref,
    kv_ref,
    query_ref,
    probs_ref,
    inverse_sum_ref,
    attended_ref,
    project_ref,
    combine_ref,
    mixed_out_ref,
    dact_ref,
    to_left_ref,
    to_right_ref,
    grads_ref,
    keys_t,
    dscores_s,
    dkv_s,
    grads_s,
):
    frame = pl.program_id(0)
    row_count, features = mixed_out_ref.shape[1:]
    width = features // HEADS
    block_count = row_count // BLOCK
    rim = HREACH * BLOCK
    mixed_out_ref[0] = mixed_in_ref[:, 0].reshape(row_count, features)
    mixed_grad = grad_in_ref[:, 0].reshape(row_count, features)
    for place in range(block_count + 2 * HREACH):
        keys_t[place] = flip(kv_ref[0, place * BLOCK : (place + 1) * BLOCK, :features])
    dkv_s[...] = jnp.zeros(dkv_s.shape, F32)

    @pl.when(frame == 0)
    def _():
        grads_s[...] = jnp.zeros(grads_s.shape, F32)

    dquery_blocks = []
    for block in range(block_count):
        span = slice(block * BLOCK, (block + 1) * BLOCK)
        places = listed_blocks(lists_ref, frame, block)
        values = jnp.concatenate(
            [kv_ref[0, pl.ds(place * BLOCK, BLOCK), features:] for place in places], axis=0
        )
        block_keys_t = jnp.concatenate([keys_t[place] for place in places], axis=1)
        block_grad = mixed_grad[span]
        attended_t = attended_ref[0, block]
        grads_s[:, 3 * features :] += dot_nn(attended_t, block_grad)
        dattn_t = dot_nt(combine_ref[0], block_grad).astype(BF16)
        dattn_wide = dattn_t.astype(F32)
        inverse_sum = inverse_sum_ref[0, block]
        scaled_dattn = (dattn_wide * head_spread(inverse_sum, width)).T.astype(BF16)
        delta = jnp.sum(
            (dattn_wide * attended_t.astype(F32)).reshape(HEADS, width, BLOCK), axis=1
        )
        row_scale = inverse_sum * scale
        dquery_parts = []
        for pair in range(HEADS // 2):
            heads = slice(pair * 2 * width, (pair + 1) * 2 * width)
            columns = slice(pair * 2 * BLOCK, (pair + 1) * 2 * BLOCK)
            pair_delta = jnp.concatenate(
                [delta[2 * pair : 2 * pair + 1], delta[2 * pair + 1 : 2 * pair + 2]], axis=1
            )
            pair_scale = jnp.concatenate(
                [row_scale[2 * pair : 2 * pair + 1], row_scale[2 * pair + 1 : 2 * pair + 2]], axis=1
            )
            dprobs = dot_nn(pair_group(values, pair, width), pair_columns(dattn_t, pair, width))
            probs = probs_ref[0, block, :, columns].astype(F32)
            dscores = (probs * ((dprobs - pair_delta) * pair_scale)).astype(BF16)
            dscores_s[:, columns] = dscores
            dquery_parts.append(pair_diagonal(dot_nn(block_keys_t[heads], dscores), width))
        dquery_blocks.append(jnp.concatenate(dquery_parts, axis=0).T.astype(BF16))
        dkeys = dot_nn(dscores_s[...], head_rows(query_ref[0, span], width))
        dvalues = dot_nn(probs_ref[0, block], head_rows(scaled_dattn, width))
        for entry, place in enumerate(places):
            rows = pl.ds(place * BLOCK, BLOCK)
            listed = slice(entry * BLOCK, (entry + 1) * BLOCK)
            dkv_s[rows, :features] += dkeys[listed]
            dkv_s[rows, features:] += dvalues[listed]
    dquery = jnp.concatenate(dquery_blocks, axis=0)
    dkv = dkv_s[...].astype(BF16)
    grads_s[:, :features] += dot_tn(act_ref[0, rim : rim + row_count], dquery)
    grads_s[:, features : 3 * features] += dot_tn(act_ref[0], dkv)
    dact = dot_nt(dkv, project_ref[0, :, features:])
    to_left_ref[0] = dact[:rim].astype(BF16)
    to_right_ref[0] = dact[rim + row_count :].astype(BF16)
    dact_ref[0] = dact[rim : rim + row_count] + dot_nt(dquery, project_ref[0, :, :features])

    @pl.when(frame == pl.num_programs(0) - 1)
    def _():
        for group in range(4 * features // LANES):
            grads_ref[group * features : (group + 1) * features] = (
                grads_s[:, group * LANES : (group + 1) * LANES] * factor
            ).astype(BF16)


def field_kernel(wave_ref, grad_in_ref, dact_ref, from_left_ref, from_right_ref, field_ref):
    row_count, features = wave_ref.shape[1:]
    normed, inverse = layer_norm(wave_ref[0])
    mixed_grad = grad_in_ref[:, 0].reshape(row_count, features).astype(F32)
    dact = dact_ref[0] + from_left_ref[0].astype(F32) + from_right_ref[0].astype(F32)
    field_ref[0] = (mixed_grad + norm_backward(dact, normed, inverse)).astype(BF16)


def grads_kernel(space_ref, time_ref, project_ref, combine_ref):
    features = combine_ref.shape[1]
    for group in range(4 * features // LANES):
        piece = space_ref[group * features : (group + 1) * features].astype(F32)
        start = group * LANES
        if start < 3 * features:
            project_ref[0, :, start : start + LANES] = piece
        else:
            combine_ref[0, :, start - 3 * features : start - 3 * features + LANES] = piece
    project_ref[1] = time_ref[:, : 3 * features].astype(F32)
    combine_ref[1] = time_ref[:, 3 * features :].astype(F32)


def shift(cells, axis, step):
    count = lax.axis_size(axis)
    if step > 0:
        moves = [(i, i + 1) for i in range(count - 1)]
    else:
        moves = [(i + 1, i) for i in range(count - 1)]
    return lax.ppermute(cells, axis, moves)


def swap(parts, axis):
    return lax.all_to_all(parts, axis, split_axis=0, concat_axis=0, tiled=True)


def sum_scattered(cells, axis):
    count = lax.axis_size(axis)
    arrived = swap(cells, axis).reshape(count, cells.shape[0] // count, cells.shape[1])
    return jnp.sum(arrived.astype(F32), axis=0).astype(cells.dtype)


def gathered(cells, axis):
    count = lax.axis_size(axis)
    return swap(jnp.broadcast_to(cells[None], (count, *cells.shape)), axis).reshape(
        count * cells.shape[0], cells.shape[1]
    )


def per_device(wave_field, cotangent, block_lists, project_weights, combine_weights):
    frame_count, row_count, features = wave_field.shape
    width = features // HEADS
    scale = 1.0 / math.sqrt(width)
    block_count = row_count // BLOCK
    list_length = block_lists.shape[-1]
    rim = HREACH * BLOCK
    extended = row_count + 2 * rim
    keys_count = list_length * BLOCK
    time_count = lax.axis_size("tm")
    all_frames = frame_count * time_count
    sent_rows = row_count // time_count
    factor = 1.0 / math.sqrt(frame_count * row_count * time_count * lax.axis_size("space"))
    params = pltpu.CompilerParams(vmem_limit_bytes=VMEM_BYTES)

    def whole(*shape):
        return pl.BlockSpec(shape, lambda f: (0,) * len(shape))

    def framed(*shape):
        return pl.BlockSpec((1, *shape), lambda f: (f,) + (0,) * len(shape))

    def parted(lane_block):
        return pl.BlockSpec((time_count, 1, sent_rows, features), lambda f: (0, f, 0, lane_block))

    lists_spec = pl.BlockSpec(memory_space=pltpu.SMEM)
    project_spec = whole(1, features, 3 * features)
    combine_spec = whole(1, features, features)

    from_left = shift(wave_field[:, row_count - rim :], "space", 1)
    from_right = shift(wave_field[:, :rim], "space", -1)
    history_cot = lax.all_to_all(cotangent, "tm", split_axis=1, concat_axis=0, tiled=True)

    mixed_space, act, keys_values, queries, probs, inverse_sum, attended = pl.pallas_call(
        space_forward_kernel,
        grid=(frame_count,),
        in_specs=[
            lists_spec,
            framed(rim, features),
            framed(row_count, features),
            framed(rim, features),
            project_spec,
            combine_spec,
        ],
        out_specs=[
            parted(0),
            framed(extended, features),
            framed(extended, 2 * features),
            framed(row_count, features),
            framed(block_count, keys_count, HEADS * BLOCK),
            framed(block_count, HEADS, BLOCK),
            framed(block_count, features, BLOCK),
        ],
        out_shape=[
            jax.ShapeDtypeStruct((time_count, frame_count, sent_rows, features), BF16),
            jax.ShapeDtypeStruct((frame_count, extended, features), BF16),
            jax.ShapeDtypeStruct((frame_count, extended, 2 * features), BF16),
            jax.ShapeDtypeStruct((frame_count, row_count, features), BF16),
            jax.ShapeDtypeStruct((frame_count, block_count, keys_count, HEADS * BLOCK), BF16),
            jax.ShapeDtypeStruct((frame_count, block_count, HEADS, BLOCK), F32),
            jax.ShapeDtypeStruct((frame_count, block_count, features, BLOCK), BF16),
        ],
        scratch_shapes=[pltpu.VMEM((block_count + 2 * HREACH, features, BLOCK), BF16)],
        compiler_params=params,
        name="space_forward",
    )(block_lists, from_left, wave_field, from_right, project_weights, combine_weights)

    history = swap(mixed_space, "tm").reshape(all_frames, sent_rows, features)

    def time_body(*refs):
        time_kernel(scale, factor, *refs)

    both, time_grads = pl.pallas_call(
        time_body,
        grid=(1,),
        in_specs=[
            whole(all_frames, sent_rows, features),
            whole(all_frames, sent_rows, features),
            pl.BlockSpec((1, features, 3 * features), lambda f: (1, 0, 0)),
            pl.BlockSpec((1, features, features), lambda f: (1, 0, 0)),
        ],
        out_specs=[whole(all_frames, sent_rows, 2 * features), whole(features, 4 * features)],
        out_shape=[
            jax.ShapeDtypeStruct((all_frames, sent_rows, 2 * features), BF16),
            jax.ShapeDtypeStruct((features, 4 * features), BF16),
        ],
        scratch_shapes=[
            pltpu.VMEM((all_frames, sent_rows, 3 * features), BF16),
            pltpu.VMEM((all_frames, sent_rows, features), BF16),
            pltpu.VMEM((all_frames, sent_rows, features), BF16),
            pltpu.VMEM((all_frames, sent_rows, 3 * features), BF16),
        ],
        compiler_params=params,
        name="time_pair",
    )(history, history_cot, project_weights, combine_weights)

    returned = swap(both.reshape(time_count, frame_count, sent_rows, 2 * features), "tm")
    time_sum = lax.psum(time_grads, ("tm", "space"))

    def backward_body(*refs):
        space_backward_kernel(scale, factor, *refs)

    mixed_field, dact, to_left, to_right, space_grads = pl.pallas_call(
        backward_body,
        grid=(frame_count,),
        in_specs=[
            lists_spec,
            parted(0),
            parted(1),
            framed(extended, features),
            framed(extended, 2 * features),
            framed(row_count, features),
            framed(block_count, keys_count, HEADS * BLOCK),
            framed(block_count, HEADS, BLOCK),
            framed(block_count, features, BLOCK),
            project_spec,
            combine_spec,
        ],
        out_specs=[
            framed(row_count, features),
            framed(row_count, features),
            framed(rim, features),
            framed(rim, features),
            whole(4 * features // LANES * features, LANES),
        ],
        out_shape=[
            jax.ShapeDtypeStruct((frame_count, row_count, features), BF16),
            jax.ShapeDtypeStruct((frame_count, row_count, features), F32),
            jax.ShapeDtypeStruct((frame_count, rim, features), BF16),
            jax.ShapeDtypeStruct((frame_count, rim, features), BF16),
            jax.ShapeDtypeStruct((4 * features // LANES * features, LANES), BF16),
        ],
        scratch_shapes=[
            pltpu.VMEM((block_count + 2 * HREACH, features, BLOCK), BF16),
            pltpu.VMEM((keys_count, HEADS * BLOCK), BF16),
            pltpu.VMEM((extended, 2 * features), F32),
            pltpu.VMEM((features, 4 * features), F32),
        ],
        compiler_params=params,
        name="space_backward",
    )(
        block_lists,
        returned,
        returned,
        act,
        keys_values,
        queries,
        probs,
        inverse_sum,
        attended,
        project_weights,
        combine_weights,
    )

    edge_left = shift(to_right, "space", 1)
    edge_right = shift(to_left, "space", -1)
    space_sum = sum_scattered(sum_scattered(space_grads, "tm"), "space")
    space_sum = gathered(gathered(space_sum, "space"), "tm")

    field_grad = pl.pallas_call(
        field_kernel,
        grid=(frame_count,),
        in_specs=[
            framed(row_count, features),
            parted(1),
            framed(row_count, features),
            framed(row_count, features),
            framed(row_count, features),
        ],
        out_specs=framed(row_count, features),
        out_shape=jax.ShapeDtypeStruct((frame_count, row_count, features), BF16),
        compiler_params=params,
        name="field_grad",
    )(wave_field, returned, dact, edge_left, edge_right)

    project_grad, combine_grad = pl.pallas_call(
        grads_kernel,
        out_shape=[
            jax.ShapeDtypeStruct((2, features, 3 * features), F32),
            jax.ShapeDtypeStruct((2, features, features), F32),
        ],
        compiler_params=params,
        name="weight_grads",
    )(space_sum, time_sum)
    return (mixed_field, field_grad, project_grad, combine_grad)


def solution(mesh):
    in_specs = (P("tm", "space", None), P("tm", "space", None), P("tm", "space", None), P(), P())
    out_specs = (P("tm", "space", None), P("tm", "space", None), P(), P())
    return jax.shard_map(
        per_device, mesh=mesh, in_specs=in_specs, out_specs=out_specs, check_vma=False
    )
```

```python
import math

import jax
import jax.numpy as jnp
from jax import lax
from jax.experimental import pallas as pl
from jax.experimental.pallas import tpu as pltpu
from jax.sharding import PartitionSpec as P

HEADS = 8
BLOCK = 128
HREACH = 2
LANES = 128
GROUP_ROWS = 16
VMEM_BYTES = 48 * 1024 * 1024
BF16 = jnp.bfloat16
F32 = jnp.float32


epsilon = 1e-05


def dot_nn(left, right):
    return lax.dot_general(left, right, (((1,), (0,)), ((), ())), preferred_element_type=F32)


def dot_nt(left, right):
    return lax.dot_general(left, right, (((1,), (1,)), ((), ())), preferred_element_type=F32)


def dot_tn(left, right):
    return lax.dot_general(left, right, (((0,), (0,)), ((), ())), preferred_element_type=F32)


def layer_norm(rows):
    widened = rows.astype(F32)
    centered = widened - jnp.mean(widened, axis=-1, keepdims=True)
    inverse = lax.rsqrt(jnp.mean(centered * centered, axis=-1, keepdims=True) + epsilon)
    return (centered * inverse, inverse)


def norm_backward(upstream, normed, inverse):
    mean_grad = jnp.mean(upstream, axis=-1, keepdims=True)
    mean_cross = jnp.mean(upstream * normed, axis=-1, keepdims=True)
    return inverse * (upstream - mean_grad - normed * mean_cross)


def flip(matrix):
    return matrix.astype(F32).T.astype(BF16)


def pair_columns(rows_t, pair, width):
    count = rows_t.shape[1]
    base = (pair * 2 * width) // LANES * LANES
    parts = []
    for head in (2 * pair, 2 * pair + 1):
        start = head * width - base
        pieces = []
        if start:
            pieces.append(jnp.zeros((start, count), rows_t.dtype))
        pieces.append(rows_t[head * width : (head + 1) * width])
        if start + width < LANES:
            pieces.append(jnp.zeros((LANES - start - width, count), rows_t.dtype))
        parts.append(jnp.concatenate(pieces, axis=0))
    return jnp.concatenate(parts, axis=1)


def pair_group(matrix, pair, width):
    base = (pair * 2 * width) // LANES * LANES
    return matrix[:, base : base + LANES]


def pair_diagonal(product, width):
    count = product.shape[1] // 2
    return jnp.concatenate([product[:width, :count], product[width:, count:]], axis=0)


def head_rows(rows, width):
    column = lax.broadcasted_iota(jnp.int32, (1, rows.shape[1]), 1) // width
    return jnp.concatenate(
        [rows * (column == head).astype(F32).astype(BF16) for head in range(HEADS)], axis=0
    )


def head_spread(per_head, width):
    return jnp.concatenate(
        [
            jnp.broadcast_to(per_head[head : head + 1], (width, per_head.shape[1]))
            for head in range(HEADS)
        ],
        axis=0,
    )


def listed_blocks(lists_ref, frame, block):
    own = lists_ref[frame, block, 0]
    return [
        lists_ref[frame, block, entry] - own + (block + HREACH)
        for entry in range(lists_ref.shape[2])
    ]


def space_forward_kernel(
    lists_ref,
    place_ref,
    left_ref,
    wave_ref,
    right_ref,
    cot_ref,
    project_ref,
    combine_ref,
    act_ref,
    kv_ref,
    query_ref,
    probs_ref,
    inverse_sum_ref,
    attended_ref,
    *rest,
):
    *sent_refs, values_t, mixed_s = rest
    frame = pl.program_id(0)
    me = place_ref[0]
    row_count, features = wave_ref.shape[1:]
    width = features // HEADS
    block_count = row_count // BLOCK
    exponent_scale = math.log2(math.e) / math.sqrt(width)
    rows = jnp.concatenate([left_ref[0], wave_ref[0], right_ref[0]], axis=0)
    normed, _ = layer_norm(rows)
    act = normed.astype(BF16)
    act_ref[0] = act
    keys_values = dot_nn(act, project_ref[0, :, features:]).astype(BF16)
    kv_ref[0] = keys_values
    rim = left_ref.shape[1]
    queries = dot_nn(act[rim : rim + row_count], project_ref[0, :, :features]).astype(BF16)
    query_ref[0] = queries
    for place in range(block_count + 2 * HREACH):
        values_t[place] = flip(keys_values[place * BLOCK : (place + 1) * BLOCK, features:])
    for block in range(block_count):
        places = listed_blocks(lists_ref, frame, block)
        keys = jnp.concatenate(
            [kv_ref[0, pl.ds(place * BLOCK, BLOCK), :features] for place in places], axis=0
        )
        block_values_t = jnp.concatenate([values_t[place] for place in places], axis=1)
        query_t = flip(queries[block * BLOCK : (block + 1) * BLOCK])
        outs = []
        for pair in range(HEADS // 2):
            scores = dot_nn(pair_group(keys, pair, width), pair_columns(query_t, pair, width))
            top = jnp.max(scores, axis=0, keepdims=True)
            exp_scores = jnp.exp2((scores - top) * exponent_scale)
            inverse_sum = 1.0 / jnp.sum(exp_scores, axis=0, keepdims=True)
            probs = exp_scores.astype(BF16)
            probs_ref[0, block, :, pair * 2 * BLOCK : (pair + 1) * 2 * BLOCK] = probs
            inverse_sum_ref[0, block, 2 * pair : 2 * pair + 1] = inverse_sum[:, :BLOCK]
            inverse_sum_ref[0, block, 2 * pair + 1 : 2 * pair + 2] = inverse_sum[:, BLOCK:]
            out = dot_nn(block_values_t[pair * 2 * width : (pair + 1) * 2 * width], probs)
            outs.append(pair_diagonal(out * inverse_sum, width))
        attended_t = jnp.concatenate(outs, axis=0)
        attended_ref[0, block] = attended_t.astype(BF16)
        attended = attended_t.T.astype(BF16)
        mixed = (
            wave_ref[0, block * BLOCK : (block + 1) * BLOCK].astype(F32)
            + dot_nn(attended, combine_ref[0])
        ).astype(BF16)
        mixed_s[block * BLOCK : (block + 1) * BLOCK] = mixed
    for distance, sent_ref in enumerate(sent_refs):
        sent_rows = sent_ref.shape[1]
        span = pl.ds(pl.multiple_of((me ^ distance) * sent_rows, GROUP_ROWS), sent_rows)
        sent_ref[0, :, :features] = mixed_s[span]
        sent_ref[0, :, features:] = cot_ref[0, span]


def time_kernel(
    scale,
    factor,
    count_in,
    *refs,
):
    arrived_refs = refs[:count_in]
    project_ref, combine_ref = refs[count_in : count_in + 2]
    returned_refs = refs[count_in + 2 : 2 * count_in + 2]
    grads_ref, proj_s, dattn_s, attended_s, dproj_s = refs[2 * count_in + 2 :]
    part_frames, row_count, features = arrived_refs[0].shape
    features //= 2
    frames = part_frames * count_in
    width = features // HEADS
    tokens = frames * row_count
    exponent_scale = scale * math.log2(math.e)
    part_tokens = part_frames * row_count
    rows = jnp.concatenate(
        [ref[:, :, :features].reshape(part_tokens, features) for ref in arrived_refs], axis=0
    )
    cot = jnp.concatenate(
        [ref[:, :, features:].reshape(part_tokens, features) for ref in arrived_refs], axis=0
    )
    normed, inverse = layer_norm(rows)
    act = normed.astype(BF16)
    proj_s[...] = dot_nn(act, project_ref[0]).astype(BF16).reshape(proj_s.shape)
    dattn_s[...] = dot_nt(cot, combine_ref[0]).astype(BF16).reshape(dattn_s.shape)
    count = frames * GROUP_ROWS
    key_row = lax.broadcasted_iota(jnp.int32, (count, 2 * count), 0) % GROUP_ROWS
    query_row = lax.broadcasted_iota(jnp.int32, (count, 2 * count), 1) % GROUP_ROWS
    same_row = key_row == query_row
    for group in range(row_count // GROUP_ROWS):
        span = slice(group * GROUP_ROWS, (group + 1) * GROUP_ROWS)
        queries = proj_s[:, span, :features].reshape(count, features)
        keys = proj_s[:, span, features : 2 * features].reshape(count, features)
        values = proj_s[:, span, 2 * features :].reshape(count, features)
        dattn = dattn_s[:, span].reshape(count, features)
        query_t, keys_t, values_t, dattn_t = flip(queries), flip(keys), flip(values), flip(dattn)
        outs, probs_parts, dscore_parts, dquery_parts = [], [], [], []
        for pair in range(HEADS // 2):
            heads = slice(pair * 2 * width, (pair + 1) * 2 * width)
            scores = dot_nn(pair_group(keys, pair, width), pair_columns(query_t, pair, width))
            scores = jnp.where(same_row, scores, -3e38)
            top = jnp.max(scores, axis=0, keepdims=True)
            exp_scores = jnp.exp2((scores - top) * exponent_scale)
            probs = (exp_scores * (1.0 / jnp.sum(exp_scores, axis=0, keepdims=True))).astype(BF16)
            probs_wide = probs.astype(F32)
            outs.append(pair_diagonal(dot_nn(values_t[heads], probs), width))
            dprobs = dot_nn(pair_group(values, pair, width), pair_columns(dattn_t, pair, width))
            delta = jnp.sum(probs_wide * dprobs, axis=0, keepdims=True)
            dscores = (probs_wide * (dprobs - delta) * scale).astype(BF16)
            dquery_parts.append(pair_diagonal(dot_nn(keys_t[heads], dscores), width))
            probs_parts.append(probs)
            dscore_parts.append(dscores)
        attended_s[:, span] = (
            jnp.concatenate(outs, axis=0).T.astype(BF16).reshape(frames, GROUP_ROWS, features)
        )
        dquery = jnp.concatenate(dquery_parts, axis=0).T
        dkeys = dot_nn(jnp.concatenate(dscore_parts, axis=1), head_rows(queries, width))
        dvalues = dot_nn(jnp.concatenate(probs_parts, axis=1), head_rows(dattn, width))
        dproj = jnp.concatenate([dquery, dkeys, dvalues], axis=1).astype(BF16)
        dproj_s[:, span] = dproj.reshape(frames, GROUP_ROWS, 3 * features)
    attended = attended_s[...].reshape(tokens, features)
    mixed = (rows.astype(F32) + dot_nn(attended, combine_ref[0])).astype(BF16)
    dproj = dproj_s[...].reshape(tokens, 3 * features)
    dact = dot_nt(dproj, project_ref[0])
    mixed_grad = (cot.astype(F32) + norm_backward(dact, normed, inverse)).astype(BF16)
    for part, ref in enumerate(returned_refs):
        span = slice(part * part_tokens, (part + 1) * part_tokens)
        ref[:, :, :features] = mixed[span].reshape(part_frames, row_count, features)
        ref[:, :, features:] = mixed_grad[span].reshape(part_frames, row_count, features)
    grads_ref[:, : 3 * features] = (dot_tn(act, dproj) * factor).astype(BF16)
    grads_ref[:, 3 * features :] = (dot_tn(attended, cot) * factor).astype(BF16)


def space_backward_kernel(
    scale,
    factor,
    count_in,
    lists_ref,
    place_ref,
    *refs,
):
    returned_refs = refs[:count_in]
    (
        act_ref,
        kv_ref,
        query_ref,
        probs_ref,
        inverse_sum_ref,
        attended_ref,
        project_ref,
        combine_ref,
        mixed_out_ref,
        mixed_grad_ref,
        dact_ref,
        to_left_ref,
        to_right_ref,
        kept_ref,
        sent_ref,
        keys_t,
        dscores_s,
        dkv_s,
        grads_s,
        rounded_s,
    ) = refs[count_in:]
    frame = pl.program_id(0)
    me = place_ref[0]
    core = place_ref[1] % 2
    row_count, features = mixed_out_ref.shape[1:]
    width = features // HEADS
    block_count = row_count // BLOCK
    rim = HREACH * BLOCK
    for distance, ref in enumerate(returned_refs):
        sent_rows = ref.shape[1]
        span = pl.ds(pl.multiple_of((me ^ distance) * sent_rows, GROUP_ROWS), sent_rows)
        mixed_out_ref[0, span] = ref[0, :, :features]
        mixed_grad_ref[0, span] = ref[0, :, features:]
    mixed_grad = mixed_grad_ref[0]
    for place in range(block_count + 2 * HREACH):
        keys_t[place] = flip(kv_ref[0, place * BLOCK : (place + 1) * BLOCK, :features])
    dkv_s[...] = jnp.zeros(dkv_s.shape, F32)

    @pl.when(frame == 0)
    def _():
        grads_s[...] = jnp.zeros(grads_s.shape, F32)

    dquery_blocks = []
    for block in range(block_count):
        span = slice(block * BLOCK, (block + 1) * BLOCK)
        places = listed_blocks(lists_ref, frame, block)
        values = jnp.concatenate(
            [kv_ref[0, pl.ds(place * BLOCK, BLOCK), features:] for place in places], axis=0
        )
        block_keys_t = jnp.concatenate([keys_t[place] for place in places], axis=1)
        block_grad = mixed_grad[span]
        attended_t = attended_ref[0, block]
        grads_s[:, 3 * features :] += dot_nn(attended_t, block_grad)
        dattn_t = dot_nt(combine_ref[0], block_grad).astype(BF16)
        dattn_wide = dattn_t.astype(F32)
        inverse_sum = inverse_sum_ref[0, block]
        scaled_dattn = (dattn_wide * head_spread(inverse_sum, width)).T.astype(BF16)
        delta = jnp.sum(
            (dattn_wide * attended_t.astype(F32)).reshape(HEADS, width, BLOCK), axis=1
        )
        row_scale = inverse_sum * scale
        dquery_parts = []
        for pair in range(HEADS // 2):
            heads = slice(pair * 2 * width, (pair + 1) * 2 * width)
            columns = slice(pair * 2 * BLOCK, (pair + 1) * 2 * BLOCK)
            pair_delta = jnp.concatenate(
                [delta[2 * pair : 2 * pair + 1], delta[2 * pair + 1 : 2 * pair + 2]], axis=1
            )
            pair_scale = jnp.concatenate(
                [row_scale[2 * pair : 2 * pair + 1], row_scale[2 * pair + 1 : 2 * pair + 2]], axis=1
            )
            dprobs = dot_nn(pair_group(values, pair, width), pair_columns(dattn_t, pair, width))
            probs = probs_ref[0, block, :, columns].astype(F32)
            dscores = (probs * ((dprobs - pair_delta) * pair_scale)).astype(BF16)
            dscores_s[:, columns] = dscores
            dquery_parts.append(pair_diagonal(dot_nn(block_keys_t[heads], dscores), width))
        dquery_blocks.append(jnp.concatenate(dquery_parts, axis=0).T.astype(BF16))
        dkeys = dot_nn(dscores_s[...], head_rows(query_ref[0, span], width))
        dvalues = dot_nn(probs_ref[0, block], head_rows(scaled_dattn, width))
        for entry, place in enumerate(places):
            rows = pl.ds(place * BLOCK, BLOCK)
            listed = slice(entry * BLOCK, (entry + 1) * BLOCK)
            dkv_s[rows, :features] += dkeys[listed]
            dkv_s[rows, features:] += dvalues[listed]
    dquery = jnp.concatenate(dquery_blocks, axis=0)
    dkv = dkv_s[...].astype(BF16)
    grads_s[:, :features] += dot_tn(act_ref[0, rim : rim + row_count], dquery)
    grads_s[:, features : 3 * features] += dot_tn(act_ref[0], dkv)
    dact = dot_nt(dkv, project_ref[0, :, features:])
    to_left_ref[0] = dact[:rim].astype(BF16)
    to_right_ref[0] = dact[rim + row_count :].astype(BF16)
    dact_ref[0] = dact[rim : rim + row_count] + dot_nt(dquery, project_ref[0, :, :features])

    @pl.when(frame == pl.num_programs(0) - 1)
    def _():
        for group in range(4 * features // LANES):
            rounded_s[group * features : (group + 1) * features] = (
                grads_s[:, group * LANES : (group + 1) * LANES] * factor
            ).astype(BF16)
        half = kept_ref.shape[0]
        kept_ref[...] = rounded_s[pl.ds(pl.multiple_of(core * half, GROUP_ROWS), half)]
        sent_ref[...] = rounded_s[pl.ds(pl.multiple_of((1 - core) * half, GROUP_ROWS), half)]


def field_kernel(wave_ref, mixed_grad_ref, dact_ref, from_left_ref, from_right_ref, field_ref):
    normed, inverse = layer_norm(wave_ref[0])
    dact = dact_ref[0] + from_left_ref[0].astype(F32) + from_right_ref[0].astype(F32)
    field_ref[0] = (
        mixed_grad_ref[0].astype(F32) + norm_backward(dact, normed, inverse)
    ).astype(BF16)


def split_kernel(place_ref, kept_ref, arrived_ref, *refs):
    *part_refs, sum_s = refs
    sum_s[...] = (kept_ref[...].astype(F32) + arrived_ref[...].astype(F32)).astype(BF16)
    for distance, ref in enumerate(part_refs):
        rows = ref.shape[0]
        ref[...] = sum_s[pl.ds(pl.multiple_of((place_ref[0] ^ distance) * rows, GROUP_ROWS), rows)]


def sum_kernel(axis, group, place_ref, *refs):
    *part_refs, total_ref, parts_s = refs
    me = place_ref[axis] // group
    for distance, ref in enumerate(part_refs):
        parts_s[me ^ distance] = ref[...]
    total = parts_s[0].astype(F32)
    for part in range(1, len(part_refs)):
        total = total + parts_s[part].astype(F32)
    total_ref[...] = total.astype(BF16)


def join_kernel(place_ref, *refs):
    *part_refs, joined_ref = refs
    for distance, ref in enumerate(part_refs):
        rows = ref.shape[0]
        span = pl.ds(pl.multiple_of((place_ref[0] ^ distance) * rows, GROUP_ROWS), rows)
        joined_ref[span] = ref[...]


def grads_kernel(place_ref, own_ref, other_ref, time_ref, project_ref, combine_ref, space_s):
    features = combine_ref.shape[1]
    core = place_ref[1] % 2
    half = own_ref.shape[0]
    space_s[pl.ds(pl.multiple_of(core * half, GROUP_ROWS), half)] = own_ref[...]
    space_s[pl.ds(pl.multiple_of((1 - core) * half, GROUP_ROWS), half)] = other_ref[...]
    for group in range(4 * features // LANES):
        piece = space_s[group * features : (group + 1) * features].astype(F32)
        start = group * LANES
        if start < 3 * features:
            project_ref[0, :, start : start + LANES] = piece
        else:
            combine_ref[0, :, start - 3 * features : start - 3 * features + LANES] = piece
    project_ref[1] = time_ref[:, : 3 * features].astype(F32)
    combine_ref[1] = time_ref[:, 3 * features :].astype(F32)


def shift(cells, axis, step):
    count = lax.axis_size(axis)
    if step > 0:
        moves = [(i, i + 1) for i in range(count - 1)]
    else:
        moves = [(i + 1, i) for i in range(count - 1)]
    return lax.ppermute(cells, axis, moves)


def exchange(cells, axis, distance):
    return lax.ppermute(cells, axis, [(i, i ^ distance) for i in range(lax.axis_size(axis))])


def per_device(wave_field, cotangent, block_lists, project_weights, combine_weights):
    frame_count, row_count, features = wave_field.shape
    width = features // HEADS
    scale = 1.0 / math.sqrt(width)
    block_count = row_count // BLOCK
    list_length = block_lists.shape[-1]
    rim = HREACH * BLOCK
    extended = row_count + 2 * rim
    keys_count = list_length * BLOCK
    time_count = lax.axis_size("tm")
    all_frames = frame_count * time_count
    sent_rows = row_count // time_count
    factor = 1.0 / math.sqrt(frame_count * row_count * time_count * lax.axis_size("space"))
    params = pltpu.CompilerParams(vmem_limit_bytes=VMEM_BYTES)

    def whole(*shape):
        return pl.BlockSpec(shape, lambda f: (0,) * len(shape))

    def framed(*shape):
        return pl.BlockSpec((1, *shape), lambda f: (f,) + (0,) * len(shape))

    lists_spec = pl.BlockSpec(memory_space=pltpu.SMEM)
    project_spec = whole(1, features, 3 * features)
    combine_spec = whole(1, features, features)
    part_spec = framed(sent_rows, 2 * features)
    part_shape = jax.ShapeDtypeStruct((frame_count, sent_rows, 2 * features), BF16)
    place = jnp.stack([lax.axis_index("tm"), lax.axis_index("space")]).astype(jnp.int32)

    from_left = shift(wave_field[:, row_count - rim :], "space", 1)
    from_right = shift(wave_field[:, :rim], "space", -1)

    act, keys_values, queries, probs, inverse_sum, attended, *parts = pl.pallas_call(
        space_forward_kernel,
        grid=(frame_count,),
        in_specs=[
            lists_spec,
            lists_spec,
            framed(rim, features),
            framed(row_count, features),
            framed(rim, features),
            framed(row_count, features),
            project_spec,
            combine_spec,
        ],
        out_specs=[
            framed(extended, features),
            framed(extended, 2 * features),
            framed(row_count, features),
            framed(block_count, keys_count, HEADS * BLOCK),
            framed(block_count, HEADS, BLOCK),
            framed(block_count, features, BLOCK),
            *[part_spec] * time_count,
        ],
        out_shape=[
            jax.ShapeDtypeStruct((frame_count, extended, features), BF16),
            jax.ShapeDtypeStruct((frame_count, extended, 2 * features), BF16),
            jax.ShapeDtypeStruct((frame_count, row_count, features), BF16),
            jax.ShapeDtypeStruct((frame_count, block_count, keys_count, HEADS * BLOCK), BF16),
            jax.ShapeDtypeStruct((frame_count, block_count, HEADS, BLOCK), F32),
            jax.ShapeDtypeStruct((frame_count, block_count, features, BLOCK), BF16),
            *[part_shape] * time_count,
        ],
        scratch_shapes=[
            pltpu.VMEM((block_count + 2 * HREACH, features, BLOCK), BF16),
            pltpu.VMEM((row_count, features), BF16),
        ],
        compiler_params=params,
        name="space_forward",
    )(
        block_lists,
        place,
        from_left,
        wave_field,
        from_right,
        cotangent,
        project_weights,
        combine_weights,
    )

    arrived = [parts[0]] + [exchange(parts[d], "tm", d) for d in range(1, time_count)]

    def time_body(*refs):
        time_kernel(scale, factor, time_count, *refs)

    whole_part = whole(frame_count, sent_rows, 2 * features)
    *parts, time_grads = pl.pallas_call(
        time_body,
        grid=(1,),
        in_specs=[
            *[whole_part] * time_count,
            pl.BlockSpec((1, features, 3 * features), lambda f: (1, 0, 0)),
            pl.BlockSpec((1, features, features), lambda f: (1, 0, 0)),
        ],
        out_specs=[*[whole_part] * time_count, whole(features, 4 * features)],
        out_shape=[
            *[part_shape] * time_count,
            jax.ShapeDtypeStruct((features, 4 * features), BF16),
        ],
        scratch_shapes=[
            pltpu.VMEM((all_frames, sent_rows, 3 * features), BF16),
            pltpu.VMEM((all_frames, sent_rows, features), BF16),
            pltpu.VMEM((all_frames, sent_rows, features), BF16),
            pltpu.VMEM((all_frames, sent_rows, 3 * features), BF16),
        ],
        compiler_params=params,
        name="time_pair",
    )(*arrived, project_weights, combine_weights)

    returned = [parts[0]] + [exchange(parts[d], "tm", d) for d in range(1, time_count)]
    time_sum = lax.psum(lax.psum(time_grads, "tm"), "space")

    def backward_body(*refs):
        space_backward_kernel(scale, factor, time_count, *refs)

    grad_rows = 4 * features // LANES * features
    half_shape = jax.ShapeDtypeStruct((grad_rows // 2, LANES), BF16)
    mixed_field, mixed_grad, dact, to_left, to_right, kept, sent = pl.pallas_call(
        backward_body,
        grid=(frame_count,),
        in_specs=[
            lists_spec,
            lists_spec,
            *[part_spec] * time_count,
            framed(extended, features),
            framed(extended, 2 * features),
            framed(row_count, features),
            framed(block_count, keys_count, HEADS * BLOCK),
            framed(block_count, HEADS, BLOCK),
            framed(block_count, features, BLOCK),
            project_spec,
            combine_spec,
        ],
        out_specs=[
            framed(row_count, features),
            framed(row_count, features),
            framed(row_count, features),
            framed(rim, features),
            framed(rim, features),
            whole(grad_rows // 2, LANES),
            whole(grad_rows // 2, LANES),
        ],
        out_shape=[
            jax.ShapeDtypeStruct((frame_count, row_count, features), BF16),
            jax.ShapeDtypeStruct((frame_count, row_count, features), BF16),
            jax.ShapeDtypeStruct((frame_count, row_count, features), F32),
            jax.ShapeDtypeStruct((frame_count, rim, features), BF16),
            jax.ShapeDtypeStruct((frame_count, rim, features), BF16),
            half_shape,
            half_shape,
        ],
        scratch_shapes=[
            pltpu.VMEM((block_count + 2 * HREACH, features, BLOCK), BF16),
            pltpu.VMEM((keys_count, HEADS * BLOCK), BF16),
            pltpu.VMEM((extended, 2 * features), F32),
            pltpu.VMEM((features, 4 * features), F32),
            pltpu.VMEM((grad_rows, LANES), BF16),
        ],
        compiler_params=params,
        name="space_backward",
    )(
        block_lists,
        place,
        *returned,
        act,
        keys_values,
        queries,
        probs,
        inverse_sum,
        attended,
        project_weights,
        combine_weights,
    )

    other = exchange(sent, "space", 1)
    edge_left = shift(to_right, "space", 1)
    edge_right = shift(to_left, "space", -1)
    vmem_spec = pl.BlockSpec(memory_space=pltpu.VMEM)
    piece_rows = grad_rows // 2 // time_count
    piece_shape = jax.ShapeDtypeStruct((piece_rows, LANES), BF16)
    pieces = pl.pallas_call(
        split_kernel,
        in_specs=[lists_spec, vmem_spec, vmem_spec],
        out_specs=[vmem_spec] * time_count,
        out_shape=[piece_shape] * time_count,
        scratch_shapes=[pltpu.VMEM((grad_rows // 2, LANES), BF16)],
        compiler_params=params,
        name="add_cores",
    )(place, kept, other)

    def summed(pieces, axis, group, name):
        def body(*refs):
            sum_kernel(axis, group, *refs)

        return pl.pallas_call(
            body,
            in_specs=[lists_spec, *[vmem_spec] * len(pieces)],
            out_specs=vmem_spec,
            out_shape=piece_shape,
            scratch_shapes=[pltpu.VMEM((len(pieces), piece_rows, LANES), BF16)],
            compiler_params=params,
            name=name,
        )(place, *pieces)

    pieces = [pieces[0]] + [exchange(pieces[d], "tm", d) for d in range(1, time_count)]
    piece = summed(pieces, 0, 1, "add_tm")
    pieces = [piece] + [exchange(piece, "space", d) for d in range(2, lax.axis_size("space"), 2)]
    piece = summed(pieces, 1, 2, "add_space")
    pieces = [piece] + [exchange(piece, "tm", d) for d in range(1, time_count)]
    own_half = pl.pallas_call(
        join_kernel,
        in_specs=[lists_spec, *[vmem_spec] * time_count],
        out_specs=vmem_spec,
        out_shape=half_shape,
        compiler_params=params,
        name="join_tm",
    )(place, *pieces)
    other_half = exchange(own_half, "space", 1)

    field_grad = pl.pallas_call(
        field_kernel,
        grid=(frame_count,),
        in_specs=[framed(row_count, features)] * 5,
        out_specs=framed(row_count, features),
        out_shape=jax.ShapeDtypeStruct((frame_count, row_count, features), BF16),
        compiler_params=params,
        name="field_grad",
    )(wave_field, mixed_grad, dact, edge_left, edge_right)

    project_grad, combine_grad = pl.pallas_call(
        grads_kernel,
        in_specs=[lists_spec, vmem_spec, vmem_spec, vmem_spec],
        out_specs=[vmem_spec, vmem_spec],
        out_shape=[
            jax.ShapeDtypeStruct((2, features, 3 * features), F32),
            jax.ShapeDtypeStruct((2, features, features), F32),
        ],
        scratch_shapes=[pltpu.VMEM((grad_rows, LANES), BF16)],
        compiler_params=params,
        name="weight_grads",
    )(place, own_half, other_half, time_sum)
    return (mixed_field, field_grad, project_grad, combine_grad)


def solution(mesh):
    in_specs = (P("tm", "space", None), P("tm", "space", None), P("tm", "space", None), P(), P())
    out_specs = (P("tm", "space", None), P("tm", "space", None), P(), P())
    return jax.shard_map(
        per_device, mesh=mesh, in_specs=in_specs, out_specs=out_specs, check_vma=False
    )
```

```python
import math

import jax
import jax.numpy as jnp
from jax import lax
from jax.experimental import pallas as pl
from jax.experimental.pallas import tpu as pltpu
from jax.sharding import PartitionSpec as P

HEADS = 8
BLOCK = 128
HREACH = 2
LANES = 128
GROUP_ROWS = 16
VMEM_BYTES = 24 * 1024 * 1024
BF16 = jnp.bfloat16
F32 = jnp.float32


epsilon = 1e-05


def dot_nn(left, right):
    return lax.dot_general(left, right, (((1,), (0,)), ((), ())), preferred_element_type=F32)


def dot_nt(left, right):
    return lax.dot_general(left, right, (((1,), (1,)), ((), ())), preferred_element_type=F32)


def dot_tn(left, right):
    return lax.dot_general(left, right, (((0,), (0,)), ((), ())), preferred_element_type=F32)


def layer_norm(rows):
    widened = rows.astype(F32)
    centered = widened - jnp.mean(widened, axis=-1, keepdims=True)
    inverse = lax.rsqrt(jnp.mean(centered * centered, axis=-1, keepdims=True) + epsilon)
    return (centered * inverse, inverse)


def norm_backward(upstream, normed, inverse):
    mean_grad = jnp.mean(upstream, axis=-1, keepdims=True)
    mean_cross = jnp.mean(upstream * normed, axis=-1, keepdims=True)
    return inverse * (upstream - mean_grad - normed * mean_cross)


def flip(matrix):
    return matrix.astype(F32).T.astype(BF16)


def pair_columns(rows_t, pair, width):
    count = rows_t.shape[1]
    base = (pair * 2 * width) // LANES * LANES
    parts = []
    for head in (2 * pair, 2 * pair + 1):
        start = head * width - base
        pieces = []
        if start:
            pieces.append(jnp.zeros((start, count), rows_t.dtype))
        pieces.append(rows_t[head * width : (head + 1) * width])
        if start + width < LANES:
            pieces.append(jnp.zeros((LANES - start - width, count), rows_t.dtype))
        parts.append(jnp.concatenate(pieces, axis=0))
    return jnp.concatenate(parts, axis=1)


def pair_group(matrix, pair, width):
    base = (pair * 2 * width) // LANES * LANES
    return matrix[:, base : base + LANES]


def pair_diagonal(product, width):
    count = product.shape[1] // 2
    return jnp.concatenate([product[:width, :count], product[width:, count:]], axis=0)


def head_rows(rows, width):
    column = lax.broadcasted_iota(jnp.int32, (1, rows.shape[1]), 1) // width
    return jnp.concatenate(
        [rows * (column == head).astype(F32).astype(BF16) for head in range(HEADS)], axis=0
    )


def head_spread(per_head, width):
    return jnp.concatenate(
        [
            jnp.broadcast_to(per_head[head : head + 1], (width, per_head.shape[1]))
            for head in range(HEADS)
        ],
        axis=0,
    )


def listed_blocks(lists_ref, frame, block):
    own = lists_ref[frame, block, 0]
    return [
        lists_ref[frame, block, entry] - own + (block + HREACH)
        for entry in range(lists_ref.shape[2])
    ]


def space_forward_kernel(
    lists_ref,
    place_ref,
    left_ref,
    wave_ref,
    right_ref,
    cot_ref,
    project_ref,
    combine_ref,
    act_ref,
    kv_ref,
    query_ref,
    probs_ref,
    inverse_sum_ref,
    attended_ref,
    *rest,
):
    *sent_refs, values_t, mixed_s = rest
    frame = pl.program_id(0)
    me = place_ref[0]
    row_count, features = wave_ref.shape[1:]
    width = features // HEADS
    block_count = row_count // BLOCK
    exponent_scale = math.log2(math.e) / math.sqrt(width)
    rows = jnp.concatenate([left_ref[0], wave_ref[0], right_ref[0]], axis=0)
    normed, _ = layer_norm(rows)
    act = normed.astype(BF16)
    act_ref[0] = act
    keys_values = dot_nn(act, project_ref[0, :, features:]).astype(BF16)
    kv_ref[0] = keys_values
    rim = left_ref.shape[1]
    queries = dot_nn(act[rim : rim + row_count], project_ref[0, :, :features]).astype(BF16)
    query_ref[0] = queries
    for place in range(block_count + 2 * HREACH):
        values_t[place] = flip(keys_values[place * BLOCK : (place + 1) * BLOCK, features:])
    for block in range(block_count):
        places = listed_blocks(lists_ref, frame, block)
        keys = jnp.concatenate(
            [kv_ref[0, pl.ds(place * BLOCK, BLOCK), :features] for place in places], axis=0
        )
        block_values_t = jnp.concatenate([values_t[place] for place in places], axis=1)
        query_t = flip(queries[block * BLOCK : (block + 1) * BLOCK])
        outs = []
        for pair in range(HEADS // 2):
            scores = dot_nn(pair_group(keys, pair, width), pair_columns(query_t, pair, width))
            top = jnp.max(scores, axis=0, keepdims=True)
            exp_scores = jnp.exp2((scores - top) * exponent_scale)
            inverse_sum = 1.0 / jnp.sum(exp_scores, axis=0, keepdims=True)
            probs = exp_scores.astype(BF16)
            probs_ref[0, block, :, pair * 2 * BLOCK : (pair + 1) * 2 * BLOCK] = probs
            inverse_sum_ref[0, block, 2 * pair : 2 * pair + 1] = inverse_sum[:, :BLOCK]
            inverse_sum_ref[0, block, 2 * pair + 1 : 2 * pair + 2] = inverse_sum[:, BLOCK:]
            out = dot_nn(block_values_t[pair * 2 * width : (pair + 1) * 2 * width], probs)
            outs.append(pair_diagonal(out * inverse_sum, width))
        attended_t = jnp.concatenate(outs, axis=0)
        attended_ref[0, block] = attended_t.astype(BF16)
        attended = attended_t.T.astype(BF16)
        mixed = (
            wave_ref[0, block * BLOCK : (block + 1) * BLOCK].astype(F32)
            + dot_nn(attended, combine_ref[0])
        ).astype(BF16)
        mixed_s[block * BLOCK : (block + 1) * BLOCK] = mixed
    for distance, sent_ref in enumerate(sent_refs):
        sent_rows = sent_ref.shape[1]
        span = pl.ds(pl.multiple_of((me ^ distance) * sent_rows, GROUP_ROWS), sent_rows)
        sent_ref[0, :, :features] = mixed_s[span]
        sent_ref[0, :, features:] = cot_ref[0, span]


def time_kernel(
    scale,
    factor,
    count_in,
    place_ref,
    *refs,
):
    arrived_refs = refs[:count_in]
    project_ref, combine_ref = refs[count_in : count_in + 2]
    grad_refs = refs[count_in + 2 : 2 * count_in + 2]
    mixed_refs = refs[2 * count_in + 2 : 3 * count_in + 2]
    kept_ref, sent_ref, proj_s, dattn_s, attended_s, dproj_s, rounded_s = refs[3 * count_in + 2 :]
    part_frames, row_count, features = arrived_refs[0].shape
    features //= 2
    frames = part_frames * count_in
    width = features // HEADS
    tokens = frames * row_count
    exponent_scale = scale * math.log2(math.e)
    part_tokens = part_frames * row_count
    rows = jnp.concatenate(
        [ref[:, :, :features].reshape(part_tokens, features) for ref in arrived_refs], axis=0
    )
    cot = jnp.concatenate(
        [ref[:, :, features:].reshape(part_tokens, features) for ref in arrived_refs], axis=0
    )
    normed, inverse = layer_norm(rows)
    act = normed.astype(BF16)
    proj_s[...] = dot_nn(act, project_ref[0]).astype(BF16).reshape(proj_s.shape)
    dattn_s[...] = dot_nt(cot, combine_ref[0]).astype(BF16).reshape(dattn_s.shape)
    count = frames * GROUP_ROWS
    key_row = lax.broadcasted_iota(jnp.int32, (count, 2 * count), 0) % GROUP_ROWS
    query_row = lax.broadcasted_iota(jnp.int32, (count, 2 * count), 1) % GROUP_ROWS
    same_row = key_row == query_row
    for group in range(row_count // GROUP_ROWS):
        span = slice(group * GROUP_ROWS, (group + 1) * GROUP_ROWS)
        queries = proj_s[:, span, :features].reshape(count, features)
        keys = proj_s[:, span, features : 2 * features].reshape(count, features)
        values = proj_s[:, span, 2 * features :].reshape(count, features)
        dattn = dattn_s[:, span].reshape(count, features)
        query_t, keys_t, values_t, dattn_t = flip(queries), flip(keys), flip(values), flip(dattn)
        outs, probs_parts, dscore_parts, dquery_parts = [], [], [], []
        for pair in range(HEADS // 2):
            heads = slice(pair * 2 * width, (pair + 1) * 2 * width)
            scores = dot_nn(pair_group(keys, pair, width), pair_columns(query_t, pair, width))
            scores = jnp.where(same_row, scores, -3e38)
            top = jnp.max(scores, axis=0, keepdims=True)
            exp_scores = jnp.exp2((scores - top) * exponent_scale)
            probs = (exp_scores * (1.0 / jnp.sum(exp_scores, axis=0, keepdims=True))).astype(BF16)
            probs_wide = probs.astype(F32)
            outs.append(pair_diagonal(dot_nn(values_t[heads], probs), width))
            dprobs = dot_nn(pair_group(values, pair, width), pair_columns(dattn_t, pair, width))
            delta = jnp.sum(probs_wide * dprobs, axis=0, keepdims=True)
            dscores = (probs_wide * (dprobs - delta) * scale).astype(BF16)
            dquery_parts.append(pair_diagonal(dot_nn(keys_t[heads], dscores), width))
            probs_parts.append(probs)
            dscore_parts.append(dscores)
        attended_s[:, span] = (
            jnp.concatenate(outs, axis=0).T.astype(BF16).reshape(frames, GROUP_ROWS, features)
        )
        dquery = jnp.concatenate(dquery_parts, axis=0).T
        dkeys = dot_nn(jnp.concatenate(dscore_parts, axis=1), head_rows(queries, width))
        dvalues = dot_nn(jnp.concatenate(probs_parts, axis=1), head_rows(dattn, width))
        dproj = jnp.concatenate([dquery, dkeys, dvalues], axis=1).astype(BF16)
        dproj_s[:, span] = dproj.reshape(frames, GROUP_ROWS, 3 * features)
    attended = attended_s[...].reshape(tokens, features)
    mixed = (rows.astype(F32) + dot_nn(attended, combine_ref[0])).astype(BF16)
    dproj = dproj_s[...].reshape(tokens, 3 * features)
    dact = dot_nt(dproj, project_ref[0])
    mixed_grad = (cot.astype(F32) + norm_backward(dact, normed, inverse)).astype(BF16)
    for part, (grad_ref, mixed_ref) in enumerate(zip(grad_refs, mixed_refs)):
        span = slice(part * part_tokens, (part + 1) * part_tokens)
        mixed_ref[...] = mixed[span].reshape(part_frames, row_count, features)
        grad_ref[...] = mixed_grad[span].reshape(part_frames, row_count, features)
    grads = jnp.concatenate([dot_tn(act, dproj), dot_tn(attended, cot)], axis=1) * factor
    halve_grads(grads, place_ref[1] % 2, rounded_s, kept_ref, sent_ref)


def space_backward_kernel(
    scale,
    factor,
    count_in,
    lists_ref,
    place_ref,
    *refs,
):
    returned_refs = refs[:count_in]
    (
        act_ref,
        kv_ref,
        query_ref,
        probs_ref,
        inverse_sum_ref,
        attended_ref,
        project_ref,
        combine_ref,
        mixed_grad_ref,
        dact_ref,
        to_left_ref,
        to_right_ref,
        kept_ref,
        sent_ref,
        keys_t,
        dscores_s,
        dkv_s,
        grads_s,
        rounded_s,
    ) = refs[count_in:]
    frame = pl.program_id(0)
    me = place_ref[0]
    core = place_ref[1] % 2
    row_count, features = mixed_grad_ref.shape[1:]
    width = features // HEADS
    block_count = row_count // BLOCK
    rim = HREACH * BLOCK
    for distance, ref in enumerate(returned_refs):
        sent_rows = ref.shape[1]
        span = pl.ds(pl.multiple_of((me ^ distance) * sent_rows, GROUP_ROWS), sent_rows)
        mixed_grad_ref[0, span] = ref[0]
    mixed_grad = mixed_grad_ref[0]
    for place in range(block_count + 2 * HREACH):
        keys_t[place] = flip(kv_ref[0, place * BLOCK : (place + 1) * BLOCK, :features])
    dkv_s[...] = jnp.zeros(dkv_s.shape, F32)

    @pl.when(frame == 0)
    def _():
        grads_s[...] = jnp.zeros(grads_s.shape, F32)

    dquery_blocks = []
    for block in range(block_count):
        span = slice(block * BLOCK, (block + 1) * BLOCK)
        places = listed_blocks(lists_ref, frame, block)
        values = jnp.concatenate(
            [kv_ref[0, pl.ds(place * BLOCK, BLOCK), features:] for place in places], axis=0
        )
        block_keys_t = jnp.concatenate([keys_t[place] for place in places], axis=1)
        block_grad = mixed_grad[span]
        attended_t = attended_ref[0, block]
        grads_s[:, 3 * features :] += dot_nn(attended_t, block_grad)
        dattn_t = dot_nt(combine_ref[0], block_grad).astype(BF16)
        dattn_wide = dattn_t.astype(F32)
        inverse_sum = inverse_sum_ref[0, block]
        scaled_dattn = (dattn_wide * head_spread(inverse_sum, width)).T.astype(BF16)
        delta = jnp.sum(
            (dattn_wide * attended_t.astype(F32)).reshape(HEADS, width, BLOCK), axis=1
        )
        row_scale = inverse_sum * scale
        dquery_parts = []
        for pair in range(HEADS // 2):
            heads = slice(pair * 2 * width, (pair + 1) * 2 * width)
            columns = slice(pair * 2 * BLOCK, (pair + 1) * 2 * BLOCK)
            pair_delta = jnp.concatenate(
                [delta[2 * pair : 2 * pair + 1], delta[2 * pair + 1 : 2 * pair + 2]], axis=1
            )
            pair_scale = jnp.concatenate(
                [row_scale[2 * pair : 2 * pair + 1], row_scale[2 * pair + 1 : 2 * pair + 2]], axis=1
            )
            dprobs = dot_nn(pair_group(values, pair, width), pair_columns(dattn_t, pair, width))
            probs = probs_ref[0, block, :, columns].astype(F32)
            dscores = (probs * ((dprobs - pair_delta) * pair_scale)).astype(BF16)
            dscores_s[:, columns] = dscores
            dquery_parts.append(pair_diagonal(dot_nn(block_keys_t[heads], dscores), width))
        dquery_blocks.append(jnp.concatenate(dquery_parts, axis=0).T.astype(BF16))
        dkeys = dot_nn(dscores_s[...], head_rows(query_ref[0, span], width))
        dvalues = dot_nn(probs_ref[0, block], head_rows(scaled_dattn, width))
        for entry, place in enumerate(places):
            rows = pl.ds(place * BLOCK, BLOCK)
            listed = slice(entry * BLOCK, (entry + 1) * BLOCK)
            dkv_s[rows, :features] += dkeys[listed]
            dkv_s[rows, features:] += dvalues[listed]
    dquery = jnp.concatenate(dquery_blocks, axis=0)
    dkv = dkv_s[...].astype(BF16)
    grads_s[:, :features] += dot_tn(act_ref[0, rim : rim + row_count], dquery)
    grads_s[:, features : 3 * features] += dot_tn(act_ref[0], dkv)
    dact = dot_nt(dkv, project_ref[0, :, features:])
    to_left_ref[0] = dact[:rim].astype(BF16)
    to_right_ref[0] = dact[rim + row_count :].astype(BF16)
    dact_ref[0] = dact[rim : rim + row_count] + dot_nt(dquery, project_ref[0, :, :features])

    @pl.when(frame == pl.num_programs(0) - 1)
    def _():
        halve_grads(grads_s[...] * factor, core, rounded_s, kept_ref, sent_ref)


def field_kernel(place_ref, wave_ref, mixed_grad_ref, dact_ref, from_left_ref, from_right_ref, *refs):
    *mixed_refs, field_ref, mixed_ref = refs
    normed, inverse = layer_norm(wave_ref[0])
    dact = dact_ref[0] + from_left_ref[0].astype(F32) + from_right_ref[0].astype(F32)
    field_ref[0] = (
        mixed_grad_ref[0].astype(F32) + norm_backward(dact, normed, inverse)
    ).astype(BF16)
    for distance, ref in enumerate(mixed_refs):
        rows = ref.shape[1]
        span = pl.ds(pl.multiple_of((place_ref[0] ^ distance) * rows, GROUP_ROWS), rows)
        mixed_ref[0, span] = ref[0]


def split_kernel(place_ref, kept_ref, arrived_ref, *refs):
    *part_refs, sum_s = refs
    sum_s[...] = (kept_ref[...].astype(F32) + arrived_ref[...].astype(F32)).astype(BF16)
    for distance, ref in enumerate(part_refs):
        rows = ref.shape[0]
        ref[...] = sum_s[pl.ds(pl.multiple_of((place_ref[0] ^ distance) * rows, GROUP_ROWS), rows)]


def sum_kernel(axis, group, place_ref, *refs):
    *part_refs, total_ref, parts_s = refs
    me = place_ref[axis] // group
    for distance, ref in enumerate(part_refs):
        parts_s[me ^ distance] = ref[...]
    total = parts_s[0].astype(F32)
    for part in range(1, len(part_refs)):
        total = total + parts_s[part].astype(F32)
    total_ref[...] = total.astype(BF16)


def join_kernel(place_ref, *refs):
    *part_refs, joined_ref = refs
    for distance, ref in enumerate(part_refs):
        rows = ref.shape[0]
        span = pl.ds(pl.multiple_of((place_ref[0] ^ distance) * rows, GROUP_ROWS), rows)
        joined_ref[span] = ref[...]


def grads_kernel(place_ref, *refs):
    *half_refs, project_ref, combine_ref, joined_s = refs
    features = combine_ref.shape[1]
    core = place_ref[1] % 2
    half = half_refs[0].shape[0]
    for layer in range(2):
        own_ref, other_ref = half_refs[2 * layer : 2 * layer + 2]
        joined_s[pl.ds(pl.multiple_of(core * half, GROUP_ROWS), half)] = own_ref[...]
        joined_s[pl.ds(pl.multiple_of((1 - core) * half, GROUP_ROWS), half)] = other_ref[...]
        for group in range(4 * features // LANES):
            piece = joined_s[group * features : (group + 1) * features].astype(F32)
            start = group * LANES
            if start < 3 * features:
                project_ref[layer, :, start : start + LANES] = piece
            else:
                combine_ref[layer, :, start - 3 * features : start - 3 * features + LANES] = piece


def halve_grads(grads, core, rounded_s, kept_ref, sent_ref):
    features = grads.shape[0]
    for group in range(grads.shape[1] // LANES):
        rounded_s[group * features : (group + 1) * features] = grads[
            :, group * LANES : (group + 1) * LANES
        ].astype(BF16)
    half = kept_ref.shape[0]
    kept_ref[...] = rounded_s[pl.ds(pl.multiple_of(core * half, GROUP_ROWS), half)]
    sent_ref[...] = rounded_s[pl.ds(pl.multiple_of((1 - core) * half, GROUP_ROWS), half)]


def in_hbm(cells):
    return pltpu.with_memory_space_constraint(cells, pltpu.HBM)


def shift(cells, axis, step):
    count = lax.axis_size(axis)
    if step > 0:
        moves = [(i, i + 1) for i in range(count - 1)]
    else:
        moves = [(i + 1, i) for i in range(count - 1)]
    return lax.ppermute(cells, axis, moves)


def exchange(cells, axis, distance):
    return lax.ppermute(cells, axis, [(i, i ^ distance) for i in range(lax.axis_size(axis))])


def per_device(wave_field, cotangent, block_lists, project_weights, combine_weights):
    frame_count, row_count, features = wave_field.shape
    width = features // HEADS
    scale = 1.0 / math.sqrt(width)
    block_count = row_count // BLOCK
    list_length = block_lists.shape[-1]
    rim = HREACH * BLOCK
    extended = row_count + 2 * rim
    keys_count = list_length * BLOCK
    time_count = lax.axis_size("tm")
    all_frames = frame_count * time_count
    sent_rows = row_count // time_count
    factor = 1.0 / math.sqrt(frame_count * row_count * time_count * lax.axis_size("space"))
    params = pltpu.CompilerParams(vmem_limit_bytes=VMEM_BYTES)

    def whole(*shape):
        return pl.BlockSpec(shape, lambda f: (0,) * len(shape))

    def framed(*shape):
        return pl.BlockSpec((1, *shape), lambda f: (f,) + (0,) * len(shape))

    lists_spec = pl.BlockSpec(memory_space=pltpu.SMEM)
    project_spec = whole(1, features, 3 * features)
    combine_spec = whole(1, features, features)
    part_spec = framed(sent_rows, 2 * features)
    part_shape = jax.ShapeDtypeStruct((frame_count, sent_rows, 2 * features), BF16)
    place = jnp.stack([lax.axis_index("tm"), lax.axis_index("space")]).astype(jnp.int32)
    wave_field, cotangent, block_lists, project_weights, combine_weights = (
        in_hbm(cells)
        for cells in (wave_field, cotangent, block_lists, project_weights, combine_weights)
    )

    from_left, from_right = (
        pltpu.with_memory_space_constraint(cells, pltpu.VMEM)
        for cells in (
            shift(wave_field[:, row_count - rim :], "space", 1),
            shift(wave_field[:, :rim], "space", -1),
        )
    )

    act, keys_values, queries, probs, inverse_sum, attended, *parts = pl.pallas_call(
        space_forward_kernel,
        grid=(frame_count,),
        in_specs=[
            lists_spec,
            lists_spec,
            framed(rim, features),
            framed(row_count, features),
            framed(rim, features),
            framed(row_count, features),
            project_spec,
            combine_spec,
        ],
        out_specs=[
            framed(extended, features),
            framed(extended, 2 * features),
            framed(row_count, features),
            framed(block_count, keys_count, HEADS * BLOCK),
            framed(block_count, HEADS, BLOCK),
            framed(block_count, features, BLOCK),
            *[part_spec] * time_count,
        ],
        out_shape=[
            jax.ShapeDtypeStruct((frame_count, extended, features), BF16),
            jax.ShapeDtypeStruct((frame_count, extended, 2 * features), BF16),
            jax.ShapeDtypeStruct((frame_count, row_count, features), BF16),
            jax.ShapeDtypeStruct((frame_count, block_count, keys_count, HEADS * BLOCK), BF16),
            jax.ShapeDtypeStruct((frame_count, block_count, HEADS, BLOCK), F32),
            jax.ShapeDtypeStruct((frame_count, block_count, features, BLOCK), BF16),
            *[part_shape] * time_count,
        ],
        scratch_shapes=[
            pltpu.VMEM((block_count + 2 * HREACH, features, BLOCK), BF16),
            pltpu.VMEM((row_count, features), BF16),
        ],
        compiler_params=params,
        name="space_forward",
    )(
        block_lists,
        place,
        from_left,
        wave_field,
        from_right,
        cotangent,
        project_weights,
        combine_weights,
    )

    arrived = [parts[0]] + [exchange(parts[d], "tm", d) for d in range(1, time_count)]

    def time_body(*refs):
        time_kernel(scale, factor, time_count, *refs)

    whole_part = whole(frame_count, sent_rows, 2 * features)
    whole_back = whole(frame_count, sent_rows, features)
    back_shape = jax.ShapeDtypeStruct((frame_count, sent_rows, features), BF16)
    grad_rows = 4 * features // LANES * features
    half_shape = jax.ShapeDtypeStruct((grad_rows // 2, LANES), BF16)
    grad_parts = pl.pallas_call(
        time_body,
        grid=(1,),
        in_specs=[
            lists_spec,
            *[whole_part] * time_count,
            pl.BlockSpec((1, features, 3 * features), lambda f: (1, 0, 0)),
            pl.BlockSpec((1, features, features), lambda f: (1, 0, 0)),
        ],
        out_specs=[*[whole_back] * (2 * time_count), *[whole(grad_rows // 2, LANES)] * 2],
        out_shape=[*[back_shape] * (2 * time_count), half_shape, half_shape],
        scratch_shapes=[
            pltpu.VMEM((all_frames, sent_rows, 3 * features), BF16),
            pltpu.VMEM((all_frames, sent_rows, features), BF16),
            pltpu.VMEM((all_frames, sent_rows, features), BF16),
            pltpu.VMEM((all_frames, sent_rows, 3 * features), BF16),
            pltpu.VMEM((grad_rows, LANES), BF16),
        ],
        compiler_params=params,
        name="time_pair",
    )(place, *arrived, project_weights, combine_weights)
    *parts, time_kept, time_sent = grad_parts

    def over_tm(pieces):
        return [pieces[0]] + [exchange(pieces[d], "tm", d) for d in range(1, time_count)]

    returned = over_tm(parts[:time_count])
    mixed_parts = over_tm(parts[time_count:])
    time_other = exchange(time_sent, "space", 1)

    def backward_body(*refs):
        space_backward_kernel(scale, factor, time_count, *refs)

    back_spec = framed(sent_rows, features)
    mixed_grad, dact, to_left, to_right, space_kept, space_sent = pl.pallas_call(
        backward_body,
        grid=(frame_count,),
        in_specs=[
            lists_spec,
            lists_spec,
            *[back_spec] * time_count,
            framed(extended, features),
            framed(extended, 2 * features),
            framed(row_count, features),
            framed(block_count, keys_count, HEADS * BLOCK),
            framed(block_count, HEADS, BLOCK),
            framed(block_count, features, BLOCK),
            project_spec,
            combine_spec,
        ],
        out_specs=[
            framed(row_count, features),
            framed(row_count, features),
            framed(rim, features),
            framed(rim, features),
            whole(grad_rows // 2, LANES),
            whole(grad_rows // 2, LANES),
        ],
        out_shape=[
            jax.ShapeDtypeStruct((frame_count, row_count, features), BF16),
            jax.ShapeDtypeStruct((frame_count, row_count, features), F32),
            jax.ShapeDtypeStruct((frame_count, rim, features), BF16),
            jax.ShapeDtypeStruct((frame_count, rim, features), BF16),
            half_shape,
            half_shape,
        ],
        scratch_shapes=[
            pltpu.VMEM((block_count + 2 * HREACH, features, BLOCK), BF16),
            pltpu.VMEM((keys_count, HEADS * BLOCK), BF16),
            pltpu.VMEM((extended, 2 * features), F32),
            pltpu.VMEM((features, 4 * features), F32),
            pltpu.VMEM((grad_rows, LANES), BF16),
        ],
        compiler_params=params,
        name="space_backward",
    )(
        block_lists,
        place,
        *returned,
        act,
        keys_values,
        queries,
        probs,
        inverse_sum,
        attended,
        project_weights,
        combine_weights,
    )

    vmem_spec = pl.BlockSpec(memory_space=pltpu.VMEM)
    piece_rows = grad_rows // 2 // time_count
    piece_shape = jax.ShapeDtypeStruct((piece_rows, LANES), BF16)

    def split(kept, other, name):
        return pl.pallas_call(
            split_kernel,
            in_specs=[lists_spec, vmem_spec, vmem_spec],
            out_specs=[vmem_spec] * time_count,
            out_shape=[piece_shape] * time_count,
            scratch_shapes=[pltpu.VMEM((grad_rows // 2, LANES), BF16)],
            compiler_params=params,
            name=name,
        )(place, kept, other)

    def summed(pieces, axis, group, name):
        def body(*refs):
            sum_kernel(axis, group, *refs)

        return pl.pallas_call(
            body,
            in_specs=[lists_spec, *[vmem_spec] * len(pieces)],
            out_specs=vmem_spec,
            out_shape=piece_shape,
            scratch_shapes=[pltpu.VMEM((len(pieces), piece_rows, LANES), BF16)],
            compiler_params=params,
            name=name,
        )(place, *pieces)

    def over_space(piece):
        return [piece] + [
            exchange(piece, "space", d) for d in range(2, lax.axis_size("space"), 2)
        ]

    def joined(pieces, name):
        return pl.pallas_call(
            join_kernel,
            in_specs=[lists_spec, *[vmem_spec] * time_count],
            out_specs=vmem_spec,
            out_shape=half_shape,
            compiler_params=params,
            name=name,
        )(place, *pieces)

    space_sent, *mixed_parts = lax.optimization_barrier((space_sent, *mixed_parts))
    space_other = exchange(space_sent, "space", 1)
    edge_left = shift(to_right, "space", 1)
    edge_right = shift(to_left, "space", -1)
    time_pieces = over_tm(split(time_kept, time_other, "add_cores_time"))
    space_pieces = over_tm(split(space_kept, space_other, "add_cores_space"))
    edge_left, edge_right, *space_pieces = lax.optimization_barrier(
        (edge_left, edge_right, *space_pieces)
    )
    time_pieces = over_space(summed(time_pieces, 0, 1, "add_tm_time"))
    space_pieces = over_space(summed(space_pieces, 0, 1, "add_tm_space"))
    time_pieces = over_tm([summed(time_pieces, 1, 2, "add_space_time")] * time_count)
    space_pieces = over_tm([summed(space_pieces, 1, 2, "add_space_space")] * time_count)
    time_half = joined(time_pieces, "join_time")
    time_half_other = exchange(time_half, "space", 1)
    space_half = joined(space_pieces, "join_space")
    space_half_other = exchange(space_half, "space", 1)

    field_grad, mixed_field = pl.pallas_call(
        field_kernel,
        grid=(frame_count,),
        in_specs=[lists_spec, *[framed(row_count, features)] * 5, *[back_spec] * time_count],
        out_specs=[framed(row_count, features)] * 2,
        out_shape=[jax.ShapeDtypeStruct((frame_count, row_count, features), BF16)] * 2,
        compiler_params=params,
        name="field_grad",
    )(place, wave_field, mixed_grad, dact, edge_left, edge_right, *mixed_parts)

    project_grad, combine_grad = pl.pallas_call(
        grads_kernel,
        in_specs=[lists_spec, *[vmem_spec] * 4],
        out_specs=[vmem_spec, vmem_spec],
        out_shape=[
            jax.ShapeDtypeStruct((2, features, 3 * features), F32),
            jax.ShapeDtypeStruct((2, features, features), F32),
        ],
        scratch_shapes=[pltpu.VMEM((grad_rows, LANES), BF16)],
        compiler_params=params,
        name="weight_grads",
    )(place, space_half, space_half_other, time_half, time_half_other)
    return (mixed_field, field_grad, project_grad, combine_grad)


def solution(mesh):
    in_specs = (P("tm", "space", None), P("tm", "space", None), P("tm", "space", None), P(), P())
    out_specs = (P("tm", "space", None), P("tm", "space", None), P(), P())
    return jax.shard_map(
        per_device, mesh=mesh, in_specs=in_specs, out_specs=out_specs, check_vma=False
    )
```

```python
import math

import jax
import jax.numpy as jnp
from jax import lax
from jax.experimental import pallas as pl
from jax.experimental.pallas import tpu as pltpu
from jax.sharding import PartitionSpec as P

HEADS = 8
BLOCK = 128
HREACH = 2
LANES = 128
GROUP_ROWS = 16
VMEM_BYTES = 24 * 1024 * 1024
BF16 = jnp.bfloat16
F32 = jnp.float32


epsilon = 1e-05


def cost(matmuls):
    flops = matmuls * 2 * 1024 * 256 * 512
    return pl.CostEstimate(flops=flops, bytes_accessed=flops // 256, transcendentals=flops // 1024)


def dot_nn(left, right):
    return lax.dot_general(left, right, (((1,), (0,)), ((), ())), preferred_element_type=F32)


def dot_nt(left, right):
    return lax.dot_general(left, right, (((1,), (1,)), ((), ())), preferred_element_type=F32)


def dot_tn(left, right):
    return lax.dot_general(left, right, (((0,), (0,)), ((), ())), preferred_element_type=F32)


def layer_norm(rows):
    widened = rows.astype(F32)
    centered = widened - jnp.mean(widened, axis=-1, keepdims=True)
    inverse = lax.rsqrt(jnp.mean(centered * centered, axis=-1, keepdims=True) + epsilon)
    return (centered * inverse, inverse)


def norm_backward(upstream, normed, inverse):
    mean_grad = jnp.mean(upstream, axis=-1, keepdims=True)
    mean_cross = jnp.mean(upstream * normed, axis=-1, keepdims=True)
    return inverse * (upstream - mean_grad - normed * mean_cross)


def flip(matrix):
    return matrix.astype(BF16).T


def pair_columns(rows_t, pair, width):
    count = rows_t.shape[1]
    base = (pair * 2 * width) // LANES * LANES
    parts = []
    for head in (2 * pair, 2 * pair + 1):
        start = head * width - base
        pieces = []
        if start:
            pieces.append(jnp.zeros((start, count), rows_t.dtype))
        pieces.append(rows_t[head * width : (head + 1) * width])
        if start + width < LANES:
            pieces.append(jnp.zeros((LANES - start - width, count), rows_t.dtype))
        parts.append(jnp.concatenate(pieces, axis=0))
    return jnp.concatenate(parts, axis=1)


def pair_group(matrix, pair, width):
    base = (pair * 2 * width) // LANES * LANES
    return matrix[:, base : base + LANES]


def pair_diagonal(product, width):
    count = product.shape[1] // 2
    return jnp.concatenate([product[:width, :count], product[width:, count:]], axis=0)


def head_rows(rows, width):
    column = lax.broadcasted_iota(jnp.int32, (1, rows.shape[1]), 1) // width
    return jnp.concatenate(
        [rows * (column == head).astype(F32).astype(BF16) for head in range(HEADS)], axis=0
    )


def head_spread(per_head, width):
    return jnp.concatenate(
        [
            jnp.broadcast_to(per_head[head : head + 1], (width, per_head.shape[1]))
            for head in range(HEADS)
        ],
        axis=0,
    )


def listed_blocks(lists_ref, frame, block):
    own = lists_ref[frame, block, 0]
    return [
        lists_ref[frame, block, entry] - own + (block + HREACH)
        for entry in range(lists_ref.shape[2])
    ]


def cut_kernel(place_ref, rows_ref, *sent_refs):
    for distance, ref in enumerate(sent_refs):
        rows = ref.shape[1]
        ref[...] = rows_ref[
            :, pl.ds(pl.multiple_of((place_ref[0] ^ distance) * rows, GROUP_ROWS), rows)
        ]


def space_forward_kernel(
    lists_ref,
    place_ref,
    left_ref,
    wave_ref,
    right_ref,
    project_ref,
    turned_ref,
    combine_ref,
    act_ref,
    kv_ref,
    keys_t_ref,
    query_ref,
    probs_ref,
    inverse_sum_ref,
    attended_ref,
    *rest,
):
    *sent_refs, values_t, mixed_s = rest
    frame = pl.program_id(0)
    me = place_ref[0]
    row_count, features = wave_ref.shape[1:]
    width = features // HEADS
    block_count = row_count // BLOCK
    exponent_scale = math.log2(math.e) / math.sqrt(width)
    rows = jnp.concatenate([left_ref[0], wave_ref[0], right_ref[0]], axis=0)
    normed, _ = layer_norm(rows)
    act = normed.astype(BF16)
    act_ref[0] = act
    keys_values = dot_nn(act, project_ref[0, :, features:]).astype(BF16)
    kv_ref[0] = keys_values
    rim = left_ref.shape[1]
    own_act = act[rim : rim + row_count]
    query_ref[0] = dot_nn(own_act, project_ref[0, :, :features]).astype(BF16)
    queries_t = dot_nt(turned_ref[0, :features], own_act).astype(BF16)
    all_keys_t = dot_nt(turned_ref[0, features : 2 * features], act).astype(BF16)
    all_values_t = dot_nt(turned_ref[0, 2 * features :], act).astype(BF16)
    for place in range(block_count + 2 * HREACH):
        keys_t_ref[0, place] = all_keys_t[:, place * BLOCK : (place + 1) * BLOCK]
        values_t[place] = all_values_t[:, place * BLOCK : (place + 1) * BLOCK]
    for block in range(block_count):
        places = listed_blocks(lists_ref, frame, block)
        keys = jnp.concatenate(
            [kv_ref[0, pl.ds(place * BLOCK, BLOCK), :features] for place in places], axis=0
        )
        block_values_t = jnp.concatenate([values_t[place] for place in places], axis=1)
        query_t = queries_t[:, block * BLOCK : (block + 1) * BLOCK]
        outs = []
        for pair in range(HEADS // 2):
            scores = dot_nn(pair_group(keys, pair, width), pair_columns(query_t, pair, width))
            top = jnp.max(scores, axis=0, keepdims=True)
            exp_scores = jnp.exp2((scores - top) * exponent_scale)
            inverse_sum = 1.0 / jnp.sum(exp_scores, axis=0, keepdims=True)
            probs = exp_scores.astype(BF16)
            probs_ref[0, block, :, pair * 2 * BLOCK : (pair + 1) * 2 * BLOCK] = probs
            inverse_sum_ref[0, block, 2 * pair : 2 * pair + 1] = inverse_sum[:, :BLOCK]
            inverse_sum_ref[0, block, 2 * pair + 1 : 2 * pair + 2] = inverse_sum[:, BLOCK:]
            out = dot_nn(block_values_t[pair * 2 * width : (pair + 1) * 2 * width], probs)
            outs.append(pair_diagonal(out * inverse_sum, width))
        attended_t = jnp.concatenate(outs, axis=0)
        attended_ref[0, block] = attended_t.astype(BF16)
        mixed = (
            wave_ref[0, block * BLOCK : (block + 1) * BLOCK].astype(F32)
            + dot_nn(flip(attended_t), combine_ref[0])
        ).astype(BF16)
        mixed_s[block * BLOCK : (block + 1) * BLOCK] = mixed
    for distance, sent_ref in enumerate(sent_refs):
        sent_rows = sent_ref.shape[1]
        span = pl.ds(pl.multiple_of((me ^ distance) * sent_rows, GROUP_ROWS), sent_rows)
        sent_ref[0] = mixed_s[span]


def time_kernel(
    scale,
    count_in,
    *refs,
):
    arrived_refs, cot_refs = refs[:count_in], refs[count_in : 2 * count_in]
    project_ref, turned_ref, combine_ref = refs[2 * count_in : 2 * count_in + 3]
    grad_refs = refs[2 * count_in + 3 : 3 * count_in + 3]
    act_ref, dproj_ref, attended_t_ref, cot_ref, mixed_ref = refs[3 * count_in + 3 :]
    part_frames, row_count, features = grad_refs[0].shape
    width = features // HEADS
    count = part_frames * count_in * GROUP_ROWS
    groups = row_count // GROUP_ROWS
    exponent_scale = scale * math.log2(math.e)

    def grouped(part_refs):
        return jnp.concatenate(
            [
                ref[:, group * GROUP_ROWS : (group + 1) * GROUP_ROWS].reshape(
                    part_frames * GROUP_ROWS, features
                )
                for group in range(groups)
                for ref in part_refs
            ],
            axis=0,
        )

    rows = grouped(arrived_refs)
    cot = grouped(cot_refs)
    cot_ref[...] = cot
    normed, inverse = layer_norm(rows)
    act = normed.astype(BF16)
    act_ref[...] = act
    projected = dot_nn(act, project_ref[0]).astype(BF16)
    projected_t = dot_nt(turned_ref[0], act).astype(BF16)
    all_dattn = dot_nt(cot, combine_ref[0]).astype(BF16)
    all_dattn_t = dot_nt(combine_ref[0], cot).astype(BF16)
    key_row = lax.broadcasted_iota(jnp.int32, (count, 2 * count), 0) % GROUP_ROWS
    query_row = lax.broadcasted_iota(jnp.int32, (count, 2 * count), 1) % GROUP_ROWS
    same_row = key_row == query_row
    attended_groups, dquery_groups, dkey_groups, dvalue_groups = [], [], [], []
    for group in range(groups):
        span = slice(group * count, (group + 1) * count)
        queries = projected[span, :features]
        keys = projected[span, features : 2 * features]
        values = projected[span, 2 * features :]
        query_t = projected_t[:features, span]
        keys_t = projected_t[features : 2 * features, span]
        values_t = projected_t[2 * features :, span]
        dattn_t = all_dattn_t[:, span]
        outs, probs_parts, dscore_parts, dquery_parts = [], [], [], []
        for pair in range(HEADS // 2):
            heads = slice(pair * 2 * width, (pair + 1) * 2 * width)
            scores = dot_nn(pair_group(keys, pair, width), pair_columns(query_t, pair, width))
            scores = jnp.where(same_row, scores, -3e38)
            top = jnp.max(scores, axis=0, keepdims=True)
            exp_scores = jnp.exp2((scores - top) * exponent_scale)
            probs = (exp_scores * (1.0 / jnp.sum(exp_scores, axis=0, keepdims=True))).astype(BF16)
            probs_wide = probs.astype(F32)
            outs.append(pair_diagonal(dot_nn(values_t[heads], probs), width))
            dprobs = dot_nn(pair_group(values, pair, width), pair_columns(dattn_t, pair, width))
            delta = jnp.sum(probs_wide * dprobs, axis=0, keepdims=True)
            dscores = (probs_wide * (dprobs - delta) * scale).astype(BF16)
            dquery_parts.append(pair_diagonal(dot_nn(keys_t[heads], dscores), width))
            probs_parts.append(probs)
            dscore_parts.append(dscores)
        attended_groups.append(jnp.concatenate(outs, axis=0).astype(BF16))
        dquery_groups.append(flip(jnp.concatenate(dquery_parts, axis=0)))
        dkey_groups.append(
            dot_nn(jnp.concatenate(dscore_parts, axis=1), head_rows(queries, width)).astype(BF16)
        )
        dvalue_groups.append(
            dot_nn(jnp.concatenate(probs_parts, axis=1), head_rows(all_dattn[span], width)).astype(BF16)
        )
    attended = jnp.concatenate([flip(attended_t) for attended_t in attended_groups], axis=0)
    mixed_ref[...] = (rows.astype(F32) + dot_nn(attended, combine_ref[0])).astype(BF16)
    attended_t_ref[...] = jnp.concatenate(attended_groups, axis=1)
    dproj = jnp.concatenate(
        [jnp.concatenate(parts, axis=0) for parts in (dquery_groups, dkey_groups, dvalue_groups)],
        axis=1,
    )
    dproj_ref[...] = dproj
    dact = dot_nt(dproj, project_ref[0])
    mixed_grad = (cot.astype(F32) + norm_backward(dact, normed, inverse)).astype(BF16)
    for part, ref in enumerate(grad_refs):
        for group in range(groups):
            span = slice(group * GROUP_ROWS, (group + 1) * GROUP_ROWS)
            for frame in range(part_frames):
                start = ((group * count_in + part) * part_frames + frame) * GROUP_ROWS
                ref[frame, span] = mixed_grad[start : start + GROUP_ROWS]


def time_grads_kernel(
    factor, part_frames, row_count, place_ref, act_ref, dproj_ref, attended_t_ref, cot_ref, mixed_ref, *refs
):
    *ride_refs, stacked_s = refs
    count_in = len(ride_refs)
    features = act_ref.shape[1]
    groups = row_count // GROUP_ROWS
    grads = jnp.concatenate(
        [dot_tn(act_ref[...], dproj_ref[...]), dot_nn(attended_t_ref[...], cot_ref[...])], axis=1
    )
    stack_grads(grads * factor, stacked_s)
    chunk = stacked_s.shape[0] // count_in
    part_rows = part_frames * row_count
    for part, ref in enumerate(ride_refs):
        for group in range(groups):
            for frame in range(part_frames):
                start = ((group * count_in + part) * part_frames + frame) * GROUP_ROWS
                for lane_group in range(features // LANES):
                    row = chunk + lane_group * part_rows + frame * row_count + group * GROUP_ROWS
                    ref[row : row + GROUP_ROWS] = mixed_ref[
                        start : start + GROUP_ROWS, lane_group * LANES : (lane_group + 1) * LANES
                    ]
        ref[:chunk] = stacked_s[
            pl.ds(pl.multiple_of((place_ref[0] ^ part) * chunk, GROUP_ROWS), chunk)
        ]


def space_backward_kernel(
    scale,
    factor,
    count_in,
    lists_ref,
    place_ref,
    *refs,
):
    returned_refs = refs[:count_in]
    (
        act_ref,
        kv_ref,
        keys_t_ref,
        query_ref,
        probs_ref,
        inverse_sum_ref,
        attended_ref,
        combine_ref,
        mixed_grad_ref,
        dquery_ref,
        dkv_ref,
        stacked_ref,
        dscores_s,
        dkv_s,
        grads_s,
    ) = refs[count_in:]
    frame = pl.program_id(0)
    me = place_ref[0]
    row_count, features = mixed_grad_ref.shape[1:]
    width = features // HEADS
    block_count = row_count // BLOCK
    rim = HREACH * BLOCK
    for distance, ref in enumerate(returned_refs):
        sent_rows = ref.shape[1]
        span = pl.ds(pl.multiple_of((me ^ distance) * sent_rows, GROUP_ROWS), sent_rows)
        mixed_grad_ref[0, span] = ref[0]
    mixed_grad = mixed_grad_ref[0]
    dkv_s[...] = jnp.zeros(dkv_s.shape, F32)

    @pl.when(frame == 0)
    def _():
        grads_s[...] = jnp.zeros(grads_s.shape, F32)

    dquery_blocks = []
    for block in range(block_count):
        span = slice(block * BLOCK, (block + 1) * BLOCK)
        places = listed_blocks(lists_ref, frame, block)
        values = jnp.concatenate(
            [kv_ref[0, pl.ds(place * BLOCK, BLOCK), features:] for place in places], axis=0
        )
        block_keys_t = jnp.concatenate([keys_t_ref[0, place] for place in places], axis=1)
        block_grad = mixed_grad[span]
        attended_t = attended_ref[0, block]
        grads_s[:, 3 * features :] += dot_nn(attended_t, block_grad)
        dattn_t = dot_nt(combine_ref[0], block_grad).astype(BF16)
        dattn_wide = dattn_t.astype(F32)
        inverse_sum = inverse_sum_ref[0, block]
        scaled_dattn = flip(dattn_wide * head_spread(inverse_sum, width))
        delta = jnp.sum(
            (dattn_wide * attended_t.astype(F32)).reshape(HEADS, width, BLOCK), axis=1
        )
        row_scale = inverse_sum * scale
        dquery_parts = []
        for pair in range(HEADS // 2):
            heads = slice(pair * 2 * width, (pair + 1) * 2 * width)
            columns = slice(pair * 2 * BLOCK, (pair + 1) * 2 * BLOCK)
            pair_delta = jnp.concatenate(
                [delta[2 * pair : 2 * pair + 1], delta[2 * pair + 1 : 2 * pair + 2]], axis=1
            )
            pair_scale = jnp.concatenate(
                [row_scale[2 * pair : 2 * pair + 1], row_scale[2 * pair + 1 : 2 * pair + 2]], axis=1
            )
            dprobs = dot_nn(pair_group(values, pair, width), pair_columns(dattn_t, pair, width))
            probs = probs_ref[0, block, :, columns].astype(F32)
            dscores = (probs * ((dprobs - pair_delta) * pair_scale)).astype(BF16)
            dscores_s[:, columns] = dscores
            dquery_parts.append(pair_diagonal(dot_nn(block_keys_t[heads], dscores), width))
        dquery_blocks.append(flip(jnp.concatenate(dquery_parts, axis=0)))
        dkeys = dot_nn(dscores_s[...], head_rows(query_ref[0, span], width))
        dvalues = dot_nn(probs_ref[0, block], head_rows(scaled_dattn, width))
        for entry, place in enumerate(places):
            rows = pl.ds(place * BLOCK, BLOCK)
            listed = slice(entry * BLOCK, (entry + 1) * BLOCK)
            dkv_s[rows, :features] += dkeys[listed]
            dkv_s[rows, features:] += dvalues[listed]
    dquery = jnp.concatenate(dquery_blocks, axis=0)
    dkv = dkv_s[...].astype(BF16)
    dquery_ref[0] = dquery
    dkv_ref[0] = dkv
    grads_s[:, :features] += dot_tn(act_ref[0, rim : rim + row_count], dquery)
    grads_s[:, features : 3 * features] += dot_tn(act_ref[0], dkv)

    @pl.when(frame == pl.num_programs(0) - 1)
    def _():
        stack_grads(grads_s[...] * factor, stacked_ref)


def dact_kernel(dquery_ref, dkv_ref, project_ref, dact_ref, to_left_ref, to_right_ref):
    row_count, features = dquery_ref.shape[1:]
    rim = to_left_ref.shape[1]
    dact = dot_nt(dkv_ref[0], project_ref[0, :, features:])
    to_left_ref[0] = dact[:rim].astype(BF16)
    to_right_ref[0] = dact[rim + row_count :].astype(BF16)
    dact_ref[0] = dact[rim : rim + row_count] + dot_nt(
        dquery_ref[0], project_ref[0, :, :features]
    )


def field_kernel(place_ref, wave_ref, mixed_grad_ref, dact_ref, from_left_ref, from_right_ref, *refs):
    *ride_refs, field_ref, mixed_ref = refs
    frame = pl.program_id(0)
    row_count, features = wave_ref.shape[1:]
    normed, inverse = layer_norm(wave_ref[0])
    dact = dact_ref[0] + from_left_ref[0].astype(F32) + from_right_ref[0].astype(F32)
    field_ref[0] = (
        mixed_grad_ref[0].astype(F32) + norm_backward(dact, normed, inverse)
    ).astype(BF16)
    rows = row_count // len(ride_refs)
    lane_groups = features // LANES
    part_rows = pl.num_programs(0) * rows
    for distance, ref in enumerate(ride_refs):
        span = pl.ds(pl.multiple_of((place_ref[0] ^ distance) * rows, GROUP_ROWS), rows)
        for lane_group in range(lane_groups):
            start = ref.shape[0] - (lane_groups - lane_group) * part_rows + frame * rows
            mixed_ref[0, span, lane_group * LANES : (lane_group + 1) * LANES] = ref[
                pl.ds(pl.multiple_of(start, GROUP_ROWS), rows)
            ]


def ordered_sum(me, refs, parts_s):
    rows = parts_s.shape[1]
    for distance, ref in enumerate(refs):
        parts_s[me ^ distance] = ref[:rows]
    total = parts_s[0].astype(F32)
    for part in range(1, len(refs)):
        total = total + parts_s[part].astype(F32)
    return total.astype(BF16)


def cores_kernel(place_ref, space_ref, *refs):
    *ride_refs, kept_ref, sent_ref, parts_s, time_s = refs
    core = place_ref[1] % 2
    time_s[...] = ordered_sum(place_ref[0], ride_refs, parts_s)
    space_half, time_half = space_ref.shape[0] // 2, time_s.shape[0] // 2
    for half, ref in ((core, kept_ref), (1 - core, sent_ref)):
        ref[:space_half] = space_ref[
            pl.ds(pl.multiple_of(half * space_half, GROUP_ROWS), space_half)
        ]
        ref[space_half:] = time_s[pl.ds(pl.multiple_of(half * time_half, GROUP_ROWS), time_half)]


def split_kernel(place_ref, kept_ref, arrived_ref, *refs):
    *part_refs, time_ref, sum_s = refs
    sum_s[...] = (kept_ref[...].astype(F32) + arrived_ref[...].astype(F32)).astype(BF16)
    rows = part_refs[0].shape[0]
    for distance, ref in enumerate(part_refs):
        ref[...] = sum_s[pl.ds(pl.multiple_of((place_ref[0] ^ distance) * rows, GROUP_ROWS), rows)]
    time_ref[...] = sum_s[rows * len(part_refs) :]


def tm_kernel(count_in, place_ref, *refs):
    part_refs, time_ref, out_refs = refs[:count_in], refs[count_in], refs[count_in + 1 : -2]
    parts_s, both_s = refs[-2:]
    rows = time_ref.shape[0]
    both_s[:rows] = ordered_sum(place_ref[0], part_refs, parts_s)
    both_s[rows:] = time_ref[...]
    rows = out_refs[0].shape[0]
    me = place_ref[1] // 2
    for distance, ref in enumerate(out_refs):
        ref[...] = both_s[pl.ds(pl.multiple_of((me ^ distance) * rows, GROUP_ROWS), rows)]


def space_sum_kernel(place_ref, *refs):
    *part_refs, total_ref, parts_s = refs
    total_ref[...] = ordered_sum(place_ref[1] // 2, part_refs, parts_s)


def join_kernel(axis, group, place_ref, *refs):
    *part_refs, joined_ref = refs
    me = place_ref[axis] // group
    for distance, ref in enumerate(part_refs):
        rows = ref.shape[0]
        joined_ref[pl.ds(pl.multiple_of((me ^ distance) * rows, GROUP_ROWS), rows)] = ref[...]


def grads_kernel(time_count, place_ref, own_ref, other_ref, project_ref, combine_ref, halves_s):
    features = combine_ref.shape[1]
    core = place_ref[1] % 2
    halves_s[core] = own_ref[...]
    halves_s[1 - core] = other_ref[...]
    rows = halves_s.shape[1] // time_count // 2

    def place_rows(layer, row, piece):
        while piece.shape[0]:
            group, inner = divmod(row, features)
            taken = min(piece.shape[0], features - inner)
            start = group * LANES
            target, start = (
                (project_ref, start) if start < 3 * features else (combine_ref, start - 3 * features)
            )
            target[layer, inner : inner + taken, start : start + LANES] = piece[:taken].astype(F32)
            row, piece = row + taken, piece[taken:]

    for half in range(2):
        for part in range(time_count):
            start = 2 * part * rows
            place_rows(0, (half * time_count + part) * rows, halves_s[half, start : start + rows])
            place_rows(1, (2 * part + half) * rows, halves_s[half, start + rows : start + 2 * rows])


def stack_grads(grads, stacked_ref):
    features = grads.shape[0]
    for group in range(grads.shape[1] // LANES):
        stacked_ref[group * features : (group + 1) * features] = grads[
            :, group * LANES : (group + 1) * LANES
        ].astype(BF16)


def in_hbm(cells):
    return pltpu.with_memory_space_constraint(cells, pltpu.HBM)


def shift(cells, axis, step):
    count = lax.axis_size(axis)
    if step > 0:
        moves = [(i, i + 1) for i in range(count - 1)]
    else:
        moves = [(i + 1, i) for i in range(count - 1)]
    return lax.ppermute(cells, axis, moves)


def exchange(cells, axis, distance):
    return lax.ppermute(cells, axis, [(i, i ^ distance) for i in range(lax.axis_size(axis))])


def per_device(wave_field, cotangent, block_lists, project_weights, combine_weights):
    frame_count, row_count, features = wave_field.shape
    width = features // HEADS
    scale = 1.0 / math.sqrt(width)
    block_count = row_count // BLOCK
    list_length = block_lists.shape[-1]
    rim = HREACH * BLOCK
    extended = row_count + 2 * rim
    keys_count = list_length * BLOCK
    time_count = lax.axis_size("tm")
    all_frames = frame_count * time_count
    sent_rows = row_count // time_count
    factor = 1.0 / math.sqrt(frame_count * row_count * time_count * lax.axis_size("space"))
    params = pltpu.CompilerParams(vmem_limit_bytes=VMEM_BYTES)

    def whole(*shape):
        return pl.BlockSpec(shape, lambda f: (0,) * len(shape))

    def framed(*shape):
        return pl.BlockSpec((1, *shape), lambda f: (f,) + (0,) * len(shape))

    lists_spec = pl.BlockSpec(memory_space=pltpu.SMEM)
    project_spec = whole(1, features, 3 * features)
    turned_spec = whole(1, 3 * features, features)
    combine_spec = whole(1, features, features)
    part_spec = framed(sent_rows, features)
    whole_part = whole(frame_count, sent_rows, features)
    part_shape = jax.ShapeDtypeStruct((frame_count, sent_rows, features), BF16)
    place = jnp.stack([lax.axis_index("tm"), lax.axis_index("space")]).astype(jnp.int32)
    turned_weights = jnp.swapaxes(project_weights, 1, 2)
    wave_field, cotangent, block_lists, project_weights, combine_weights = (
        in_hbm(cells)
        for cells in (wave_field, cotangent, block_lists, project_weights, combine_weights)
    )

    from_left, from_right = (
        pltpu.with_memory_space_constraint(cells, pltpu.VMEM)
        for cells in (
            shift(wave_field[:, row_count - rim :], "space", 1),
            shift(wave_field[:, :rim], "space", -1),
        )
    )

    def over_tm(pieces):
        return [pieces[0]] + [exchange(pieces[d], "tm", d) for d in range(1, time_count)]

    vmem_spec = pl.BlockSpec(memory_space=pltpu.VMEM)
    cot_parts = pl.pallas_call(
        cut_kernel,
        grid=(1,),
        in_specs=[lists_spec, whole(frame_count, row_count, features)],
        out_specs=[whole_part] * time_count,
        out_shape=[part_shape] * time_count,
        compiler_params=params,
        name="cut_cotangent",
    )(place, cotangent)
    arrived_cot = over_tm(cot_parts)

    act, keys_values, keys_t, queries, probs, inverse_sum, attended, *parts = pl.pallas_call(
        space_forward_kernel,
        grid=(frame_count,),
        in_specs=[
            lists_spec,
            lists_spec,
            framed(rim, features),
            framed(row_count, features),
            framed(rim, features),
            project_spec,
            turned_spec,
            combine_spec,
        ],
        out_specs=[
            framed(extended, features),
            framed(extended, 2 * features),
            framed(extended // BLOCK, features, BLOCK),
            framed(row_count, features),
            framed(block_count, keys_count, HEADS * BLOCK),
            framed(block_count, HEADS, BLOCK),
            framed(block_count, features, BLOCK),
            *[part_spec] * time_count,
        ],
        out_shape=[
            jax.ShapeDtypeStruct((frame_count, extended, features), BF16),
            jax.ShapeDtypeStruct((frame_count, extended, 2 * features), BF16),
            jax.ShapeDtypeStruct((frame_count, extended // BLOCK, features, BLOCK), BF16),
            jax.ShapeDtypeStruct((frame_count, row_count, features), BF16),
            jax.ShapeDtypeStruct((frame_count, block_count, keys_count, HEADS * BLOCK), BF16),
            jax.ShapeDtypeStruct((frame_count, block_count, HEADS, BLOCK), F32),
            jax.ShapeDtypeStruct((frame_count, block_count, features, BLOCK), BF16),
            *[part_shape] * time_count,
        ],
        scratch_shapes=[
            pltpu.VMEM((block_count + 2 * HREACH, features, BLOCK), BF16),
            pltpu.VMEM((row_count, features), BF16),
        ],
        compiler_params=params,
        cost_estimate=cost(40),
        name="space_forward",
    )(
        block_lists,
        place,
        from_left,
        wave_field,
        from_right,
        project_weights,
        turned_weights,
        combine_weights,
    )

    arrived = over_tm(parts)

    def time_body(*refs):
        time_kernel(scale, time_count, *refs)

    def time_grads_body(*refs):
        time_grads_kernel(factor, frame_count, sent_rows, *refs)

    tokens = all_frames * sent_rows
    grad_rows = 4 * features // LANES * features
    ride_rows = grad_rows // time_count + frame_count * sent_rows * features // LANES
    time_shapes = [
        (tokens, features),
        (tokens, 3 * features),
        (features, tokens),
        (tokens, features),
        (tokens, features),
    ]
    time_outs = pl.pallas_call(
        time_body,
        grid=(1,),
        in_specs=[
            *[whole_part] * (2 * time_count),
            pl.BlockSpec((1, features, 3 * features), lambda f: (1, 0, 0)),
            pl.BlockSpec((1, 3 * features, features), lambda f: (1, 0, 0)),
            pl.BlockSpec((1, features, features), lambda f: (1, 0, 0)),
        ],
        out_specs=[*[whole_part] * time_count, *[whole(*shape) for shape in time_shapes]],
        out_shape=[
            *[part_shape] * time_count,
            *[jax.ShapeDtypeStruct(shape, BF16) for shape in time_shapes],
        ],
        compiler_params=params,
        cost_estimate=cost(36),
        name="time_pair",
    )(*arrived, *arrived_cot, project_weights, turned_weights, combine_weights)
    parts, time_kept = time_outs[:time_count], time_outs[time_count:]
    rides = pl.pallas_call(
        time_grads_body,
        in_specs=[lists_spec] + [vmem_spec] * len(time_kept),
        out_specs=[vmem_spec] * time_count,
        out_shape=[jax.ShapeDtypeStruct((ride_rows, LANES), BF16)] * time_count,
        scratch_shapes=[pltpu.VMEM((grad_rows, LANES), BF16)],
        compiler_params=params,
        cost_estimate=cost(6),
        name="time_grads",
    )(place, *time_kept)

    returned = over_tm(parts)
    rides = over_tm(rides)

    def backward_body(*refs):
        space_backward_kernel(scale, factor, time_count, *refs)

    mixed_grad, dquery, dkv, space_grads = pl.pallas_call(
        backward_body,
        grid=(frame_count,),
        in_specs=[
            lists_spec,
            lists_spec,
            *[part_spec] * time_count,
            framed(extended, features),
            framed(extended, 2 * features),
            framed(extended // BLOCK, features, BLOCK),
            framed(row_count, features),
            framed(block_count, keys_count, HEADS * BLOCK),
            framed(block_count, HEADS, BLOCK),
            framed(block_count, features, BLOCK),
            combine_spec,
        ],
        out_specs=[
            framed(row_count, features),
            framed(row_count, features),
            framed(extended, 2 * features),
            whole(grad_rows, LANES),
        ],
        out_shape=[
            jax.ShapeDtypeStruct((frame_count, row_count, features), BF16),
            jax.ShapeDtypeStruct((frame_count, row_count, features), BF16),
            jax.ShapeDtypeStruct((frame_count, extended, 2 * features), BF16),
            jax.ShapeDtypeStruct((grad_rows, LANES), BF16),
        ],
        scratch_shapes=[
            pltpu.VMEM((keys_count, HEADS * BLOCK), BF16),
            pltpu.VMEM((extended, 2 * features), F32),
            pltpu.VMEM((features, 4 * features), F32),
        ],
        compiler_params=params,
        cost_estimate=cost(44),
        name="space_backward",
    )(
        block_lists,
        place,
        *returned,
        act,
        keys_values,
        keys_t,
        queries,
        probs,
        inverse_sum,
        attended,
        combine_weights,
    )

    space_count = lax.axis_size("space") // 2

    def small(body, out_rows, scratch, name, *operands):
        return pl.pallas_call(
            body,
            in_specs=[lists_spec] + [vmem_spec] * len(operands),
            out_specs=[vmem_spec] * len(out_rows),
            out_shape=[jax.ShapeDtypeStruct((rows, LANES), BF16) for rows in out_rows],
            scratch_shapes=[pltpu.VMEM((*shape, LANES), BF16) for shape in scratch],
            compiler_params=params,
            name=name,
        )(place, *operands)

    def over_space(pieces):
        return [pieces[0]] + [
            exchange(pieces[d], "space", 2 * d) for d in range(1, space_count)
        ]

    def tm_body(*refs):
        tm_kernel(time_count, *refs)

    def join_space(*refs):
        join_kernel(1, 2, *refs)

    def join_tm(*refs):
        join_kernel(0, 1, *refs)

    chunk = grad_rows // time_count
    half_rows = grad_rows // 2 + chunk // 2
    kept, sent = small(
        cores_kernel,
        [half_rows] * 2,
        [(time_count, chunk), (chunk,)],
        "add_tm_time",
        space_grads,
        *rides,
    )
    other = exchange(sent, "space", 1)
    dact, to_left, to_right = pl.pallas_call(
        dact_kernel,
        grid=(frame_count,),
        in_specs=[framed(row_count, features), framed(extended, 2 * features), project_spec],
        out_specs=[framed(row_count, features), framed(rim, features), framed(rim, features)],
        out_shape=[
            jax.ShapeDtypeStruct((frame_count, row_count, features), F32),
            jax.ShapeDtypeStruct((frame_count, rim, features), BF16),
            jax.ShapeDtypeStruct((frame_count, rim, features), BF16),
        ],
        compiler_params=params,
        name="space_dact",
    )(dquery, dkv, project_weights)
    edge_left = shift(to_right, "space", 1)
    edge_right = shift(to_left, "space", -1)
    *pieces, time_piece = small(
        split_kernel, [chunk // 2] * (time_count + 1), [(half_rows,)], "add_cores", kept, other
    )
    edge_left, edge_right, *pieces = lax.optimization_barrier(
        (edge_left, edge_right, *over_tm(pieces))
    )
    pieces = small(
        tm_body,
        [chunk // space_count] * space_count,
        [(time_count, chunk // 2), (chunk,)],
        "add_tm_space",
        *pieces,
        time_piece,
    )
    (piece,) = small(
        space_sum_kernel,
        [chunk // space_count],
        [(space_count, chunk // space_count)],
        "add_space",
        *over_space(pieces),
    )
    (piece,) = small(join_space, [chunk], [], "join_space", *over_space([piece] * space_count))
    (own_half,) = small(join_tm, [grad_rows], [], "join_tm", *over_tm([piece] * time_count))
    other_half = exchange(own_half, "space", 1)

    field_grad, mixed_field = pl.pallas_call(
        field_kernel,
        grid=(frame_count,),
        in_specs=[
            lists_spec,
            *[framed(row_count, features)] * 5,
            *[whole(ride_rows, LANES)] * time_count,
        ],
        out_specs=[framed(row_count, features)] * 2,
        out_shape=[jax.ShapeDtypeStruct((frame_count, row_count, features), BF16)] * 2,
        compiler_params=params,
        name="field_grad",
    )(place, wave_field, mixed_grad, dact, edge_left, edge_right, *rides)

    def grads_body(*refs):
        grads_kernel(time_count, *refs)

    project_grad, combine_grad = pl.pallas_call(
        grads_body,
        in_specs=[lists_spec, vmem_spec, vmem_spec],
        out_specs=[vmem_spec, vmem_spec],
        out_shape=[
            jax.ShapeDtypeStruct((2, features, 3 * features), F32),
            jax.ShapeDtypeStruct((2, features, features), F32),
        ],
        scratch_shapes=[pltpu.VMEM((2, grad_rows, LANES), BF16)],
        compiler_params=params,
        name="weight_grads",
    )(place, own_half, other_half)
    return (mixed_field, field_grad, project_grad, combine_grad)


def solution(mesh):
    in_specs = (P("tm", "space", None), P("tm", "space", None), P("tm", "space", None), P(), P())
    out_specs = (P("tm", "space", None), P("tm", "space", None), P(), P())
    return jax.shard_map(
        per_device, mesh=mesh, in_specs=in_specs, out_specs=out_specs, check_vma=False
    )
```

```python
import math

import jax
import jax.numpy as jnp
from jax import lax
from jax.experimental import pallas as pl
from jax.experimental.pallas import tpu as pltpu
from jax.sharding import PartitionSpec as P

HEADS = 8
BLOCK = 128
HREACH = 2
LANES = 128
GROUP_ROWS = 16
VMEM_BYTES = 24 * 1024 * 1024
BF16 = jnp.bfloat16
F32 = jnp.float32


epsilon = 1e-05


def cost(matmuls):
    flops = matmuls * 2 * 1024 * 256 * 512
    return pl.CostEstimate(flops=flops, bytes_accessed=flops // 256, transcendentals=flops // 1024)


def dot_nn(left, right):
    return lax.dot_general(left, right, (((1,), (0,)), ((), ())), preferred_element_type=F32)


def dot_nt(left, right):
    return lax.dot_general(left, right, (((1,), (1,)), ((), ())), preferred_element_type=F32)


def dot_tn(left, right):
    return lax.dot_general(left, right, (((0,), (0,)), ((), ())), preferred_element_type=F32)


def layer_norm(rows):
    widened = rows.astype(F32)
    centered = widened - jnp.mean(widened, axis=-1, keepdims=True)
    inverse = lax.rsqrt(jnp.mean(centered * centered, axis=-1, keepdims=True) + epsilon)
    return (centered * inverse, inverse)


def norm_backward(upstream, normed, inverse):
    mean_grad = jnp.mean(upstream, axis=-1, keepdims=True)
    mean_cross = jnp.mean(upstream * normed, axis=-1, keepdims=True)
    return inverse * (upstream - mean_grad - normed * mean_cross)


def flip(matrix):
    return matrix.astype(BF16).T


def pair_columns(rows_t, pair, width):
    count = rows_t.shape[1]
    base = (pair * 2 * width) // LANES * LANES
    parts = []
    for head in (2 * pair, 2 * pair + 1):
        start = head * width - base
        pieces = []
        if start:
            pieces.append(jnp.zeros((start, count), rows_t.dtype))
        pieces.append(rows_t[head * width : (head + 1) * width])
        if start + width < LANES:
            pieces.append(jnp.zeros((LANES - start - width, count), rows_t.dtype))
        parts.append(jnp.concatenate(pieces, axis=0))
    return jnp.concatenate(parts, axis=1)


def pair_group(matrix, pair, width):
    base = (pair * 2 * width) // LANES * LANES
    return matrix[:, base : base + LANES]


def pair_diagonal(product, width):
    count = product.shape[1] // 2
    return jnp.concatenate([product[:width, :count], product[width:, count:]], axis=0)


def head_rows(rows, width):
    column = lax.broadcasted_iota(jnp.int32, (1, rows.shape[1]), 1) // width
    return jnp.concatenate(
        [rows * (column == head).astype(F32).astype(BF16) for head in range(HEADS)], axis=0
    )


def head_spread(per_head, width):
    return jnp.concatenate(
        [
            jnp.broadcast_to(per_head[head : head + 1], (width, per_head.shape[1]))
            for head in range(HEADS)
        ],
        axis=0,
    )


def listed_blocks(lists_ref, frame, block):
    own = lists_ref[frame, block, 0]
    return [
        lists_ref[frame, block, entry] - own + (block + HREACH)
        for entry in range(lists_ref.shape[2])
    ]


def prepare_kernel(
    place_ref,
    wave_hbm,
    cot_hbm,
    project_hbm,
    combine_hbm,
    wave_ref,
    project_ref,
    turned_ref,
    combine_ref,
    *rest,
):
    *sent_refs, cot_s, sems = rest
    moves = [
        pltpu.make_async_copy(source, target, sems.at[index])
        for index, (source, target) in enumerate(
            (
                (cot_hbm, cot_s),
                (project_hbm, project_ref),
                (wave_hbm, wave_ref),
                (combine_hbm, combine_ref),
            )
        )
    ]
    for move in moves:
        move.start()
    moves[0].wait()
    for distance, ref in enumerate(sent_refs):
        rows = ref.shape[1]
        ref[...] = cot_s[
            :, pl.ds(pl.multiple_of((place_ref[0] ^ distance) * rows, GROUP_ROWS), rows)
        ]
    moves[1].wait()
    for layer in range(2):
        turned_ref[layer] = flip(project_ref[layer])
    moves[2].wait()
    moves[3].wait()


def halo_start(core, rim, row_count, near):
    after = core == 0 if near else core != 0
    return pl.multiple_of(jnp.where(after, rim + row_count, 0), BLOCK)


def space_forward_kernel(
    lists_ref,
    place_ref,
    near_ref,
    far_ref,
    wave_ref,
    project_ref,
    turned_ref,
    combine_ref,
    act_ref,
    kv_ref,
    keys_t_ref,
    query_ref,
    probs_ref,
    inverse_sum_ref,
    attended_ref,
    *rest,
):
    *sent_refs, values_t, mixed_s, extended_s = rest
    me = place_ref[0]
    core = place_ref[1] % 2
    frame_count, row_count, features = wave_ref.shape
    rim = near_ref.shape[1]
    width = features // HEADS
    block_count = row_count // BLOCK
    exponent_scale = math.log2(math.e) / math.sqrt(width)
    for frame in range(frame_count):
        extended_s[frame, rim : rim + row_count] = wave_ref[frame]
        extended_s[frame, pl.ds(halo_start(core, rim, row_count, True), rim)] = near_ref[frame]
        extended_s[frame, pl.ds(halo_start(core, rim, row_count, False), rim)] = far_ref[frame]
        normed, _ = layer_norm(extended_s[frame])
        act = normed.astype(BF16)
        act_ref[frame] = act
        kv_ref[frame] = dot_nn(act, project_ref[0, :, features:]).astype(BF16)
        own_act = act[rim : rim + row_count]
        query_ref[frame] = dot_nn(own_act, project_ref[0, :, :features]).astype(BF16)
        queries_t = dot_nt(turned_ref[0, :features], own_act).astype(BF16)
        all_keys_t = dot_nt(turned_ref[0, features : 2 * features], act).astype(BF16)
        all_values_t = dot_nt(turned_ref[0, 2 * features :], act).astype(BF16)
        for place in range(block_count + 2 * HREACH):
            keys_t_ref[frame, place] = all_keys_t[:, place * BLOCK : (place + 1) * BLOCK]
            values_t[frame, place] = all_values_t[:, place * BLOCK : (place + 1) * BLOCK]
        for block in range(block_count):
            places = listed_blocks(lists_ref, frame, block)
            keys = jnp.concatenate(
                [kv_ref[frame, pl.ds(place * BLOCK, BLOCK), :features] for place in places], axis=0
            )
            block_values_t = jnp.concatenate([values_t[frame, place] for place in places], axis=1)
            query_t = queries_t[:, block * BLOCK : (block + 1) * BLOCK]
            outs = []
            for pair in range(HEADS // 2):
                scores = dot_nn(pair_group(keys, pair, width), pair_columns(query_t, pair, width))
                top = jnp.max(scores, axis=0, keepdims=True)
                exp_scores = jnp.exp2((scores - top) * exponent_scale)
                inverse_sum = 1.0 / jnp.sum(exp_scores, axis=0, keepdims=True)
                probs = exp_scores.astype(BF16)
                probs_ref[frame, block, :, pair * 2 * BLOCK : (pair + 1) * 2 * BLOCK] = probs
                inverse_sum_ref[frame, block, 2 * pair : 2 * pair + 1] = inverse_sum[:, :BLOCK]
                inverse_sum_ref[frame, block, 2 * pair + 1 : 2 * pair + 2] = inverse_sum[:, BLOCK:]
                out = dot_nn(block_values_t[pair * 2 * width : (pair + 1) * 2 * width], probs)
                outs.append(pair_diagonal(out * inverse_sum, width))
            attended_t = jnp.concatenate(outs, axis=0)
            attended_ref[frame, :, block * BLOCK : (block + 1) * BLOCK] = attended_t.astype(BF16)
            mixed_s[frame, block * BLOCK : (block + 1) * BLOCK] = (
                wave_ref[frame, block * BLOCK : (block + 1) * BLOCK].astype(F32)
                + dot_nn(flip(attended_t), combine_ref[0])
            ).astype(BF16)
    for distance, ref in enumerate(sent_refs):
        rows = ref.shape[1]
        ref[...] = mixed_s[
            :, pl.ds(pl.multiple_of((me ^ distance) * rows, GROUP_ROWS), rows)
        ]


def time_kernel(
    scale,
    count_in,
    *refs,
):
    arrived_refs, cot_refs = refs[:count_in], refs[count_in : 2 * count_in]
    project_ref, turned_ref, combine_ref = refs[2 * count_in : 2 * count_in + 3]
    grad_refs = refs[2 * count_in + 3 : 3 * count_in + 3]
    act_ref, dproj_ref, attended_t_ref, cot_ref, mixed_ref = refs[3 * count_in + 3 :]
    part_frames, row_count, features = grad_refs[0].shape
    width = features // HEADS
    count = part_frames * count_in * GROUP_ROWS
    groups = row_count // GROUP_ROWS
    exponent_scale = scale * math.log2(math.e)

    def grouped(part_refs):
        return jnp.concatenate(
            [
                ref[:, group * GROUP_ROWS : (group + 1) * GROUP_ROWS].reshape(
                    part_frames * GROUP_ROWS, features
                )
                for group in range(groups)
                for ref in part_refs
            ],
            axis=0,
        )

    rows = grouped(arrived_refs)
    cot = grouped(cot_refs)
    cot_ref[...] = cot
    normed, inverse = layer_norm(rows)
    act = normed.astype(BF16)
    act_ref[...] = act
    projected = dot_nn(act, project_ref[1]).astype(BF16)
    projected_t = dot_nt(turned_ref[1], act).astype(BF16)
    all_dattn = dot_nt(cot, combine_ref[1]).astype(BF16)
    all_dattn_t = dot_nt(combine_ref[1], cot).astype(BF16)
    key_row = lax.broadcasted_iota(jnp.int32, (count, 2 * count), 0) % GROUP_ROWS
    query_row = lax.broadcasted_iota(jnp.int32, (count, 2 * count), 1) % GROUP_ROWS
    same_row = key_row == query_row
    attended_groups, dquery_groups, dkey_groups, dvalue_groups = [], [], [], []
    for group in range(groups):
        span = slice(group * count, (group + 1) * count)
        queries = projected[span, :features]
        keys = projected[span, features : 2 * features]
        values = projected[span, 2 * features :]
        query_t = projected_t[:features, span]
        keys_t = projected_t[features : 2 * features, span]
        values_t = projected_t[2 * features :, span]
        dattn_t = all_dattn_t[:, span]
        outs, probs_parts, dscore_parts, dquery_parts = [], [], [], []
        for pair in range(HEADS // 2):
            heads = slice(pair * 2 * width, (pair + 1) * 2 * width)
            scores = dot_nn(pair_group(keys, pair, width), pair_columns(query_t, pair, width))
            scores = jnp.where(same_row, scores, -3e38)
            top = jnp.max(scores, axis=0, keepdims=True)
            exp_scores = jnp.exp2((scores - top) * exponent_scale)
            probs = (exp_scores * (1.0 / jnp.sum(exp_scores, axis=0, keepdims=True))).astype(BF16)
            probs_wide = probs.astype(F32)
            outs.append(pair_diagonal(dot_nn(values_t[heads], probs), width))
            dprobs = dot_nn(pair_group(values, pair, width), pair_columns(dattn_t, pair, width))
            delta = jnp.sum(probs_wide * dprobs, axis=0, keepdims=True)
            dscores = (probs_wide * (dprobs - delta) * scale).astype(BF16)
            dquery_parts.append(pair_diagonal(dot_nn(keys_t[heads], dscores), width))
            probs_parts.append(probs)
            dscore_parts.append(dscores)
        attended_groups.append(jnp.concatenate(outs, axis=0).astype(BF16))
        dquery_groups.append(flip(jnp.concatenate(dquery_parts, axis=0)))
        dkey_groups.append(
            dot_nn(jnp.concatenate(dscore_parts, axis=1), head_rows(queries, width)).astype(BF16)
        )
        dvalue_groups.append(
            dot_nn(jnp.concatenate(probs_parts, axis=1), head_rows(all_dattn[span], width)).astype(BF16)
        )
    attended = jnp.concatenate([flip(attended_t) for attended_t in attended_groups], axis=0)
    mixed_ref[...] = (rows.astype(F32) + dot_nn(attended, combine_ref[1])).astype(BF16)
    attended_t_ref[...] = jnp.concatenate(attended_groups, axis=1)
    dproj = jnp.concatenate(
        [jnp.concatenate(parts, axis=0) for parts in (dquery_groups, dkey_groups, dvalue_groups)],
        axis=1,
    )
    dproj_ref[...] = dproj
    dact = dot_nt(dproj, project_ref[1])
    mixed_grad = (cot.astype(F32) + norm_backward(dact, normed, inverse)).astype(BF16)
    for part, ref in enumerate(grad_refs):
        for group in range(groups):
            span = slice(group * GROUP_ROWS, (group + 1) * GROUP_ROWS)
            for frame in range(part_frames):
                start = ((group * count_in + part) * part_frames + frame) * GROUP_ROWS
                ref[frame, span] = mixed_grad[start : start + GROUP_ROWS]


def time_grads_kernel(
    factor, part_frames, row_count, place_ref, act_ref, dproj_ref, attended_t_ref, cot_ref, mixed_ref, *refs
):
    *ride_refs, stacked_s = refs
    count_in = len(ride_refs)
    features = act_ref.shape[1]
    groups = row_count // GROUP_ROWS
    stack_grads(
        [dot_tn(act_ref[...], dproj_ref[...]), dot_nn(attended_t_ref[...], cot_ref[...])],
        factor,
        stacked_s,
    )
    chunk = stacked_s.shape[0] // count_in
    part_rows = part_frames * row_count
    for part, ref in enumerate(ride_refs):
        for group in range(groups):
            for frame in range(part_frames):
                start = ((group * count_in + part) * part_frames + frame) * GROUP_ROWS
                for lane_group in range(features // LANES):
                    row = chunk + lane_group * part_rows + frame * row_count + group * GROUP_ROWS
                    ref[row : row + GROUP_ROWS] = mixed_ref[
                        start : start + GROUP_ROWS, lane_group * LANES : (lane_group + 1) * LANES
                    ]
        ref[:chunk] = stacked_s[
            pl.ds(pl.multiple_of((place_ref[0] ^ part) * chunk, GROUP_ROWS), chunk)
        ]


def space_backward_kernel(
    scale,
    factor,
    count_in,
    lists_ref,
    place_ref,
    *refs,
):
    returned_refs = refs[:count_in]
    (
        act_ref,
        kv_ref,
        keys_t_ref,
        query_ref,
        probs_ref,
        inverse_sum_ref,
        attended_ref,
        combine_ref,
        mixed_grad_ref,
        dquery_ref,
        dkv_ref,
        stacked_ref,
        dscores_s,
        dkv_s,
    ) = refs[count_in:]
    me = place_ref[0]
    frame_count, row_count, features = mixed_grad_ref.shape
    width = features // HEADS
    block_count = row_count // BLOCK
    rim = HREACH * BLOCK
    for distance, ref in enumerate(returned_refs):
        rows = ref.shape[1]
        span = pl.ds(pl.multiple_of((me ^ distance) * rows, GROUP_ROWS), rows)
        mixed_grad_ref[:, span] = ref[...]
    for frame in range(frame_count):
        dkv_s[frame] = jnp.zeros(dkv_s.shape[1:], F32)
        all_dattn_t = dot_nt(combine_ref[0], mixed_grad_ref[frame]).astype(BF16)
        for block in range(block_count):
            span = slice(block * BLOCK, (block + 1) * BLOCK)
            places = listed_blocks(lists_ref, frame, block)
            values = jnp.concatenate(
                [kv_ref[frame, pl.ds(place * BLOCK, BLOCK), features:] for place in places], axis=0
            )
            block_keys_t = jnp.concatenate([keys_t_ref[frame, place] for place in places], axis=1)
            dattn_t = all_dattn_t[:, span]
            dattn_wide = dattn_t.astype(F32)
            inverse_sum = inverse_sum_ref[frame, block]
            scaled_dattn = flip(dattn_wide * head_spread(inverse_sum, width))
            delta = jnp.sum(
                (dattn_wide * attended_ref[frame, :, span].astype(F32)).reshape(
                    HEADS, width, BLOCK
                ),
                axis=1,
            )
            row_scale = inverse_sum * scale
            dquery_parts = []
            for pair in range(HEADS // 2):
                heads = slice(pair * 2 * width, (pair + 1) * 2 * width)
                columns = slice(pair * 2 * BLOCK, (pair + 1) * 2 * BLOCK)
                pair_delta = jnp.concatenate(
                    [delta[2 * pair : 2 * pair + 1], delta[2 * pair + 1 : 2 * pair + 2]], axis=1
                )
                pair_scale = jnp.concatenate(
                    [row_scale[2 * pair : 2 * pair + 1], row_scale[2 * pair + 1 : 2 * pair + 2]],
                    axis=1,
                )
                dprobs = dot_nn(pair_group(values, pair, width), pair_columns(dattn_t, pair, width))
                probs = probs_ref[frame, block, :, columns].astype(F32)
                dscores = (probs * ((dprobs - pair_delta) * pair_scale)).astype(BF16)
                dscores_s[frame, block, :, columns] = dscores
                dquery_parts.append(pair_diagonal(dot_nn(block_keys_t[heads], dscores), width))
            dquery_ref[frame, span] = flip(jnp.concatenate(dquery_parts, axis=0))
            dkeys = dot_nn(dscores_s[frame, block], head_rows(query_ref[frame, span], width))
            dvalues = dot_nn(probs_ref[frame, block], head_rows(scaled_dattn, width))
            for entry, place in enumerate(places):
                rows = pl.ds(place * BLOCK, BLOCK)
                listed = slice(entry * BLOCK, (entry + 1) * BLOCK)
                dkv_s[frame, rows, :features] += dkeys[listed]
                dkv_s[frame, rows, features:] += dvalues[listed]
        dkv_ref[frame] = dkv_s[frame].astype(BF16)
    extended = dkv_ref.shape[1]
    act = act_ref[...]
    own_act = act[:, rim : rim + row_count].reshape(frame_count * row_count, features)
    stack_grads(
        [
            dot_tn(own_act, dquery_ref[...].reshape(frame_count * row_count, features)),
            dot_tn(
                act.reshape(frame_count * extended, features),
                dkv_ref[...].reshape(frame_count * extended, 2 * features),
            ),
            sum(
                dot_nn(attended_ref[frame], mixed_grad_ref[frame]) for frame in range(frame_count)
            ),
        ],
        factor,
        stacked_ref,
    )


def dact_kernel(place_ref, dquery_ref, dkv_ref, project_ref, dact_ref, near_ref, far_ref, dact_s):
    frame_count, row_count, features = dquery_ref.shape
    rim = near_ref.shape[1]
    core = place_ref[1] % 2
    for frame in range(frame_count):
        dact = dot_nt(dkv_ref[frame], project_ref[0, :, features:])
        dact_s[frame] = dact.astype(BF16)
        dact_ref[frame] = dact[rim : rim + row_count] + dot_nt(
            dquery_ref[frame], project_ref[0, :, :features]
        )
    near_ref[...] = dact_s[:, pl.ds(halo_start(core, rim, row_count, True), rim)]
    far_ref[...] = dact_s[:, pl.ds(halo_start(core, rim, row_count, False), rim)]


def field_kernel(place_ref, wave_ref, mixed_grad_ref, dact_ref, near_ref, far_ref, *refs):
    *ride_refs, field_ref, mixed_ref = refs
    frame_count, row_count, features = wave_ref.shape
    rows = row_count // len(ride_refs)
    lane_groups = features // LANES
    part_rows = frame_count * rows
    for frame in range(frame_count):
        normed, inverse = layer_norm(wave_ref[frame])
        dact = dact_ref[frame] + near_ref[frame].astype(F32) + far_ref[frame].astype(F32)
        field_ref[frame] = (
            mixed_grad_ref[frame].astype(F32) + norm_backward(dact, normed, inverse)
        ).astype(BF16)
        for distance, ref in enumerate(ride_refs):
            span = pl.ds(pl.multiple_of((place_ref[0] ^ distance) * rows, GROUP_ROWS), rows)
            for lane_group in range(lane_groups):
                start = ref.shape[0] - (lane_groups - lane_group) * part_rows + frame * rows
                mixed_ref[frame, span, lane_group * LANES : (lane_group + 1) * LANES] = ref[
                    start : start + rows
                ]


def ordered_sum(me, refs, parts_s):
    rows = parts_s.shape[1]
    for distance, ref in enumerate(refs):
        parts_s[me ^ distance] = ref[:rows]
    total = parts_s[0].astype(F32)
    for part in range(1, len(refs)):
        total = total + parts_s[part].astype(F32)
    return total.astype(BF16)


def cores_kernel(place_ref, space_ref, *refs):
    *ride_refs, kept_ref, sent_ref, parts_s, time_s = refs
    core = place_ref[1] % 2
    time_s[...] = ordered_sum(place_ref[0], ride_refs, parts_s)
    space_half, time_half = space_ref.shape[0] // 2, time_s.shape[0] // 2
    for half, ref in ((core, kept_ref), (1 - core, sent_ref)):
        ref[:space_half] = space_ref[
            pl.ds(pl.multiple_of(half * space_half, GROUP_ROWS), space_half)
        ]
        ref[space_half:] = time_s[pl.ds(pl.multiple_of(half * time_half, GROUP_ROWS), time_half)]


def split_kernel(place_ref, kept_ref, arrived_ref, *refs):
    *part_refs, time_ref, sum_s = refs
    sum_s[...] = (kept_ref[...].astype(F32) + arrived_ref[...].astype(F32)).astype(BF16)
    rows = part_refs[0].shape[0]
    for distance, ref in enumerate(part_refs):
        ref[...] = sum_s[pl.ds(pl.multiple_of((place_ref[0] ^ distance) * rows, GROUP_ROWS), rows)]
    time_ref[...] = sum_s[rows * len(part_refs) :]


def tm_sum_kernel(place_ref, *refs):
    *part_refs, total_ref, parts_s = refs
    total_ref[...] = ordered_sum(place_ref[0], part_refs, parts_s)


def space_sum_kernel(place_ref, *refs):
    *part_refs, total_ref, parts_s = refs
    count_in = len(part_refs) // 2
    rows = parts_s.shape[1]
    me = place_ref[1] // 2
    total_ref[:rows] = ordered_sum(me, part_refs[:count_in], parts_s)
    total_ref[rows:] = ordered_sum(me, part_refs[count_in:], parts_s)


def join_kernel(place_ref, *refs):
    *part_refs, joined_ref = refs
    me = place_ref[0]
    for distance, ref in enumerate(part_refs):
        rows = ref.shape[0]
        joined_ref[pl.ds(pl.multiple_of((me ^ distance) * rows, GROUP_ROWS), rows)] = ref[...]


def grads_kernel(time_count, place_ref, own_ref, other_ref, project_ref, combine_ref, halves_s):
    features = combine_ref.shape[1]
    core = place_ref[1] % 2
    halves_s[core] = own_ref[...]
    halves_s[1 - core] = other_ref[...]
    rows = halves_s.shape[1] // time_count // 2

    def place_rows(layer, row, piece):
        while piece.shape[0]:
            group, inner = divmod(row, features)
            taken = min(piece.shape[0], features - inner)
            start = group * LANES
            target, start = (
                (project_ref, start) if start < 3 * features else (combine_ref, start - 3 * features)
            )
            target[layer, inner : inner + taken, start : start + LANES] = piece[:taken].astype(F32)
            row, piece = row + taken, piece[taken:]

    for half in range(2):
        for part in range(time_count):
            start = 2 * part * rows
            place_rows(0, (half * time_count + part) * rows, halves_s[half, start : start + rows])
            place_rows(1, (2 * part + half) * rows, halves_s[half, start + rows : start + 2 * rows])


def stack_grads(grads, factor, stacked_ref):
    row = 0
    for grad in grads:
        for lane in range(0, grad.shape[1], LANES):
            stacked_ref[row : row + grad.shape[0]] = (
                grad[:, lane : lane + LANES] * factor
            ).astype(BF16)
            row += grad.shape[0]


def in_hbm(cells):
    return pltpu.with_memory_space_constraint(cells, pltpu.HBM)


def swap_far(cells, axis):
    pairs = [(i, i + 1) for i in range(1, lax.axis_size(axis) - 1, 2)]
    return lax.ppermute(cells, axis, pairs + [(j, i) for i, j in pairs])


def exchange(cells, axis, distance):
    return lax.ppermute(cells, axis, [(i, i ^ distance) for i in range(lax.axis_size(axis))])


def per_device(wave_field, cotangent, block_lists, project_weights, combine_weights):
    frame_count, row_count, features = wave_field.shape
    width = features // HEADS
    scale = 1.0 / math.sqrt(width)
    block_count = row_count // BLOCK
    list_length = block_lists.shape[-1]
    rim = HREACH * BLOCK
    extended = row_count + 2 * rim
    keys_count = list_length * BLOCK
    time_count = lax.axis_size("tm")
    all_frames = frame_count * time_count
    sent_rows = row_count // time_count
    factor = 1.0 / math.sqrt(frame_count * row_count * time_count * lax.axis_size("space"))
    space_count = lax.axis_size("space") // 2
    grad_rows = 4 * features // LANES * features
    chunk = grad_rows // time_count
    half_rows = grad_rows // 2 + chunk // 2
    ride_rows = chunk + frame_count * sent_rows * features // LANES
    tokens = all_frames * sent_rows
    places = block_count + 2 * HREACH
    smem_spec = pl.BlockSpec(memory_space=pltpu.SMEM)
    vmem_spec = pl.BlockSpec(memory_space=pltpu.VMEM)
    hbm_spec = pl.BlockSpec(memory_space=pl.ANY)

    def call(body, name, scalars, operands, outs, scratch=(), matmuls=1, in_spec=vmem_spec):
        def typed(shape):
            return (shape[:-1], shape[-1]) if not isinstance(shape[-1], int) else (shape, BF16)

        return pl.pallas_call(
            body,
            in_specs=[smem_spec] * len(scalars) + [in_spec] * len(operands),
            out_specs=[vmem_spec] * len(outs),
            out_shape=[jax.ShapeDtypeStruct(*typed(shape)) for shape in outs],
            scratch_shapes=[
                pltpu.VMEM(*typed(shape)) if isinstance(shape, tuple) else shape
                for shape in scratch
            ],
            compiler_params=pltpu.CompilerParams(vmem_limit_bytes=VMEM_BYTES),
            cost_estimate=cost(matmuls),
            name=name,
        )(*scalars, *operands)

    def over_tm(pieces):
        return [pieces[0]] + [exchange(pieces[d], "tm", d) for d in range(1, time_count)]

    def over_space(piece):
        return [piece] + [exchange(piece, "space", 2 * d) for d in range(1, space_count)]

    own = (frame_count, row_count, features)
    part = (frame_count, sent_rows, features)
    near = exchange(wave_field, "space", 1)
    far = swap_far(wave_field, "space")
    place = jnp.stack([lax.axis_index("tm"), lax.axis_index("space")]).astype(jnp.int32)
    wave, project, turned, combine, *cot_parts = call(
        prepare_kernel,
        "prepare",
        [place],
        [in_hbm(cells) for cells in (wave_field, cotangent, project_weights, combine_weights)],
        [
            own,
            (2, features, 3 * features),
            (2, 3 * features, features),
            (2, features, features),
            *[part] * time_count,
        ],
        [own, pltpu.SemaphoreType.DMA((4,))],
        matmuls=8,
        in_spec=hbm_spec,
    )
    arrived_cot = over_tm(cot_parts)
    block_lists = in_hbm(block_lists)

    outs = call(
        space_forward_kernel,
        "space_forward",
        [block_lists, place],
        [near, far, wave, project, turned, combine],
        [
            (frame_count, extended, features),
            (frame_count, extended, 2 * features),
            (frame_count, places, features, BLOCK),
            own,
            (frame_count, block_count, keys_count, HEADS * BLOCK),
            (frame_count, block_count, HEADS, BLOCK, F32),
            (frame_count, features, row_count),
            *[part] * time_count,
        ],
        [(frame_count, places, features, BLOCK), own, (frame_count, extended, features)],
        matmuls=40,
    )
    kept_space, parts = outs[:7], outs[7:]
    arrived = over_tm(parts)

    def time_body(*refs):
        time_kernel(scale, time_count, *refs)

    outs = call(
        time_body,
        "time_pair",
        [],
        [*arrived, *arrived_cot, project, turned, combine],
        [
            *[part] * time_count,
            (tokens, features),
            (tokens, 3 * features),
            (features, tokens),
            (tokens, features),
            (tokens, features),
        ],
        matmuls=36,
    )
    parts, kept_time = outs[:time_count], outs[time_count:]

    def time_grads_body(*refs):
        time_grads_kernel(factor, frame_count, sent_rows, *refs)

    rides = call(
        time_grads_body,
        "time_grads",
        [place],
        kept_time,
        [(ride_rows, LANES)] * time_count,
        [(grad_rows, LANES)],
        matmuls=6,
    )
    returned = over_tm(parts)
    rides = over_tm(rides)

    def backward_body(*refs):
        space_backward_kernel(scale, factor, time_count, *refs)

    mixed_grad, dquery, dkv, space_grads = call(
        backward_body,
        "space_backward",
        [block_lists, place],
        [*returned, *kept_space, combine],
        [own, own, (frame_count, extended, 2 * features), (grad_rows, LANES)],
        [
            (frame_count, block_count, keys_count, HEADS * BLOCK),
            (frame_count, extended, 2 * features, F32),
        ],
        matmuls=44,
    )

    kept, sent = call(
        cores_kernel,
        "add_tm_time",
        [place],
        [space_grads, *rides],
        [(half_rows, LANES)] * 2,
        [(time_count, chunk, LANES), (chunk, LANES)],
    )
    other = exchange(sent, "space", 1)
    dact, to_near, to_far = call(
        dact_kernel,
        "space_dact",
        [place],
        [dquery, dkv, project],
        [(*own, F32), (frame_count, rim, features), (frame_count, rim, features)],
        [(frame_count, extended, features)],
        matmuls=3,
    )
    *space_pieces, time_piece = call(
        split_kernel,
        "add_cores",
        [place],
        [kept, other],
        [(chunk // 2, LANES)] * (time_count + 1),
        [(half_rows, LANES)],
    )
    to_near, to_far, *space_pieces = lax.optimization_barrier((to_near, to_far, *space_pieces))
    space_pieces = over_tm(space_pieces)
    time_pieces = over_space(time_piece)
    from_near = exchange(to_near, "space", 1)
    from_far = swap_far(to_far, "space")
    (space_piece,) = call(
        tm_sum_kernel,
        "add_tm_space",
        [place],
        space_pieces,
        [(chunk // 2, LANES)],
        [(time_count, chunk // 2, LANES)],
    )
    (piece,) = call(
        space_sum_kernel,
        "add_space",
        [place],
        over_space(space_piece) + time_pieces,
        [(chunk, LANES)],
        [(space_count, chunk // 2, LANES)],
    )
    joined = over_tm([piece] * time_count)
    field_grad, mixed_field = call(
        field_kernel,
        "field_grad",
        [place],
        [wave, mixed_grad, dact, from_near, from_far, *rides],
        [own, own],
        matmuls=3,
    )
    field_grad, mixed_field, *joined = lax.optimization_barrier((field_grad, mixed_field, *joined))
    (own_half,) = call(join_kernel, "join_tm", [place], joined, [(grad_rows, LANES)])
    other_half = exchange(own_half, "space", 1)

    def grads_body(*refs):
        grads_kernel(time_count, *refs)

    project_grad, combine_grad = call(
        grads_body,
        "weight_grads",
        [place],
        [own_half, other_half],
        [(2, features, 3 * features, F32), (2, features, features, F32)],
        [(2, grad_rows, LANES)],
    )
    return (mixed_field, field_grad, project_grad, combine_grad)


def solution(mesh):
    in_specs = (P("tm", "space", None), P("tm", "space", None), P("tm", "space", None), P(), P())
    out_specs = (P("tm", "space", None), P("tm", "space", None), P(), P())
    return jax.shard_map(
        per_device, mesh=mesh, in_specs=in_specs, out_specs=out_specs, check_vma=False
    )
```

```python
import math

import jax
import jax.numpy as jnp
from jax import lax
from jax.experimental import pallas as pl
from jax.experimental.pallas import tpu as pltpu
from jax.sharding import PartitionSpec as P

HEADS = 8
BLOCK = 128
HREACH = 2
LANES = 128
GROUP_ROWS = 16
VMEM_BYTES = 24 * 1024 * 1024
BF16 = jnp.bfloat16
F32 = jnp.float32


epsilon = 1e-05


def cost(matmuls):
    flops = matmuls * 2 * 1024 * 256 * 512
    return pl.CostEstimate(flops=flops, bytes_accessed=flops // 256, transcendentals=flops // 1024)


def dot_nn(left, right):
    return lax.dot_general(left, right, (((1,), (0,)), ((), ())), preferred_element_type=F32)


def dot_nt(left, right):
    return lax.dot_general(left, right, (((1,), (1,)), ((), ())), preferred_element_type=F32)


def dot_tn(left, right):
    return lax.dot_general(left, right, (((0,), (0,)), ((), ())), preferred_element_type=F32)


def layer_norm(rows):
    widened = rows.astype(F32)
    centered = widened - jnp.mean(widened, axis=-1, keepdims=True)
    inverse = lax.rsqrt(jnp.mean(centered * centered, axis=-1, keepdims=True) + epsilon)
    return (centered * inverse, inverse)


def norm_backward(upstream, normed, inverse):
    mean_grad = jnp.mean(upstream, axis=-1, keepdims=True)
    mean_cross = jnp.mean(upstream * normed, axis=-1, keepdims=True)
    return inverse * (upstream - mean_grad - normed * mean_cross)


def flip(matrix):
    return matrix.astype(BF16).T


def pair_columns(rows_t, pair, width):
    count = rows_t.shape[1]
    base = (pair * 2 * width) // LANES * LANES
    parts = []
    for head in (2 * pair, 2 * pair + 1):
        start = head * width - base
        pieces = []
        if start:
            pieces.append(jnp.zeros((start, count), rows_t.dtype))
        pieces.append(rows_t[head * width : (head + 1) * width])
        if start + width < LANES:
            pieces.append(jnp.zeros((LANES - start - width, count), rows_t.dtype))
        parts.append(jnp.concatenate(pieces, axis=0))
    return jnp.concatenate(parts, axis=1)


def pair_group(matrix, pair, width):
    base = (pair * 2 * width) // LANES * LANES
    return matrix[:, base : base + LANES]


def pair_diagonal(product, width):
    count = product.shape[1] // 2
    return jnp.concatenate([product[:width, :count], product[width:, count:]], axis=0)


def head_rows(rows, width):
    column = lax.broadcasted_iota(jnp.int32, (1, rows.shape[1]), 1) // width
    return jnp.concatenate(
        [rows * (column == head).astype(F32).astype(BF16) for head in range(HEADS)], axis=0
    )


def head_spread(per_head, width):
    return jnp.concatenate(
        [
            jnp.broadcast_to(per_head[head : head + 1], (width, per_head.shape[1]))
            for head in range(HEADS)
        ],
        axis=0,
    )


def listed_blocks(lists_ref, frame, block):
    own = lists_ref[frame, block, 0]
    return [
        lists_ref[frame, block, entry] - own + (block + HREACH)
        for entry in range(lists_ref.shape[2])
    ]


def prepare_kernel(
    wave_hbm,
    cot_hbm,
    project_hbm,
    combine_hbm,
    wave_ref,
    project_ref,
    turned_ref,
    combine_ref,
    cot_ref,
    sems,
):
    moves = [
        pltpu.make_async_copy(source, target, sems.at[index])
        for index, (source, target) in enumerate(
            (
                (project_hbm, project_ref),
                (wave_hbm, wave_ref),
                (combine_hbm, combine_ref),
                (cot_hbm, cot_ref),
            )
        )
    ]
    for move in moves:
        move.start()
    moves[0].wait()
    for layer in range(2):
        turned_ref[layer] = flip(project_ref[layer])
    for move in moves[1:]:
        move.wait()


def halo_start(core, rim, row_count, near):
    after = core == 0 if near else core != 0
    return pl.multiple_of(jnp.where(after, rim + row_count, 0), BLOCK)


def space_forward_kernel(
    lists_ref,
    place_ref,
    near_ref,
    far_ref,
    wave_ref,
    cot_ref,
    project_ref,
    turned_ref,
    combine_ref,
    act_ref,
    kv_ref,
    keys_t_ref,
    query_ref,
    probs_ref,
    inverse_sum_ref,
    attended_ref,
    *rest,
):
    *sent_refs, values_t, mixed_s, extended_s = rest
    me = place_ref[0]
    core = place_ref[1] % 2
    frame_count, row_count, features = wave_ref.shape
    rim = near_ref.shape[1]
    width = features // HEADS
    block_count = row_count // BLOCK
    exponent_scale = math.log2(math.e) / math.sqrt(width)
    for frame in range(frame_count):
        extended_s[frame, rim : rim + row_count] = wave_ref[frame]
        extended_s[frame, pl.ds(halo_start(core, rim, row_count, True), rim)] = near_ref[frame]
        extended_s[frame, pl.ds(halo_start(core, rim, row_count, False), rim)] = far_ref[frame]
        normed, _ = layer_norm(extended_s[frame])
        act = normed.astype(BF16)
        act_ref[frame] = act
        kv_ref[frame] = dot_nn(act, project_ref[0, :, features:]).astype(BF16)
        own_act = act[rim : rim + row_count]
        query_ref[frame] = dot_nn(own_act, project_ref[0, :, :features]).astype(BF16)
        queries_t = dot_nt(turned_ref[0, :features], own_act).astype(BF16)
        all_keys_t = dot_nt(turned_ref[0, features : 2 * features], act).astype(BF16)
        all_values_t = dot_nt(turned_ref[0, 2 * features :], act).astype(BF16)
        for place in range(block_count + 2 * HREACH):
            keys_t_ref[frame, place] = all_keys_t[:, place * BLOCK : (place + 1) * BLOCK]
            values_t[frame, place] = all_values_t[:, place * BLOCK : (place + 1) * BLOCK]
        for block in range(block_count):
            places = listed_blocks(lists_ref, frame, block)
            keys = jnp.concatenate(
                [kv_ref[frame, pl.ds(place * BLOCK, BLOCK), :features] for place in places], axis=0
            )
            block_values_t = jnp.concatenate([values_t[frame, place] for place in places], axis=1)
            query_t = queries_t[:, block * BLOCK : (block + 1) * BLOCK]
            outs = []
            for pair in range(HEADS // 2):
                scores = dot_nn(pair_group(keys, pair, width), pair_columns(query_t, pair, width))
                top = jnp.max(scores, axis=0, keepdims=True)
                exp_scores = jnp.exp2((scores - top) * exponent_scale)
                inverse_sum = 1.0 / jnp.sum(exp_scores, axis=0, keepdims=True)
                probs = exp_scores.astype(BF16)
                probs_ref[frame, block, :, pair * 2 * BLOCK : (pair + 1) * 2 * BLOCK] = probs
                inverse_sum_ref[frame, block, 2 * pair : 2 * pair + 1] = inverse_sum[:, :BLOCK]
                inverse_sum_ref[frame, block, 2 * pair + 1 : 2 * pair + 2] = inverse_sum[:, BLOCK:]
                out = dot_nn(block_values_t[pair * 2 * width : (pair + 1) * 2 * width], probs)
                outs.append(pair_diagonal(out * inverse_sum, width))
            attended_t = jnp.concatenate(outs, axis=0)
            attended_ref[frame, :, block * BLOCK : (block + 1) * BLOCK] = attended_t.astype(BF16)
            mixed_s[frame, block * BLOCK : (block + 1) * BLOCK] = (
                wave_ref[frame, block * BLOCK : (block + 1) * BLOCK].astype(F32)
                + dot_nn(flip(attended_t), combine_ref[0])
            ).astype(BF16)
    for distance, ref in enumerate(sent_refs):
        rows = ref.shape[1]
        span = pl.ds(pl.multiple_of((me ^ distance) * rows, GROUP_ROWS), rows)
        ref[:, :, :features] = mixed_s[:, span]
        ref[:, :, features:] = cot_ref[:, span]


def time_kernel(
    scale,
    count_in,
    *refs,
):
    arrived_refs = refs[:count_in]
    project_ref, turned_ref, combine_ref = refs[count_in : count_in + 3]
    grad_refs = refs[count_in + 3 : 2 * count_in + 3]
    act_ref, dproj_ref, attended_t_ref, cot_ref, mixed_ref = refs[2 * count_in + 3 :]
    part_frames, row_count, features = grad_refs[0].shape
    width = features // HEADS
    count = part_frames * count_in * GROUP_ROWS
    groups = row_count // GROUP_ROWS
    exponent_scale = scale * math.log2(math.e)

    def grouped(lanes):
        return jnp.concatenate(
            [
                ref[:, group * GROUP_ROWS : (group + 1) * GROUP_ROWS, lanes].reshape(
                    part_frames * GROUP_ROWS, features
                )
                for group in range(groups)
                for ref in arrived_refs
            ],
            axis=0,
        )

    rows = grouped(slice(0, features))
    cot = grouped(slice(features, 2 * features))
    cot_ref[...] = cot
    normed, inverse = layer_norm(rows)
    act = normed.astype(BF16)
    act_ref[...] = act
    projected = dot_nn(act, project_ref[1]).astype(BF16)
    projected_t = dot_nt(turned_ref[1], act).astype(BF16)
    all_dattn = dot_nt(cot, combine_ref[1]).astype(BF16)
    all_dattn_t = dot_nt(combine_ref[1], cot).astype(BF16)
    key_row = lax.broadcasted_iota(jnp.int32, (count, 2 * count), 0) % GROUP_ROWS
    query_row = lax.broadcasted_iota(jnp.int32, (count, 2 * count), 1) % GROUP_ROWS
    same_row = key_row == query_row
    attended_groups, dquery_groups, dkey_groups, dvalue_groups = [], [], [], []
    for group in range(groups):
        span = slice(group * count, (group + 1) * count)
        queries = projected[span, :features]
        keys = projected[span, features : 2 * features]
        values = projected[span, 2 * features :]
        query_t = projected_t[:features, span]
        keys_t = projected_t[features : 2 * features, span]
        values_t = projected_t[2 * features :, span]
        dattn_t = all_dattn_t[:, span]
        outs, probs_parts, dscore_parts, dquery_parts = [], [], [], []
        for pair in range(HEADS // 2):
            heads = slice(pair * 2 * width, (pair + 1) * 2 * width)
            scores = dot_nn(pair_group(keys, pair, width), pair_columns(query_t, pair, width))
            scores = jnp.where(same_row, scores, -3e38)
            top = jnp.max(scores, axis=0, keepdims=True)
            exp_scores = jnp.exp2((scores - top) * exponent_scale)
            probs = (exp_scores * (1.0 / jnp.sum(exp_scores, axis=0, keepdims=True))).astype(BF16)
            probs_wide = probs.astype(F32)
            outs.append(pair_diagonal(dot_nn(values_t[heads], probs), width))
            dprobs = dot_nn(pair_group(values, pair, width), pair_columns(dattn_t, pair, width))
            delta = jnp.sum(probs_wide * dprobs, axis=0, keepdims=True)
            dscores = (probs_wide * (dprobs - delta) * scale).astype(BF16)
            dquery_parts.append(pair_diagonal(dot_nn(keys_t[heads], dscores), width))
            probs_parts.append(probs)
            dscore_parts.append(dscores)
        attended_groups.append(jnp.concatenate(outs, axis=0).astype(BF16))
        dquery_groups.append(flip(jnp.concatenate(dquery_parts, axis=0)))
        dkey_groups.append(
            dot_nn(jnp.concatenate(dscore_parts, axis=1), head_rows(queries, width)).astype(BF16)
        )
        dvalue_groups.append(
            dot_nn(jnp.concatenate(probs_parts, axis=1), head_rows(all_dattn[span], width)).astype(BF16)
        )
    attended = jnp.concatenate([flip(attended_t) for attended_t in attended_groups], axis=0)
    mixed_ref[...] = (rows.astype(F32) + dot_nn(attended, combine_ref[1])).astype(BF16)
    attended_t_ref[...] = jnp.concatenate(attended_groups, axis=1)
    dproj = jnp.concatenate(
        [jnp.concatenate(parts, axis=0) for parts in (dquery_groups, dkey_groups, dvalue_groups)],
        axis=1,
    )
    dproj_ref[...] = dproj
    dact = dot_nt(dproj, project_ref[1])
    mixed_grad = (cot.astype(F32) + norm_backward(dact, normed, inverse)).astype(BF16)
    for part, ref in enumerate(grad_refs):
        for group in range(groups):
            span = slice(group * GROUP_ROWS, (group + 1) * GROUP_ROWS)
            for frame in range(part_frames):
                start = ((group * count_in + part) * part_frames + frame) * GROUP_ROWS
                ref[frame, span] = mixed_grad[start : start + GROUP_ROWS]


def time_grads_kernel(
    factor, part_frames, row_count, place_ref, act_ref, dproj_ref, attended_t_ref, cot_ref, mixed_ref, *refs
):
    *ride_refs, stacked_s = refs
    count_in = len(ride_refs)
    features = act_ref.shape[1]
    groups = row_count // GROUP_ROWS
    stack_grads(
        [dot_tn(act_ref[...], dproj_ref[...]), dot_nn(attended_t_ref[...], cot_ref[...])],
        factor,
        stacked_s,
    )
    chunk = stacked_s.shape[0] // count_in
    part_rows = part_frames * row_count
    for part, ref in enumerate(ride_refs):
        for group in range(groups):
            for frame in range(part_frames):
                start = ((group * count_in + part) * part_frames + frame) * GROUP_ROWS
                for lane_group in range(features // LANES):
                    row = chunk + lane_group * part_rows + frame * row_count + group * GROUP_ROWS
                    ref[row : row + GROUP_ROWS] = mixed_ref[
                        start : start + GROUP_ROWS, lane_group * LANES : (lane_group + 1) * LANES
                    ]
        ref[:chunk] = stacked_s[
            pl.ds(pl.multiple_of((place_ref[0] ^ part) * chunk, GROUP_ROWS), chunk)
        ]


def space_backward_kernel(
    scale,
    factor,
    count_in,
    lists_ref,
    place_ref,
    *refs,
):
    returned_refs = refs[:count_in]
    (
        act_ref,
        kv_ref,
        keys_t_ref,
        query_ref,
        probs_ref,
        inverse_sum_ref,
        attended_ref,
        combine_ref,
        mixed_grad_ref,
        dquery_ref,
        dkv_ref,
        stacked_ref,
        dscores_s,
        dkv_s,
    ) = refs[count_in:]
    me = place_ref[0]
    frame_count, row_count, features = mixed_grad_ref.shape
    width = features // HEADS
    block_count = row_count // BLOCK
    rim = HREACH * BLOCK
    for distance, ref in enumerate(returned_refs):
        rows = ref.shape[1]
        span = pl.ds(pl.multiple_of((me ^ distance) * rows, GROUP_ROWS), rows)
        mixed_grad_ref[:, span] = ref[...]
    for frame in range(frame_count):
        dkv_s[frame] = jnp.zeros(dkv_s.shape[1:], F32)
        all_dattn_t = dot_nt(combine_ref[0], mixed_grad_ref[frame]).astype(BF16)
        for block in range(block_count):
            span = slice(block * BLOCK, (block + 1) * BLOCK)
            places = listed_blocks(lists_ref, frame, block)
            values = jnp.concatenate(
                [kv_ref[frame, pl.ds(place * BLOCK, BLOCK), features:] for place in places], axis=0
            )
            block_keys_t = jnp.concatenate([keys_t_ref[frame, place] for place in places], axis=1)
            dattn_t = all_dattn_t[:, span]
            dattn_wide = dattn_t.astype(F32)
            inverse_sum = inverse_sum_ref[frame, block]
            scaled_dattn = flip(dattn_wide * head_spread(inverse_sum, width))
            delta = jnp.sum(
                (dattn_wide * attended_ref[frame, :, span].astype(F32)).reshape(
                    HEADS, width, BLOCK
                ),
                axis=1,
            )
            row_scale = inverse_sum * scale
            dquery_parts = []
            for pair in range(HEADS // 2):
                heads = slice(pair * 2 * width, (pair + 1) * 2 * width)
                columns = slice(pair * 2 * BLOCK, (pair + 1) * 2 * BLOCK)
                pair_delta = jnp.concatenate(
                    [delta[2 * pair : 2 * pair + 1], delta[2 * pair + 1 : 2 * pair + 2]], axis=1
                )
                pair_scale = jnp.concatenate(
                    [row_scale[2 * pair : 2 * pair + 1], row_scale[2 * pair + 1 : 2 * pair + 2]],
                    axis=1,
                )
                dprobs = dot_nn(pair_group(values, pair, width), pair_columns(dattn_t, pair, width))
                probs = probs_ref[frame, block, :, columns].astype(F32)
                dscores = (probs * ((dprobs - pair_delta) * pair_scale)).astype(BF16)
                dscores_s[frame, block, :, columns] = dscores
                dquery_parts.append(pair_diagonal(dot_nn(block_keys_t[heads], dscores), width))
            dquery_ref[frame, span] = flip(jnp.concatenate(dquery_parts, axis=0))
            dkeys = dot_nn(dscores_s[frame, block], head_rows(query_ref[frame, span], width))
            dvalues = dot_nn(probs_ref[frame, block], head_rows(scaled_dattn, width))
            for entry, place in enumerate(places):
                rows = pl.ds(place * BLOCK, BLOCK)
                listed = slice(entry * BLOCK, (entry + 1) * BLOCK)
                dkv_s[frame, rows, :features] += dkeys[listed]
                dkv_s[frame, rows, features:] += dvalues[listed]
        dkv_ref[frame] = dkv_s[frame].astype(BF16)
    extended = dkv_ref.shape[1]
    act = act_ref[...]
    own_act = act[:, rim : rim + row_count].reshape(frame_count * row_count, features)
    stack_grads(
        [
            dot_tn(own_act, dquery_ref[...].reshape(frame_count * row_count, features)),
            dot_tn(
                act.reshape(frame_count * extended, features),
                dkv_ref[...].reshape(frame_count * extended, 2 * features),
            ),
            sum(
                dot_nn(attended_ref[frame], mixed_grad_ref[frame]) for frame in range(frame_count)
            ),
        ],
        factor,
        stacked_ref,
    )


def dact_kernel(place_ref, dquery_ref, dkv_ref, project_ref, dact_ref, near_ref, far_ref, dact_s):
    frame_count, row_count, features = dquery_ref.shape
    rim = near_ref.shape[1]
    core = place_ref[1] % 2
    for frame in range(frame_count):
        dact = dot_nt(dkv_ref[frame], project_ref[0, :, features:])
        dact_s[frame] = dact.astype(BF16)
        dact_ref[frame] = dact[rim : rim + row_count] + dot_nt(
            dquery_ref[frame], project_ref[0, :, :features]
        )
    near_ref[...] = dact_s[:, pl.ds(halo_start(core, rim, row_count, True), rim)]
    far_ref[...] = dact_s[:, pl.ds(halo_start(core, rim, row_count, False), rim)]


def field_kernel(place_ref, wave_ref, mixed_grad_ref, dact_ref, near_ref, far_ref, *refs):
    *ride_refs, field_ref, mixed_ref = refs
    frame_count, row_count, features = wave_ref.shape
    rows = row_count // len(ride_refs)
    lane_groups = features // LANES
    part_rows = frame_count * rows
    for frame in range(frame_count):
        normed, inverse = layer_norm(wave_ref[frame])
        dact = dact_ref[frame] + near_ref[frame].astype(F32) + far_ref[frame].astype(F32)
        field_ref[frame] = (
            mixed_grad_ref[frame].astype(F32) + norm_backward(dact, normed, inverse)
        ).astype(BF16)
        for distance, ref in enumerate(ride_refs):
            span = pl.ds(pl.multiple_of((place_ref[0] ^ distance) * rows, GROUP_ROWS), rows)
            for lane_group in range(lane_groups):
                start = ref.shape[0] - (lane_groups - lane_group) * part_rows + frame * rows
                mixed_ref[frame, span, lane_group * LANES : (lane_group + 1) * LANES] = ref[
                    start : start + rows
                ]


def ordered_sum(me, refs, parts_s):
    rows = parts_s.shape[1]
    for distance, ref in enumerate(refs):
        parts_s[me ^ distance] = ref[:rows]
    total = parts_s[0].astype(F32)
    for part in range(1, len(refs)):
        total = total + parts_s[part].astype(F32)
    return total.astype(BF16)


def cores_kernel(place_ref, space_ref, *refs):
    *ride_refs, kept_ref, sent_ref, parts_s, time_s = refs
    core = place_ref[1] % 2
    time_s[...] = ordered_sum(place_ref[0], ride_refs, parts_s)
    space_half, time_half = space_ref.shape[0] // 2, time_s.shape[0] // 2
    for half, ref in ((core, kept_ref), (1 - core, sent_ref)):
        ref[:space_half] = space_ref[
            pl.ds(pl.multiple_of(half * space_half, GROUP_ROWS), space_half)
        ]
        ref[space_half:] = time_s[pl.ds(pl.multiple_of(half * time_half, GROUP_ROWS), time_half)]


def split_kernel(place_ref, kept_ref, arrived_ref, *refs):
    *part_refs, time_ref, sum_s = refs
    sum_s[...] = (kept_ref[...].astype(F32) + arrived_ref[...].astype(F32)).astype(BF16)
    rows = part_refs[0].shape[0]
    for distance, ref in enumerate(part_refs):
        ref[...] = sum_s[pl.ds(pl.multiple_of((place_ref[0] ^ distance) * rows, GROUP_ROWS), rows)]
    time_ref[...] = sum_s[rows * len(part_refs) :]


def tm_sum_kernel(place_ref, *refs):
    *part_refs, time_ref, time_other_ref, space_out_ref, time_out_ref, parts_s = refs
    space_out_ref[...] = ordered_sum(place_ref[0], part_refs, parts_s)
    time_out_ref[...] = add_rounded(time_ref, time_other_ref)


def add_rounded(left_ref, right_ref):
    return (left_ref[...].astype(F32) + right_ref[...].astype(F32)).astype(BF16)


def pairs_kernel(*refs):
    out_refs = refs[2 * len(refs) // 3 :]
    for index, ref in enumerate(out_refs):
        ref[...] = add_rounded(refs[2 * index], refs[2 * index + 1])


def both_kernel(space_ref, space_other_ref, time_ref, total_ref):
    rows = space_ref.shape[0]
    total_ref[:rows] = add_rounded(space_ref, space_other_ref)
    total_ref[rows:] = time_ref[...]


def join_kernel(place_ref, *refs):
    *part_refs, joined_ref = refs
    me = place_ref[0]
    for distance, ref in enumerate(part_refs):
        rows = ref.shape[0]
        joined_ref[pl.ds(pl.multiple_of((me ^ distance) * rows, GROUP_ROWS), rows)] = ref[...]


def grads_kernel(time_count, place_ref, own_ref, other_ref, project_ref, combine_ref, halves_s):
    features = combine_ref.shape[1]
    core = place_ref[1] % 2
    halves_s[core] = own_ref[...]
    halves_s[1 - core] = other_ref[...]
    rows = halves_s.shape[1] // time_count // 2

    def place_rows(layer, row, piece):
        while piece.shape[0]:
            group, inner = divmod(row, features)
            taken = min(piece.shape[0], features - inner)
            start = group * LANES
            target, start = (
                (project_ref, start) if start < 3 * features else (combine_ref, start - 3 * features)
            )
            target[layer, inner : inner + taken, start : start + LANES] = piece[:taken].astype(F32)
            row, piece = row + taken, piece[taken:]

    for half in range(2):
        for part in range(time_count):
            start = 2 * part * rows
            place_rows(0, (half * time_count + part) * rows, halves_s[half, start : start + rows])
            place_rows(1, (2 * part + half) * rows, halves_s[half, start + rows : start + 2 * rows])


def stack_grads(grads, factor, stacked_ref):
    row = 0
    for grad in grads:
        for lane in range(0, grad.shape[1], LANES):
            stacked_ref[row : row + grad.shape[0]] = (
                grad[:, lane : lane + LANES] * factor
            ).astype(BF16)
            row += grad.shape[0]


def in_hbm(cells):
    return pltpu.with_memory_space_constraint(cells, pltpu.HBM)


def swap_far(cells, axis):
    pairs = [(i, i + 1) for i in range(1, lax.axis_size(axis) - 1, 2)]
    return lax.ppermute(cells, axis, pairs + [(j, i) for i, j in pairs])


def exchange(cells, axis, distance):
    return lax.ppermute(cells, axis, [(i, i ^ distance) for i in range(lax.axis_size(axis))])


def per_device(wave_field, cotangent, block_lists, project_weights, combine_weights):
    frame_count, row_count, features = wave_field.shape
    width = features // HEADS
    scale = 1.0 / math.sqrt(width)
    block_count = row_count // BLOCK
    list_length = block_lists.shape[-1]
    rim = HREACH * BLOCK
    extended = row_count + 2 * rim
    keys_count = list_length * BLOCK
    time_count = lax.axis_size("tm")
    all_frames = frame_count * time_count
    sent_rows = row_count // time_count
    factor = 1.0 / math.sqrt(frame_count * row_count * time_count * lax.axis_size("space"))
    space_count = lax.axis_size("space") // 2
    grad_rows = 4 * features // LANES * features
    chunk = grad_rows // time_count
    half_rows = grad_rows // 2 + chunk // 2
    ride_rows = chunk + frame_count * sent_rows * features // LANES
    tokens = all_frames * sent_rows
    places = block_count + 2 * HREACH
    smem_spec = pl.BlockSpec(memory_space=pltpu.SMEM)
    vmem_spec = pl.BlockSpec(memory_space=pltpu.VMEM)
    hbm_spec = pl.BlockSpec(memory_space=pl.ANY)

    def call(body, name, scalars, operands, outs, scratch=(), matmuls=1, in_spec=vmem_spec):
        def typed(shape):
            return (shape[:-1], shape[-1]) if not isinstance(shape[-1], int) else (shape, BF16)

        return pl.pallas_call(
            body,
            in_specs=[smem_spec] * len(scalars) + [in_spec] * len(operands),
            out_specs=[vmem_spec] * len(outs),
            out_shape=[jax.ShapeDtypeStruct(*typed(shape)) for shape in outs],
            scratch_shapes=[
                pltpu.VMEM(*typed(shape)) if isinstance(shape, tuple) else shape
                for shape in scratch
            ],
            compiler_params=pltpu.CompilerParams(vmem_limit_bytes=VMEM_BYTES),
            cost_estimate=cost(matmuls),
            name=name,
        )(*scalars, *operands)

    def over_tm(pieces):
        return [pieces[0]] + [exchange(pieces[d], "tm", d) for d in range(1, time_count)]

    own = (frame_count, row_count, features)
    part = (frame_count, sent_rows, features)
    near = exchange(wave_field, "space", 1)
    far = swap_far(wave_field, "space")
    place = jnp.stack([lax.axis_index("tm"), lax.axis_index("space")]).astype(jnp.int32)
    wave, project, turned, combine, cot = call(
        prepare_kernel,
        "prepare",
        [],
        [in_hbm(cells) for cells in (wave_field, cotangent, project_weights, combine_weights)],
        [
            own,
            (2, features, 3 * features),
            (2, 3 * features, features),
            (2, features, features),
            own,
        ],
        [pltpu.SemaphoreType.DMA((4,))],
        matmuls=8,
        in_spec=hbm_spec,
    )
    block_lists = in_hbm(block_lists)

    outs = call(
        space_forward_kernel,
        "space_forward",
        [block_lists, place],
        [near, far, wave, cot, project, turned, combine],
        [
            (frame_count, extended, features),
            (frame_count, extended, 2 * features),
            (frame_count, places, features, BLOCK),
            own,
            (frame_count, block_count, keys_count, HEADS * BLOCK),
            (frame_count, block_count, HEADS, BLOCK, F32),
            (frame_count, features, row_count),
            *[(frame_count, sent_rows, 2 * features)] * time_count,
        ],
        [(frame_count, places, features, BLOCK), own, (frame_count, extended, features)],
        matmuls=40,
    )
    kept_space, parts = outs[:7], outs[7:]
    arrived = over_tm(parts)

    def time_body(*refs):
        time_kernel(scale, time_count, *refs)

    outs = call(
        time_body,
        "time_pair",
        [],
        [*arrived, project, turned, combine],
        [
            *[part] * time_count,
            (tokens, features),
            (tokens, 3 * features),
            (features, tokens),
            (tokens, features),
            (tokens, features),
        ],
        matmuls=36,
    )
    parts, kept_time = outs[:time_count], outs[time_count:]

    def time_grads_body(*refs):
        time_grads_kernel(factor, frame_count, sent_rows, *refs)

    rides = call(
        time_grads_body,
        "time_grads",
        [place],
        kept_time,
        [(ride_rows, LANES)] * time_count,
        [(grad_rows, LANES)],
        matmuls=6,
    )
    returned = over_tm(parts)
    rides = over_tm(rides)

    def backward_body(*refs):
        space_backward_kernel(scale, factor, time_count, *refs)

    mixed_grad, dquery, dkv, space_grads = call(
        backward_body,
        "space_backward",
        [block_lists, place],
        [*returned, *kept_space, combine],
        [own, own, (frame_count, extended, 2 * features), (grad_rows, LANES)],
        [
            (frame_count, block_count, keys_count, HEADS * BLOCK),
            (frame_count, extended, 2 * features, F32),
        ],
        matmuls=44,
    )

    kept, sent = call(
        cores_kernel,
        "add_tm_time",
        [place],
        [space_grads, *rides],
        [(half_rows, LANES)] * 2,
        [(time_count, chunk, LANES), (chunk, LANES)],
    )
    other = exchange(sent, "space", 1)
    dact, to_near, to_far = call(
        dact_kernel,
        "space_dact",
        [place],
        [dquery, dkv, project],
        [(*own, F32), (frame_count, rim, features), (frame_count, rim, features)],
        [(frame_count, extended, features)],
        matmuls=3,
    )
    *space_pieces, time_piece = call(
        split_kernel,
        "add_cores",
        [place],
        [kept, other],
        [(chunk // 2, LANES)] * (time_count + 1),
        [(half_rows, LANES)],
    )
    to_near, to_far, *space_pieces = lax.optimization_barrier((to_near, to_far, *space_pieces))
    steps = [2 << bit for bit in range((space_count - 1).bit_length())]
    space_pieces = over_tm(space_pieces)
    time_other = exchange(time_piece, "space", steps[0])
    from_far = swap_far(to_far, "space")
    from_near = exchange(to_near, "space", 1)
    space_piece, time_piece = call(
        tm_sum_kernel,
        "add_tm_space",
        [place],
        [*space_pieces, time_piece, time_other],
        [(chunk // 2, LANES)] * 2,
        [(time_count, chunk // 2, LANES)],
    )
    for step, time_step in zip(steps, steps[1:]):
        space_other = exchange(space_piece, "space", step)
        time_other = exchange(time_piece, "space", time_step)
        space_piece, time_piece = call(
            pairs_kernel,
            "add_space",
            [],
            [space_piece, space_other, time_piece, time_other],
            [(chunk // 2, LANES)] * 2,
        )
    (piece,) = call(
        both_kernel,
        "add_space_last",
        [],
        [space_piece, exchange(space_piece, "space", steps[-1]), time_piece],
        [(chunk, LANES)],
    )
    joined = over_tm([piece] * time_count)
    field_grad, mixed_field = call(
        field_kernel,
        "field_grad",
        [place],
        [wave, mixed_grad, dact, from_near, from_far, *rides],
        [own, own],
        matmuls=3,
    )
    field_grad, mixed_field, *joined = lax.optimization_barrier((field_grad, mixed_field, *joined))
    (own_half,) = call(join_kernel, "join_tm", [place], joined, [(grad_rows, LANES)])
    other_half = exchange(own_half, "space", 1)

    def grads_body(*refs):
        grads_kernel(time_count, *refs)

    project_grad, combine_grad = call(
        grads_body,
        "weight_grads",
        [place],
        [own_half, other_half],
        [(2, features, 3 * features, F32), (2, features, features, F32)],
        [(2, grad_rows, LANES)],
    )
    return (mixed_field, field_grad, project_grad, combine_grad)


def solution(mesh):
    in_specs = (P("tm", "space", None), P("tm", "space", None), P("tm", "space", None), P(), P())
    out_specs = (P("tm", "space", None), P("tm", "space", None), P(), P())
    return jax.shard_map(
        per_device, mesh=mesh, in_specs=in_specs, out_specs=out_specs, check_vma=False
    )
```

```python
import math

import jax
import jax.numpy as jnp
from jax import lax
from jax.experimental import pallas as pl
from jax.experimental.pallas import tpu as pltpu
from jax.sharding import PartitionSpec as P

HEADS = 8
BLOCK = 128
HREACH = 2
LANES = 128
GROUP_ROWS = 16
VMEM_BYTES = 24 * 1024 * 1024
BF16 = jnp.bfloat16
F32 = jnp.float32


epsilon = 1e-05


def cost(matmuls):
    flops = matmuls * 2 * 1024 * 256 * 512
    return pl.CostEstimate(flops=flops, bytes_accessed=flops // 256, transcendentals=flops // 1024)


def dot_nn(left, right):
    return lax.dot_general(left, right, (((1,), (0,)), ((), ())), preferred_element_type=F32)


def dot_nt(left, right):
    return lax.dot_general(left, right, (((1,), (1,)), ((), ())), preferred_element_type=F32)


def dot_tn(left, right):
    return lax.dot_general(left, right, (((0,), (0,)), ((), ())), preferred_element_type=F32)


def layer_norm(rows):
    widened = rows.astype(F32)
    centered = widened - jnp.mean(widened, axis=-1, keepdims=True)
    inverse = lax.rsqrt(jnp.mean(centered * centered, axis=-1, keepdims=True) + epsilon)
    return (centered * inverse, inverse)


def norm_backward(upstream, normed, inverse):
    mean_grad = jnp.mean(upstream, axis=-1, keepdims=True)
    mean_cross = jnp.mean(upstream * normed, axis=-1, keepdims=True)
    return inverse * (upstream - mean_grad - normed * mean_cross)


def flip(matrix):
    return matrix.astype(BF16).T


def pair_columns(rows_t, pair, width):
    count = rows_t.shape[1]
    base = (pair * 2 * width) // LANES * LANES
    parts = []
    for head in (2 * pair, 2 * pair + 1):
        start = head * width - base
        pieces = []
        if start:
            pieces.append(jnp.zeros((start, count), rows_t.dtype))
        pieces.append(rows_t[head * width : (head + 1) * width])
        if start + width < LANES:
            pieces.append(jnp.zeros((LANES - start - width, count), rows_t.dtype))
        parts.append(jnp.concatenate(pieces, axis=0))
    return jnp.concatenate(parts, axis=1)


def pair_group(matrix, pair, width):
    base = (pair * 2 * width) // LANES * LANES
    return matrix[:, base : base + LANES]


def pair_diagonal(product, width):
    count = product.shape[1] // 2
    return jnp.concatenate([product[:width, :count], product[width:, count:]], axis=0)


def head_rows(rows, width):
    column = lax.broadcasted_iota(jnp.int32, (1, rows.shape[1]), 1) // width
    return jnp.concatenate(
        [rows * (column == head).astype(F32).astype(BF16) for head in range(HEADS)], axis=0
    )


def head_spread(per_head, width):
    return jnp.concatenate(
        [
            jnp.broadcast_to(per_head[head : head + 1], (width, per_head.shape[1]))
            for head in range(HEADS)
        ],
        axis=0,
    )


def listed_blocks(lists_ref, frame, block):
    own = lists_ref[frame, block, 0]
    return [
        lists_ref[frame, block, entry] - own + (block + HREACH)
        for entry in range(lists_ref.shape[2])
    ]


def halo_start(core, rim, row_count, near):
    after = core == 0 if near else core != 0
    return pl.multiple_of(jnp.where(after, rim + row_count, 0), BLOCK)


def project_rows(
    frame, start, rows, project_ref, turned_ref, act_ref, kv_ref, keys_t_ref, values_t_ref
):
    features = rows.shape[1]
    normed, _ = layer_norm(rows)
    act = normed.astype(BF16)
    span = pl.ds(start, rows.shape[0])
    act_ref[frame, span] = act
    kv_ref[frame, span] = dot_nn(act, project_ref[0, :, features:]).astype(BF16)
    keys_t = dot_nt(turned_ref[0, features : 2 * features], act).astype(BF16)
    values_t = dot_nt(turned_ref[0, 2 * features :], act).astype(BF16)
    for block in range(rows.shape[0] // BLOCK):
        lanes = slice(block * BLOCK, (block + 1) * BLOCK)
        keys_t_ref[frame, start // BLOCK + block] = keys_t[:, lanes]
        values_t_ref[frame, start // BLOCK + block] = values_t[:, lanes]
    return act


def prepare_kernel(
    place_ref,
    near_ref,
    wave_hbm,
    cot_hbm,
    project_hbm,
    combine_hbm,
    wave_ref,
    project_ref,
    turned_ref,
    combine_ref,
    cot_ref,
    query_ref,
    query_t_ref,
    act_ref,
    kv_ref,
    keys_t_ref,
    values_t_ref,
    sems,
):
    moves = [
        pltpu.make_async_copy(source, target, sems.at[index])
        for index, (source, target) in enumerate(
            (
                (project_hbm, project_ref),
                (wave_hbm, wave_ref),
                (combine_hbm, combine_ref),
                (cot_hbm, cot_ref),
            )
        )
    ]
    for move in moves:
        move.start()
    frame_count, row_count, features = wave_ref.shape
    rim = near_ref.shape[1]
    core = place_ref[1] % 2
    moves[0].wait()
    turned_ref[0] = flip(project_ref[0])
    for frame in range(frame_count):
        project_rows(
            frame,
            halo_start(core, rim, row_count, True),
            near_ref[frame],
            project_ref,
            turned_ref,
            act_ref,
            kv_ref,
            keys_t_ref,
            values_t_ref,
        )
    moves[1].wait()
    for frame in range(frame_count):
        act = project_rows(
            frame, rim, wave_ref[frame], project_ref, turned_ref, act_ref, kv_ref, keys_t_ref, values_t_ref
        )
        query_ref[frame] = dot_nn(act, project_ref[0, :, :features]).astype(BF16)
        query_t_ref[frame] = dot_nt(turned_ref[0, :features], act).astype(BF16)
    turned_ref[1] = flip(project_ref[1])
    moves[2].wait()
    moves[3].wait()


def space_forward_kernel(
    lists_ref,
    place_ref,
    far_ref,
    wave_ref,
    cot_ref,
    project_ref,
    turned_ref,
    combine_ref,
    query_t_ref,
    act_in,
    kv_in,
    keys_t_in,
    values_t_in,
    act_ref,
    kv_ref,
    keys_t_ref,
    values_t_ref,
    probs_ref,
    inverse_sum_ref,
    attended_ref,
    *rest,
):
    del act_in, kv_in, keys_t_in, values_t_in
    *sent_refs, mixed_s = rest
    me = place_ref[0]
    core = place_ref[1] % 2
    frame_count, row_count, features = wave_ref.shape
    rim = far_ref.shape[1]
    width = features // HEADS
    block_count = row_count // BLOCK
    exponent_scale = math.log2(math.e) / math.sqrt(width)
    for frame in range(frame_count):
        project_rows(
            frame,
            halo_start(core, rim, row_count, False),
            far_ref[frame],
            project_ref,
            turned_ref,
            act_ref,
            kv_ref,
            keys_t_ref,
            values_t_ref,
        )
    blocks = [(frame, block) for frame in range(frame_count) for block in range(block_count)]
    loaded = {}

    def load(index):
        frame, block = blocks[index]
        places = listed_blocks(lists_ref, frame, block)
        keys = jnp.concatenate(
            [kv_ref[frame, pl.ds(place * BLOCK, BLOCK), :features] for place in places], axis=0
        )
        loaded[index] = (keys, query_t_ref[frame, :, block * BLOCK : (block + 1) * BLOCK], places)

    def pair_scores(step):
        index, pair = divmod(step, HEADS // 2)
        if index not in loaded:
            load(index)
        keys, query_t, _ = loaded[index]
        return dot_nn(pair_group(keys, pair, width), pair_columns(query_t, pair, width))

    steps = len(blocks) * HEADS // 2
    scores = pair_scores(0)
    outs = []
    for step in range(steps):
        following = pair_scores(step + 1) if step + 1 < steps else None
        index, pair = divmod(step, HEADS // 2)
        frame, block = blocks[index]
        if pair == 0:
            block_values_t = jnp.concatenate(
                [values_t_ref[frame, place] for place in loaded[index][2]], axis=1
            )
            outs = []
        top = jnp.max(scores, axis=0, keepdims=True)
        exp_scores = jnp.exp2((scores - top) * exponent_scale)
        inverse_sum = 1.0 / jnp.sum(exp_scores, axis=0, keepdims=True)
        probs = exp_scores.astype(BF16)
        probs_ref[frame, block, :, pair * 2 * BLOCK : (pair + 1) * 2 * BLOCK] = probs
        inverse_sum_ref[frame, block, 2 * pair : 2 * pair + 1] = inverse_sum[:, :BLOCK]
        inverse_sum_ref[frame, block, 2 * pair + 1 : 2 * pair + 2] = inverse_sum[:, BLOCK:]
        out = dot_nn(block_values_t[pair * 2 * width : (pair + 1) * 2 * width], probs)
        outs.append(pair_diagonal(out * inverse_sum, width))
        scores = following
        if pair == HEADS // 2 - 1:
            attended_t = jnp.concatenate(outs, axis=0)
            span = slice(block * BLOCK, (block + 1) * BLOCK)
            attended_ref[frame, :, span] = attended_t.astype(BF16)
            mixed_s[frame, span] = (
                wave_ref[frame, span].astype(F32) + dot_nn(flip(attended_t), combine_ref[0])
            ).astype(BF16)
    for distance, ref in enumerate(sent_refs):
        rows = ref.shape[1]
        span = pl.ds(pl.multiple_of((me ^ distance) * rows, GROUP_ROWS), rows)
        ref[:, :, :features] = mixed_s[:, span]
        ref[:, :, features:] = cot_ref[:, span]


def time_kernel(
    scale,
    count_in,
    *refs,
):
    arrived_refs = refs[:count_in]
    project_ref, turned_ref, combine_ref = refs[count_in : count_in + 3]
    grad_refs = refs[count_in + 3 : 2 * count_in + 3]
    act_ref, dproj_ref, attended_t_ref, cot_ref, mixed_ref = refs[2 * count_in + 3 :]
    part_frames, row_count, features = grad_refs[0].shape
    width = features // HEADS
    count = part_frames * count_in * GROUP_ROWS
    groups = row_count // GROUP_ROWS
    exponent_scale = scale * math.log2(math.e)

    def grouped(lanes):
        return jnp.concatenate(
            [
                ref[:, group * GROUP_ROWS : (group + 1) * GROUP_ROWS, lanes].reshape(
                    part_frames * GROUP_ROWS, features
                )
                for group in range(groups)
                for ref in arrived_refs
            ],
            axis=0,
        )

    rows = grouped(slice(0, features))
    cot = grouped(slice(features, 2 * features))
    cot_ref[...] = cot
    normed, inverse = layer_norm(rows)
    act = normed.astype(BF16)
    act_ref[...] = act
    projected = dot_nn(act, project_ref[1]).astype(BF16)
    projected_t = dot_nt(turned_ref[1], act).astype(BF16)
    all_dattn = dot_nt(cot, combine_ref[1]).astype(BF16)
    all_dattn_t = dot_nt(combine_ref[1], cot).astype(BF16)
    all_count = HEADS * count
    key_row = lax.broadcasted_iota(jnp.int32, (count, all_count), 0) % GROUP_ROWS
    query_row = lax.broadcasted_iota(jnp.int32, (count, all_count), 1) % GROUP_ROWS
    same_row = key_row == query_row
    attended_groups, dquery_groups, dkey_groups, dvalue_groups = [], [], [], []
    pairs = range(HEADS // 2)

    def products(group):
        span = slice(group * count, (group + 1) * count)
        return tuple(
            jnp.concatenate(
                [
                    dot_nn(pair_group(left, pair, width), pair_columns(right, pair, width))
                    for pair in pairs
                ],
                axis=1,
            )
            for left, right in (
                (projected[span, features : 2 * features], projected_t[:features, span]),
                (projected[span, 2 * features :], all_dattn_t[:, span]),
            )
        )

    def by_heads(left_t, right):
        return jnp.concatenate(
            [
                pair_diagonal(
                    dot_nn(
                        left_t[pair * 2 * width : (pair + 1) * 2 * width],
                        right[:, pair * 2 * count : (pair + 1) * 2 * count],
                    ),
                    width,
                )
                for pair in pairs
            ],
            axis=0,
        )

    scores, dprobs = products(0)
    for group in range(groups):
        following = products(group + 1) if group + 1 < groups else (None, None)
        span = slice(group * count, (group + 1) * count)
        scores = jnp.where(same_row, scores, -3e38)
        top = jnp.max(scores, axis=0, keepdims=True)
        exp_scores = jnp.exp2((scores - top) * exponent_scale)
        probs = (exp_scores * (1.0 / jnp.sum(exp_scores, axis=0, keepdims=True))).astype(BF16)
        probs_wide = probs.astype(F32)
        delta = jnp.sum(probs_wide * dprobs, axis=0, keepdims=True)
        dscores = (probs_wide * (dprobs - delta) * scale).astype(BF16)
        attended_groups.append(by_heads(projected_t[2 * features :, span], probs).astype(BF16))
        dquery_groups.append(flip(by_heads(projected_t[features : 2 * features, span], dscores)))
        dkey_groups.append(
            dot_nn(dscores, head_rows(projected[span, :features], width)).astype(BF16)
        )
        dvalue_groups.append(dot_nn(probs, head_rows(all_dattn[span], width)).astype(BF16))
        scores, dprobs = following
    attended = jnp.concatenate([flip(attended_t) for attended_t in attended_groups], axis=0)
    mixed_ref[...] = (rows.astype(F32) + dot_nn(attended, combine_ref[1])).astype(BF16)
    attended_t_ref[...] = jnp.concatenate(attended_groups, axis=1)
    dproj = jnp.concatenate(
        [jnp.concatenate(parts, axis=0) for parts in (dquery_groups, dkey_groups, dvalue_groups)],
        axis=1,
    )
    dproj_ref[...] = dproj
    dact = dot_nt(dproj, project_ref[1])
    mixed_grad = (cot.astype(F32) + norm_backward(dact, normed, inverse)).astype(BF16)
    for part, ref in enumerate(grad_refs):
        for group in range(groups):
            span = slice(group * GROUP_ROWS, (group + 1) * GROUP_ROWS)
            for frame in range(part_frames):
                start = ((group * count_in + part) * part_frames + frame) * GROUP_ROWS
                ref[frame, span] = mixed_grad[start : start + GROUP_ROWS]


def time_grads_kernel(
    factor, part_frames, row_count, place_ref, act_ref, dproj_ref, attended_t_ref, cot_ref, mixed_ref, *refs
):
    *ride_refs, stacked_s = refs
    count_in = len(ride_refs)
    features = act_ref.shape[1]
    groups = row_count // GROUP_ROWS
    stack_grads(
        [dot_tn(act_ref[...], dproj_ref[...]), dot_nn(attended_t_ref[...], cot_ref[...])],
        factor,
        stacked_s,
    )
    chunk = stacked_s.shape[0] // count_in
    part_rows = part_frames * row_count
    for part, ref in enumerate(ride_refs):
        for group in range(groups):
            for frame in range(part_frames):
                start = ((group * count_in + part) * part_frames + frame) * GROUP_ROWS
                for lane_group in range(features // LANES):
                    row = chunk + lane_group * part_rows + frame * row_count + group * GROUP_ROWS
                    ref[row : row + GROUP_ROWS] = mixed_ref[
                        start : start + GROUP_ROWS, lane_group * LANES : (lane_group + 1) * LANES
                    ]
        ref[:chunk] = stacked_s[
            pl.ds(pl.multiple_of((place_ref[0] ^ part) * chunk, GROUP_ROWS), chunk)
        ]


def space_backward_kernel(
    scale,
    factor,
    count_in,
    lists_ref,
    place_ref,
    *refs,
):
    returned_refs = refs[:count_in]
    (
        act_ref,
        kv_ref,
        keys_t_ref,
        query_ref,
        probs_ref,
        inverse_sum_ref,
        attended_ref,
        combine_ref,
        mixed_grad_ref,
        dquery_ref,
        dkv_ref,
        stacked_ref,
        dscores_s,
        dkv_s,
    ) = refs[count_in:]
    me = place_ref[0]
    frame_count, row_count, features = mixed_grad_ref.shape
    width = features // HEADS
    block_count = row_count // BLOCK
    rim = HREACH * BLOCK
    for distance, ref in enumerate(returned_refs):
        rows = ref.shape[1]
        span = pl.ds(pl.multiple_of((me ^ distance) * rows, GROUP_ROWS), rows)
        mixed_grad_ref[:, span] = ref[...]
    blocks = [(frame, block) for frame in range(frame_count) for block in range(block_count)]
    all_dattn_t = [
        dot_nt(combine_ref[0], mixed_grad_ref[frame]).astype(BF16) for frame in range(frame_count)
    ]
    loaded = {}

    def load(index):
        frame, block = blocks[index]
        places = listed_blocks(lists_ref, frame, block)
        values = jnp.concatenate(
            [kv_ref[frame, pl.ds(place * BLOCK, BLOCK), features:] for place in places], axis=0
        )
        loaded[index] = (
            values,
            all_dattn_t[frame][:, block * BLOCK : (block + 1) * BLOCK],
            places,
        )

    def pair_products(step):
        index, pair = divmod(step, HEADS // 2)
        if index not in loaded:
            load(index)
        values, dattn_t, _ = loaded[index]
        return dot_nn(pair_group(values, pair, width), pair_columns(dattn_t, pair, width))

    def add_listed(index, lanes, parts):
        frame = blocks[index][0]
        for entry, place in enumerate(loaded[index][2]):
            rows = pl.ds(place * BLOCK, BLOCK)
            dkv_s[frame, rows, lanes] += parts[entry * BLOCK : (entry + 1) * BLOCK]

    def add_keys(index):
        frame, block = blocks[index]
        queries = head_rows(query_ref[frame, block * BLOCK : (block + 1) * BLOCK], width)
        add_listed(index, slice(0, features), dot_nn(dscores_s[frame, block], queries))

    dkv_s[...] = jnp.zeros(dkv_s.shape, F32)
    steps = len(blocks) * HEADS // 2
    dprobs = pair_products(0)
    dquery_parts = []
    for step in range(steps):
        following = pair_products(step + 1) if step + 1 < steps else None
        index, pair = divmod(step, HEADS // 2)
        frame, block = blocks[index]
        _, dattn_t, places = loaded[index]
        if pair == 0:
            span = slice(block * BLOCK, (block + 1) * BLOCK)
            block_keys_t = jnp.concatenate([keys_t_ref[frame, place] for place in places], axis=1)
            dattn_wide = dattn_t.astype(F32)
            inverse_sum = inverse_sum_ref[frame, block]
            delta = jnp.sum(
                (dattn_wide * attended_ref[frame, :, span].astype(F32)).reshape(
                    HEADS, width, BLOCK
                ),
                axis=1,
            )
            row_scale = inverse_sum * scale
            dquery_parts = []
        if pair == 1:
            scaled_dattn = flip(dattn_wide * head_spread(inverse_sum, width))
            add_listed(
                index,
                slice(features, 2 * features),
                dot_nn(probs_ref[frame, block], head_rows(scaled_dattn, width)),
            )
        if pair == 2 and index:
            add_keys(index - 1)
        heads = slice(pair * 2 * width, (pair + 1) * 2 * width)
        columns = slice(pair * 2 * BLOCK, (pair + 1) * 2 * BLOCK)
        pair_delta, pair_scale = (
            jnp.concatenate([rows[2 * pair : 2 * pair + 1], rows[2 * pair + 1 : 2 * pair + 2]], axis=1)
            for rows in (delta, row_scale)
        )
        probs = probs_ref[frame, block, :, columns].astype(F32)
        dscores = (probs * ((dprobs - pair_delta) * pair_scale)).astype(BF16)
        dscores_s[frame, block, :, columns] = dscores
        dquery_parts.append(pair_diagonal(dot_nn(block_keys_t[heads], dscores), width))
        dprobs = following
        if pair == HEADS // 2 - 1:
            dquery_ref[frame, span] = flip(jnp.concatenate(dquery_parts, axis=0))
    add_keys(len(blocks) - 1)
    dkv_ref[...] = dkv_s[...].astype(BF16)
    extended = dkv_ref.shape[1]
    act = act_ref[...]
    own_act = act[:, rim : rim + row_count].reshape(frame_count * row_count, features)
    stack_grads(
        [
            dot_tn(own_act, dquery_ref[...].reshape(frame_count * row_count, features)),
            dot_tn(
                act.reshape(frame_count * extended, features),
                dkv_ref[...].reshape(frame_count * extended, 2 * features),
            ),
            sum(
                dot_nn(attended_ref[frame], mixed_grad_ref[frame]) for frame in range(frame_count)
            ),
        ],
        factor,
        stacked_ref,
    )


def dact_kernel(place_ref, dquery_ref, dkv_ref, project_ref, dact_ref, near_ref, far_ref, dact_s):
    frame_count, row_count, features = dquery_ref.shape
    rim = near_ref.shape[1]
    core = place_ref[1] % 2
    for frame in range(frame_count):
        dact = dot_nt(dkv_ref[frame], project_ref[0, :, features:])
        dact_s[frame] = dact.astype(BF16)
        dact_ref[frame] = dact[rim : rim + row_count] + dot_nt(
            dquery_ref[frame], project_ref[0, :, :features]
        )
    near_ref[...] = dact_s[:, pl.ds(halo_start(core, rim, row_count, True), rim)]
    far_ref[...] = dact_s[:, pl.ds(halo_start(core, rim, row_count, False), rim)]


def field_kernel(place_ref, wave_ref, mixed_grad_ref, dact_ref, near_ref, far_ref, *refs):
    *ride_refs, field_ref, mixed_ref = refs
    frame_count, row_count, features = wave_ref.shape
    rows = row_count // len(ride_refs)
    lane_groups = features // LANES
    part_rows = frame_count * rows
    for frame in range(frame_count):
        normed, inverse = layer_norm(wave_ref[frame])
        dact = dact_ref[frame] + near_ref[frame].astype(F32) + far_ref[frame].astype(F32)
        field_ref[frame] = (
            mixed_grad_ref[frame].astype(F32) + norm_backward(dact, normed, inverse)
        ).astype(BF16)
        for distance, ref in enumerate(ride_refs):
            span = pl.ds(pl.multiple_of((place_ref[0] ^ distance) * rows, GROUP_ROWS), rows)
            for lane_group in range(lane_groups):
                start = ref.shape[0] - (lane_groups - lane_group) * part_rows + frame * rows
                mixed_ref[frame, span, lane_group * LANES : (lane_group + 1) * LANES] = ref[
                    start : start + rows
                ]


def ordered_sum(me, refs, parts_s):
    rows = parts_s.shape[1]
    for distance, ref in enumerate(refs):
        parts_s[me ^ distance] = ref[:rows]
    total = parts_s[0].astype(F32)
    for part in range(1, len(refs)):
        total = total + parts_s[part].astype(F32)
    return total.astype(BF16)


def cores_kernel(place_ref, space_ref, *refs):
    *ride_refs, kept_ref, sent_ref, parts_s, time_s = refs
    core = place_ref[1] % 2
    time_s[...] = ordered_sum(place_ref[0], ride_refs, parts_s)
    space_half, time_half = space_ref.shape[0] // 2, time_s.shape[0] // 2
    for half, ref in ((core, kept_ref), (1 - core, sent_ref)):
        ref[:space_half] = space_ref[
            pl.ds(pl.multiple_of(half * space_half, GROUP_ROWS), space_half)
        ]
        ref[space_half:] = time_s[pl.ds(pl.multiple_of(half * time_half, GROUP_ROWS), time_half)]


def split_kernel(place_ref, kept_ref, arrived_ref, *refs):
    *part_refs, time_ref, sum_s = refs
    sum_s[...] = (kept_ref[...].astype(F32) + arrived_ref[...].astype(F32)).astype(BF16)
    rows = part_refs[0].shape[0]
    for distance, ref in enumerate(part_refs):
        ref[...] = sum_s[pl.ds(pl.multiple_of((place_ref[0] ^ distance) * rows, GROUP_ROWS), rows)]
    time_ref[...] = sum_s[rows * len(part_refs) :]


def tm_sum_kernel(place_ref, *refs):
    *part_refs, time_ref, time_other_ref, space_out_ref, time_out_ref, parts_s = refs
    space_out_ref[...] = ordered_sum(place_ref[0], part_refs, parts_s)
    time_out_ref[...] = add_rounded(time_ref, time_other_ref)


def add_rounded(left_ref, right_ref):
    return (left_ref[...].astype(F32) + right_ref[...].astype(F32)).astype(BF16)


def pairs_kernel(*refs):
    out_refs = refs[2 * len(refs) // 3 :]
    for index, ref in enumerate(out_refs):
        ref[...] = add_rounded(refs[2 * index], refs[2 * index + 1])


def join_kernel(place_ref, *refs):
    *part_refs, joined_ref = refs
    count_in = len(part_refs) // 2
    rows = part_refs[0].shape[0]
    for layer in range(2):
        for distance in range(count_in):
            start = (2 * (place_ref[0] ^ distance) + layer) * rows
            joined_ref[pl.ds(pl.multiple_of(start, GROUP_ROWS), rows)] = part_refs[
                layer * count_in + distance
            ][...]


def grads_kernel(time_count, own, place_ref, half_ref, *refs):
    project_hbm, combine_hbm, wide_s, sems = refs[-4:]
    features = combine_hbm.shape[1]
    core = place_ref[1] % 2
    rows = half_ref.shape[0] // time_count // 2
    wide_s[...] = half_ref[...].astype(F32).reshape(wide_s.shape)

    def write(half):
        moves = []
        for part in range(time_count):
            for layer, row in ((0, (half * time_count + part) * rows), (1, (2 * part + half) * rows)):
                group, inner = divmod(row, features)
                start = group * LANES
                target, start = (
                    (project_hbm, start)
                    if start < 3 * features
                    else (combine_hbm, start - 3 * features)
                )
                piece = 2 * part + layer
                moves.append(
                    pltpu.make_async_copy(
                        wide_s.at[piece],
                        target.at[layer, pl.ds(inner, rows), pl.ds(start, LANES)],
                        sems.at[piece],
                    )
                )
        for move in moves:
            move.start()
        for move in moves:
            move.wait()

    for half in range(2):

        @pl.when((core if own else 1 - core) == half)
        def _():
            write(half)


def stack_grads(grads, factor, stacked_ref):
    row = 0
    for grad in grads:
        for lane in range(0, grad.shape[1], LANES):
            stacked_ref[row : row + grad.shape[0]] = (
                grad[:, lane : lane + LANES] * factor
            ).astype(BF16)
            row += grad.shape[0]


def in_hbm(cells):
    return pltpu.with_memory_space_constraint(cells, pltpu.HBM)


def swap_far(cells, axis):
    pairs = [(i, i + 1) for i in range(1, lax.axis_size(axis) - 1, 2)]
    return lax.ppermute(cells, axis, pairs + [(j, i) for i, j in pairs])


def exchange(cells, axis, distance):
    return lax.ppermute(cells, axis, [(i, i ^ distance) for i in range(lax.axis_size(axis))])


def per_device(wave_field, cotangent, block_lists, project_weights, combine_weights):
    frame_count, row_count, features = wave_field.shape
    width = features // HEADS
    scale = 1.0 / math.sqrt(width)
    block_count = row_count // BLOCK
    list_length = block_lists.shape[-1]
    rim = HREACH * BLOCK
    extended = row_count + 2 * rim
    keys_count = list_length * BLOCK
    time_count = lax.axis_size("tm")
    all_frames = frame_count * time_count
    sent_rows = row_count // time_count
    factor = 1.0 / math.sqrt(frame_count * row_count * time_count * lax.axis_size("space"))
    space_count = lax.axis_size("space") // 2
    grad_rows = 4 * features // LANES * features
    chunk = grad_rows // time_count
    half_rows = grad_rows // 2 + chunk // 2
    ride_rows = chunk + frame_count * sent_rows * features // LANES
    tokens = all_frames * sent_rows
    places = block_count + 2 * HREACH
    smem_spec = pl.BlockSpec(memory_space=pltpu.SMEM)
    vmem_spec = pl.BlockSpec(memory_space=pltpu.VMEM)
    hbm_spec = pl.BlockSpec(memory_space=pl.ANY)

    def call(
        body, name, scalars, operands, outs, scratch=(), matmuls=1, hbm=(), aliases=None, out_spec=None
    ):
        def typed(shape):
            return (shape[:-1], shape[-1]) if not isinstance(shape[-1], int) else (shape, BF16)

        return pl.pallas_call(
            body,
            in_specs=[smem_spec] * len(scalars)
            + [vmem_spec] * len(operands)
            + [hbm_spec] * len(hbm),
            out_specs=[out_spec or vmem_spec] * len(outs),
            out_shape=[jax.ShapeDtypeStruct(*typed(shape)) for shape in outs],
            scratch_shapes=[
                pltpu.VMEM(*typed(shape)) if isinstance(shape, tuple) else shape
                for shape in scratch
            ],
            compiler_params=pltpu.CompilerParams(vmem_limit_bytes=VMEM_BYTES),
            cost_estimate=cost(matmuls),
            input_output_aliases=aliases or {},
            name=name,
        )(*scalars, *operands, *hbm)

    def over_tm(pieces):
        return [pieces[0]] + [exchange(pieces[d], "tm", d) for d in range(1, time_count)]

    own = (frame_count, row_count, features)
    part = (frame_count, sent_rows, features)
    near = exchange(wave_field, "space", 1)
    far = swap_far(wave_field, "space")
    place = jnp.stack([lax.axis_index("tm"), lax.axis_index("space")]).astype(jnp.int32)
    extended_shapes = [
        (frame_count, extended, features),
        (frame_count, extended, 2 * features),
        (frame_count, places, features, BLOCK),
        (frame_count, places, features, BLOCK),
    ]
    wave, project, turned, combine, cot, queries, queries_t, *projected = call(
        prepare_kernel,
        "prepare",
        [place],
        [near],
        [
            own,
            (2, features, 3 * features),
            (2, 3 * features, features),
            (2, features, features),
            own,
            own,
            (frame_count, features, row_count),
            *extended_shapes,
        ],
        [pltpu.SemaphoreType.DMA((4,))],
        matmuls=12,
        hbm=[in_hbm(cells) for cells in (wave_field, cotangent, project_weights, combine_weights)],
    )
    block_lists = in_hbm(block_lists)
    act, keys_values, keys_t, _, probs, inverse_sum, attended, *parts = call(
        space_forward_kernel,
        "space_forward",
        [block_lists, place],
        [far, wave, cot, project, turned, combine, queries_t, *projected],
        [
            *extended_shapes,
            (frame_count, block_count, keys_count, HEADS * BLOCK),
            (frame_count, block_count, HEADS, BLOCK, F32),
            (frame_count, features, row_count),
            *[(frame_count, sent_rows, 2 * features)] * time_count,
        ],
        [own],
        matmuls=40,
        aliases={9 + index: index for index in range(4)},
    )
    kept_space = [act, keys_values, keys_t, queries, probs, inverse_sum, attended]
    arrived = over_tm(parts)

    def time_body(*refs):
        time_kernel(scale, time_count, *refs)

    outs = call(
        time_body,
        "time_pair",
        [],
        [*arrived, project, turned, combine],
        [
            *[part] * time_count,
            (tokens, features),
            (tokens, 3 * features),
            (features, tokens),
            (tokens, features),
            (tokens, features),
        ],
        matmuls=36,
    )
    parts, kept_time = outs[:time_count], outs[time_count:]

    def time_grads_body(*refs):
        time_grads_kernel(factor, frame_count, sent_rows, *refs)

    rides = call(
        time_grads_body,
        "time_grads",
        [place],
        kept_time,
        [(ride_rows, LANES)] * time_count,
        [(grad_rows, LANES)],
        matmuls=6,
    )
    returned = over_tm(parts)
    rides = over_tm(rides)

    def backward_body(*refs):
        space_backward_kernel(scale, factor, time_count, *refs)

    mixed_grad, dquery, dkv, space_grads = call(
        backward_body,
        "space_backward",
        [block_lists, place],
        [*returned, *kept_space, combine],
        [own, own, (frame_count, extended, 2 * features), (grad_rows, LANES)],
        [
            (frame_count, block_count, keys_count, HEADS * BLOCK),
            (frame_count, extended, 2 * features, F32),
        ],
        matmuls=44,
    )

    kept, sent = call(
        cores_kernel,
        "add_tm_time",
        [place],
        [space_grads, *rides],
        [(half_rows, LANES)] * 2,
        [(time_count, chunk, LANES), (chunk, LANES)],
    )
    other = exchange(sent, "space", 1)
    dact, to_near, to_far = call(
        dact_kernel,
        "space_dact",
        [place],
        [dquery, dkv, project],
        [(*own, F32), (frame_count, rim, features), (frame_count, rim, features)],
        [(frame_count, extended, features)],
        matmuls=3,
    )
    *space_pieces, time_piece = call(
        split_kernel,
        "add_cores",
        [place],
        [kept, other],
        [(chunk // 2, LANES)] * (time_count + 1),
        [(half_rows, LANES)],
    )
    steps = [2 << bit for bit in range((space_count - 1).bit_length())]
    from_far = swap_far(to_far, "space")
    from_near = exchange(to_near, "space", 1)
    from_near, from_far, *space_pieces = lax.optimization_barrier(
        (from_near, from_far, *over_tm(space_pieces))
    )
    time_other = exchange(time_piece, "space", steps[0])
    space_piece, time_piece = call(
        tm_sum_kernel,
        "add_tm_space",
        [place],
        [*space_pieces, time_piece, time_other],
        [(chunk // 2, LANES)] * 2,
        [(time_count, chunk // 2, LANES)],
    )
    for step, time_step in zip(steps, steps[1:]):
        space_other = exchange(space_piece, "space", step)
        time_other = exchange(time_piece, "space", time_step)
        space_piece, time_piece = call(
            pairs_kernel,
            "add_space",
            [],
            [space_piece, space_other, time_piece, time_other],
            [(chunk // 2, LANES)] * 2,
        )
    space_other = exchange(space_piece, "space", steps[-1])
    time_joined = over_tm([time_piece] * time_count)
    (space_piece,) = call(
        pairs_kernel, "add_space_last", [], [space_piece, space_other], [(chunk // 2, LANES)]
    )
    joined = over_tm([space_piece] * time_count) + time_joined

    field_grad, mixed_field = call(
        field_kernel,
        "field_grad",
        [place],
        [wave, mixed_grad, dact, from_near, from_far, *rides],
        [own, own],
        matmuls=3,
    )
    field_grad, mixed_field, *joined = lax.optimization_barrier((field_grad, mixed_field, *joined))
    (own_half,) = call(join_kernel, "join_tm", [place], joined, [(grad_rows, LANES)])
    other_half = exchange(own_half, "space", 1)

    grads = ()
    for half in (own_half, other_half):

        def grads_body(*refs, mine=half is own_half):
            grads_kernel(time_count, mine, *refs)

        grads = call(
            grads_body,
            "weight_grads",
            [place],
            [half],
            [(2, features, 3 * features, F32), (2, features, features, F32)],
            [
                (2 * time_count, grad_rows // time_count // 2, LANES, F32),
                pltpu.SemaphoreType.DMA((2 * time_count,)),
            ],
            hbm=grads,
            aliases={2: 0, 3: 1} if grads else None,
            out_spec=pl.BlockSpec(memory_space=pltpu.HBM),
        )
    project_grad, combine_grad = grads
    return (mixed_field, field_grad, project_grad, combine_grad)


def solution(mesh):
    in_specs = (P("tm", "space", None), P("tm", "space", None), P("tm", "space", None), P(), P())
    out_specs = (P("tm", "space", None), P("tm", "space", None), P(), P())
    return jax.shard_map(
        per_device, mesh=mesh, in_specs=in_specs, out_specs=out_specs, check_vma=False
    )
```

```python
import math

import jax
import jax.numpy as jnp
from jax import lax
from jax.experimental import pallas as pl
from jax.experimental.pallas import tpu as pltpu
from jax.sharding import PartitionSpec as P

HEADS = 8
BLOCK = 128
HREACH = 2
LANES = 128
GROUP_ROWS = 16
VMEM_BYTES = 24 * 1024 * 1024
BF16 = jnp.bfloat16
F32 = jnp.float32


epsilon = 1e-05


def cost(matmuls):
    flops = matmuls * 2 * 1024 * 256 * 512
    return pl.CostEstimate(flops=flops, bytes_accessed=flops // 256, transcendentals=flops // 1024)


def dot_nn(left, right):
    return lax.dot_general(left, right, (((1,), (0,)), ((), ())), preferred_element_type=F32)


def dot_nt(left, right):
    return lax.dot_general(left, right, (((1,), (1,)), ((), ())), preferred_element_type=F32)


def dot_tn(left, right):
    return lax.dot_general(left, right, (((0,), (0,)), ((), ())), preferred_element_type=F32)


def layer_norm(rows):
    widened = rows.astype(F32)
    centered = widened - jnp.mean(widened, axis=-1, keepdims=True)
    inverse = lax.rsqrt(jnp.mean(centered * centered, axis=-1, keepdims=True) + epsilon)
    return (centered * inverse, inverse)


def norm_backward(upstream, normed, inverse):
    mean_grad = jnp.mean(upstream, axis=-1, keepdims=True)
    mean_cross = jnp.mean(upstream * normed, axis=-1, keepdims=True)
    return inverse * (upstream - mean_grad - normed * mean_cross)


def flip(matrix):
    return matrix.astype(BF16).T


def pair_columns(rows_t, pair, width):
    count = rows_t.shape[1]
    base = (pair * 2 * width) // LANES * LANES
    parts = []
    for head in (2 * pair, 2 * pair + 1):
        start = head * width - base
        pieces = []
        if start:
            pieces.append(jnp.zeros((start, count), rows_t.dtype))
        pieces.append(rows_t[head * width : (head + 1) * width])
        if start + width < LANES:
            pieces.append(jnp.zeros((LANES - start - width, count), rows_t.dtype))
        parts.append(jnp.concatenate(pieces, axis=0))
    return jnp.concatenate(parts, axis=1)


def pair_group(matrix, pair, width):
    base = (pair * 2 * width) // LANES * LANES
    return matrix[:, base : base + LANES]


def pair_diagonal(product, width):
    count = product.shape[1] // 2
    return jnp.concatenate([product[:width, :count], product[width:, count:]], axis=0)


def head_rows(rows, width):
    column = lax.broadcasted_iota(jnp.int32, (1, rows.shape[1]), 1) // width
    return jnp.concatenate(
        [rows * (column == head).astype(F32).astype(BF16) for head in range(HEADS)], axis=0
    )


def head_spread(per_head, width):
    return jnp.concatenate(
        [
            jnp.broadcast_to(per_head[head : head + 1], (width, per_head.shape[1]))
            for head in range(HEADS)
        ],
        axis=0,
    )


def listed_blocks(lists_ref, frame, block):
    own = lists_ref[frame, block, 0]
    return [
        lists_ref[frame, block, entry] - own + (block + HREACH)
        for entry in range(lists_ref.shape[2])
    ]


def halo_start(core, rim, row_count, near):
    after = core == 0 if near else core != 0
    return pl.multiple_of(jnp.where(after, rim + row_count, 0), BLOCK)


def project_rows(
    frame, start, rows, project_ref, turned_ref, act_ref, kv_ref, keys_t_ref, values_t_ref
):
    features = rows.shape[1]
    normed, _ = layer_norm(rows)
    act = normed.astype(BF16)
    span = pl.ds(start, rows.shape[0])
    act_ref[frame, span] = act
    kv_ref[frame, span] = dot_nn(act, project_ref[0, :, features:]).astype(BF16)
    keys_t = dot_nt(turned_ref[0, features : 2 * features], act).astype(BF16)
    values_t = dot_nt(turned_ref[0, 2 * features :], act).astype(BF16)
    for block in range(rows.shape[0] // BLOCK):
        lanes = slice(block * BLOCK, (block + 1) * BLOCK)
        keys_t_ref[frame, start // BLOCK + block] = keys_t[:, lanes]
        values_t_ref[frame, start // BLOCK + block] = values_t[:, lanes]
    return act


def prepare_kernel(
    place_ref,
    near_ref,
    wave_hbm,
    cot_hbm,
    project_hbm,
    combine_hbm,
    wave_ref,
    project_ref,
    turned_ref,
    combine_ref,
    cot_ref,
    query_ref,
    query_t_ref,
    act_ref,
    kv_ref,
    keys_t_ref,
    values_t_ref,
    sems,
):
    moves = [
        pltpu.make_async_copy(source, target, sems.at[index])
        for index, (source, target) in enumerate(
            (
                (project_hbm, project_ref),
                (wave_hbm, wave_ref),
                (combine_hbm, combine_ref),
                (cot_hbm, cot_ref),
            )
        )
    ]
    for move in moves:
        move.start()
    frame_count, row_count, features = wave_ref.shape
    rim = near_ref.shape[1]
    core = place_ref[1] % 2
    moves[0].wait()
    turned_ref[0] = flip(project_ref[0])
    for frame in range(frame_count):
        project_rows(
            frame,
            halo_start(core, rim, row_count, True),
            near_ref[frame],
            project_ref,
            turned_ref,
            act_ref,
            kv_ref,
            keys_t_ref,
            values_t_ref,
        )
    moves[1].wait()
    for frame in range(frame_count):
        act = project_rows(
            frame, rim, wave_ref[frame], project_ref, turned_ref, act_ref, kv_ref, keys_t_ref, values_t_ref
        )
        query_ref[frame] = dot_nn(act, project_ref[0, :, :features]).astype(BF16)
        query_t_ref[frame] = dot_nt(turned_ref[0, :features], act).astype(BF16)
    turned_ref[1] = flip(project_ref[1])
    moves[2].wait()
    moves[3].wait()


def space_forward_kernel(
    lists_ref,
    place_ref,
    far_ref,
    wave_ref,
    cot_ref,
    project_ref,
    turned_ref,
    combine_ref,
    query_t_ref,
    act_in,
    kv_in,
    keys_t_in,
    values_t_in,
    act_ref,
    kv_ref,
    keys_t_ref,
    values_t_ref,
    probs_ref,
    inverse_sum_ref,
    attended_ref,
    *rest,
):
    del act_in, kv_in, keys_t_in, values_t_in
    *sent_refs, mixed_s = rest
    me = place_ref[0]
    core = place_ref[1] % 2
    frame_count, row_count, features = wave_ref.shape
    rim = far_ref.shape[1]
    width = features // HEADS
    block_count = row_count // BLOCK
    exponent_scale = math.log2(math.e) / math.sqrt(width)
    for frame in range(frame_count):
        project_rows(
            frame,
            halo_start(core, rim, row_count, False),
            far_ref[frame],
            project_ref,
            turned_ref,
            act_ref,
            kv_ref,
            keys_t_ref,
            values_t_ref,
        )
    blocks = [(frame, block) for frame in range(frame_count) for block in range(block_count)]
    loaded = {}

    def load(index):
        frame, block = blocks[index]
        places = listed_blocks(lists_ref, frame, block)
        keys = jnp.concatenate(
            [kv_ref[frame, pl.ds(place * BLOCK, BLOCK), :features] for place in places], axis=0
        )
        loaded[index] = (keys, query_t_ref[frame, :, block * BLOCK : (block + 1) * BLOCK], places)

    def pair_scores(step):
        index, pair = divmod(step, HEADS // 2)
        if index not in loaded:
            load(index)
        keys, query_t, _ = loaded[index]
        return dot_nn(pair_group(keys, pair, width), pair_columns(query_t, pair, width))

    steps = len(blocks) * HEADS // 2
    scores = pair_scores(0)
    outs = []
    for step in range(steps):
        following = pair_scores(step + 1) if step + 1 < steps else None
        index, pair = divmod(step, HEADS // 2)
        frame, block = blocks[index]
        if pair == 0:
            block_values_t = jnp.concatenate(
                [values_t_ref[frame, place] for place in loaded[index][2]], axis=1
            )
            outs = []
        top = jnp.max(scores, axis=0, keepdims=True)
        exp_scores = jnp.exp2((scores - top) * exponent_scale)
        inverse_sum = 1.0 / jnp.sum(exp_scores, axis=0, keepdims=True)
        probs = exp_scores.astype(BF16)
        probs_ref[frame, block, :, pair * 2 * BLOCK : (pair + 1) * 2 * BLOCK] = probs
        inverse_sum_ref[frame, block, 2 * pair : 2 * pair + 1] = inverse_sum[:, :BLOCK]
        inverse_sum_ref[frame, block, 2 * pair + 1 : 2 * pair + 2] = inverse_sum[:, BLOCK:]
        out = dot_nn(block_values_t[pair * 2 * width : (pair + 1) * 2 * width], probs)
        outs.append(pair_diagonal(out * inverse_sum, width))
        scores = following
        if pair == HEADS // 2 - 1:
            attended_t = jnp.concatenate(outs, axis=0)
            span = slice(block * BLOCK, (block + 1) * BLOCK)
            attended_ref[frame, :, span] = attended_t.astype(BF16)
            mixed_s[frame, span] = (
                wave_ref[frame, span].astype(F32) + dot_nn(flip(attended_t), combine_ref[0])
            ).astype(BF16)
    for distance, ref in enumerate(sent_refs):
        rows = ref.shape[1]
        span = pl.ds(pl.multiple_of((me ^ distance) * rows, GROUP_ROWS), rows)
        ref[:, :, :features] = mixed_s[:, span]
        ref[:, :, features:] = cot_ref[:, span]


def time_kernel(
    scale,
    count_in,
    *refs,
):
    arrived_refs = refs[:count_in]
    project_ref, turned_ref, combine_ref = refs[count_in : count_in + 3]
    grad_refs = refs[count_in + 3 : 2 * count_in + 3]
    act_ref, dproj_ref, attended_t_ref, cot_ref, mixed_ref = refs[2 * count_in + 3 :]
    part_frames, row_count, features = grad_refs[0].shape
    width = features // HEADS
    count = part_frames * count_in * GROUP_ROWS
    groups = row_count // GROUP_ROWS
    exponent_scale = scale * math.log2(math.e)

    def grouped(lanes):
        return jnp.concatenate(
            [
                ref[:, group * GROUP_ROWS : (group + 1) * GROUP_ROWS, lanes].reshape(
                    part_frames * GROUP_ROWS, features
                )
                for group in range(groups)
                for ref in arrived_refs
            ],
            axis=0,
        )

    rows = grouped(slice(0, features))
    cot = grouped(slice(features, 2 * features))
    cot_ref[...] = cot
    normed, inverse = layer_norm(rows)
    act = normed.astype(BF16)
    act_ref[...] = act
    projected = dot_nn(act, project_ref[1]).astype(BF16)
    projected_t = dot_nt(turned_ref[1], act).astype(BF16)
    all_dattn = dot_nt(cot, combine_ref[1]).astype(BF16)
    all_dattn_t = dot_nt(combine_ref[1], cot).astype(BF16)
    all_count = HEADS * count
    key_row = lax.broadcasted_iota(jnp.int32, (count, all_count), 0) % GROUP_ROWS
    query_row = lax.broadcasted_iota(jnp.int32, (count, all_count), 1) % GROUP_ROWS
    same_row = key_row == query_row
    attended_groups, dquery_groups, dkey_groups, dvalue_groups = [], [], [], []
    pairs = range(HEADS // 2)

    def products(group):
        span = slice(group * count, (group + 1) * count)
        return tuple(
            jnp.concatenate(
                [
                    dot_nn(pair_group(left, pair, width), pair_columns(right, pair, width))
                    for pair in pairs
                ],
                axis=1,
            )
            for left, right in (
                (projected[span, features : 2 * features], projected_t[:features, span]),
                (projected[span, 2 * features :], all_dattn_t[:, span]),
            )
        )

    def by_heads(left_t, right):
        return jnp.concatenate(
            [
                pair_diagonal(
                    dot_nn(
                        left_t[pair * 2 * width : (pair + 1) * 2 * width],
                        right[:, pair * 2 * count : (pair + 1) * 2 * count],
                    ),
                    width,
                )
                for pair in pairs
            ],
            axis=0,
        )

    scores, dprobs = products(0)
    for group in range(groups):
        following = products(group + 1) if group + 1 < groups else (None, None)
        span = slice(group * count, (group + 1) * count)
        scores = jnp.where(same_row, scores, -3e38)
        top = jnp.max(scores, axis=0, keepdims=True)
        exp_scores = jnp.exp2((scores - top) * exponent_scale)
        probs = (exp_scores * (1.0 / jnp.sum(exp_scores, axis=0, keepdims=True))).astype(BF16)
        probs_wide = probs.astype(F32)
        delta = jnp.sum(probs_wide * dprobs, axis=0, keepdims=True)
        dscores = (probs_wide * (dprobs - delta) * scale).astype(BF16)
        attended_groups.append(by_heads(projected_t[2 * features :, span], probs).astype(BF16))
        dquery_groups.append(flip(by_heads(projected_t[features : 2 * features, span], dscores)))
        dkey_groups.append(
            dot_nn(dscores, head_rows(projected[span, :features], width)).astype(BF16)
        )
        dvalue_groups.append(dot_nn(probs, head_rows(all_dattn[span], width)).astype(BF16))
        scores, dprobs = following
    attended = jnp.concatenate([flip(attended_t) for attended_t in attended_groups], axis=0)
    mixed_ref[...] = (rows.astype(F32) + dot_nn(attended, combine_ref[1])).astype(BF16)
    attended_t_ref[...] = jnp.concatenate(attended_groups, axis=1)
    dproj = jnp.concatenate(
        [jnp.concatenate(parts, axis=0) for parts in (dquery_groups, dkey_groups, dvalue_groups)],
        axis=1,
    )
    dproj_ref[...] = dproj
    dact = dot_nt(dproj, project_ref[1])
    mixed_grad = (cot.astype(F32) + norm_backward(dact, normed, inverse)).astype(BF16)
    for part, ref in enumerate(grad_refs):
        for group in range(groups):
            span = slice(group * GROUP_ROWS, (group + 1) * GROUP_ROWS)
            for frame in range(part_frames):
                start = ((group * count_in + part) * part_frames + frame) * GROUP_ROWS
                ref[frame, span] = mixed_grad[start : start + GROUP_ROWS]


def time_grads_kernel(
    factor, part_frames, row_count, place_ref, act_ref, dproj_ref, attended_t_ref, cot_ref, mixed_ref, *refs
):
    *ride_refs, stacked_s = refs
    count_in = len(ride_refs)
    features = act_ref.shape[1]
    groups = row_count // GROUP_ROWS
    stack_grads(
        [dot_tn(act_ref[...], dproj_ref[...]), dot_nn(attended_t_ref[...], cot_ref[...])],
        factor,
        stacked_s,
    )
    chunk = stacked_s.shape[0] // count_in
    part_rows = part_frames * row_count
    for part, ref in enumerate(ride_refs):
        for group in range(groups):
            for frame in range(part_frames):
                start = ((group * count_in + part) * part_frames + frame) * GROUP_ROWS
                for lane_group in range(features // LANES):
                    row = chunk + lane_group * part_rows + frame * row_count + group * GROUP_ROWS
                    ref[row : row + GROUP_ROWS] = mixed_ref[
                        start : start + GROUP_ROWS, lane_group * LANES : (lane_group + 1) * LANES
                    ]
        ref[:chunk] = stacked_s[
            pl.ds(pl.multiple_of((place_ref[0] ^ part) * chunk, GROUP_ROWS), chunk)
        ]


def space_backward_kernel(
    scale,
    factor,
    count_in,
    lists_ref,
    place_ref,
    *refs,
):
    returned_refs = refs[:count_in]
    (
        act_ref,
        kv_ref,
        keys_t_ref,
        query_ref,
        probs_ref,
        inverse_sum_ref,
        attended_ref,
        combine_ref,
        mixed_grad_ref,
        dquery_ref,
        dkv_ref,
        kept_ref,
        sent_ref,
        dscores_s,
        dkv_s,
        stacked_s,
    ) = refs[count_in:]
    me = place_ref[0]
    frame_count, row_count, features = mixed_grad_ref.shape
    width = features // HEADS
    block_count = row_count // BLOCK
    rim = HREACH * BLOCK
    for distance, ref in enumerate(returned_refs):
        rows = ref.shape[1]
        span = pl.ds(pl.multiple_of((me ^ distance) * rows, GROUP_ROWS), rows)
        mixed_grad_ref[:, span] = ref[...]
    blocks = [(frame, block) for frame in range(frame_count) for block in range(block_count)]
    all_dattn_t = [
        dot_nt(combine_ref[0], mixed_grad_ref[frame]).astype(BF16) for frame in range(frame_count)
    ]
    loaded = {}

    def load(index):
        frame, block = blocks[index]
        places = listed_blocks(lists_ref, frame, block)
        values = jnp.concatenate(
            [kv_ref[frame, pl.ds(place * BLOCK, BLOCK), features:] for place in places], axis=0
        )
        loaded[index] = (
            values,
            all_dattn_t[frame][:, block * BLOCK : (block + 1) * BLOCK],
            places,
        )

    def pair_products(step):
        index, pair = divmod(step, HEADS // 2)
        if index not in loaded:
            load(index)
        values, dattn_t, _ = loaded[index]
        return dot_nn(pair_group(values, pair, width), pair_columns(dattn_t, pair, width))

    def add_listed(index, lanes, parts):
        frame = blocks[index][0]
        for entry, place in enumerate(loaded[index][2]):
            rows = pl.ds(place * BLOCK, BLOCK)
            dkv_s[frame, rows, lanes] += parts[entry * BLOCK : (entry + 1) * BLOCK]

    def add_keys(index):
        frame, block = blocks[index]
        queries = head_rows(query_ref[frame, block * BLOCK : (block + 1) * BLOCK], width)
        add_listed(index, slice(0, features), dot_nn(dscores_s[frame, block], queries))

    dkv_s[...] = jnp.zeros(dkv_s.shape, F32)
    steps = len(blocks) * HEADS // 2
    dprobs = pair_products(0)
    dquery_parts = []
    for step in range(steps):
        following = pair_products(step + 1) if step + 1 < steps else None
        index, pair = divmod(step, HEADS // 2)
        frame, block = blocks[index]
        _, dattn_t, places = loaded[index]
        if pair == 0:
            span = slice(block * BLOCK, (block + 1) * BLOCK)
            block_keys_t = jnp.concatenate([keys_t_ref[frame, place] for place in places], axis=1)
            dattn_wide = dattn_t.astype(F32)
            inverse_sum = inverse_sum_ref[frame, block]
            delta = jnp.sum(
                (dattn_wide * attended_ref[frame, :, span].astype(F32)).reshape(
                    HEADS, width, BLOCK
                ),
                axis=1,
            )
            row_scale = inverse_sum * scale
            dquery_parts = []
        if pair == 1:
            scaled_dattn = flip(dattn_wide * head_spread(inverse_sum, width))
            add_listed(
                index,
                slice(features, 2 * features),
                dot_nn(probs_ref[frame, block], head_rows(scaled_dattn, width)),
            )
        if pair == 2 and index:
            add_keys(index - 1)
        heads = slice(pair * 2 * width, (pair + 1) * 2 * width)
        columns = slice(pair * 2 * BLOCK, (pair + 1) * 2 * BLOCK)
        pair_delta, pair_scale = (
            jnp.concatenate([rows[2 * pair : 2 * pair + 1], rows[2 * pair + 1 : 2 * pair + 2]], axis=1)
            for rows in (delta, row_scale)
        )
        probs = probs_ref[frame, block, :, columns].astype(F32)
        dscores = (probs * ((dprobs - pair_delta) * pair_scale)).astype(BF16)
        dscores_s[frame, block, :, columns] = dscores
        dquery_parts.append(pair_diagonal(dot_nn(block_keys_t[heads], dscores), width))
        dprobs = following
        if pair == HEADS // 2 - 1:
            dquery_ref[frame, span] = flip(jnp.concatenate(dquery_parts, axis=0))
    add_keys(len(blocks) - 1)
    dkv_ref[...] = dkv_s[...].astype(BF16)
    extended = dkv_ref.shape[1]
    act = act_ref[...]
    own_act = act[:, rim : rim + row_count].reshape(frame_count * row_count, features)
    stack_grads(
        [
            dot_tn(own_act, dquery_ref[...].reshape(frame_count * row_count, features)),
            dot_tn(
                act.reshape(frame_count * extended, features),
                dkv_ref[...].reshape(frame_count * extended, 2 * features),
            ),
            sum(
                dot_nn(attended_ref[frame], mixed_grad_ref[frame]) for frame in range(frame_count)
            ),
        ],
        factor,
        stacked_s,
    )
    halve(place_ref[1] % 2, stacked_s, kept_ref, sent_ref)


def dact_kernel(place_ref, dquery_ref, dkv_ref, project_ref, dact_ref, near_ref, far_ref, dact_s):
    frame_count, row_count, features = dquery_ref.shape
    rim = near_ref.shape[1]
    core = place_ref[1] % 2
    for frame in range(frame_count):
        dact = dot_nt(dkv_ref[frame], project_ref[0, :, features:])
        dact_s[frame] = dact.astype(BF16)
        dact_ref[frame] = dact[rim : rim + row_count] + dot_nt(
            dquery_ref[frame], project_ref[0, :, :features]
        )
    near_ref[...] = dact_s[:, pl.ds(halo_start(core, rim, row_count, True), rim)]
    far_ref[...] = dact_s[:, pl.ds(halo_start(core, rim, row_count, False), rim)]


def field_kernel(place_ref, wave_ref, mixed_grad_ref, dact_ref, near_ref, far_ref, *refs):
    *ride_refs, field_ref, mixed_ref = refs
    frame_count, row_count, features = wave_ref.shape
    rows = row_count // len(ride_refs)
    lane_groups = features // LANES
    part_rows = frame_count * rows
    for frame in range(frame_count):
        normed, inverse = layer_norm(wave_ref[frame])
        dact = dact_ref[frame] + near_ref[frame].astype(F32) + far_ref[frame].astype(F32)
        field_ref[frame] = (
            mixed_grad_ref[frame].astype(F32) + norm_backward(dact, normed, inverse)
        ).astype(BF16)
        for distance, ref in enumerate(ride_refs):
            span = pl.ds(pl.multiple_of((place_ref[0] ^ distance) * rows, GROUP_ROWS), rows)
            for lane_group in range(lane_groups):
                start = ref.shape[0] - (lane_groups - lane_group) * part_rows + frame * rows
                mixed_ref[frame, span, lane_group * LANES : (lane_group + 1) * LANES] = ref[
                    start : start + rows
                ]


def ordered_sum(me, refs, parts_s):
    rows = parts_s.shape[1]
    for distance, ref in enumerate(refs):
        parts_s[me ^ distance] = ref[:rows]
    total = parts_s[0].astype(F32)
    for part in range(1, len(refs)):
        total = total + parts_s[part].astype(F32)
    return total.astype(BF16)


def halve(core, whole_s, kept_ref, sent_ref):
    half = kept_ref.shape[0]
    kept_ref[...] = whole_s[pl.ds(pl.multiple_of(core * half, GROUP_ROWS), half)]
    sent_ref[...] = whole_s[pl.ds(pl.multiple_of((1 - core) * half, GROUP_ROWS), half)]


def cores_kernel(place_ref, *refs):
    *ride_refs, kept_ref, sent_ref, parts_s, time_s = refs
    time_s[...] = ordered_sum(place_ref[0], ride_refs, parts_s)
    halve(place_ref[1] % 2, time_s, kept_ref, sent_ref)


def split_kernel(place_ref, kept_ref, arrived_ref, *refs):
    *part_refs, sum_s = refs
    sum_s[...] = add_rounded(kept_ref, arrived_ref)
    rows = part_refs[0].shape[0]
    for distance, ref in enumerate(part_refs):
        ref[...] = sum_s[pl.ds(pl.multiple_of((place_ref[0] ^ distance) * rows, GROUP_ROWS), rows)]


def tm_sum_kernel(place_ref, *refs):
    *part_refs, time_ref, time_other_ref, space_out_ref, time_out_ref, parts_s = refs
    space_out_ref[...] = ordered_sum(place_ref[0], part_refs, parts_s)
    time_out_ref[...] = add_rounded(time_ref, time_other_ref)


def add_rounded(left_ref, right_ref):
    return (left_ref[...].astype(F32) + right_ref[...].astype(F32)).astype(BF16)


def pairs_kernel(*refs):
    out_refs = refs[2 * len(refs) // 3 :]
    for index, ref in enumerate(out_refs):
        ref[...] = add_rounded(refs[2 * index], refs[2 * index + 1])


def both_kernel(space_ref, space_other_ref, time_ref, total_ref):
    rows = space_ref.shape[0]
    total_ref[:rows] = add_rounded(space_ref, space_other_ref)
    total_ref[rows:] = time_ref[...]


def join_kernel(place_ref, *refs):
    *part_refs, joined_ref = refs
    for distance, ref in enumerate(part_refs):
        rows = ref.shape[0]
        joined_ref[pl.ds(pl.multiple_of((place_ref[0] ^ distance) * rows, GROUP_ROWS), rows)] = ref[
            ...
        ]


def grads_kernel(time_count, own, place_ref, half_ref, *refs):
    project_hbm, combine_hbm, wide_s, sems = refs[-4:]
    features = combine_hbm.shape[1]
    core = place_ref[1] % 2
    rows = half_ref.shape[0] // time_count // 2
    wide_s[...] = half_ref[...].astype(F32).reshape(wide_s.shape)

    def write(half):
        moves = []
        for part in range(time_count):
            for layer, row in ((0, (half * time_count + part) * rows), (1, (2 * part + half) * rows)):
                group, inner = divmod(row, features)
                start = group * LANES
                target, start = (
                    (project_hbm, start)
                    if start < 3 * features
                    else (combine_hbm, start - 3 * features)
                )
                piece = 2 * part + layer
                moves.append(
                    pltpu.make_async_copy(
                        wide_s.at[piece],
                        target.at[layer, pl.ds(inner, rows), pl.ds(start, LANES)],
                        sems.at[piece],
                    )
                )
        for move in moves:
            move.start()
        for move in moves:
            move.wait()

    for half in range(2):

        @pl.when((core if own else 1 - core) == half)
        def _():
            write(half)


def stack_grads(grads, factor, stacked_ref):
    row = 0
    for grad in grads:
        for lane in range(0, grad.shape[1], LANES):
            stacked_ref[row : row + grad.shape[0]] = (
                grad[:, lane : lane + LANES] * factor
            ).astype(BF16)
            row += grad.shape[0]


def in_hbm(cells):
    return pltpu.with_memory_space_constraint(cells, pltpu.HBM)


def swap_far(cells, axis):
    pairs = [(i, i + 1) for i in range(1, lax.axis_size(axis) - 1, 2)]
    return lax.ppermute(cells, axis, pairs + [(j, i) for i, j in pairs])


def exchange(cells, axis, distance):
    return lax.ppermute(cells, axis, [(i, i ^ distance) for i in range(lax.axis_size(axis))])


def per_device(wave_field, cotangent, block_lists, project_weights, combine_weights):
    frame_count, row_count, features = wave_field.shape
    width = features // HEADS
    scale = 1.0 / math.sqrt(width)
    block_count = row_count // BLOCK
    list_length = block_lists.shape[-1]
    rim = HREACH * BLOCK
    extended = row_count + 2 * rim
    keys_count = list_length * BLOCK
    time_count = lax.axis_size("tm")
    all_frames = frame_count * time_count
    sent_rows = row_count // time_count
    factor = 1.0 / math.sqrt(frame_count * row_count * time_count * lax.axis_size("space"))
    space_count = lax.axis_size("space") // 2
    grad_rows = 4 * features // LANES * features
    chunk = grad_rows // time_count
    ride_rows = chunk + frame_count * sent_rows * features // LANES
    tokens = all_frames * sent_rows
    places = block_count + 2 * HREACH
    smem_spec = pl.BlockSpec(memory_space=pltpu.SMEM)
    vmem_spec = pl.BlockSpec(memory_space=pltpu.VMEM)
    hbm_spec = pl.BlockSpec(memory_space=pl.ANY)

    def call(
        body, name, scalars, operands, outs, scratch=(), matmuls=1, hbm=(), aliases=None, out_spec=None
    ):
        def typed(shape):
            return (shape[:-1], shape[-1]) if not isinstance(shape[-1], int) else (shape, BF16)

        return pl.pallas_call(
            body,
            in_specs=[smem_spec] * len(scalars)
            + [vmem_spec] * len(operands)
            + [hbm_spec] * len(hbm),
            out_specs=[out_spec or vmem_spec] * len(outs),
            out_shape=[jax.ShapeDtypeStruct(*typed(shape)) for shape in outs],
            scratch_shapes=[
                pltpu.VMEM(*typed(shape)) if isinstance(shape, tuple) else shape
                for shape in scratch
            ],
            compiler_params=pltpu.CompilerParams(vmem_limit_bytes=VMEM_BYTES),
            cost_estimate=cost(matmuls),
            input_output_aliases=aliases or {},
            name=name,
        )(*scalars, *operands, *hbm)

    def over_tm(pieces):
        return [pieces[0]] + [exchange(pieces[d], "tm", d) for d in range(1, time_count)]

    own = (frame_count, row_count, features)
    part = (frame_count, sent_rows, features)
    near = exchange(wave_field, "space", 1)
    far = swap_far(wave_field, "space")
    place = jnp.stack([lax.axis_index("tm"), lax.axis_index("space")]).astype(jnp.int32)
    extended_shapes = [
        (frame_count, extended, features),
        (frame_count, extended, 2 * features),
        (frame_count, places, features, BLOCK),
        (frame_count, places, features, BLOCK),
    ]
    wave, project, turned, combine, cot, queries, queries_t, *projected = call(
        prepare_kernel,
        "prepare",
        [place],
        [near],
        [
            own,
            (2, features, 3 * features),
            (2, 3 * features, features),
            (2, features, features),
            own,
            own,
            (frame_count, features, row_count),
            *extended_shapes,
        ],
        [pltpu.SemaphoreType.DMA((4,))],
        matmuls=12,
        hbm=[in_hbm(cells) for cells in (wave_field, cotangent, project_weights, combine_weights)],
    )
    block_lists = in_hbm(block_lists)
    act, keys_values, keys_t, _, probs, inverse_sum, attended, *parts = call(
        space_forward_kernel,
        "space_forward",
        [block_lists, place],
        [far, wave, cot, project, turned, combine, queries_t, *projected],
        [
            *extended_shapes,
            (frame_count, block_count, keys_count, HEADS * BLOCK),
            (frame_count, block_count, HEADS, BLOCK, F32),
            (frame_count, features, row_count),
            *[(frame_count, sent_rows, 2 * features)] * time_count,
        ],
        [own],
        matmuls=40,
        aliases={9 + index: index for index in range(4)},
    )
    kept_space = [act, keys_values, keys_t, queries, probs, inverse_sum, attended]
    arrived = over_tm(parts)

    def time_body(*refs):
        time_kernel(scale, time_count, *refs)

    outs = call(
        time_body,
        "time_pair",
        [],
        [*arrived, project, turned, combine],
        [
            *[part] * time_count,
            (tokens, features),
            (tokens, 3 * features),
            (features, tokens),
            (tokens, features),
            (tokens, features),
        ],
        matmuls=36,
    )
    parts, kept_time = outs[:time_count], outs[time_count:]

    def time_grads_body(*refs):
        time_grads_kernel(factor, frame_count, sent_rows, *refs)

    rides = call(
        time_grads_body,
        "time_grads",
        [place],
        kept_time,
        [(ride_rows, LANES)] * time_count,
        [(grad_rows, LANES)],
        matmuls=6,
    )
    returned = over_tm(parts)
    rides = over_tm(rides)
    returned[1], rides[0] = lax.optimization_barrier((returned[1], rides[0]))

    def backward_body(*refs):
        space_backward_kernel(scale, factor, time_count, *refs)

    mixed_grad, dquery, dkv, space_kept, space_sent = call(
        backward_body,
        "space_backward",
        [block_lists, place],
        [*returned, *kept_space, combine],
        [own, own, (frame_count, extended, 2 * features), *[(grad_rows // 2, LANES)] * 2],
        [
            (frame_count, block_count, keys_count, HEADS * BLOCK),
            (frame_count, extended, 2 * features, F32),
            (grad_rows, LANES),
        ],
        matmuls=44,
    )

    def add_pair(name, piece, other):
        (total,) = call(pairs_kernel, name, [], [piece, other], [(chunk // 2, LANES)])
        return total

    space_other = exchange(space_sent, "space", 1)
    time_kept, time_sent = call(
        cores_kernel,
        "add_tm_time",
        [place],
        rides,
        [(chunk // 2, LANES)] * 2,
        [(time_count, chunk, LANES), (chunk, LANES)],
        matmuls=24,
    )
    time_other = exchange(time_sent, "space", 1)
    space_other, time_kept = lax.optimization_barrier((space_other, time_kept))
    space_pieces = call(
        split_kernel,
        "add_cores",
        [place],
        [space_kept, space_other],
        [(chunk // 2, LANES)] * time_count,
        [(grad_rows // 2, LANES)],
    )
    space_pieces = over_tm(space_pieces)
    time_piece = add_pair("add_cores_time", time_kept, time_other)
    steps = [2 << bit for bit in range((space_count - 1).bit_length())]
    time_other = exchange(time_piece, "space", steps[0])
    space_piece, time_piece = call(
        tm_sum_kernel,
        "add_tm_space",
        [place],
        [*space_pieces, time_piece, time_other],
        [(chunk // 2, LANES)] * 2,
        [(time_count, chunk // 2, LANES)],
    )

    space_piece, dquery = lax.optimization_barrier((space_piece, dquery))
    dact, to_near, to_far = call(
        dact_kernel,
        "space_dact",
        [place],
        [dquery, dkv, project],
        [(*own, F32), (frame_count, rim, features), (frame_count, rim, features)],
        [(frame_count, extended, features)],
        matmuls=3,
    )
    for step, time_step in zip(steps, steps[1:]):
        space_other = exchange(space_piece, "space", step)
        time_other = exchange(time_piece, "space", time_step)
        space_other, to_near, to_far = lax.optimization_barrier((space_other, to_near, to_far))
        space_piece = add_pair("add_space", space_piece, space_other)
        space_piece, time_other = lax.optimization_barrier((space_piece, time_other))
        time_piece = add_pair("add_space_time", time_piece, time_other)
    space_other = exchange(space_piece, "space", steps[-1])
    time_piece, to_near, to_far = lax.optimization_barrier((time_piece, to_near, to_far))
    from_far = swap_far(to_far, "space")
    from_near = exchange(to_near, "space", 1)
    (piece,) = call(
        both_kernel,
        "add_space_last",
        [],
        [space_piece, space_other, time_piece],
        [(chunk, LANES)],
        matmuls=64,
    )
    joined = over_tm([piece] * time_count)

    field_grad, mixed_field = call(
        field_kernel,
        "field_grad",
        [place],
        [wave, mixed_grad, dact, from_near, from_far, *rides],
        [own, own],
        matmuls=3,
    )
    field_grad, mixed_field, *joined = lax.optimization_barrier((field_grad, mixed_field, *joined))
    (own_half,) = call(join_kernel, "join_tm", [place], joined, [(grad_rows, LANES)])
    other_half = exchange(own_half, "space", 1)

    grads = ()
    for half in (own_half, other_half):

        def grads_body(*refs, mine=half is own_half):
            grads_kernel(time_count, mine, *refs)

        grads = call(
            grads_body,
            "weight_grads",
            [place],
            [half],
            [(2, features, 3 * features, F32), (2, features, features, F32)],
            [
                (2 * time_count, grad_rows // time_count // 2, LANES, F32),
                pltpu.SemaphoreType.DMA((2 * time_count,)),
            ],
            hbm=grads,
            aliases={2: 0, 3: 1} if grads else None,
            out_spec=pl.BlockSpec(memory_space=pltpu.HBM),
        )
    project_grad, combine_grad = grads
    return (mixed_field, field_grad, project_grad, combine_grad)


def solution(mesh):
    in_specs = (P("tm", "space", None), P("tm", "space", None), P("tm", "space", None), P(), P())
    out_specs = (P("tm", "space", None), P("tm", "space", None), P(), P())
    return jax.shard_map(
        per_device, mesh=mesh, in_specs=in_specs, out_specs=out_specs, check_vma=False
    )
```

```python
import math

import jax
import jax.numpy as jnp
from jax import lax
from jax.experimental import pallas as pl
from jax.experimental.pallas import tpu as pltpu
from jax.sharding import PartitionSpec as P

HEADS = 8
BLOCK = 128
HREACH = 2
LANES = 128
GROUP_ROWS = 16
VMEM_BYTES = 24 * 1024 * 1024
BF16 = jnp.bfloat16
F32 = jnp.float32


epsilon = 1e-05


def cost(matmuls):
    flops = matmuls * 2 * 1024 * 256 * 512
    return pl.CostEstimate(flops=flops, bytes_accessed=flops // 256, transcendentals=flops // 1024)


def dot_nn(left, right):
    return lax.dot_general(left, right, (((1,), (0,)), ((), ())), preferred_element_type=F32)


def dot_nt(left, right):
    return lax.dot_general(left, right, (((1,), (1,)), ((), ())), preferred_element_type=F32)


def dot_tn(left, right):
    return lax.dot_general(left, right, (((0,), (0,)), ((), ())), preferred_element_type=F32)


def layer_norm(rows):
    widened = rows.astype(F32)
    centered = widened - jnp.mean(widened, axis=-1, keepdims=True)
    inverse = lax.rsqrt(jnp.mean(centered * centered, axis=-1, keepdims=True) + epsilon)
    return (centered * inverse, inverse)


def norm_backward(upstream, normed, inverse):
    mean_grad = jnp.mean(upstream, axis=-1, keepdims=True)
    mean_cross = jnp.mean(upstream * normed, axis=-1, keepdims=True)
    return inverse * (upstream - mean_grad - normed * mean_cross)


def flip(matrix):
    return matrix.astype(BF16).T


def pair_columns(rows_t, pair, width):
    count = rows_t.shape[1]
    base = (pair * 2 * width) // LANES * LANES
    parts = []
    for head in (2 * pair, 2 * pair + 1):
        start = head * width - base
        pieces = []
        if start:
            pieces.append(jnp.zeros((start, count), rows_t.dtype))
        pieces.append(rows_t[head * width : (head + 1) * width])
        if start + width < LANES:
            pieces.append(jnp.zeros((LANES - start - width, count), rows_t.dtype))
        parts.append(jnp.concatenate(pieces, axis=0))
    return jnp.concatenate(parts, axis=1)


def pair_group(matrix, pair, width):
    base = (pair * 2 * width) // LANES * LANES
    return matrix[:, base : base + LANES]


def pair_diagonal(product, width):
    count = product.shape[1] // 2
    return jnp.concatenate([product[:width, :count], product[width:, count:]], axis=0)


def head_rows(rows, width):
    column = lax.broadcasted_iota(jnp.int32, (1, rows.shape[1]), 1) // width
    return jnp.concatenate(
        [rows * (column == head).astype(F32).astype(BF16) for head in range(HEADS)], axis=0
    )


def head_spread(per_head, width):
    return jnp.concatenate(
        [
            jnp.broadcast_to(per_head[head : head + 1], (width, per_head.shape[1]))
            for head in range(HEADS)
        ],
        axis=0,
    )


def listed_blocks(lists_ref, frame, block):
    own = lists_ref[frame, block, 0]
    return [
        lists_ref[frame, block, entry] - own + (block + HREACH)
        for entry in range(lists_ref.shape[2])
    ]


def halo_start(core, rim, row_count, near):
    after = core == 0 if near else core != 0
    return pl.multiple_of(jnp.where(after, rim + row_count, 0), BLOCK)


def project_rows(
    frame, start, rows, project_ref, turned_ref, act_ref, kv_ref, keys_t_ref, values_t_ref
):
    features = rows.shape[1]
    normed, _ = layer_norm(rows)
    act = normed.astype(BF16)
    span = pl.ds(start, rows.shape[0])
    act_ref[frame, span] = act
    kv_ref[frame, span] = dot_nn(act, project_ref[0, :, features:]).astype(BF16)
    keys_t = dot_nt(turned_ref[0, features : 2 * features], act).astype(BF16)
    values_t = dot_nt(turned_ref[0, 2 * features :], act).astype(BF16)
    for block in range(rows.shape[0] // BLOCK):
        lanes = slice(block * BLOCK, (block + 1) * BLOCK)
        keys_t_ref[frame, start // BLOCK + block] = keys_t[:, lanes]
        values_t_ref[frame, start // BLOCK + block] = values_t[:, lanes]
    return act


def prepare_kernel(
    place_ref,
    near_ref,
    wave_hbm,
    cot_hbm,
    project_hbm,
    combine_hbm,
    wave_ref,
    project_ref,
    turned_ref,
    combine_ref,
    cot_ref,
    query_ref,
    query_t_ref,
    act_ref,
    kv_ref,
    keys_t_ref,
    values_t_ref,
    sems,
):
    moves = [
        pltpu.make_async_copy(source, target, sems.at[index])
        for index, (source, target) in enumerate(
            (
                (project_hbm, project_ref),
                (wave_hbm, wave_ref),
                (combine_hbm, combine_ref),
                (cot_hbm, cot_ref),
            )
        )
    ]
    for move in moves:
        move.start()
    frame_count, row_count, features = wave_ref.shape
    rim = near_ref.shape[1]
    core = place_ref[1] % 2
    moves[0].wait()
    turned_ref[0] = flip(project_ref[0])
    for frame in range(frame_count):
        project_rows(
            frame,
            halo_start(core, rim, row_count, True),
            near_ref[frame],
            project_ref,
            turned_ref,
            act_ref,
            kv_ref,
            keys_t_ref,
            values_t_ref,
        )
    moves[1].wait()
    for frame in range(frame_count):
        act = project_rows(
            frame, rim, wave_ref[frame], project_ref, turned_ref, act_ref, kv_ref, keys_t_ref, values_t_ref
        )
        query_ref[frame] = dot_nn(act, project_ref[0, :, :features]).astype(BF16)
        query_t_ref[frame] = dot_nt(turned_ref[0, :features], act).astype(BF16)
    turned_ref[1] = flip(project_ref[1])
    moves[2].wait()
    moves[3].wait()


def space_forward_kernel(
    frame,
    sent_rows,
    lists_ref,
    place_ref,
    far_ref,
    wave_ref,
    cot_ref,
    project_ref,
    turned_ref,
    combine_ref,
    query_t_ref,
    *rest,
):
    me = place_ref[0]
    core = place_ref[1] % 2
    _, row_count, features = wave_ref.shape
    mixed_s = rest[-1]
    refs = rest[-8 - row_count // sent_rows : -1]
    act_ref, kv_ref, keys_t_ref, values_t_ref, probs_ref, inverse_sum_ref, attended_ref = refs[:7]
    sent_refs = refs[7:]
    rim = far_ref.shape[1]
    width = features // HEADS
    block_count = row_count // BLOCK
    exponent_scale = math.log2(math.e) / math.sqrt(width)
    project_rows(
        frame,
        halo_start(core, rim, row_count, False),
        far_ref[0],
        project_ref,
        turned_ref,
        act_ref,
        kv_ref,
        keys_t_ref,
        values_t_ref,
    )
    loaded = {}

    def load(block):
        places = listed_blocks(lists_ref, frame, block)
        keys = jnp.concatenate(
            [kv_ref[frame, pl.ds(place * BLOCK, BLOCK), :features] for place in places], axis=0
        )
        loaded[block] = (keys, query_t_ref[frame, :, block * BLOCK : (block + 1) * BLOCK], places)

    def pair_scores(step):
        block, pair = divmod(step, HEADS // 2)
        if block not in loaded:
            load(block)
        keys, query_t, _ = loaded[block]
        return dot_nn(pair_group(keys, pair, width), pair_columns(query_t, pair, width))

    steps = block_count * HEADS // 2
    scores = pair_scores(0)
    outs = []
    for step in range(steps):
        following = pair_scores(step + 1) if step + 1 < steps else None
        block, pair = divmod(step, HEADS // 2)
        if pair == 0:
            block_values_t = jnp.concatenate(
                [values_t_ref[frame, place] for place in loaded[block][2]], axis=1
            )
            outs = []
        top = jnp.max(scores, axis=0, keepdims=True)
        exp_scores = jnp.exp2((scores - top) * exponent_scale)
        inverse_sum = 1.0 / jnp.sum(exp_scores, axis=0, keepdims=True)
        probs = exp_scores.astype(BF16)
        probs_ref[frame, block, :, pair * 2 * BLOCK : (pair + 1) * 2 * BLOCK] = probs
        inverse_sum_ref[frame, block, 2 * pair : 2 * pair + 1] = inverse_sum[:, :BLOCK]
        inverse_sum_ref[frame, block, 2 * pair + 1 : 2 * pair + 2] = inverse_sum[:, BLOCK:]
        out = dot_nn(block_values_t[pair * 2 * width : (pair + 1) * 2 * width], probs)
        outs.append(pair_diagonal(out * inverse_sum, width))
        scores = following
        if pair == HEADS // 2 - 1:
            attended_t = jnp.concatenate(outs, axis=0)
            span = slice(block * BLOCK, (block + 1) * BLOCK)
            attended_ref[frame, :, span] = attended_t.astype(BF16)
            mixed_s[span] = (
                wave_ref[frame, span].astype(F32) + dot_nn(flip(attended_t), combine_ref[0])
            ).astype(BF16)
    for distance, ref in enumerate(sent_refs):
        span = pl.ds(pl.multiple_of((me ^ distance) * sent_rows, GROUP_ROWS), sent_rows)
        ref[frame, :, :features] = mixed_s[span]
        ref[frame, :, features:] = cot_ref[frame, span]


def time_kernel(
    scale,
    count_in,
    *refs,
):
    arrived_refs = refs[:count_in]
    project_ref, turned_ref, combine_ref = refs[count_in : count_in + 3]
    grad_refs = refs[count_in + 3 : 2 * count_in + 3]
    act_ref, dproj_ref, attended_t_ref, cot_ref, mixed_ref = refs[2 * count_in + 3 :]
    part_frames, row_count, features = grad_refs[0].shape
    width = features // HEADS
    count = part_frames * count_in * GROUP_ROWS
    groups = row_count // GROUP_ROWS
    exponent_scale = scale * math.log2(math.e)

    def grouped(lanes):
        return jnp.concatenate(
            [
                ref[:, group * GROUP_ROWS : (group + 1) * GROUP_ROWS, lanes].reshape(
                    part_frames * GROUP_ROWS, features
                )
                for group in range(groups)
                for ref in arrived_refs
            ],
            axis=0,
        )

    rows = grouped(slice(0, features))
    cot = grouped(slice(features, 2 * features))
    cot_ref[...] = cot
    normed, inverse = layer_norm(rows)
    act = normed.astype(BF16)
    act_ref[...] = act
    projected = dot_nn(act, project_ref[1]).astype(BF16)
    projected_t = dot_nt(turned_ref[1], act).astype(BF16)
    all_dattn = dot_nt(cot, combine_ref[1]).astype(BF16)
    all_dattn_t = dot_nt(combine_ref[1], cot).astype(BF16)
    all_count = HEADS * count
    key_row = lax.broadcasted_iota(jnp.int32, (count, all_count), 0) % GROUP_ROWS
    query_row = lax.broadcasted_iota(jnp.int32, (count, all_count), 1) % GROUP_ROWS
    same_row = key_row == query_row
    attended_groups, dquery_groups, dkey_groups, dvalue_groups = [], [], [], []
    pairs = range(HEADS // 2)

    def products(group):
        span = slice(group * count, (group + 1) * count)
        return tuple(
            jnp.concatenate(
                [
                    dot_nn(pair_group(left, pair, width), pair_columns(right, pair, width))
                    for pair in pairs
                ],
                axis=1,
            )
            for left, right in (
                (projected[span, features : 2 * features], projected_t[:features, span]),
                (projected[span, 2 * features :], all_dattn_t[:, span]),
            )
        )

    def by_heads(left_t, right):
        return jnp.concatenate(
            [
                pair_diagonal(
                    dot_nn(
                        left_t[pair * 2 * width : (pair + 1) * 2 * width],
                        right[:, pair * 2 * count : (pair + 1) * 2 * count],
                    ),
                    width,
                )
                for pair in pairs
            ],
            axis=0,
        )

    scores, dprobs = products(0)
    for group in range(groups):
        following = products(group + 1) if group + 1 < groups else (None, None)
        span = slice(group * count, (group + 1) * count)
        scores = jnp.where(same_row, scores, -3e38)
        top = jnp.max(scores, axis=0, keepdims=True)
        exp_scores = jnp.exp2((scores - top) * exponent_scale)
        probs = (exp_scores * (1.0 / jnp.sum(exp_scores, axis=0, keepdims=True))).astype(BF16)
        probs_wide = probs.astype(F32)
        delta = jnp.sum(probs_wide * dprobs, axis=0, keepdims=True)
        dscores = (probs_wide * (dprobs - delta) * scale).astype(BF16)
        attended_groups.append(by_heads(projected_t[2 * features :, span], probs).astype(BF16))
        dquery_groups.append(flip(by_heads(projected_t[features : 2 * features, span], dscores)))
        dkey_groups.append(
            dot_nn(dscores, head_rows(projected[span, :features], width)).astype(BF16)
        )
        dvalue_groups.append(dot_nn(probs, head_rows(all_dattn[span], width)).astype(BF16))
        scores, dprobs = following
    attended = jnp.concatenate([flip(attended_t) for attended_t in attended_groups], axis=0)
    mixed_ref[...] = (rows.astype(F32) + dot_nn(attended, combine_ref[1])).astype(BF16)
    attended_t_ref[...] = jnp.concatenate(attended_groups, axis=1)
    dproj = jnp.concatenate(
        [jnp.concatenate(parts, axis=0) for parts in (dquery_groups, dkey_groups, dvalue_groups)],
        axis=1,
    )
    dproj_ref[...] = dproj
    dact = dot_nt(dproj, project_ref[1])
    mixed_grad = (cot.astype(F32) + norm_backward(dact, normed, inverse)).astype(BF16)
    for part, ref in enumerate(grad_refs):
        for group in range(groups):
            span = slice(group * GROUP_ROWS, (group + 1) * GROUP_ROWS)
            for frame in range(part_frames):
                start = ((group * count_in + part) * part_frames + frame) * GROUP_ROWS
                ref[frame, span] = mixed_grad[start : start + GROUP_ROWS]


def time_grads_kernel(
    factor, part_frames, row_count, place_ref, act_ref, dproj_ref, attended_t_ref, cot_ref, mixed_ref, *refs
):
    *ride_refs, stacked_s = refs
    count_in = len(ride_refs)
    features = act_ref.shape[1]
    groups = row_count // GROUP_ROWS
    stack_grads(
        [dot_tn(act_ref[...], dproj_ref[...]), dot_nn(attended_t_ref[...], cot_ref[...])],
        factor,
        stacked_s,
    )
    chunk = stacked_s.shape[0] // count_in
    part_rows = part_frames * row_count
    for part, ref in enumerate(ride_refs):
        for group in range(groups):
            for frame in range(part_frames):
                start = ((group * count_in + part) * part_frames + frame) * GROUP_ROWS
                for lane_group in range(features // LANES):
                    row = chunk + lane_group * part_rows + frame * row_count + group * GROUP_ROWS
                    ref[row : row + GROUP_ROWS] = mixed_ref[
                        start : start + GROUP_ROWS, lane_group * LANES : (lane_group + 1) * LANES
                    ]
        ref[:chunk] = stacked_s[
            pl.ds(pl.multiple_of((place_ref[0] ^ part) * chunk, GROUP_ROWS), chunk)
        ]


def space_backward_kernel(
    scale,
    factor,
    count_in,
    lists_ref,
    place_ref,
    *refs,
):
    returned_refs = refs[:count_in]
    (
        act_ref,
        kv_ref,
        keys_t_ref,
        query_ref,
        probs_ref,
        inverse_sum_ref,
        attended_ref,
        combine_ref,
        mixed_grad_ref,
        dquery_ref,
        dkv_ref,
        kept_ref,
        sent_ref,
        dscores_s,
        dkv_s,
        stacked_s,
    ) = refs[count_in:]
    me = place_ref[0]
    frame_count, row_count, features = mixed_grad_ref.shape
    width = features // HEADS
    block_count = row_count // BLOCK
    rim = HREACH * BLOCK
    for distance, ref in enumerate(returned_refs):
        rows = ref.shape[1]
        span = pl.ds(pl.multiple_of((me ^ distance) * rows, GROUP_ROWS), rows)
        mixed_grad_ref[:, span] = ref[...]
    blocks = [(frame, block) for frame in range(frame_count) for block in range(block_count)]
    all_dattn_t = [
        dot_nt(combine_ref[0], mixed_grad_ref[frame]).astype(BF16) for frame in range(frame_count)
    ]
    loaded = {}

    def load(index):
        frame, block = blocks[index]
        places = listed_blocks(lists_ref, frame, block)
        values = jnp.concatenate(
            [kv_ref[frame, pl.ds(place * BLOCK, BLOCK), features:] for place in places], axis=0
        )
        loaded[index] = (
            values,
            all_dattn_t[frame][:, block * BLOCK : (block + 1) * BLOCK],
            places,
        )

    def pair_products(step):
        index, pair = divmod(step, HEADS // 2)
        if index not in loaded:
            load(index)
        values, dattn_t, _ = loaded[index]
        return dot_nn(pair_group(values, pair, width), pair_columns(dattn_t, pair, width))

    def add_listed(index, lanes, parts):
        frame = blocks[index][0]
        for entry, place in enumerate(loaded[index][2]):
            rows = pl.ds(place * BLOCK, BLOCK)
            dkv_s[frame, rows, lanes] += parts[entry * BLOCK : (entry + 1) * BLOCK]

    def add_keys(index):
        frame, block = blocks[index]
        queries = head_rows(query_ref[frame, block * BLOCK : (block + 1) * BLOCK], width)
        add_listed(index, slice(0, features), dot_nn(dscores_s[frame, block], queries))

    dkv_s[...] = jnp.zeros(dkv_s.shape, F32)
    steps = len(blocks) * HEADS // 2
    dprobs = pair_products(0)
    dquery_parts = []
    for step in range(steps):
        following = pair_products(step + 1) if step + 1 < steps else None
        index, pair = divmod(step, HEADS // 2)
        frame, block = blocks[index]
        _, dattn_t, places = loaded[index]
        if pair == 0:
            span = slice(block * BLOCK, (block + 1) * BLOCK)
            block_keys_t = jnp.concatenate([keys_t_ref[frame, place] for place in places], axis=1)
            dattn_wide = dattn_t.astype(F32)
            inverse_sum = inverse_sum_ref[frame, block]
            delta = jnp.sum(
                (dattn_wide * attended_ref[frame, :, span].astype(F32)).reshape(
                    HEADS, width, BLOCK
                ),
                axis=1,
            )
            row_scale = inverse_sum * scale
            dquery_parts = []
        if pair == 1:
            scaled_dattn = flip(dattn_wide * head_spread(inverse_sum, width))
            add_listed(
                index,
                slice(features, 2 * features),
                dot_nn(probs_ref[frame, block], head_rows(scaled_dattn, width)),
            )
        if pair == 2 and index:
            add_keys(index - 1)
        heads = slice(pair * 2 * width, (pair + 1) * 2 * width)
        columns = slice(pair * 2 * BLOCK, (pair + 1) * 2 * BLOCK)
        pair_delta, pair_scale = (
            jnp.concatenate([rows[2 * pair : 2 * pair + 1], rows[2 * pair + 1 : 2 * pair + 2]], axis=1)
            for rows in (delta, row_scale)
        )
        probs = probs_ref[frame, block, :, columns].astype(F32)
        dscores = (probs * ((dprobs - pair_delta) * pair_scale)).astype(BF16)
        dscores_s[frame, block, :, columns] = dscores
        dquery_parts.append(pair_diagonal(dot_nn(block_keys_t[heads], dscores), width))
        dprobs = following
        if pair == HEADS // 2 - 1:
            dquery_ref[frame, span] = flip(jnp.concatenate(dquery_parts, axis=0))
    add_keys(len(blocks) - 1)
    dkv_ref[...] = dkv_s[...].astype(BF16)
    extended = dkv_ref.shape[1]
    act = act_ref[...]
    own_act = act[:, rim : rim + row_count].reshape(frame_count * row_count, features)
    stack_grads(
        [
            dot_tn(own_act, dquery_ref[...].reshape(frame_count * row_count, features)),
            dot_tn(
                act.reshape(frame_count * extended, features),
                dkv_ref[...].reshape(frame_count * extended, 2 * features),
            ),
            sum(
                dot_nn(attended_ref[frame], mixed_grad_ref[frame]) for frame in range(frame_count)
            ),
        ],
        factor,
        stacked_s,
    )
    halve(place_ref[1] % 2, stacked_s, kept_ref, sent_ref)


def dact_kernel(place_ref, dquery_ref, dkv_ref, project_ref, dact_ref, near_ref, far_ref, dact_s):
    frame_count, row_count, features = dquery_ref.shape
    rim = near_ref.shape[1]
    core = place_ref[1] % 2
    for frame in range(frame_count):
        dact = dot_nt(dkv_ref[frame], project_ref[0, :, features:])
        dact_s[frame] = dact.astype(BF16)
        dact_ref[frame] = dact[rim : rim + row_count] + dot_nt(
            dquery_ref[frame], project_ref[0, :, :features]
        )
    near_ref[...] = dact_s[:, pl.ds(halo_start(core, rim, row_count, True), rim)]
    far_ref[...] = dact_s[:, pl.ds(halo_start(core, rim, row_count, False), rim)]


def field_kernel(place_ref, wave_ref, mixed_grad_ref, dact_ref, near_ref, far_ref, *refs):
    *ride_refs, field_ref, mixed_ref = refs
    frame_count, row_count, features = wave_ref.shape
    rows = row_count // len(ride_refs)
    lane_groups = features // LANES
    part_rows = frame_count * rows
    for frame in range(frame_count):
        normed, inverse = layer_norm(wave_ref[frame])
        dact = dact_ref[frame] + near_ref[frame].astype(F32) + far_ref[frame].astype(F32)
        field_ref[frame] = (
            mixed_grad_ref[frame].astype(F32) + norm_backward(dact, normed, inverse)
        ).astype(BF16)
        for distance, ref in enumerate(ride_refs):
            span = pl.ds(pl.multiple_of((place_ref[0] ^ distance) * rows, GROUP_ROWS), rows)
            for lane_group in range(lane_groups):
                start = ref.shape[0] - (lane_groups - lane_group) * part_rows + frame * rows
                mixed_ref[frame, span, lane_group * LANES : (lane_group + 1) * LANES] = ref[
                    start : start + rows
                ]


def ordered_sum(me, refs, parts_s):
    rows = parts_s.shape[1]
    for distance, ref in enumerate(refs):
        parts_s[me ^ distance] = ref[:rows]
    total = parts_s[0].astype(F32)
    for part in range(1, len(refs)):
        total = total + parts_s[part].astype(F32)
    return total.astype(BF16)


def halve(core, whole_s, kept_ref, sent_ref):
    half = kept_ref.shape[0]
    kept_ref[...] = whole_s[pl.ds(pl.multiple_of(core * half, GROUP_ROWS), half)]
    sent_ref[...] = whole_s[pl.ds(pl.multiple_of((1 - core) * half, GROUP_ROWS), half)]


def cores_kernel(place_ref, *refs):
    *ride_refs, kept_ref, sent_ref, parts_s, time_s = refs
    time_s[...] = ordered_sum(place_ref[0], ride_refs, parts_s)
    halve(place_ref[1] % 2, time_s, kept_ref, sent_ref)


def split_kernel(place_ref, kept_ref, arrived_ref, *refs):
    *part_refs, sum_s = refs
    sum_s[...] = add_rounded(kept_ref, arrived_ref)
    rows = part_refs[0].shape[0]
    for distance, ref in enumerate(part_refs):
        ref[...] = sum_s[pl.ds(pl.multiple_of((place_ref[0] ^ distance) * rows, GROUP_ROWS), rows)]


def tm_sum_kernel(place_ref, *refs):
    *part_refs, time_ref, time_other_ref, space_out_ref, time_out_ref, parts_s = refs
    space_out_ref[...] = ordered_sum(place_ref[0], part_refs, parts_s)
    time_out_ref[...] = add_rounded(time_ref, time_other_ref)


def add_rounded(left_ref, right_ref):
    return (left_ref[...].astype(F32) + right_ref[...].astype(F32)).astype(BF16)


def pairs_kernel(*refs):
    out_refs = refs[2 * len(refs) // 3 :]
    for index, ref in enumerate(out_refs):
        ref[...] = add_rounded(refs[2 * index], refs[2 * index + 1])


def both_kernel(space_ref, space_other_ref, time_ref, total_ref):
    rows = space_ref.shape[0]
    total_ref[:rows] = add_rounded(space_ref, space_other_ref)
    total_ref[rows:] = time_ref[...]


def grads_kernel(time_count, own, place_ref, *refs):
    project_hbm, combine_hbm, wide_s, sems = refs[-4:]
    features = combine_hbm.shape[1]
    core = place_ref[1] % 2
    rows = wide_s.shape[1] // 2
    for distance, ref in enumerate(refs[:time_count]):
        wide_s[place_ref[0] ^ distance] = ref[...].astype(F32)

    def write(half):
        moves = []
        for part in range(time_count):
            for layer, row in ((0, (half * time_count + part) * rows), (1, (2 * part + half) * rows)):
                group, inner = divmod(row, features)
                start = group * LANES
                target, start = (
                    (project_hbm, start)
                    if start < 3 * features
                    else (combine_hbm, start - 3 * features)
                )
                piece = 2 * part + layer
                moves.append(
                    pltpu.make_async_copy(
                        wide_s.at[part, pl.ds(layer * rows, rows)],
                        target.at[layer, pl.ds(inner, rows), pl.ds(start, LANES)],
                        sems.at[piece],
                    )
                )
        for move in moves:
            move.start()
        for move in moves:
            move.wait()

    for half in range(2):

        @pl.when((core if own else 1 - core) == half)
        def _():
            write(half)


def stack_grads(grads, factor, stacked_ref):
    row = 0
    for grad in grads:
        for lane in range(0, grad.shape[1], LANES):
            stacked_ref[row : row + grad.shape[0]] = (
                grad[:, lane : lane + LANES] * factor
            ).astype(BF16)
            row += grad.shape[0]


def in_hbm(cells):
    return pltpu.with_memory_space_constraint(cells, pltpu.HBM)


def swap_far(cells, axis):
    pairs = [(i, i + 1) for i in range(1, lax.axis_size(axis) - 1, 2)]
    return lax.ppermute(cells, axis, pairs + [(j, i) for i, j in pairs])


def exchange(cells, axis, distance):
    return lax.ppermute(cells, axis, [(i, i ^ distance) for i in range(lax.axis_size(axis))])


def per_device(wave_field, cotangent, block_lists, project_weights, combine_weights):
    frame_count, row_count, features = wave_field.shape
    width = features // HEADS
    scale = 1.0 / math.sqrt(width)
    block_count = row_count // BLOCK
    list_length = block_lists.shape[-1]
    rim = HREACH * BLOCK
    extended = row_count + 2 * rim
    keys_count = list_length * BLOCK
    time_count = lax.axis_size("tm")
    all_frames = frame_count * time_count
    sent_rows = row_count // time_count
    factor = 1.0 / math.sqrt(frame_count * row_count * time_count * lax.axis_size("space"))
    space_count = lax.axis_size("space") // 2
    grad_rows = 4 * features // LANES * features
    chunk = grad_rows // time_count
    ride_rows = chunk + frame_count * sent_rows * features // LANES
    tokens = all_frames * sent_rows
    places = block_count + 2 * HREACH
    smem_spec = pl.BlockSpec(memory_space=pltpu.SMEM)
    vmem_spec = pl.BlockSpec(memory_space=pltpu.VMEM)
    hbm_spec = pl.BlockSpec(memory_space=pl.ANY)

    def call(
        body, name, scalars, operands, outs, scratch=(), matmuls=1, hbm=(), aliases=None, out_spec=None
    ):
        def typed(shape):
            return (shape[:-1], shape[-1]) if not isinstance(shape[-1], int) else (shape, BF16)

        return pl.pallas_call(
            body,
            in_specs=[smem_spec] * len(scalars)
            + [vmem_spec] * len(operands)
            + [hbm_spec] * len(hbm),
            out_specs=[out_spec or vmem_spec] * len(outs),
            out_shape=[jax.ShapeDtypeStruct(*typed(shape)) for shape in outs],
            scratch_shapes=[
                pltpu.VMEM(*typed(shape)) if isinstance(shape, tuple) else shape
                for shape in scratch
            ],
            compiler_params=pltpu.CompilerParams(vmem_limit_bytes=VMEM_BYTES),
            cost_estimate=cost(matmuls),
            input_output_aliases=aliases or {},
            name=name,
        )(*scalars, *operands, *hbm)

    def over_tm(pieces):
        return [pieces[0]] + [exchange(pieces[d], "tm", d) for d in range(1, time_count)]

    own = (frame_count, row_count, features)
    part = (frame_count, sent_rows, features)
    near = exchange(wave_field, "space", 1)
    fars = [swap_far(wave_field[frame : frame + 1], "space") for frame in range(frame_count)]
    place = jnp.stack([lax.axis_index("tm"), lax.axis_index("space")]).astype(jnp.int32)
    extended_shapes = [
        (frame_count, extended, features),
        (frame_count, extended, 2 * features),
        (frame_count, places, features, BLOCK),
        (frame_count, places, features, BLOCK),
    ]
    wave, project, turned, combine, cot, queries, queries_t, *projected = call(
        prepare_kernel,
        "prepare",
        [place],
        [near],
        [
            own,
            (2, features, 3 * features),
            (2, 3 * features, features),
            (2, features, features),
            own,
            own,
            (frame_count, features, row_count),
            *extended_shapes,
        ],
        [pltpu.SemaphoreType.DMA((4,))],
        matmuls=12,
        hbm=[in_hbm(cells) for cells in (wave_field, cotangent, project_weights, combine_weights)],
    )
    block_lists = in_hbm(block_lists)
    space_outs = projected
    for frame, far in enumerate(fars):

        def forward_body(*refs, frame=frame):
            space_forward_kernel(frame, sent_rows, *refs)

        space_outs = call(
            forward_body,
            "space_forward",
            [block_lists, place],
            [far, wave, cot, project, turned, combine, queries_t, *space_outs],
            [
                *extended_shapes,
                (frame_count, block_count, keys_count, HEADS * BLOCK),
                (frame_count, block_count, HEADS, BLOCK, F32),
                (frame_count, features, row_count),
                *[(frame_count, sent_rows, 2 * features)] * time_count,
            ],
            [(row_count, features)],
            matmuls=20,
            aliases={9 + index: index for index in range(len(space_outs))},
        )
    act, keys_values, keys_t, _, probs, inverse_sum, attended, *parts = space_outs
    kept_space = [act, keys_values, keys_t, queries, probs, inverse_sum, attended]
    arrived = over_tm(parts)

    def time_body(*refs):
        time_kernel(scale, time_count, *refs)

    outs = call(
        time_body,
        "time_pair",
        [],
        [*arrived, project, turned, combine],
        [
            *[part] * time_count,
            (tokens, features),
            (tokens, 3 * features),
            (features, tokens),
            (tokens, features),
            (tokens, features),
        ],
        matmuls=36,
    )
    parts, kept_time = outs[:time_count], outs[time_count:]

    def time_grads_body(*refs):
        time_grads_kernel(factor, frame_count, sent_rows, *refs)

    rides = call(
        time_grads_body,
        "time_grads",
        [place],
        kept_time,
        [(ride_rows, LANES)] * time_count,
        [(grad_rows, LANES)],
        matmuls=6,
    )
    returned = over_tm(parts)
    rides = over_tm(rides)
    returned[1], rides[0] = lax.optimization_barrier((returned[1], rides[0]))

    def backward_body(*refs):
        space_backward_kernel(scale, factor, time_count, *refs)

    mixed_grad, dquery, dkv, space_kept, space_sent = call(
        backward_body,
        "space_backward",
        [block_lists, place],
        [*returned, *kept_space, combine],
        [own, own, (frame_count, extended, 2 * features), *[(grad_rows // 2, LANES)] * 2],
        [
            (frame_count, block_count, keys_count, HEADS * BLOCK),
            (frame_count, extended, 2 * features, F32),
            (grad_rows, LANES),
        ],
        matmuls=44,
    )

    def add_pair(name, piece, other):
        (total,) = call(pairs_kernel, name, [], [piece, other], [(chunk // 2, LANES)])
        return total

    space_other = exchange(space_sent, "space", 1)
    time_kept, time_sent = call(
        cores_kernel,
        "add_tm_time",
        [place],
        rides,
        [(chunk // 2, LANES)] * 2,
        [(time_count, chunk, LANES), (chunk, LANES)],
        matmuls=24,
    )
    time_other = exchange(time_sent, "space", 1)
    space_other, time_kept = lax.optimization_barrier((space_other, time_kept))
    space_pieces = call(
        split_kernel,
        "add_cores",
        [place],
        [space_kept, space_other],
        [(chunk // 2, LANES)] * time_count,
        [(grad_rows // 2, LANES)],
    )
    space_pieces = over_tm(space_pieces)
    time_piece = add_pair("add_cores_time", time_kept, time_other)
    steps = [2 << bit for bit in range((space_count - 1).bit_length())]
    time_other = exchange(time_piece, "space", steps[0])
    space_piece, time_piece = call(
        tm_sum_kernel,
        "add_tm_space",
        [place],
        [*space_pieces, time_piece, time_other],
        [(chunk // 2, LANES)] * 2,
        [(time_count, chunk // 2, LANES)],
    )

    space_piece, dquery = lax.optimization_barrier((space_piece, dquery))
    dact, to_near, to_far = call(
        dact_kernel,
        "space_dact",
        [place],
        [dquery, dkv, project],
        [(*own, F32), (frame_count, rim, features), (frame_count, rim, features)],
        [(frame_count, extended, features)],
        matmuls=3,
    )
    sent_piece = space_piece
    for step, time_step in zip(steps, steps[1:]):
        space_other = exchange(sent_piece, "space", step)
        time_other = exchange(time_piece, "space", time_step)
        space_other, to_near, to_far = lax.optimization_barrier((space_other, to_near, to_far))
        sent_piece = add_pair("add_space", space_piece, space_other)
        space_piece, time_other = lax.optimization_barrier((sent_piece, time_other))
        time_piece = add_pair("add_space_time", time_piece, time_other)
    space_other = exchange(sent_piece, "space", steps[-1])
    time_piece, to_near, to_far = lax.optimization_barrier((time_piece, to_near, to_far))
    from_far = swap_far(to_far, "space")
    from_near = exchange(to_near, "space", 1)
    (piece,) = call(
        both_kernel,
        "add_space_last",
        [],
        [space_piece, space_other, time_piece],
        [(chunk, LANES)],
        matmuls=64,
    )
    joined = over_tm([piece] * time_count)

    others = exchange(piece, "space", 1)
    from_near, others = lax.optimization_barrier((from_near, others))

    field_grad, mixed_field = call(
        field_kernel,
        "field_grad",
        [place],
        [wave, mixed_grad, dact, from_near, from_far, *rides],
        [own, own],
        matmuls=3,
    )
    field_grad, mixed_field, *joined = lax.optimization_barrier((field_grad, mixed_field, *joined))
    others = [others] + [exchange(part, "space", 1) for part in joined[1:]]

    grads = ()
    for half in (joined, others):

        def grads_body(*refs, mine=half is joined):
            grads_kernel(time_count, mine, *refs)

        grads = call(
            grads_body,
            "weight_grads",
            [place],
            half,
            [(2, features, 3 * features, F32), (2, features, features, F32)],
            [
                (time_count, chunk, LANES, F32),
                pltpu.SemaphoreType.DMA((2 * time_count,)),
            ],
            hbm=grads,
            aliases={1 + time_count: 0, 2 + time_count: 1} if grads else None,
            out_spec=pl.BlockSpec(memory_space=pltpu.HBM),
        )
    project_grad, combine_grad = grads
    return (mixed_field, field_grad, project_grad, combine_grad)


def solution(mesh):
    in_specs = (P("tm", "space", None), P("tm", "space", None), P("tm", "space", None), P(), P())
    out_specs = (P("tm", "space", None), P("tm", "space", None), P(), P())
    return jax.shard_map(
        per_device, mesh=mesh, in_specs=in_specs, out_specs=out_specs, check_vma=False
    )
```

```python
import math

import jax
import jax.numpy as jnp
from jax import lax
from jax.experimental import pallas as pl
from jax.experimental.pallas import tpu as pltpu
from jax.sharding import PartitionSpec as P

HEADS = 8
BLOCK = 128
HREACH = 2
LANES = 128
GROUP_ROWS = 16
VMEM_BYTES = 24 * 1024 * 1024
BF16 = jnp.bfloat16
F32 = jnp.float32


epsilon = 1e-05


def cost(matmuls):
    flops = matmuls * 2 * 1024 * 256 * 512
    return pl.CostEstimate(flops=flops, bytes_accessed=flops // 256, transcendentals=flops // 1024)


def dot_nn(left, right):
    return lax.dot_general(left, right, (((1,), (0,)), ((), ())), preferred_element_type=F32)


def dot_nt(left, right):
    return lax.dot_general(left, right, (((1,), (1,)), ((), ())), preferred_element_type=F32)


def dot_tn(left, right):
    return lax.dot_general(left, right, (((0,), (0,)), ((), ())), preferred_element_type=F32)


def layer_norm(rows):
    widened = rows.astype(F32)
    centered = widened - jnp.mean(widened, axis=-1, keepdims=True)
    inverse = lax.rsqrt(jnp.mean(centered * centered, axis=-1, keepdims=True) + epsilon)
    return (centered * inverse, inverse)


def norm_backward(upstream, normed, inverse):
    mean_grad = jnp.mean(upstream, axis=-1, keepdims=True)
    mean_cross = jnp.mean(upstream * normed, axis=-1, keepdims=True)
    return inverse * (upstream - mean_grad - normed * mean_cross)


def flip(matrix):
    return matrix.astype(BF16).T


def pair_columns(rows_t, pair, width):
    count = rows_t.shape[1]
    base = (pair * 2 * width) // LANES * LANES
    parts = []
    for head in (2 * pair, 2 * pair + 1):
        start = head * width - base
        pieces = []
        if start:
            pieces.append(jnp.zeros((start, count), rows_t.dtype))
        pieces.append(rows_t[head * width : (head + 1) * width])
        if start + width < LANES:
            pieces.append(jnp.zeros((LANES - start - width, count), rows_t.dtype))
        parts.append(jnp.concatenate(pieces, axis=0))
    return jnp.concatenate(parts, axis=1)


def pair_group(matrix, pair, width):
    base = (pair * 2 * width) // LANES * LANES
    return matrix[:, base : base + LANES]


def pair_diagonal(product, width):
    count = product.shape[1] // 2
    return jnp.concatenate([product[:width, :count], product[width:, count:]], axis=0)


def head_rows(rows, width):
    column = lax.broadcasted_iota(jnp.int32, (1, rows.shape[1]), 1) // width
    return jnp.concatenate(
        [rows * (column == head).astype(F32).astype(BF16) for head in range(HEADS)], axis=0
    )


def head_spread(per_head, width):
    return jnp.concatenate(
        [
            jnp.broadcast_to(per_head[head : head + 1], (width, per_head.shape[1]))
            for head in range(HEADS)
        ],
        axis=0,
    )


def listed_blocks(lists_ref, frame, block):
    own = lists_ref[frame, block, 0]
    return [
        lists_ref[frame, block, entry] - own + (block + HREACH)
        for entry in range(lists_ref.shape[2])
    ]


def halo_start(core, rim, row_count, near):
    after = core == 0 if near else core != 0
    return pl.multiple_of(jnp.where(after, rim + row_count, 0), BLOCK)


def project_rows(
    frame, start, rows, project_ref, turned_ref, act_ref, kv_ref, keys_t_ref, values_t_ref
):
    features = rows.shape[1]
    normed, _ = layer_norm(rows)
    act = normed.astype(BF16)
    span = pl.ds(start, rows.shape[0])
    act_ref[frame, span] = act
    kv_ref[frame, span] = dot_nn(act, project_ref[0, :, features:]).astype(BF16)
    keys_t = dot_nt(turned_ref[0, features : 2 * features], act).astype(BF16)
    values_t = dot_nt(turned_ref[0, 2 * features :], act).astype(BF16)
    for block in range(rows.shape[0] // BLOCK):
        lanes = slice(block * BLOCK, (block + 1) * BLOCK)
        keys_t_ref[frame, start // BLOCK + block] = keys_t[:, lanes]
        values_t_ref[frame, start // BLOCK + block] = values_t[:, lanes]
    return act


def prepare_kernel(
    place_ref,
    near_ref,
    wave_hbm,
    cot_hbm,
    project_hbm,
    combine_hbm,
    wave_ref,
    project_ref,
    turned_ref,
    combine_ref,
    cot_ref,
    query_ref,
    query_t_ref,
    act_ref,
    kv_ref,
    keys_t_ref,
    values_t_ref,
    sems,
):
    moves = [
        pltpu.make_async_copy(source, target, sems.at[index])
        for index, (source, target) in enumerate(
            (
                (project_hbm, project_ref),
                (wave_hbm, wave_ref),
                (combine_hbm, combine_ref),
                (cot_hbm, cot_ref),
            )
        )
    ]
    for move in moves:
        move.start()
    frame_count, row_count, features = wave_ref.shape
    rim = near_ref.shape[1]
    core = place_ref[1] % 2
    moves[0].wait()
    turned_ref[0] = flip(project_ref[0])
    for frame in range(frame_count):
        project_rows(
            frame,
            halo_start(core, rim, row_count, True),
            near_ref[frame],
            project_ref,
            turned_ref,
            act_ref,
            kv_ref,
            keys_t_ref,
            values_t_ref,
        )
    moves[1].wait()
    for frame in range(frame_count):
        act = project_rows(
            frame, rim, wave_ref[frame], project_ref, turned_ref, act_ref, kv_ref, keys_t_ref, values_t_ref
        )
        query_ref[frame] = dot_nn(act, project_ref[0, :, :features]).astype(BF16)
        query_t_ref[frame] = dot_nt(turned_ref[0, :features], act).astype(BF16)
    turned_ref[1] = flip(project_ref[1])
    moves[2].wait()
    moves[3].wait()


def space_forward_kernel(
    lists_ref,
    place_ref,
    far_ref,
    wave_ref,
    cot_ref,
    project_ref,
    turned_ref,
    combine_ref,
    query_t_ref,
    act_in,
    kv_in,
    keys_t_in,
    values_t_in,
    act_ref,
    kv_ref,
    keys_t_ref,
    values_t_ref,
    probs_ref,
    inverse_sum_ref,
    attended_ref,
    *rest,
):
    del act_in, kv_in, keys_t_in, values_t_in
    *sent_refs, mixed_s = rest
    me = place_ref[0]
    core = place_ref[1] % 2
    frame_count, row_count, features = wave_ref.shape
    rim = far_ref.shape[1]
    width = features // HEADS
    block_count = row_count // BLOCK
    exponent_scale = math.log2(math.e) / math.sqrt(width)
    for frame in range(frame_count):
        project_rows(
            frame,
            halo_start(core, rim, row_count, False),
            far_ref[frame],
            project_ref,
            turned_ref,
            act_ref,
            kv_ref,
            keys_t_ref,
            values_t_ref,
        )
    blocks = [(frame, block) for frame in range(frame_count) for block in range(block_count)]
    loaded = {}

    def load(index):
        frame, block = blocks[index]
        places = listed_blocks(lists_ref, frame, block)
        keys = jnp.concatenate(
            [kv_ref[frame, pl.ds(place * BLOCK, BLOCK), :features] for place in places], axis=0
        )
        loaded[index] = (keys, query_t_ref[frame, :, block * BLOCK : (block + 1) * BLOCK], places)

    def pair_scores(step):
        index, pair = divmod(step, HEADS // 2)
        if index not in loaded:
            load(index)
        keys, query_t, _ = loaded[index]
        return dot_nn(pair_group(keys, pair, width), pair_columns(query_t, pair, width))

    steps = len(blocks) * HEADS // 2
    scores = pair_scores(0)
    outs = []
    for step in range(steps):
        following = pair_scores(step + 1) if step + 1 < steps else None
        index, pair = divmod(step, HEADS // 2)
        frame, block = blocks[index]
        if pair == 0:
            block_values_t = jnp.concatenate(
                [values_t_ref[frame, place] for place in loaded[index][2]], axis=1
            )
            outs = []
        top = jnp.max(scores, axis=0, keepdims=True)
        exp_scores = jnp.exp2((scores - top) * exponent_scale)
        inverse_sum = 1.0 / jnp.sum(exp_scores, axis=0, keepdims=True)
        probs = exp_scores.astype(BF16)
        probs_ref[frame, block, :, pair * 2 * BLOCK : (pair + 1) * 2 * BLOCK] = probs
        inverse_sum_ref[frame, block, 2 * pair : 2 * pair + 1] = inverse_sum[:, :BLOCK]
        inverse_sum_ref[frame, block, 2 * pair + 1 : 2 * pair + 2] = inverse_sum[:, BLOCK:]
        out = dot_nn(block_values_t[pair * 2 * width : (pair + 1) * 2 * width], probs)
        outs.append(pair_diagonal(out * inverse_sum, width))
        scores = following
        if pair == HEADS // 2 - 1:
            attended_t = jnp.concatenate(outs, axis=0)
            span = slice(block * BLOCK, (block + 1) * BLOCK)
            attended_ref[frame, :, span] = attended_t.astype(BF16)
            mixed_s[frame, span] = (
                wave_ref[frame, span].astype(F32) + dot_nn(flip(attended_t), combine_ref[0])
            ).astype(BF16)
    for distance, ref in enumerate(sent_refs):
        rows = ref.shape[1]
        span = pl.ds(pl.multiple_of((me ^ distance) * rows, GROUP_ROWS), rows)
        ref[:, :, :features] = mixed_s[:, span]
        ref[:, :, features:] = cot_ref[:, span]


def time_kernel(
    scale,
    count_in,
    *refs,
):
    arrived_refs = refs[:count_in]
    project_ref, turned_ref, combine_ref = refs[count_in : count_in + 3]
    grad_refs = refs[count_in + 3 : 2 * count_in + 3]
    act_ref, dproj_ref, attended_t_ref, cot_ref, mixed_ref = refs[2 * count_in + 3 :]
    part_frames, row_count, features = grad_refs[0].shape
    width = features // HEADS
    count = part_frames * count_in * GROUP_ROWS
    groups = row_count // GROUP_ROWS
    exponent_scale = scale * math.log2(math.e)

    def grouped(lanes):
        return jnp.concatenate(
            [
                ref[:, group * GROUP_ROWS : (group + 1) * GROUP_ROWS, lanes].reshape(
                    part_frames * GROUP_ROWS, features
                )
                for group in range(groups)
                for ref in arrived_refs
            ],
            axis=0,
        )

    rows = grouped(slice(0, features))
    cot = grouped(slice(features, 2 * features))
    cot_ref[...] = cot
    normed, inverse = layer_norm(rows)
    act = normed.astype(BF16)
    act_ref[...] = act
    projected = dot_nn(act, project_ref[1]).astype(BF16)
    projected_t = dot_nt(turned_ref[1], act).astype(BF16)
    all_dattn = dot_nt(cot, combine_ref[1]).astype(BF16)
    all_dattn_t = dot_nt(combine_ref[1], cot).astype(BF16)
    all_count = HEADS * count
    key_row = lax.broadcasted_iota(jnp.int32, (count, all_count), 0) % GROUP_ROWS
    query_row = lax.broadcasted_iota(jnp.int32, (count, all_count), 1) % GROUP_ROWS
    same_row = key_row == query_row
    attended_groups, dquery_groups, dkey_groups, dvalue_groups = [], [], [], []
    pairs = range(HEADS // 2)

    def products(group):
        span = slice(group * count, (group + 1) * count)
        return tuple(
            jnp.concatenate(
                [
                    dot_nn(pair_group(left, pair, width), pair_columns(right, pair, width))
                    for pair in pairs
                ],
                axis=1,
            )
            for left, right in (
                (projected[span, features : 2 * features], projected_t[:features, span]),
                (projected[span, 2 * features :], all_dattn_t[:, span]),
            )
        )

    def by_heads(left_t, right):
        return jnp.concatenate(
            [
                pair_diagonal(
                    dot_nn(
                        left_t[pair * 2 * width : (pair + 1) * 2 * width],
                        right[:, pair * 2 * count : (pair + 1) * 2 * count],
                    ),
                    width,
                )
                for pair in pairs
            ],
            axis=0,
        )

    scores, dprobs = products(0)
    for group in range(groups):
        following = products(group + 1) if group + 1 < groups else (None, None)
        span = slice(group * count, (group + 1) * count)
        scores = jnp.where(same_row, scores, -3e38)
        top = jnp.max(scores, axis=0, keepdims=True)
        exp_scores = jnp.exp2((scores - top) * exponent_scale)
        probs = (exp_scores * (1.0 / jnp.sum(exp_scores, axis=0, keepdims=True))).astype(BF16)
        probs_wide = probs.astype(F32)
        delta = jnp.sum(probs_wide * dprobs, axis=0, keepdims=True)
        dscores = (probs_wide * (dprobs - delta) * scale).astype(BF16)
        attended_groups.append(by_heads(projected_t[2 * features :, span], probs).astype(BF16))
        dquery_groups.append(flip(by_heads(projected_t[features : 2 * features, span], dscores)))
        dkey_groups.append(
            dot_nn(dscores, head_rows(projected[span, :features], width)).astype(BF16)
        )
        dvalue_groups.append(dot_nn(probs, head_rows(all_dattn[span], width)).astype(BF16))
        scores, dprobs = following
    attended = jnp.concatenate([flip(attended_t) for attended_t in attended_groups], axis=0)
    mixed_ref[...] = (rows.astype(F32) + dot_nn(attended, combine_ref[1])).astype(BF16)
    attended_t_ref[...] = jnp.concatenate(attended_groups, axis=1)
    dproj = jnp.concatenate(
        [jnp.concatenate(parts, axis=0) for parts in (dquery_groups, dkey_groups, dvalue_groups)],
        axis=1,
    )
    dproj_ref[...] = dproj
    dact = dot_nt(dproj, project_ref[1])
    mixed_grad = (cot.astype(F32) + norm_backward(dact, normed, inverse)).astype(BF16)
    for part, ref in enumerate(grad_refs):
        for group in range(groups):
            span = slice(group * GROUP_ROWS, (group + 1) * GROUP_ROWS)
            for frame in range(part_frames):
                start = ((group * count_in + part) * part_frames + frame) * GROUP_ROWS
                ref[frame, span] = mixed_grad[start : start + GROUP_ROWS]


def time_grads_kernel(
    factor, part_frames, row_count, place_ref, act_ref, dproj_ref, attended_t_ref, cot_ref, mixed_ref, *refs
):
    *ride_refs, stacked_s = refs
    count_in = len(ride_refs)
    features = act_ref.shape[1]
    groups = row_count // GROUP_ROWS
    stack_grads(
        [dot_tn(act_ref[...], dproj_ref[...]), dot_nn(attended_t_ref[...], cot_ref[...])],
        factor,
        stacked_s,
    )
    chunk = stacked_s.shape[0] // count_in
    part_rows = part_frames * row_count
    for part, ref in enumerate(ride_refs):
        for group in range(groups):
            for frame in range(part_frames):
                start = ((group * count_in + part) * part_frames + frame) * GROUP_ROWS
                for lane_group in range(features // LANES):
                    row = chunk + lane_group * part_rows + frame * row_count + group * GROUP_ROWS
                    ref[row : row + GROUP_ROWS] = mixed_ref[
                        start : start + GROUP_ROWS, lane_group * LANES : (lane_group + 1) * LANES
                    ]
        ref[:chunk] = stacked_s[
            pl.ds(pl.multiple_of((place_ref[0] ^ part) * chunk, GROUP_ROWS), chunk)
        ]


def space_backward_kernel(
    scale,
    count_in,
    lists_ref,
    place_ref,
    *refs,
):
    returned_refs = refs[:count_in]
    (
        act_ref,
        kv_ref,
        keys_t_ref,
        query_ref,
        probs_ref,
        inverse_sum_ref,
        attended_ref,
        project_ref,
        combine_ref,
        mixed_grad_ref,
        dquery_ref,
        dkv_ref,
        dact_ref,
        near_ref,
        far_ref,
        dscores_s,
        dkv_s,
        dact_s,
    ) = refs[count_in:]
    me = place_ref[0]
    frame_count, row_count, features = mixed_grad_ref.shape
    width = features // HEADS
    block_count = row_count // BLOCK
    rim = HREACH * BLOCK
    for distance, ref in enumerate(returned_refs):
        rows = ref.shape[1]
        span = pl.ds(pl.multiple_of((me ^ distance) * rows, GROUP_ROWS), rows)
        mixed_grad_ref[:, span] = ref[...]
    blocks = [(frame, block) for frame in range(frame_count) for block in range(block_count)]
    all_dattn_t = [
        dot_nt(combine_ref[0], mixed_grad_ref[frame]).astype(BF16) for frame in range(frame_count)
    ]
    loaded = {}

    def load(index):
        frame, block = blocks[index]
        places = listed_blocks(lists_ref, frame, block)
        values = jnp.concatenate(
            [kv_ref[frame, pl.ds(place * BLOCK, BLOCK), features:] for place in places], axis=0
        )
        loaded[index] = (
            values,
            all_dattn_t[frame][:, block * BLOCK : (block + 1) * BLOCK],
            places,
        )

    def pair_products(step):
        index, pair = divmod(step, HEADS // 2)
        if index not in loaded:
            load(index)
        values, dattn_t, _ = loaded[index]
        return dot_nn(pair_group(values, pair, width), pair_columns(dattn_t, pair, width))

    def add_listed(index, lanes, parts):
        frame = blocks[index][0]
        for entry, place in enumerate(loaded[index][2]):
            rows = pl.ds(place * BLOCK, BLOCK)
            dkv_s[frame, rows, lanes] += parts[entry * BLOCK : (entry + 1) * BLOCK]

    def add_keys(index):
        frame, block = blocks[index]
        queries = head_rows(query_ref[frame, block * BLOCK : (block + 1) * BLOCK], width)
        add_listed(index, slice(0, features), dot_nn(dscores_s[frame, block], queries))

    dkv_s[...] = jnp.zeros(dkv_s.shape, F32)
    steps = len(blocks) * HEADS // 2
    dprobs = pair_products(0)
    dquery_parts = []
    for step in range(steps):
        following = pair_products(step + 1) if step + 1 < steps else None
        index, pair = divmod(step, HEADS // 2)
        frame, block = blocks[index]
        _, dattn_t, places = loaded[index]
        if pair == 0:
            span = slice(block * BLOCK, (block + 1) * BLOCK)
            block_keys_t = jnp.concatenate([keys_t_ref[frame, place] for place in places], axis=1)
            dattn_wide = dattn_t.astype(F32)
            inverse_sum = inverse_sum_ref[frame, block]
            delta = jnp.sum(
                (dattn_wide * attended_ref[frame, :, span].astype(F32)).reshape(
                    HEADS, width, BLOCK
                ),
                axis=1,
            )
            row_scale = inverse_sum * scale
            dquery_parts = []
        if pair == 1:
            scaled_dattn = flip(dattn_wide * head_spread(inverse_sum, width))
            add_listed(
                index,
                slice(features, 2 * features),
                dot_nn(probs_ref[frame, block], head_rows(scaled_dattn, width)),
            )
        if pair == 2 and index:
            add_keys(index - 1)
        heads = slice(pair * 2 * width, (pair + 1) * 2 * width)
        columns = slice(pair * 2 * BLOCK, (pair + 1) * 2 * BLOCK)
        pair_delta, pair_scale = (
            jnp.concatenate([rows[2 * pair : 2 * pair + 1], rows[2 * pair + 1 : 2 * pair + 2]], axis=1)
            for rows in (delta, row_scale)
        )
        probs = probs_ref[frame, block, :, columns].astype(F32)
        dscores = (probs * ((dprobs - pair_delta) * pair_scale)).astype(BF16)
        dscores_s[frame, block, :, columns] = dscores
        dquery_parts.append(pair_diagonal(dot_nn(block_keys_t[heads], dscores), width))
        dprobs = following
        if pair == HEADS // 2 - 1:
            dquery_ref[frame, span] = flip(jnp.concatenate(dquery_parts, axis=0))
    add_keys(len(blocks) - 1)
    dkv_ref[...] = dkv_s[...].astype(BF16)
    core = place_ref[1] % 2
    for frame in range(frame_count):
        dact = dot_nt(dkv_ref[frame], project_ref[0, :, features:])
        dact_s[frame] = dact.astype(BF16)
        dact_ref[frame] = dact[rim : rim + row_count] + dot_nt(
            dquery_ref[frame], project_ref[0, :, :features]
        )
    near_ref[...] = dact_s[:, pl.ds(halo_start(core, rim, row_count, True), rim)]
    far_ref[...] = dact_s[:, pl.ds(halo_start(core, rim, row_count, False), rim)]


def space_grads_kernel(
    factor,
    place_ref,
    act_ref,
    dquery_ref,
    dkv_ref,
    attended_ref,
    mixed_grad_ref,
    kept_ref,
    sent_ref,
    stacked_s,
):
    frame_count, row_count, features = mixed_grad_ref.shape
    extended = dkv_ref.shape[1]
    rim = (extended - row_count) // 2
    act = act_ref[...]
    own_act = act[:, rim : rim + row_count].reshape(frame_count * row_count, features)
    stack_grads(
        [
            dot_tn(own_act, dquery_ref[...].reshape(frame_count * row_count, features)),
            dot_tn(
                act.reshape(frame_count * extended, features),
                dkv_ref[...].reshape(frame_count * extended, 2 * features),
            ),
            sum(
                dot_nn(attended_ref[frame], mixed_grad_ref[frame]) for frame in range(frame_count)
            ),
        ],
        factor,
        stacked_s,
    )
    halve(place_ref[1] % 2, stacked_s, kept_ref, sent_ref)


def field_kernel(place_ref, wave_ref, mixed_grad_ref, dact_ref, near_ref, far_ref, *refs):
    *ride_refs, field_ref, mixed_ref = refs
    frame_count, row_count, features = wave_ref.shape
    rows = row_count // len(ride_refs)
    lane_groups = features // LANES
    part_rows = frame_count * rows
    for frame in range(frame_count):
        normed, inverse = layer_norm(wave_ref[frame])
        dact = dact_ref[frame] + near_ref[frame].astype(F32) + far_ref[frame].astype(F32)
        field_ref[frame] = (
            mixed_grad_ref[frame].astype(F32) + norm_backward(dact, normed, inverse)
        ).astype(BF16)
        for distance, ref in enumerate(ride_refs):
            span = pl.ds(pl.multiple_of((place_ref[0] ^ distance) * rows, GROUP_ROWS), rows)
            for lane_group in range(lane_groups):
                start = ref.shape[0] - (lane_groups - lane_group) * part_rows + frame * rows
                mixed_ref[frame, span, lane_group * LANES : (lane_group + 1) * LANES] = ref[
                    start : start + rows
                ]


def ordered_sum(me, refs, parts_s):
    rows = parts_s.shape[1]
    for distance, ref in enumerate(refs):
        parts_s[me ^ distance] = ref[:rows]
    total = parts_s[0].astype(F32)
    for part in range(1, len(refs)):
        total = total + parts_s[part].astype(F32)
    return total.astype(BF16)


def halve(core, whole_s, kept_ref, sent_ref):
    half = kept_ref.shape[0]
    kept_ref[...] = whole_s[pl.ds(pl.multiple_of(core * half, GROUP_ROWS), half)]
    sent_ref[...] = whole_s[pl.ds(pl.multiple_of((1 - core) * half, GROUP_ROWS), half)]


def cores_kernel(place_ref, *refs):
    *ride_refs, kept_ref, sent_ref, parts_s, time_s = refs
    time_s[...] = ordered_sum(place_ref[0], ride_refs, parts_s)
    halve(place_ref[1] % 2, time_s, kept_ref, sent_ref)


def split_kernel(place_ref, kept_ref, arrived_ref, *refs):
    *part_refs, sum_s = refs
    sum_s[...] = add_rounded(kept_ref, arrived_ref)
    rows = part_refs[0].shape[0]
    for distance, ref in enumerate(part_refs):
        ref[...] = sum_s[pl.ds(pl.multiple_of((place_ref[0] ^ distance) * rows, GROUP_ROWS), rows)]


def tm_sum_kernel(place_ref, *refs):
    *part_refs, time_ref, time_other_ref, space_out_ref, time_out_ref, parts_s = refs
    space_out_ref[...] = ordered_sum(place_ref[0], part_refs, parts_s)
    time_out_ref[...] = add_rounded(time_ref, time_other_ref)


def add_rounded(left_ref, right_ref):
    return (left_ref[...].astype(F32) + right_ref[...].astype(F32)).astype(BF16)


def pairs_kernel(*refs):
    out_refs = refs[2 * len(refs) // 3 :]
    for index, ref in enumerate(out_refs):
        ref[...] = add_rounded(refs[2 * index], refs[2 * index + 1])


def join_kernel(place_ref, *refs):
    *part_refs, joined_ref = refs
    count_in = len(part_refs) // 2
    rows = part_refs[0].shape[0]
    for layer in range(2):
        for distance in range(count_in):
            start = (2 * (place_ref[0] ^ distance) + layer) * rows
            joined_ref[pl.ds(pl.multiple_of(start, GROUP_ROWS), rows)] = part_refs[
                layer * count_in + distance
            ][...]


def grads_kernel(time_count, own, place_ref, half_ref, *refs):
    project_hbm, combine_hbm, wide_s, sems = refs[-4:]
    features = combine_hbm.shape[1]
    core = place_ref[1] % 2
    rows = half_ref.shape[0] // time_count // 2
    wide_s[...] = half_ref[...].astype(F32).reshape(wide_s.shape)

    def write(half):
        moves = []
        for part in range(time_count):
            for layer, row in ((0, (half * time_count + part) * rows), (1, (2 * part + half) * rows)):
                group, inner = divmod(row, features)
                start = group * LANES
                target, start = (
                    (project_hbm, start)
                    if start < 3 * features
                    else (combine_hbm, start - 3 * features)
                )
                piece = 2 * part + layer
                moves.append(
                    pltpu.make_async_copy(
                        wide_s.at[piece],
                        target.at[layer, pl.ds(inner, rows), pl.ds(start, LANES)],
                        sems.at[piece],
                    )
                )
        for move in moves:
            move.start()
        for move in moves:
            move.wait()

    for half in range(2):

        @pl.when((core if own else 1 - core) == half)
        def _():
            write(half)


def stack_grads(grads, factor, stacked_ref):
    row = 0
    for grad in grads:
        for lane in range(0, grad.shape[1], LANES):
            stacked_ref[row : row + grad.shape[0]] = (
                grad[:, lane : lane + LANES] * factor
            ).astype(BF16)
            row += grad.shape[0]


def in_hbm(cells):
    return pltpu.with_memory_space_constraint(cells, pltpu.HBM)


def swap_far(cells, axis):
    pairs = [(i, i + 1) for i in range(1, lax.axis_size(axis) - 1, 2)]
    return lax.ppermute(cells, axis, pairs + [(j, i) for i, j in pairs])


def exchange(cells, axis, distance):
    return lax.ppermute(cells, axis, [(i, i ^ distance) for i in range(lax.axis_size(axis))])


def per_device(wave_field, cotangent, block_lists, project_weights, combine_weights):
    frame_count, row_count, features = wave_field.shape
    width = features // HEADS
    scale = 1.0 / math.sqrt(width)
    block_count = row_count // BLOCK
    list_length = block_lists.shape[-1]
    rim = HREACH * BLOCK
    extended = row_count + 2 * rim
    keys_count = list_length * BLOCK
    time_count = lax.axis_size("tm")
    all_frames = frame_count * time_count
    sent_rows = row_count // time_count
    factor = 1.0 / math.sqrt(frame_count * row_count * time_count * lax.axis_size("space"))
    space_count = lax.axis_size("space") // 2
    grad_rows = 4 * features // LANES * features
    chunk = grad_rows // time_count
    ride_rows = chunk + frame_count * sent_rows * features // LANES
    tokens = all_frames * sent_rows
    places = block_count + 2 * HREACH
    smem_spec = pl.BlockSpec(memory_space=pltpu.SMEM)
    vmem_spec = pl.BlockSpec(memory_space=pltpu.VMEM)
    hbm_spec = pl.BlockSpec(memory_space=pl.ANY)

    def call(
        body, name, scalars, operands, outs, scratch=(), matmuls=1, hbm=(), aliases=None, out_spec=None
    ):
        def typed(shape):
            return (shape[:-1], shape[-1]) if not isinstance(shape[-1], int) else (shape, BF16)

        return pl.pallas_call(
            body,
            in_specs=[smem_spec] * len(scalars)
            + [vmem_spec] * len(operands)
            + [hbm_spec] * len(hbm),
            out_specs=[out_spec or vmem_spec] * len(outs),
            out_shape=[jax.ShapeDtypeStruct(*typed(shape)) for shape in outs],
            scratch_shapes=[
                pltpu.VMEM(*typed(shape)) if isinstance(shape, tuple) else shape
                for shape in scratch
            ],
            compiler_params=pltpu.CompilerParams(vmem_limit_bytes=VMEM_BYTES),
            cost_estimate=cost(matmuls),
            input_output_aliases=aliases or {},
            name=name,
        )(*scalars, *operands, *hbm)

    def over_tm(pieces):
        return [pieces[0]] + [exchange(pieces[d], "tm", d) for d in range(1, time_count)]

    own = (frame_count, row_count, features)
    part = (frame_count, sent_rows, features)
    near = exchange(wave_field, "space", 1)
    far = swap_far(wave_field, "space")
    place = jnp.stack([lax.axis_index("tm"), lax.axis_index("space")]).astype(jnp.int32)
    extended_shapes = [
        (frame_count, extended, features),
        (frame_count, extended, 2 * features),
        (frame_count, places, features, BLOCK),
        (frame_count, places, features, BLOCK),
    ]
    wave, project, turned, combine, cot, queries, queries_t, *projected = call(
        prepare_kernel,
        "prepare",
        [place],
        [near],
        [
            own,
            (2, features, 3 * features),
            (2, 3 * features, features),
            (2, features, features),
            own,
            own,
            (frame_count, features, row_count),
            *extended_shapes,
        ],
        [pltpu.SemaphoreType.DMA((4,))],
        matmuls=12,
        hbm=[in_hbm(cells) for cells in (wave_field, cotangent, project_weights, combine_weights)],
    )
    block_lists = in_hbm(block_lists)
    act, keys_values, keys_t, _, probs, inverse_sum, attended, *parts = call(
        space_forward_kernel,
        "space_forward",
        [block_lists, place],
        [far, wave, cot, project, turned, combine, queries_t, *projected],
        [
            *extended_shapes,
            (frame_count, block_count, keys_count, HEADS * BLOCK),
            (frame_count, block_count, HEADS, BLOCK, F32),
            (frame_count, features, row_count),
            *[(frame_count, sent_rows, 2 * features)] * time_count,
        ],
        [own],
        matmuls=40,
        aliases={9 + index: index for index in range(4)},
    )
    kept_space = [act, keys_values, keys_t, queries, probs, inverse_sum, attended]
    arrived = over_tm(parts)

    def time_body(*refs):
        time_kernel(scale, time_count, *refs)

    outs = call(
        time_body,
        "time_pair",
        [],
        [*arrived, project, turned, combine],
        [
            *[part] * time_count,
            (tokens, features),
            (tokens, 3 * features),
            (features, tokens),
            (tokens, features),
            (tokens, features),
        ],
        matmuls=36,
    )
    parts, kept_time = outs[:time_count], outs[time_count:]

    def time_grads_body(*refs):
        time_grads_kernel(factor, frame_count, sent_rows, *refs)

    rides = call(
        time_grads_body,
        "time_grads",
        [place],
        kept_time,
        [(ride_rows, LANES)] * time_count,
        [(grad_rows, LANES)],
        matmuls=6,
    )
    returned = over_tm(parts)
    rides = over_tm(rides)
    returned[1], rides[0] = lax.optimization_barrier((returned[1], rides[0]))

    def backward_body(*refs):
        space_backward_kernel(scale, time_count, *refs)

    mixed_grad, dquery, dkv, dact, to_near, to_far = call(
        backward_body,
        "space_backward",
        [block_lists, place],
        [*returned, *kept_space, project, combine],
        [
            own,
            own,
            (frame_count, extended, 2 * features),
            (*own, F32),
            *[(frame_count, rim, features)] * 2,
        ],
        [
            (frame_count, block_count, keys_count, HEADS * BLOCK),
            (frame_count, extended, 2 * features, F32),
            (frame_count, extended, features),
        ],
        matmuls=44,
    )
    from_far = swap_far(to_far, "space")
    from_near = exchange(to_near, "space", 1)

    def space_grads_body(*refs):
        space_grads_kernel(factor, *refs)

    space_kept, space_sent = call(
        space_grads_body,
        "space_grads",
        [place],
        [act, dquery, dkv, attended, mixed_grad],
        [(grad_rows // 2, LANES)] * 2,
        [(grad_rows, LANES)],
        matmuls=8,
    )

    def add_pair(name, piece, other):
        (total,) = call(pairs_kernel, name, [], [piece, other], [(chunk // 2, LANES)])
        return total

    space_other = exchange(space_sent, "space", 1)
    time_kept, time_sent = call(
        cores_kernel,
        "add_tm_time",
        [place],
        rides,
        [(chunk // 2, LANES)] * 2,
        [(time_count, chunk, LANES), (chunk, LANES)],
        matmuls=24,
    )
    time_other = exchange(time_sent, "space", 1)
    space_other, time_kept = lax.optimization_barrier((space_other, time_kept))
    space_pieces = call(
        split_kernel,
        "add_cores",
        [place],
        [space_kept, space_other],
        [(chunk // 2, LANES)] * time_count,
        [(grad_rows // 2, LANES)],
    )
    space_pieces = over_tm(space_pieces)
    time_piece = add_pair("add_cores_time", time_kept, time_other)
    steps = [2 << bit for bit in range((space_count - 1).bit_length())]
    from_near, from_far, *space_pieces = lax.optimization_barrier(
        (from_near, from_far, *space_pieces)
    )
    time_other = exchange(time_piece, "space", steps[0])
    space_piece, time_piece = call(
        tm_sum_kernel,
        "add_tm_space",
        [place],
        [*space_pieces, time_piece, time_other],
        [(chunk // 2, LANES)] * 2,
        [(time_count, chunk // 2, LANES)],
    )
    sent_piece = space_piece
    for step, time_step in zip(steps, steps[1:]):
        space_other = exchange(sent_piece, "space", step)
        time_other = exchange(time_piece, "space", time_step)
        sent_piece = add_pair("add_space", space_piece, space_other)
        space_piece, time_other = lax.optimization_barrier((sent_piece, time_other))
        time_piece = add_pair("add_space_time", time_piece, time_other)
    space_other = exchange(sent_piece, "space", steps[-1])
    time_joined = over_tm([time_piece] * time_count)
    space_piece = add_pair("add_space_last", space_piece, space_other)
    joined = over_tm([space_piece] * time_count) + time_joined

    field_grad, mixed_field = call(
        field_kernel,
        "field_grad",
        [place],
        [wave, mixed_grad, dact, from_near, from_far, *rides],
        [own, own],
        matmuls=3,
    )
    field_grad, mixed_field, *joined = lax.optimization_barrier((field_grad, mixed_field, *joined))
    (own_half,) = call(join_kernel, "join_tm", [place], joined, [(grad_rows, LANES)])
    other_half = exchange(own_half, "space", 1)

    grads = ()
    for half in (own_half, other_half):

        def grads_body(*refs, mine=half is own_half):
            grads_kernel(time_count, mine, *refs)

        grads = call(
            grads_body,
            "weight_grads",
            [place],
            [half],
            [(2, features, 3 * features, F32), (2, features, features, F32)],
            [
                (2 * time_count, grad_rows // time_count // 2, LANES, F32),
                pltpu.SemaphoreType.DMA((2 * time_count,)),
            ],
            hbm=grads,
            aliases={2: 0, 3: 1} if grads else None,
            out_spec=pl.BlockSpec(memory_space=pltpu.HBM),
        )
    project_grad, combine_grad = grads
    return (mixed_field, field_grad, project_grad, combine_grad)


def solution(mesh):
    in_specs = (P("tm", "space", None), P("tm", "space", None), P("tm", "space", None), P(), P())
    out_specs = (P("tm", "space", None), P("tm", "space", None), P(), P())
    return jax.shard_map(
        per_device, mesh=mesh, in_specs=in_specs, out_specs=out_specs, check_vma=False
    )
```

```python
import math

import jax
import jax.numpy as jnp
from jax import lax
from jax.experimental import pallas as pl
from jax.experimental.pallas import tpu as pltpu
from jax.sharding import PartitionSpec as P

HEADS = 8
BLOCK = 128
HREACH = 2
LANES = 128
GROUP_ROWS = 16
VMEM_BYTES = 24 * 1024 * 1024
BF16 = jnp.bfloat16
F32 = jnp.float32


epsilon = 1e-05


def cost(matmuls):
    flops = matmuls * 2 * 1024 * 256 * 512
    return pl.CostEstimate(flops=flops, bytes_accessed=flops // 256, transcendentals=flops // 1024)


def dot_nn(left, right):
    return lax.dot_general(left, right, (((1,), (0,)), ((), ())), preferred_element_type=F32)


def dot_nt(left, right):
    return lax.dot_general(left, right, (((1,), (1,)), ((), ())), preferred_element_type=F32)


def dot_tn(left, right):
    return lax.dot_general(left, right, (((0,), (0,)), ((), ())), preferred_element_type=F32)


def layer_norm(rows):
    widened = rows.astype(F32)
    centered = widened - jnp.mean(widened, axis=-1, keepdims=True)
    inverse = lax.rsqrt(jnp.mean(centered * centered, axis=-1, keepdims=True) + epsilon)
    return (centered * inverse, inverse)


def norm_backward(upstream, normed, inverse):
    mean_grad = jnp.mean(upstream, axis=-1, keepdims=True)
    mean_cross = jnp.mean(upstream * normed, axis=-1, keepdims=True)
    return inverse * (upstream - mean_grad - normed * mean_cross)


def flip(matrix):
    return matrix.astype(BF16).T


def pair_columns(rows_t, pair, width):
    count = rows_t.shape[1]
    base = (pair * 2 * width) // LANES * LANES
    parts = []
    for head in (2 * pair, 2 * pair + 1):
        start = head * width - base
        pieces = []
        if start:
            pieces.append(jnp.zeros((start, count), rows_t.dtype))
        pieces.append(rows_t[head * width : (head + 1) * width])
        if start + width < LANES:
            pieces.append(jnp.zeros((LANES - start - width, count), rows_t.dtype))
        parts.append(jnp.concatenate(pieces, axis=0))
    return jnp.concatenate(parts, axis=1)


def pair_group(matrix, pair, width):
    base = (pair * 2 * width) // LANES * LANES
    return matrix[:, base : base + LANES]


def pair_diagonal(product, width):
    count = product.shape[1] // 2
    return jnp.concatenate([product[:width, :count], product[width:, count:]], axis=0)


def head_rows(rows, width):
    column = lax.broadcasted_iota(jnp.int32, (1, rows.shape[1]), 1) // width
    return jnp.concatenate(
        [rows * (column == head).astype(F32).astype(BF16) for head in range(HEADS)], axis=0
    )


def head_spread(per_head, width):
    return jnp.concatenate(
        [
            jnp.broadcast_to(per_head[head : head + 1], (width, per_head.shape[1]))
            for head in range(HEADS)
        ],
        axis=0,
    )


def listed_blocks(lists_ref, frame, block):
    own = lists_ref[frame, block, 0]
    return [
        lists_ref[frame, block, entry] - own + (block + HREACH)
        for entry in range(lists_ref.shape[2])
    ]


def halo_start(core, rim, row_count, near):
    after = core == 0 if near else core != 0
    return pl.multiple_of(jnp.where(after, rim + row_count, 0), BLOCK)


def project_rows(
    frame, start, rows, project_ref, turned_ref, act_ref, kv_ref, keys_t_ref, values_t_ref
):
    features = rows.shape[1]
    normed, _ = layer_norm(rows)
    act = normed.astype(BF16)
    span = pl.ds(start, rows.shape[0])
    act_ref[frame, span] = act
    kv_ref[frame, span] = dot_nn(act, project_ref[0, :, features:]).astype(BF16)
    keys_t = dot_nt(turned_ref[0, features : 2 * features], act).astype(BF16)
    values_t = dot_nt(turned_ref[0, 2 * features :], act).astype(BF16)
    for block in range(rows.shape[0] // BLOCK):
        lanes = slice(block * BLOCK, (block + 1) * BLOCK)
        keys_t_ref[frame, start // BLOCK + block] = keys_t[:, lanes]
        values_t_ref[frame, start // BLOCK + block] = values_t[:, lanes]
    return act


def prepare_kernel(
    place_ref,
    near_ref,
    wave_hbm,
    cot_hbm,
    project_hbm,
    combine_hbm,
    wave_ref,
    project_ref,
    turned_ref,
    combine_ref,
    cot_ref,
    query_ref,
    query_t_ref,
    act_ref,
    kv_ref,
    keys_t_ref,
    values_t_ref,
    sems,
):
    moves = [
        pltpu.make_async_copy(source, target, sems.at[index])
        for index, (source, target) in enumerate(
            (
                (project_hbm, project_ref),
                (wave_hbm, wave_ref),
                (combine_hbm, combine_ref),
                (cot_hbm, cot_ref),
            )
        )
    ]
    for move in moves:
        move.start()
    frame_count, row_count, features = wave_ref.shape
    rim = near_ref.shape[1]
    core = place_ref[1] % 2
    moves[0].wait()
    turned_ref[0] = flip(project_ref[0])
    for frame in range(frame_count):
        project_rows(
            frame,
            halo_start(core, rim, row_count, True),
            near_ref[frame],
            project_ref,
            turned_ref,
            act_ref,
            kv_ref,
            keys_t_ref,
            values_t_ref,
        )
    moves[1].wait()
    for frame in range(frame_count):
        act = project_rows(
            frame, rim, wave_ref[frame], project_ref, turned_ref, act_ref, kv_ref, keys_t_ref, values_t_ref
        )
        query_ref[frame] = dot_nn(act, project_ref[0, :, :features]).astype(BF16)
        query_t_ref[frame] = dot_nt(turned_ref[0, :features], act).astype(BF16)
    turned_ref[1] = flip(project_ref[1])
    moves[2].wait()
    moves[3].wait()


def space_forward_kernel(
    lists_ref,
    place_ref,
    far_ref,
    wave_ref,
    cot_ref,
    project_ref,
    turned_ref,
    combine_ref,
    query_t_ref,
    act_in,
    kv_in,
    keys_t_in,
    values_t_in,
    act_ref,
    kv_ref,
    keys_t_ref,
    values_t_ref,
    probs_ref,
    inverse_sum_ref,
    attended_ref,
    *rest,
):
    del act_in, kv_in, keys_t_in, values_t_in
    *sent_refs, mixed_s = rest
    me = place_ref[0]
    core = place_ref[1] % 2
    frame_count, row_count, features = wave_ref.shape
    rim = far_ref.shape[1]
    width = features // HEADS
    block_count = row_count // BLOCK
    exponent_scale = math.log2(math.e) / math.sqrt(width)
    for frame in range(frame_count):
        project_rows(
            frame,
            halo_start(core, rim, row_count, False),
            far_ref[frame],
            project_ref,
            turned_ref,
            act_ref,
            kv_ref,
            keys_t_ref,
            values_t_ref,
        )
    blocks = [(frame, block) for frame in range(frame_count) for block in range(block_count)]
    loaded = {}

    def load(index):
        frame, block = blocks[index]
        places = listed_blocks(lists_ref, frame, block)
        keys = jnp.concatenate(
            [kv_ref[frame, pl.ds(place * BLOCK, BLOCK), :features] for place in places], axis=0
        )
        loaded[index] = (keys, query_t_ref[frame, :, block * BLOCK : (block + 1) * BLOCK], places)

    def pair_scores(step):
        index, pair = divmod(step, HEADS // 2)
        if index not in loaded:
            load(index)
        keys, query_t, _ = loaded[index]
        return dot_nn(pair_group(keys, pair, width), pair_columns(query_t, pair, width))

    steps = len(blocks) * HEADS // 2
    scores = pair_scores(0)
    outs = []
    for step in range(steps):
        following = pair_scores(step + 1) if step + 1 < steps else None
        index, pair = divmod(step, HEADS // 2)
        frame, block = blocks[index]
        if pair == 0:
            block_values_t = jnp.concatenate(
                [values_t_ref[frame, place] for place in loaded[index][2]], axis=1
            )
            outs = []
        top = jnp.max(scores, axis=0, keepdims=True)
        exp_scores = jnp.exp2((scores - top) * exponent_scale)
        inverse_sum = 1.0 / jnp.sum(exp_scores, axis=0, keepdims=True)
        probs = exp_scores.astype(BF16)
        probs_ref[frame, block, :, pair * 2 * BLOCK : (pair + 1) * 2 * BLOCK] = probs
        inverse_sum_ref[frame, block, 2 * pair : 2 * pair + 1] = inverse_sum[:, :BLOCK]
        inverse_sum_ref[frame, block, 2 * pair + 1 : 2 * pair + 2] = inverse_sum[:, BLOCK:]
        out = dot_nn(block_values_t[pair * 2 * width : (pair + 1) * 2 * width], probs)
        outs.append(pair_diagonal(out * inverse_sum, width))
        scores = following
        if pair == HEADS // 2 - 1:
            attended_t = jnp.concatenate(outs, axis=0)
            span = slice(block * BLOCK, (block + 1) * BLOCK)
            attended_ref[frame, :, span] = attended_t.astype(BF16)
            mixed_s[frame, span] = (
                wave_ref[frame, span].astype(F32) + dot_nn(flip(attended_t), combine_ref[0])
            ).astype(BF16)
    for distance, ref in enumerate(sent_refs):
        rows = ref.shape[1]
        span = pl.ds(pl.multiple_of((me ^ distance) * rows, GROUP_ROWS), rows)
        ref[:, :, :features] = mixed_s[:, span]
        ref[:, :, features:] = cot_ref[:, span]


def time_kernel(
    scale,
    count_in,
    *refs,
):
    arrived_refs = refs[:count_in]
    project_ref, turned_ref, combine_ref = refs[count_in : count_in + 3]
    grad_refs = refs[count_in + 3 : 2 * count_in + 3]
    act_ref, dproj_ref, attended_t_ref, cot_ref, mixed_ref = refs[2 * count_in + 3 :]
    part_frames, row_count, features = grad_refs[0].shape
    width = features // HEADS
    count = part_frames * count_in * GROUP_ROWS
    groups = row_count // GROUP_ROWS
    exponent_scale = scale * math.log2(math.e)

    def grouped(lanes):
        return jnp.concatenate(
            [
                ref[:, group * GROUP_ROWS : (group + 1) * GROUP_ROWS, lanes].reshape(
                    part_frames * GROUP_ROWS, features
                )
                for group in range(groups)
                for ref in arrived_refs
            ],
            axis=0,
        )

    rows = grouped(slice(0, features))
    cot = grouped(slice(features, 2 * features))
    cot_ref[...] = cot
    normed, inverse = layer_norm(rows)
    act = normed.astype(BF16)
    act_ref[...] = act
    projected = dot_nn(act, project_ref[1]).astype(BF16)
    projected_t = dot_nt(turned_ref[1], act).astype(BF16)
    all_dattn = dot_nt(cot, combine_ref[1]).astype(BF16)
    all_dattn_t = dot_nt(combine_ref[1], cot).astype(BF16)
    all_count = HEADS * count
    key_row = lax.broadcasted_iota(jnp.int32, (count, all_count), 0) % GROUP_ROWS
    query_row = lax.broadcasted_iota(jnp.int32, (count, all_count), 1) % GROUP_ROWS
    same_row = key_row == query_row
    attended_groups, dquery_groups, dkey_groups, dvalue_groups = [], [], [], []
    pairs = range(HEADS // 2)

    def products(group):
        span = slice(group * count, (group + 1) * count)
        return tuple(
            jnp.concatenate(
                [
                    dot_nn(pair_group(left, pair, width), pair_columns(right, pair, width))
                    for pair in pairs
                ],
                axis=1,
            )
            for left, right in (
                (projected[span, features : 2 * features], projected_t[:features, span]),
                (projected[span, 2 * features :], all_dattn_t[:, span]),
            )
        )

    def by_heads(left_t, right):
        return jnp.concatenate(
            [
                pair_diagonal(
                    dot_nn(
                        left_t[pair * 2 * width : (pair + 1) * 2 * width],
                        right[:, pair * 2 * count : (pair + 1) * 2 * count],
                    ),
                    width,
                )
                for pair in pairs
            ],
            axis=0,
        )

    scores, dprobs = products(0)
    for group in range(groups):
        following = products(group + 1) if group + 1 < groups else (None, None)
        span = slice(group * count, (group + 1) * count)
        scores = jnp.where(same_row, scores, -3e38)
        top = jnp.max(scores, axis=0, keepdims=True)
        exp_scores = jnp.exp2((scores - top) * exponent_scale)
        probs = (exp_scores * (1.0 / jnp.sum(exp_scores, axis=0, keepdims=True))).astype(BF16)
        probs_wide = probs.astype(F32)
        delta = jnp.sum(probs_wide * dprobs, axis=0, keepdims=True)
        dscores = (probs_wide * (dprobs - delta) * scale).astype(BF16)
        attended_groups.append(by_heads(projected_t[2 * features :, span], probs).astype(BF16))
        dquery_groups.append(flip(by_heads(projected_t[features : 2 * features, span], dscores)))
        dkey_groups.append(
            dot_nn(dscores, head_rows(projected[span, :features], width)).astype(BF16)
        )
        dvalue_groups.append(dot_nn(probs, head_rows(all_dattn[span], width)).astype(BF16))
        scores, dprobs = following
    attended = jnp.concatenate([flip(attended_t) for attended_t in attended_groups], axis=0)
    mixed_ref[...] = (rows.astype(F32) + dot_nn(attended, combine_ref[1])).astype(BF16)
    attended_t_ref[...] = jnp.concatenate(attended_groups, axis=1)
    dproj = jnp.concatenate(
        [jnp.concatenate(parts, axis=0) for parts in (dquery_groups, dkey_groups, dvalue_groups)],
        axis=1,
    )
    dproj_ref[...] = dproj
    dact = dot_nt(dproj, project_ref[1])
    mixed_grad = (cot.astype(F32) + norm_backward(dact, normed, inverse)).astype(BF16)
    for part, ref in enumerate(grad_refs):
        for group in range(groups):
            span = slice(group * GROUP_ROWS, (group + 1) * GROUP_ROWS)
            for frame in range(part_frames):
                start = ((group * count_in + part) * part_frames + frame) * GROUP_ROWS
                ref[frame, span] = mixed_grad[start : start + GROUP_ROWS]


def time_grads_kernel(
    factor, part_frames, row_count, place_ref, act_ref, dproj_ref, attended_t_ref, cot_ref, mixed_ref, *refs
):
    *ride_refs, stacked_s = refs
    count_in = len(ride_refs)
    features = act_ref.shape[1]
    groups = row_count // GROUP_ROWS
    stack_grads(
        [dot_tn(act_ref[...], dproj_ref[...]), dot_nn(attended_t_ref[...], cot_ref[...])],
        factor,
        stacked_s,
    )
    chunk = stacked_s.shape[0] // count_in
    part_rows = part_frames * row_count
    for part, ref in enumerate(ride_refs):
        for group in range(groups):
            for frame in range(part_frames):
                start = ((group * count_in + part) * part_frames + frame) * GROUP_ROWS
                for lane_group in range(features // LANES):
                    row = chunk + lane_group * part_rows + frame * row_count + group * GROUP_ROWS
                    ref[row : row + GROUP_ROWS] = mixed_ref[
                        start : start + GROUP_ROWS, lane_group * LANES : (lane_group + 1) * LANES
                    ]
        ref[:chunk] = stacked_s[
            pl.ds(pl.multiple_of((place_ref[0] ^ part) * chunk, GROUP_ROWS), chunk)
        ]


def space_backward_kernel(
    scale,
    factor,
    count_in,
    lists_ref,
    place_ref,
    *refs,
):
    returned_refs = refs[:count_in]
    (
        act_ref,
        kv_ref,
        keys_t_ref,
        query_ref,
        probs_ref,
        inverse_sum_ref,
        attended_ref,
        combine_ref,
        mixed_grad_ref,
        dquery_ref,
        dkv_ref,
        kept_ref,
        sent_ref,
        dscores_s,
        dkv_s,
        stacked_s,
    ) = refs[count_in:]
    me = place_ref[0]
    frame_count, row_count, features = mixed_grad_ref.shape
    width = features // HEADS
    block_count = row_count // BLOCK
    rim = HREACH * BLOCK
    for distance, ref in enumerate(returned_refs):
        rows = ref.shape[1]
        span = pl.ds(pl.multiple_of((me ^ distance) * rows, GROUP_ROWS), rows)
        mixed_grad_ref[:, span] = ref[...]
    blocks = [(frame, block) for frame in range(frame_count) for block in range(block_count)]
    all_dattn_t = [
        dot_nt(combine_ref[0], mixed_grad_ref[frame]).astype(BF16) for frame in range(frame_count)
    ]
    loaded = {}

    def load(index):
        frame, block = blocks[index]
        places = listed_blocks(lists_ref, frame, block)
        values = jnp.concatenate(
            [kv_ref[frame, pl.ds(place * BLOCK, BLOCK), features:] for place in places], axis=0
        )
        loaded[index] = (
            values,
            all_dattn_t[frame][:, block * BLOCK : (block + 1) * BLOCK],
            places,
        )

    def pair_products(step):
        index, pair = divmod(step, HEADS // 2)
        if index not in loaded:
            load(index)
        values, dattn_t, _ = loaded[index]
        return dot_nn(pair_group(values, pair, width), pair_columns(dattn_t, pair, width))

    def add_listed(index, lanes, parts):
        frame = blocks[index][0]
        for entry, place in enumerate(loaded[index][2]):
            rows = pl.ds(place * BLOCK, BLOCK)
            dkv_s[frame, rows, lanes] += parts[entry * BLOCK : (entry + 1) * BLOCK]

    def add_keys(index):
        frame, block = blocks[index]
        queries = head_rows(query_ref[frame, block * BLOCK : (block + 1) * BLOCK], width)
        add_listed(index, slice(0, features), dot_nn(dscores_s[frame, block], queries))

    dkv_s[...] = jnp.zeros(dkv_s.shape, F32)
    steps = len(blocks) * HEADS // 2
    dprobs = pair_products(0)
    dquery_parts = []
    for step in range(steps):
        following = pair_products(step + 1) if step + 1 < steps else None
        index, pair = divmod(step, HEADS // 2)
        frame, block = blocks[index]
        _, dattn_t, places = loaded[index]
        if pair == 0:
            span = slice(block * BLOCK, (block + 1) * BLOCK)
            block_keys_t = jnp.concatenate([keys_t_ref[frame, place] for place in places], axis=1)
            dattn_wide = dattn_t.astype(F32)
            inverse_sum = inverse_sum_ref[frame, block]
            delta = jnp.sum(
                (dattn_wide * attended_ref[frame, :, span].astype(F32)).reshape(
                    HEADS, width, BLOCK
                ),
                axis=1,
            )
            row_scale = inverse_sum * scale
            dquery_parts = []
        if pair == 1:
            scaled_dattn = flip(dattn_wide * head_spread(inverse_sum, width))
            add_listed(
                index,
                slice(features, 2 * features),
                dot_nn(probs_ref[frame, block], head_rows(scaled_dattn, width)),
            )
        if pair == 2 and index:
            add_keys(index - 1)
        heads = slice(pair * 2 * width, (pair + 1) * 2 * width)
        columns = slice(pair * 2 * BLOCK, (pair + 1) * 2 * BLOCK)
        pair_delta, pair_scale = (
            jnp.concatenate([rows[2 * pair : 2 * pair + 1], rows[2 * pair + 1 : 2 * pair + 2]], axis=1)
            for rows in (delta, row_scale)
        )
        probs = probs_ref[frame, block, :, columns].astype(F32)
        dscores = (probs * ((dprobs - pair_delta) * pair_scale)).astype(BF16)
        dscores_s[frame, block, :, columns] = dscores
        dquery_parts.append(pair_diagonal(dot_nn(block_keys_t[heads], dscores), width))
        dprobs = following
        if pair == HEADS // 2 - 1:
            dquery_ref[frame, span] = flip(jnp.concatenate(dquery_parts, axis=0))
    add_keys(len(blocks) - 1)
    dkv_ref[...] = dkv_s[...].astype(BF16)
    extended = dkv_ref.shape[1]
    act = act_ref[...]
    own_act = act[:, rim : rim + row_count].reshape(frame_count * row_count, features)
    stack_grads(
        [
            dot_tn(own_act, dquery_ref[...].reshape(frame_count * row_count, features)),
            dot_tn(
                act.reshape(frame_count * extended, features),
                dkv_ref[...].reshape(frame_count * extended, 2 * features),
            ),
            sum(
                dot_nn(attended_ref[frame], mixed_grad_ref[frame]) for frame in range(frame_count)
            ),
        ],
        factor,
        stacked_s,
    )
    halve(place_ref[1] % 2, stacked_s, kept_ref, sent_ref)


def dact_kernel(place_ref, dquery_ref, dkv_ref, project_ref, dact_ref, near_ref, far_ref, dact_s):
    frame_count, row_count, features = dquery_ref.shape
    rim = near_ref.shape[1]
    core = place_ref[1] % 2
    for frame in range(frame_count):
        dact = dot_nt(dkv_ref[frame], project_ref[0, :, features:])
        dact_s[frame] = dact.astype(BF16)
        dact_ref[frame] = dact[rim : rim + row_count] + dot_nt(
            dquery_ref[frame], project_ref[0, :, :features]
        )
    near_ref[...] = dact_s[:, pl.ds(halo_start(core, rim, row_count, True), rim)]
    far_ref[...] = dact_s[:, pl.ds(halo_start(core, rim, row_count, False), rim)]


def field_kernel(place_ref, wave_ref, mixed_grad_ref, dact_ref, near_ref, far_ref, *refs):
    *ride_refs, field_ref, mixed_ref = refs
    frame_count, row_count, features = wave_ref.shape
    rows = row_count // len(ride_refs)
    lane_groups = features // LANES
    part_rows = frame_count * rows
    for frame in range(frame_count):
        normed, inverse = layer_norm(wave_ref[frame])
        dact = dact_ref[frame] + near_ref[frame].astype(F32) + far_ref[frame].astype(F32)
        field_ref[frame] = (
            mixed_grad_ref[frame].astype(F32) + norm_backward(dact, normed, inverse)
        ).astype(BF16)
        for distance, ref in enumerate(ride_refs):
            span = pl.ds(pl.multiple_of((place_ref[0] ^ distance) * rows, GROUP_ROWS), rows)
            for lane_group in range(lane_groups):
                start = ref.shape[0] - (lane_groups - lane_group) * part_rows + frame * rows
                mixed_ref[frame, span, lane_group * LANES : (lane_group + 1) * LANES] = ref[
                    start : start + rows
                ]


def ordered_sum(me, refs, parts_s):
    rows = parts_s.shape[1]
    for distance, ref in enumerate(refs):
        parts_s[me ^ distance] = ref[:rows]
    total = parts_s[0].astype(F32)
    for part in range(1, len(refs)):
        total = total + parts_s[part].astype(F32)
    return total.astype(BF16)


def halve(core, whole_s, kept_ref, sent_ref):
    half = kept_ref.shape[0]
    kept_ref[...] = whole_s[pl.ds(pl.multiple_of(core * half, GROUP_ROWS), half)]
    sent_ref[...] = whole_s[pl.ds(pl.multiple_of((1 - core) * half, GROUP_ROWS), half)]


def cores_kernel(place_ref, *refs):
    *ride_refs, kept_ref, sent_ref, parts_s, time_s = refs
    time_s[...] = ordered_sum(place_ref[0], ride_refs, parts_s)
    halve(place_ref[1] % 2, time_s, kept_ref, sent_ref)


def split_kernel(place_ref, kept_ref, arrived_ref, *refs):
    *part_refs, sum_s = refs
    sum_s[...] = add_rounded(kept_ref, arrived_ref)
    rows = part_refs[0].shape[0]
    for distance, ref in enumerate(part_refs):
        ref[...] = sum_s[pl.ds(pl.multiple_of((place_ref[0] ^ distance) * rows, GROUP_ROWS), rows)]


def tm_sum_kernel(place_ref, *refs):
    *part_refs, time_ref, time_other_ref, space_out_ref, time_out_ref, parts_s = refs
    space_out_ref[...] = ordered_sum(place_ref[0], part_refs, parts_s)
    time_out_ref[...] = add_rounded(time_ref, time_other_ref)


def add_rounded(left_ref, right_ref):
    return (left_ref[...].astype(F32) + right_ref[...].astype(F32)).astype(BF16)


def pairs_kernel(*refs):
    out_refs = refs[2 * len(refs) // 3 :]
    for index, ref in enumerate(out_refs):
        ref[...] = add_rounded(refs[2 * index], refs[2 * index + 1])


def join_kernel(place_ref, *refs):
    *part_refs, joined_ref = refs
    count_in = len(part_refs) // 2
    rows = part_refs[0].shape[0]
    for layer in range(2):
        for distance in range(count_in):
            start = (2 * (place_ref[0] ^ distance) + layer) * rows
            joined_ref[pl.ds(pl.multiple_of(start, GROUP_ROWS), rows)] = part_refs[
                layer * count_in + distance
            ][...]


def grads_kernel(time_count, own, place_ref, half_ref, *refs):
    project_hbm, combine_hbm, wide_s, sems = refs[-4:]
    features = combine_hbm.shape[1]
    core = place_ref[1] % 2
    rows = half_ref.shape[0] // time_count // 2
    wide_s[...] = half_ref[...].astype(F32).reshape(wide_s.shape)

    def write(half):
        moves = []
        for part in range(time_count):
            for layer, row in ((0, (half * time_count + part) * rows), (1, (2 * part + half) * rows)):
                group, inner = divmod(row, features)
                start = group * LANES
                target, start = (
                    (project_hbm, start)
                    if start < 3 * features
                    else (combine_hbm, start - 3 * features)
                )
                piece = 2 * part + layer
                moves.append(
                    pltpu.make_async_copy(
                        wide_s.at[piece],
                        target.at[layer, pl.ds(inner, rows), pl.ds(start, LANES)],
                        sems.at[piece],
                    )
                )
        for move in moves:
            move.start()
        for move in moves:
            move.wait()

    for half in range(2):

        @pl.when((core if own else 1 - core) == half)
        def _():
            write(half)


def stack_grads(grads, factor, stacked_ref):
    row = 0
    for grad in grads:
        for lane in range(0, grad.shape[1], LANES):
            stacked_ref[row : row + grad.shape[0]] = (
                grad[:, lane : lane + LANES] * factor
            ).astype(BF16)
            row += grad.shape[0]


def in_hbm(cells):
    return pltpu.with_memory_space_constraint(cells, pltpu.HBM)


def swap_far(cells, axis):
    pairs = [(i, i + 1) for i in range(1, lax.axis_size(axis) - 1, 2)]
    return lax.ppermute(cells, axis, pairs + [(j, i) for i, j in pairs])


def exchange(cells, axis, distance):
    return lax.ppermute(cells, axis, [(i, i ^ distance) for i in range(lax.axis_size(axis))])


def per_device(wave_field, cotangent, block_lists, project_weights, combine_weights):
    frame_count, row_count, features = wave_field.shape
    width = features // HEADS
    scale = 1.0 / math.sqrt(width)
    block_count = row_count // BLOCK
    list_length = block_lists.shape[-1]
    rim = HREACH * BLOCK
    extended = row_count + 2 * rim
    keys_count = list_length * BLOCK
    time_count = lax.axis_size("tm")
    all_frames = frame_count * time_count
    sent_rows = row_count // time_count
    factor = 1.0 / math.sqrt(frame_count * row_count * time_count * lax.axis_size("space"))
    space_count = lax.axis_size("space") // 2
    grad_rows = 4 * features // LANES * features
    chunk = grad_rows // time_count
    ride_rows = chunk + frame_count * sent_rows * features // LANES
    tokens = all_frames * sent_rows
    places = block_count + 2 * HREACH
    smem_spec = pl.BlockSpec(memory_space=pltpu.SMEM)
    vmem_spec = pl.BlockSpec(memory_space=pltpu.VMEM)
    hbm_spec = pl.BlockSpec(memory_space=pl.ANY)

    def call(
        body, name, scalars, operands, outs, scratch=(), matmuls=1, hbm=(), aliases=None, out_spec=None
    ):
        def typed(shape):
            return (shape[:-1], shape[-1]) if not isinstance(shape[-1], int) else (shape, BF16)

        return pl.pallas_call(
            body,
            in_specs=[smem_spec] * len(scalars)
            + [vmem_spec] * len(operands)
            + [hbm_spec] * len(hbm),
            out_specs=[out_spec or vmem_spec] * len(outs),
            out_shape=[jax.ShapeDtypeStruct(*typed(shape)) for shape in outs],
            scratch_shapes=[
                pltpu.VMEM(*typed(shape)) if isinstance(shape, tuple) else shape
                for shape in scratch
            ],
            compiler_params=pltpu.CompilerParams(vmem_limit_bytes=VMEM_BYTES),
            cost_estimate=cost(matmuls),
            input_output_aliases=aliases or {},
            name=name,
        )(*scalars, *operands, *hbm)

    def over_tm(pieces):
        return [pieces[0]] + [exchange(pieces[d], "tm", d) for d in range(1, time_count)]

    own = (frame_count, row_count, features)
    part = (frame_count, sent_rows, features)
    near = exchange(wave_field, "space", 1)
    far = swap_far(wave_field, "space")
    place = jnp.stack([lax.axis_index("tm"), lax.axis_index("space")]).astype(jnp.int32)
    extended_shapes = [
        (frame_count, extended, features),
        (frame_count, extended, 2 * features),
        (frame_count, places, features, BLOCK),
        (frame_count, places, features, BLOCK),
    ]
    wave, project, turned, combine, cot, queries, queries_t, *projected = call(
        prepare_kernel,
        "prepare",
        [place],
        [near],
        [
            own,
            (2, features, 3 * features),
            (2, 3 * features, features),
            (2, features, features),
            own,
            own,
            (frame_count, features, row_count),
            *extended_shapes,
        ],
        [pltpu.SemaphoreType.DMA((4,))],
        matmuls=12,
        hbm=[in_hbm(cells) for cells in (wave_field, cotangent, project_weights, combine_weights)],
    )
    block_lists = in_hbm(block_lists)
    act, keys_values, keys_t, _, probs, inverse_sum, attended, *parts = call(
        space_forward_kernel,
        "space_forward",
        [block_lists, place],
        [far, wave, cot, project, turned, combine, queries_t, *projected],
        [
            *extended_shapes,
            (frame_count, block_count, keys_count, HEADS * BLOCK),
            (frame_count, block_count, HEADS, BLOCK, F32),
            (frame_count, features, row_count),
            *[(frame_count, sent_rows, 2 * features)] * time_count,
        ],
        [own],
        matmuls=40,
        aliases={9 + index: index for index in range(4)},
    )
    kept_space = [act, keys_values, keys_t, queries, probs, inverse_sum, attended]
    arrived = over_tm(parts)

    def time_body(*refs):
        time_kernel(scale, time_count, *refs)

    outs = call(
        time_body,
        "time_pair",
        [],
        [*arrived, project, turned, combine],
        [
            *[part] * time_count,
            (tokens, features),
            (tokens, 3 * features),
            (features, tokens),
            (tokens, features),
            (tokens, features),
        ],
        matmuls=36,
    )
    parts, kept_time = outs[:time_count], outs[time_count:]

    def time_grads_body(*refs):
        time_grads_kernel(factor, frame_count, sent_rows, *refs)

    rides = call(
        time_grads_body,
        "time_grads",
        [place],
        kept_time,
        [(ride_rows, LANES)] * time_count,
        [(grad_rows, LANES)],
        matmuls=6,
    )
    returned = over_tm(parts)
    rides = over_tm(rides)
    returned[1], rides[0] = lax.optimization_barrier((returned[1], rides[0]))

    def backward_body(*refs):
        space_backward_kernel(scale, factor, time_count, *refs)

    mixed_grad, dquery, dkv, space_kept, space_sent = call(
        backward_body,
        "space_backward",
        [block_lists, place],
        [*returned, *kept_space, combine],
        [own, own, (frame_count, extended, 2 * features), *[(grad_rows // 2, LANES)] * 2],
        [
            (frame_count, block_count, keys_count, HEADS * BLOCK),
            (frame_count, extended, 2 * features, F32),
            (grad_rows, LANES),
        ],
        matmuls=44,
    )

    def add_pair(name, piece, other):
        (total,) = call(pairs_kernel, name, [], [piece, other], [(chunk // 2, LANES)])
        return total

    space_other = exchange(space_sent, "space", 1)
    dact, to_near, to_far = call(
        dact_kernel,
        "space_dact",
        [place],
        [dquery, dkv, project],
        [(*own, F32), (frame_count, rim, features), (frame_count, rim, features)],
        [(frame_count, extended, features)],
        matmuls=3,
    )
    rides[0], to_near, to_far = lax.optimization_barrier((rides[0], to_near, to_far))
    time_kept, time_sent = call(
        cores_kernel,
        "add_tm_time",
        [place],
        rides,
        [(chunk // 2, LANES)] * 2,
        [(time_count, chunk, LANES), (chunk, LANES)],
        matmuls=24,
    )
    time_other = exchange(time_sent, "space", 1)
    space_other, time_kept = lax.optimization_barrier((space_other, time_kept))
    space_pieces = call(
        split_kernel,
        "add_cores",
        [place],
        [space_kept, space_other],
        [(chunk // 2, LANES)] * time_count,
        [(grad_rows // 2, LANES)],
    )
    to_near, to_far, *space_pieces = lax.optimization_barrier((to_near, to_far, *space_pieces))
    space_pieces = over_tm(space_pieces)
    from_far = swap_far(to_far, "space")
    from_near = exchange(to_near, "space", 1)
    time_piece = add_pair("add_cores_time", time_kept, time_other)
    steps = [2 << bit for bit in range((space_count - 1).bit_length())]
    time_other = exchange(time_piece, "space", steps[0])
    space_piece, time_piece = call(
        tm_sum_kernel,
        "add_tm_space",
        [place],
        [*space_pieces, time_piece, time_other],
        [(chunk // 2, LANES)] * 2,
        [(time_count, chunk // 2, LANES)],
    )

    sent_piece = space_piece
    for step, time_step in zip(steps, steps[1:]):
        space_other = exchange(sent_piece, "space", step)
        time_other = exchange(time_piece, "space", time_step)
        sent_piece = add_pair("add_space", space_piece, space_other)
        space_piece, time_other = lax.optimization_barrier((sent_piece, time_other))
        time_piece = add_pair("add_space_time", time_piece, time_other)
    space_other = exchange(sent_piece, "space", steps[-1])
    time_joined = over_tm([time_piece] * time_count)
    space_piece = add_pair("add_space_last", space_piece, space_other)
    joined = over_tm([space_piece] * time_count) + time_joined

    field_grad, mixed_field = call(
        field_kernel,
        "field_grad",
        [place],
        [wave, mixed_grad, dact, from_near, from_far, *rides],
        [own, own],
        matmuls=3,
    )
    field_grad, mixed_field, *joined = lax.optimization_barrier((field_grad, mixed_field, *joined))
    (own_half,) = call(join_kernel, "join_tm", [place], joined, [(grad_rows, LANES)])
    other_half = exchange(own_half, "space", 1)

    grads = ()
    for half in (own_half, other_half):

        def grads_body(*refs, mine=half is own_half):
            grads_kernel(time_count, mine, *refs)

        grads = call(
            grads_body,
            "weight_grads",
            [place],
            [half],
            [(2, features, 3 * features, F32), (2, features, features, F32)],
            [
                (2 * time_count, grad_rows // time_count // 2, LANES, F32),
                pltpu.SemaphoreType.DMA((2 * time_count,)),
            ],
            hbm=grads,
            aliases={2: 0, 3: 1} if grads else None,
            out_spec=pl.BlockSpec(memory_space=pltpu.HBM),
        )
    project_grad, combine_grad = grads
    return (mixed_field, field_grad, project_grad, combine_grad)


def solution(mesh):
    in_specs = (P("tm", "space", None), P("tm", "space", None), P("tm", "space", None), P(), P())
    out_specs = (P("tm", "space", None), P("tm", "space", None), P(), P())
    return jax.shard_map(
        per_device, mesh=mesh, in_specs=in_specs, out_specs=out_specs, check_vma=False
    )
```

```python
import math

import jax
import jax.numpy as jnp
from jax import lax
from jax.experimental import pallas as pl
from jax.experimental.pallas import tpu as pltpu
from jax.sharding import PartitionSpec as P

HEADS = 8
BLOCK = 128
HREACH = 2
LANES = 128
GROUP_ROWS = 16
VMEM_BYTES = 24 * 1024 * 1024
BF16 = jnp.bfloat16
F32 = jnp.float32


epsilon = 1e-05


def cost(matmuls):
    flops = matmuls * 2 * 1024 * 256 * 512
    return pl.CostEstimate(flops=flops, bytes_accessed=flops // 256, transcendentals=flops // 1024)


def dot_nn(left, right):
    return lax.dot_general(left, right, (((1,), (0,)), ((), ())), preferred_element_type=F32)


def dot_nt(left, right):
    return lax.dot_general(left, right, (((1,), (1,)), ((), ())), preferred_element_type=F32)


def dot_tn(left, right):
    return lax.dot_general(left, right, (((0,), (0,)), ((), ())), preferred_element_type=F32)


def layer_norm(rows):
    widened = rows.astype(F32)
    centered = widened - jnp.mean(widened, axis=-1, keepdims=True)
    inverse = lax.rsqrt(jnp.mean(centered * centered, axis=-1, keepdims=True) + epsilon)
    return (centered * inverse, inverse)


def norm_backward(upstream, normed, inverse):
    mean_grad = jnp.mean(upstream, axis=-1, keepdims=True)
    mean_cross = jnp.mean(upstream * normed, axis=-1, keepdims=True)
    return inverse * (upstream - mean_grad - normed * mean_cross)


def flip(matrix):
    return matrix.astype(BF16).T


def pair_columns(rows_t, pair, width):
    count = rows_t.shape[1]
    base = (pair * 2 * width) // LANES * LANES
    parts = []
    for head in (2 * pair, 2 * pair + 1):
        start = head * width - base
        pieces = []
        if start:
            pieces.append(jnp.zeros((start, count), rows_t.dtype))
        pieces.append(rows_t[head * width : (head + 1) * width])
        if start + width < LANES:
            pieces.append(jnp.zeros((LANES - start - width, count), rows_t.dtype))
        parts.append(jnp.concatenate(pieces, axis=0))
    return jnp.concatenate(parts, axis=1)


def pair_group(matrix, pair, width):
    base = (pair * 2 * width) // LANES * LANES
    return matrix[:, base : base + LANES]


def pair_diagonal(product, width):
    count = product.shape[1] // 2
    return jnp.concatenate([product[:width, :count], product[width:, count:]], axis=0)


def head_rows(rows, width):
    column = lax.broadcasted_iota(jnp.int32, (1, rows.shape[1]), 1) // width
    return jnp.concatenate(
        [rows * (column == head).astype(F32).astype(BF16) for head in range(HEADS)], axis=0
    )


def head_spread(per_head, width):
    return jnp.concatenate(
        [
            jnp.broadcast_to(per_head[head : head + 1], (width, per_head.shape[1]))
            for head in range(HEADS)
        ],
        axis=0,
    )


def listed_blocks(lists_ref, frame, block):
    own = lists_ref[frame, block, 0]
    return [
        lists_ref[frame, block, entry] - own + (block + HREACH)
        for entry in range(lists_ref.shape[2])
    ]


def halo_start(core, rim, row_count, near):
    after = core == 0 if near else core != 0
    return pl.multiple_of(jnp.where(after, rim + row_count, 0), BLOCK)


def project_rows(
    frame, start, rows, project_ref, turned_ref, act_ref, kv_ref, keys_t_ref, values_t_ref
):
    features = rows.shape[1]
    normed, _ = layer_norm(rows)
    act = normed.astype(BF16)
    span = pl.ds(start, rows.shape[0])
    act_ref[frame, span] = act
    kv_ref[frame, span] = dot_nn(act, project_ref[0, :, features:]).astype(BF16)
    keys_t = dot_nt(turned_ref[0, features : 2 * features], act).astype(BF16)
    values_t = dot_nt(turned_ref[0, 2 * features :], act).astype(BF16)
    for block in range(rows.shape[0] // BLOCK):
        lanes = slice(block * BLOCK, (block + 1) * BLOCK)
        keys_t_ref[frame, start // BLOCK + block] = keys_t[:, lanes]
        values_t_ref[frame, start // BLOCK + block] = values_t[:, lanes]
    return act


def prepare_kernel(
    place_ref,
    near_ref,
    wave_hbm,
    cot_hbm,
    project_hbm,
    combine_hbm,
    wave_ref,
    project_ref,
    turned_ref,
    combine_ref,
    cot_ref,
    query_ref,
    query_t_ref,
    act_ref,
    kv_ref,
    keys_t_ref,
    values_t_ref,
    sems,
):
    moves = [
        pltpu.make_async_copy(source, target, sems.at[index])
        for index, (source, target) in enumerate(
            (
                (project_hbm, project_ref),
                (wave_hbm, wave_ref),
                (combine_hbm, combine_ref),
                (cot_hbm, cot_ref),
            )
        )
    ]
    for move in moves:
        move.start()
    frame_count, row_count, features = wave_ref.shape
    rim = near_ref.shape[1]
    core = place_ref[1] % 2
    moves[0].wait()
    turned_ref[0] = flip(project_ref[0])
    for frame in range(frame_count):
        project_rows(
            frame,
            halo_start(core, rim, row_count, True),
            near_ref[frame],
            project_ref,
            turned_ref,
            act_ref,
            kv_ref,
            keys_t_ref,
            values_t_ref,
        )
    moves[1].wait()
    for frame in range(frame_count):
        act = project_rows(
            frame, rim, wave_ref[frame], project_ref, turned_ref, act_ref, kv_ref, keys_t_ref, values_t_ref
        )
        query_ref[frame] = dot_nn(act, project_ref[0, :, :features]).astype(BF16)
        query_t_ref[frame] = dot_nt(turned_ref[0, :features], act).astype(BF16)
    turned_ref[1] = flip(project_ref[1])
    moves[2].wait()
    moves[3].wait()


def space_forward_kernel(
    lists_ref,
    place_ref,
    far_ref,
    wave_ref,
    cot_ref,
    project_ref,
    turned_ref,
    combine_ref,
    query_t_ref,
    act_in,
    kv_in,
    keys_t_in,
    values_t_in,
    act_ref,
    kv_ref,
    keys_t_ref,
    values_t_ref,
    probs_ref,
    inverse_sum_ref,
    attended_ref,
    *rest,
):
    del act_in, kv_in, keys_t_in, values_t_in
    *sent_refs, mixed_s = rest
    me = place_ref[0]
    core = place_ref[1] % 2
    frame_count, row_count, features = wave_ref.shape
    rim = far_ref.shape[1]
    width = features // HEADS
    block_count = row_count // BLOCK
    exponent_scale = math.log2(math.e) / math.sqrt(width)
    for frame in range(frame_count):
        project_rows(
            frame,
            halo_start(core, rim, row_count, False),
            far_ref[frame],
            project_ref,
            turned_ref,
            act_ref,
            kv_ref,
            keys_t_ref,
            values_t_ref,
        )
    blocks = [(frame, block) for frame in range(frame_count) for block in range(block_count)]
    loaded = {}

    def load(index):
        frame, block = blocks[index]
        places = listed_blocks(lists_ref, frame, block)
        keys = jnp.concatenate(
            [kv_ref[frame, pl.ds(place * BLOCK, BLOCK), :features] for place in places], axis=0
        )
        loaded[index] = (keys, query_t_ref[frame, :, block * BLOCK : (block + 1) * BLOCK], places)

    def pair_scores(step):
        index, pair = divmod(step, HEADS // 2)
        if index not in loaded:
            load(index)
        keys, query_t, _ = loaded[index]
        return dot_nn(pair_group(keys, pair, width), pair_columns(query_t, pair, width))

    steps = len(blocks) * HEADS // 2
    scores = pair_scores(0)
    outs = []
    for step in range(steps):
        following = pair_scores(step + 1) if step + 1 < steps else None
        index, pair = divmod(step, HEADS // 2)
        frame, block = blocks[index]
        if pair == 0:
            block_values_t = jnp.concatenate(
                [values_t_ref[frame, place] for place in loaded[index][2]], axis=1
            )
            outs = []
        top = jnp.max(scores, axis=0, keepdims=True)
        exp_scores = jnp.exp2((scores - top) * exponent_scale)
        inverse_sum = 1.0 / jnp.sum(exp_scores, axis=0, keepdims=True)
        probs = exp_scores.astype(BF16)
        probs_ref[frame, block, :, pair * 2 * BLOCK : (pair + 1) * 2 * BLOCK] = probs
        inverse_sum_ref[frame, block, 2 * pair : 2 * pair + 1] = inverse_sum[:, :BLOCK]
        inverse_sum_ref[frame, block, 2 * pair + 1 : 2 * pair + 2] = inverse_sum[:, BLOCK:]
        out = dot_nn(block_values_t[pair * 2 * width : (pair + 1) * 2 * width], probs)
        outs.append(pair_diagonal(out * inverse_sum, width))
        scores = following
        if pair == HEADS // 2 - 1:
            attended_t = jnp.concatenate(outs, axis=0)
            span = slice(block * BLOCK, (block + 1) * BLOCK)
            attended_ref[frame, :, span] = attended_t.astype(BF16)
            mixed_s[frame, span] = (
                wave_ref[frame, span].astype(F32) + dot_nn(flip(attended_t), combine_ref[0])
            ).astype(BF16)
    for distance, ref in enumerate(sent_refs):
        rows = ref.shape[1]
        span = pl.ds(pl.multiple_of((me ^ distance) * rows, GROUP_ROWS), rows)
        ref[:, :, :features] = mixed_s[:, span]
        ref[:, :, features:] = cot_ref[:, span]


def time_kernel(
    scale,
    count_in,
    *refs,
):
    arrived_refs = refs[:count_in]
    project_ref, turned_ref, combine_ref = refs[count_in : count_in + 3]
    grad_refs = refs[count_in + 3 : 2 * count_in + 3]
    act_ref, dproj_ref, attended_t_ref, cot_ref, mixed_ref = refs[2 * count_in + 3 :]
    part_frames, row_count, features = grad_refs[0].shape
    width = features // HEADS
    count = part_frames * count_in * GROUP_ROWS
    groups = row_count // GROUP_ROWS
    exponent_scale = scale * math.log2(math.e)

    def grouped(lanes):
        return jnp.concatenate(
            [
                ref[:, group * GROUP_ROWS : (group + 1) * GROUP_ROWS, lanes].reshape(
                    part_frames * GROUP_ROWS, features
                )
                for group in range(groups)
                for ref in arrived_refs
            ],
            axis=0,
        )

    rows = grouped(slice(0, features))
    cot = grouped(slice(features, 2 * features))
    cot_ref[...] = cot
    normed, inverse = layer_norm(rows)
    act = normed.astype(BF16)
    act_ref[...] = act
    projected = dot_nn(act, project_ref[1]).astype(BF16)
    projected_t = dot_nt(turned_ref[1], act).astype(BF16)
    all_dattn = dot_nt(cot, combine_ref[1]).astype(BF16)
    all_dattn_t = dot_nt(combine_ref[1], cot).astype(BF16)
    all_count = HEADS * count
    key_row = lax.broadcasted_iota(jnp.int32, (count, all_count), 0) % GROUP_ROWS
    query_row = lax.broadcasted_iota(jnp.int32, (count, all_count), 1) % GROUP_ROWS
    same_row = key_row == query_row
    attended_groups, dquery_groups, dkey_groups, dvalue_groups = [], [], [], []
    pairs = range(HEADS // 2)

    def products(group):
        span = slice(group * count, (group + 1) * count)
        return tuple(
            jnp.concatenate(
                [
                    dot_nn(pair_group(left, pair, width), pair_columns(right, pair, width))
                    for pair in pairs
                ],
                axis=1,
            )
            for left, right in (
                (projected[span, features : 2 * features], projected_t[:features, span]),
                (projected[span, 2 * features :], all_dattn_t[:, span]),
            )
        )

    def by_heads(left_t, right):
        return jnp.concatenate(
            [
                pair_diagonal(
                    dot_nn(
                        left_t[pair * 2 * width : (pair + 1) * 2 * width],
                        right[:, pair * 2 * count : (pair + 1) * 2 * count],
                    ),
                    width,
                )
                for pair in pairs
            ],
            axis=0,
        )

    scores, dprobs = products(0)
    for group in range(groups):
        following = products(group + 1) if group + 1 < groups else (None, None)
        span = slice(group * count, (group + 1) * count)
        scores = jnp.where(same_row, scores, -3e38)
        top = jnp.max(scores, axis=0, keepdims=True)
        exp_scores = jnp.exp2((scores - top) * exponent_scale)
        probs = (exp_scores * (1.0 / jnp.sum(exp_scores, axis=0, keepdims=True))).astype(BF16)
        probs_wide = probs.astype(F32)
        delta = jnp.sum(probs_wide * dprobs, axis=0, keepdims=True)
        dscores = (probs_wide * (dprobs - delta) * scale).astype(BF16)
        attended_groups.append(by_heads(projected_t[2 * features :, span], probs).astype(BF16))
        dquery_groups.append(flip(by_heads(projected_t[features : 2 * features, span], dscores)))
        dkey_groups.append(
            dot_nn(dscores, head_rows(projected[span, :features], width)).astype(BF16)
        )
        dvalue_groups.append(dot_nn(probs, head_rows(all_dattn[span], width)).astype(BF16))
        scores, dprobs = following
    attended = jnp.concatenate([flip(attended_t) for attended_t in attended_groups], axis=0)
    mixed_ref[...] = (rows.astype(F32) + dot_nn(attended, combine_ref[1])).astype(BF16)
    attended_t_ref[...] = jnp.concatenate(attended_groups, axis=1)
    dproj = jnp.concatenate(
        [jnp.concatenate(parts, axis=0) for parts in (dquery_groups, dkey_groups, dvalue_groups)],
        axis=1,
    )
    dproj_ref[...] = dproj
    dact = dot_nt(dproj, project_ref[1])
    mixed_grad = (cot.astype(F32) + norm_backward(dact, normed, inverse)).astype(BF16)
    for part, ref in enumerate(grad_refs):
        for group in range(groups):
            span = slice(group * GROUP_ROWS, (group + 1) * GROUP_ROWS)
            for frame in range(part_frames):
                start = ((group * count_in + part) * part_frames + frame) * GROUP_ROWS
                ref[frame, span] = mixed_grad[start : start + GROUP_ROWS]


def time_grads_kernel(
    factor, part_frames, row_count, place_ref, act_ref, dproj_ref, attended_t_ref, cot_ref, mixed_ref, *refs
):
    *ride_refs, stacked_s = refs
    count_in = len(ride_refs)
    features = act_ref.shape[1]
    groups = row_count // GROUP_ROWS
    stack_grads(
        [dot_tn(act_ref[...], dproj_ref[...]), dot_nn(attended_t_ref[...], cot_ref[...])],
        factor,
        stacked_s,
    )
    chunk = stacked_s.shape[0] // count_in
    part_rows = part_frames * row_count
    for part, ref in enumerate(ride_refs):
        for group in range(groups):
            for frame in range(part_frames):
                start = ((group * count_in + part) * part_frames + frame) * GROUP_ROWS
                for lane_group in range(features // LANES):
                    row = chunk + lane_group * part_rows + frame * row_count + group * GROUP_ROWS
                    ref[row : row + GROUP_ROWS] = mixed_ref[
                        start : start + GROUP_ROWS, lane_group * LANES : (lane_group + 1) * LANES
                    ]
        half = chunk // 2
        for core in range(2):
            start = pl.multiple_of((core * count_in + (place_ref[0] ^ part)) * half, GROUP_ROWS)
            ref[core * half : (core + 1) * half] = stacked_s[pl.ds(start, half)]


def space_backward_kernel(
    scale,
    factor,
    count_in,
    lists_ref,
    place_ref,
    *refs,
):
    returned_refs = refs[:count_in]
    (
        act_ref,
        kv_ref,
        keys_t_ref,
        query_ref,
        probs_ref,
        inverse_sum_ref,
        attended_ref,
        combine_ref,
        mixed_grad_ref,
        dquery_ref,
        dkv_ref,
        kept_ref,
        sent_ref,
        dscores_s,
        dkv_s,
        stacked_s,
    ) = refs[count_in:]
    me = place_ref[0]
    frame_count, row_count, features = mixed_grad_ref.shape
    width = features // HEADS
    block_count = row_count // BLOCK
    rim = HREACH * BLOCK
    for distance, ref in enumerate(returned_refs):
        rows = ref.shape[1]
        span = pl.ds(pl.multiple_of((me ^ distance) * rows, GROUP_ROWS), rows)
        mixed_grad_ref[:, span] = ref[...]
    blocks = [(frame, block) for frame in range(frame_count) for block in range(block_count)]
    all_dattn_t = [
        dot_nt(combine_ref[0], mixed_grad_ref[frame]).astype(BF16) for frame in range(frame_count)
    ]
    loaded = {}

    def load(index):
        frame, block = blocks[index]
        places = listed_blocks(lists_ref, frame, block)
        values = jnp.concatenate(
            [kv_ref[frame, pl.ds(place * BLOCK, BLOCK), features:] for place in places], axis=0
        )
        loaded[index] = (
            values,
            all_dattn_t[frame][:, block * BLOCK : (block + 1) * BLOCK],
            places,
        )

    def pair_products(step):
        index, pair = divmod(step, HEADS // 2)
        if index not in loaded:
            load(index)
        values, dattn_t, _ = loaded[index]
        return dot_nn(pair_group(values, pair, width), pair_columns(dattn_t, pair, width))

    def add_listed(index, lanes, parts):
        frame = blocks[index][0]
        for entry, place in enumerate(loaded[index][2]):
            rows = pl.ds(place * BLOCK, BLOCK)
            dkv_s[frame, rows, lanes] += parts[entry * BLOCK : (entry + 1) * BLOCK]

    def add_keys(index):
        frame, block = blocks[index]
        queries = head_rows(query_ref[frame, block * BLOCK : (block + 1) * BLOCK], width)
        add_listed(index, slice(0, features), dot_nn(dscores_s[frame, block], queries))

    dkv_s[...] = jnp.zeros(dkv_s.shape, F32)
    steps = len(blocks) * HEADS // 2
    dprobs = pair_products(0)
    dquery_parts = []
    for step in range(steps):
        following = pair_products(step + 1) if step + 1 < steps else None
        index, pair = divmod(step, HEADS // 2)
        frame, block = blocks[index]
        _, dattn_t, places = loaded[index]
        if pair == 0:
            span = slice(block * BLOCK, (block + 1) * BLOCK)
            block_keys_t = jnp.concatenate([keys_t_ref[frame, place] for place in places], axis=1)
            dattn_wide = dattn_t.astype(F32)
            inverse_sum = inverse_sum_ref[frame, block]
            delta = jnp.sum(
                (dattn_wide * attended_ref[frame, :, span].astype(F32)).reshape(
                    HEADS, width, BLOCK
                ),
                axis=1,
            )
            row_scale = inverse_sum * scale
            dquery_parts = []
        if pair == 1:
            scaled_dattn = flip(dattn_wide * head_spread(inverse_sum, width))
            add_listed(
                index,
                slice(features, 2 * features),
                dot_nn(probs_ref[frame, block], head_rows(scaled_dattn, width)),
            )
        if pair == 2 and index:
            add_keys(index - 1)
        heads = slice(pair * 2 * width, (pair + 1) * 2 * width)
        columns = slice(pair * 2 * BLOCK, (pair + 1) * 2 * BLOCK)
        pair_delta, pair_scale = (
            jnp.concatenate([rows[2 * pair : 2 * pair + 1], rows[2 * pair + 1 : 2 * pair + 2]], axis=1)
            for rows in (delta, row_scale)
        )
        probs = probs_ref[frame, block, :, columns].astype(F32)
        dscores = (probs * ((dprobs - pair_delta) * pair_scale)).astype(BF16)
        dscores_s[frame, block, :, columns] = dscores
        dquery_parts.append(pair_diagonal(dot_nn(block_keys_t[heads], dscores), width))
        dprobs = following
        if pair == HEADS // 2 - 1:
            dquery_ref[frame, span] = flip(jnp.concatenate(dquery_parts, axis=0))
    add_keys(len(blocks) - 1)
    dkv_ref[...] = dkv_s[...].astype(BF16)
    extended = dkv_ref.shape[1]
    act = act_ref[...]
    own_act = act[:, rim : rim + row_count].reshape(frame_count * row_count, features)
    stack_grads(
        [
            dot_tn(own_act, dquery_ref[...].reshape(frame_count * row_count, features)),
            dot_tn(
                act.reshape(frame_count * extended, features),
                dkv_ref[...].reshape(frame_count * extended, 2 * features),
            ),
            sum(
                dot_nn(attended_ref[frame], mixed_grad_ref[frame]) for frame in range(frame_count)
            ),
        ],
        factor,
        stacked_s,
    )
    halve(place_ref[1] % 2, stacked_s, kept_ref, sent_ref)


def dact_kernel(place_ref, dquery_ref, dkv_ref, project_ref, dact_ref, near_ref, far_ref, dact_s):
    frame_count, row_count, features = dquery_ref.shape
    rim = near_ref.shape[1]
    core = place_ref[1] % 2
    for frame in range(frame_count):
        dact = dot_nt(dkv_ref[frame], project_ref[0, :, features:])
        dact_s[frame] = dact.astype(BF16)
        dact_ref[frame] = dact[rim : rim + row_count] + dot_nt(
            dquery_ref[frame], project_ref[0, :, :features]
        )
    near_ref[...] = dact_s[:, pl.ds(halo_start(core, rim, row_count, True), rim)]
    far_ref[...] = dact_s[:, pl.ds(halo_start(core, rim, row_count, False), rim)]


def field_kernel(place_ref, wave_ref, mixed_grad_ref, dact_ref, near_ref, far_ref, *refs):
    *ride_refs, field_ref, mixed_ref = refs
    frame_count, row_count, features = wave_ref.shape
    rows = row_count // len(ride_refs)
    lane_groups = features // LANES
    part_rows = frame_count * rows
    for frame in range(frame_count):
        normed, inverse = layer_norm(wave_ref[frame])
        dact = dact_ref[frame] + near_ref[frame].astype(F32) + far_ref[frame].astype(F32)
        field_ref[frame] = (
            mixed_grad_ref[frame].astype(F32) + norm_backward(dact, normed, inverse)
        ).astype(BF16)
        for distance, ref in enumerate(ride_refs):
            span = pl.ds(pl.multiple_of((place_ref[0] ^ distance) * rows, GROUP_ROWS), rows)
            for lane_group in range(lane_groups):
                start = ref.shape[0] - (lane_groups - lane_group) * part_rows + frame * rows
                mixed_ref[frame, span, lane_group * LANES : (lane_group + 1) * LANES] = ref[
                    start : start + rows
                ]


def ordered_sum(me, refs, parts_s):
    rows = parts_s.shape[1]
    for distance, ref in enumerate(refs):
        parts_s[me ^ distance] = ref[:rows]
    total = parts_s[0].astype(F32)
    for part in range(1, len(refs)):
        total = total + parts_s[part].astype(F32)
    return total.astype(BF16)


def halve(core, whole_s, kept_ref, sent_ref):
    half = kept_ref.shape[0]
    kept_ref[...] = whole_s[pl.ds(pl.multiple_of(core * half, GROUP_ROWS), half)]
    sent_ref[...] = whole_s[pl.ds(pl.multiple_of((1 - core) * half, GROUP_ROWS), half)]


def cores_kernel(place_ref, *refs):
    *ride_refs, kept_ref, sent_ref, parts_s, time_s = refs
    time_s[...] = ordered_sum(place_ref[0], ride_refs, parts_s)
    halve(place_ref[1] % 2, time_s, kept_ref, sent_ref)


def split_kernel(place_ref, kept_ref, arrived_ref, *refs):
    *part_refs, sum_s = refs
    sum_s[...] = add_rounded(kept_ref, arrived_ref)
    rows = part_refs[0].shape[0]
    for distance, ref in enumerate(part_refs):
        ref[...] = sum_s[pl.ds(pl.multiple_of((place_ref[0] ^ distance) * rows, GROUP_ROWS), rows)]


def tm_sum_kernel(place_ref, *refs):
    *part_refs, time_ref, time_other_ref, space_out_ref, time_out_ref, parts_s = refs
    space_out_ref[...] = ordered_sum(place_ref[0], part_refs, parts_s)
    time_out_ref[...] = add_rounded(time_ref, time_other_ref)


def add_rounded(left_ref, right_ref):
    return (left_ref[...].astype(F32) + right_ref[...].astype(F32)).astype(BF16)


def pairs_kernel(*refs):
    out_refs = refs[2 * len(refs) // 3 :]
    for index, ref in enumerate(out_refs):
        ref[...] = add_rounded(refs[2 * index], refs[2 * index + 1])


def both_kernel(space_ref, space_other_ref, time_ref, total_ref):
    rows = space_ref.shape[0]
    total_ref[:rows] = add_rounded(space_ref, space_other_ref)
    total_ref[rows:] = time_ref[...]


def join_kernel(place_ref, *refs):
    *part_refs, joined_ref = refs
    for distance, ref in enumerate(part_refs):
        rows = ref.shape[0]
        joined_ref[pl.ds(pl.multiple_of((place_ref[0] ^ distance) * rows, GROUP_ROWS), rows)] = ref[
            ...
        ]


def grads_kernel(time_count, own, place_ref, half_ref, *refs):
    project_hbm, combine_hbm, wide_s, sems = refs[-4:]
    features = combine_hbm.shape[1]
    core = place_ref[1] % 2
    rows = half_ref.shape[0] // time_count // 2
    for part in range(time_count):
        group, inner = divmod(part * rows, features)
        for layer in range(2):
            wide_s[layer, inner : inner + rows, group * LANES : (group + 1) * LANES] = half_ref[
                (2 * part + layer) * rows : (2 * part + layer + 1) * rows
            ].astype(F32)

    def write(half):
        moves = []
        for layer in range(2):
            if half:
                pieces = [
                    (slice(0, features), project_hbm.at[layer, :, 2 * features :]),
                    (slice(features, 2 * features), combine_hbm.at[layer]),
                ]
            else:
                pieces = [(slice(0, 2 * features), project_hbm.at[layer, :, : 2 * features])]
            for lanes, target in pieces:
                moves.append(
                    pltpu.make_async_copy(
                        wide_s.at[layer, :, lanes], target, sems.at[len(moves)]
                    )
                )
        for move in moves:
            move.start()
        for move in moves:
            move.wait()

    for half in range(2):

        @pl.when((core if own else 1 - core) == half)
        def _():
            write(half)


def stack_grads(grads, factor, stacked_ref):
    row = 0
    for grad in grads:
        for lane in range(0, grad.shape[1], LANES):
            stacked_ref[row : row + grad.shape[0]] = (
                grad[:, lane : lane + LANES] * factor
            ).astype(BF16)
            row += grad.shape[0]


def in_hbm(cells):
    return pltpu.with_memory_space_constraint(cells, pltpu.HBM)


def swap_far(cells, axis):
    pairs = [(i, i + 1) for i in range(1, lax.axis_size(axis) - 1, 2)]
    return lax.ppermute(cells, axis, pairs + [(j, i) for i, j in pairs])


def exchange(cells, axis, distance):
    return lax.ppermute(cells, axis, [(i, i ^ distance) for i in range(lax.axis_size(axis))])


def per_device(wave_field, cotangent, block_lists, project_weights, combine_weights):
    frame_count, row_count, features = wave_field.shape
    width = features // HEADS
    scale = 1.0 / math.sqrt(width)
    block_count = row_count // BLOCK
    list_length = block_lists.shape[-1]
    rim = HREACH * BLOCK
    extended = row_count + 2 * rim
    keys_count = list_length * BLOCK
    time_count = lax.axis_size("tm")
    all_frames = frame_count * time_count
    sent_rows = row_count // time_count
    factor = 1.0 / math.sqrt(frame_count * row_count * time_count * lax.axis_size("space"))
    space_count = lax.axis_size("space") // 2
    grad_rows = 4 * features // LANES * features
    chunk = grad_rows // time_count
    ride_rows = chunk + frame_count * sent_rows * features // LANES
    tokens = all_frames * sent_rows
    places = block_count + 2 * HREACH
    smem_spec = pl.BlockSpec(memory_space=pltpu.SMEM)
    vmem_spec = pl.BlockSpec(memory_space=pltpu.VMEM)
    hbm_spec = pl.BlockSpec(memory_space=pl.ANY)

    def call(
        body, name, scalars, operands, outs, scratch=(), matmuls=1, hbm=(), aliases=None, out_spec=None
    ):
        def typed(shape):
            return (shape[:-1], shape[-1]) if not isinstance(shape[-1], int) else (shape, BF16)

        return pl.pallas_call(
            body,
            in_specs=[smem_spec] * len(scalars)
            + [vmem_spec] * len(operands)
            + [hbm_spec] * len(hbm),
            out_specs=[out_spec or vmem_spec] * len(outs),
            out_shape=[jax.ShapeDtypeStruct(*typed(shape)) for shape in outs],
            scratch_shapes=[
                pltpu.VMEM(*typed(shape)) if isinstance(shape, tuple) else shape
                for shape in scratch
            ],
            compiler_params=pltpu.CompilerParams(vmem_limit_bytes=VMEM_BYTES),
            cost_estimate=cost(matmuls),
            input_output_aliases=aliases or {},
            name=name,
        )(*scalars, *operands, *hbm)

    def over_tm(pieces):
        return [pieces[0]] + [exchange(pieces[d], "tm", d) for d in range(1, time_count)]

    own = (frame_count, row_count, features)
    part = (frame_count, sent_rows, features)
    far = swap_far(wave_field, "space")
    near = exchange(wave_field, "space", 1)
    place = jnp.stack([lax.axis_index("tm"), lax.axis_index("space")]).astype(jnp.int32)
    extended_shapes = [
        (frame_count, extended, features),
        (frame_count, extended, 2 * features),
        (frame_count, places, features, BLOCK),
        (frame_count, places, features, BLOCK),
    ]
    wave, project, turned, combine, cot, queries, queries_t, *projected = call(
        prepare_kernel,
        "prepare",
        [place],
        [near],
        [
            own,
            (2, features, 3 * features),
            (2, 3 * features, features),
            (2, features, features),
            own,
            own,
            (frame_count, features, row_count),
            *extended_shapes,
        ],
        [pltpu.SemaphoreType.DMA((4,))],
        matmuls=12,
        hbm=[in_hbm(cells) for cells in (wave_field, cotangent, project_weights, combine_weights)],
    )
    block_lists = in_hbm(block_lists)
    act, keys_values, keys_t, _, probs, inverse_sum, attended, *parts = call(
        space_forward_kernel,
        "space_forward",
        [block_lists, place],
        [far, wave, cot, project, turned, combine, queries_t, *projected],
        [
            *extended_shapes,
            (frame_count, block_count, keys_count, HEADS * BLOCK),
            (frame_count, block_count, HEADS, BLOCK, F32),
            (frame_count, features, row_count),
            *[(frame_count, sent_rows, 2 * features)] * time_count,
        ],
        [own],
        matmuls=40,
        aliases={9 + index: index for index in range(4)},
    )
    kept_space = [act, keys_values, keys_t, queries, probs, inverse_sum, attended]
    arrived = over_tm(parts)

    def time_body(*refs):
        time_kernel(scale, time_count, *refs)

    outs = call(
        time_body,
        "time_pair",
        [],
        [*arrived, project, turned, combine],
        [
            *[part] * time_count,
            (tokens, features),
            (tokens, 3 * features),
            (features, tokens),
            (tokens, features),
            (tokens, features),
        ],
        matmuls=36,
    )
    parts, kept_time = outs[:time_count], outs[time_count:]

    def time_grads_body(*refs):
        time_grads_kernel(factor, frame_count, sent_rows, *refs)

    rides = call(
        time_grads_body,
        "time_grads",
        [place],
        kept_time,
        [(ride_rows, LANES)] * time_count,
        [(grad_rows, LANES)],
        matmuls=6,
    )
    returned = over_tm(parts)
    rides = over_tm(rides)
    returned[1], rides[0] = lax.optimization_barrier((returned[1], rides[0]))

    def backward_body(*refs):
        space_backward_kernel(scale, factor, time_count, *refs)

    mixed_grad, dquery, dkv, space_kept, space_sent = call(
        backward_body,
        "space_backward",
        [block_lists, place],
        [*returned, *kept_space, combine],
        [own, own, (frame_count, extended, 2 * features), *[(grad_rows // 2, LANES)] * 2],
        [
            (frame_count, block_count, keys_count, HEADS * BLOCK),
            (frame_count, extended, 2 * features, F32),
            (grad_rows, LANES),
        ],
        matmuls=44,
    )

    def add_pair(name, piece, other):
        (total,) = call(pairs_kernel, name, [], [piece, other], [(chunk // 2, LANES)])
        return total

    space_other = exchange(space_sent, "space", 1)
    time_kept, time_sent = call(
        cores_kernel,
        "add_tm_time",
        [place],
        rides,
        [(chunk // 2, LANES)] * 2,
        [(time_count, chunk, LANES), (chunk, LANES)],
        matmuls=24,
    )
    time_other = exchange(time_sent, "space", 1)
    space_other, time_kept = lax.optimization_barrier((space_other, time_kept))
    space_pieces = call(
        split_kernel,
        "add_cores",
        [place],
        [space_kept, space_other],
        [(chunk // 2, LANES)] * time_count,
        [(grad_rows // 2, LANES)],
    )
    space_pieces = over_tm(space_pieces)
    time_piece = add_pair("add_cores_time", time_kept, time_other)
    steps = [2 << bit for bit in range((space_count - 1).bit_length())]
    time_other = exchange(time_piece, "space", steps[0])
    space_piece, time_piece = call(
        tm_sum_kernel,
        "add_tm_space",
        [place],
        [*space_pieces, time_piece, time_other],
        [(chunk // 2, LANES)] * 2,
        [(time_count, chunk // 2, LANES)],
    )

    space_piece, dquery = lax.optimization_barrier((space_piece, dquery))
    dact, to_near, to_far = call(
        dact_kernel,
        "space_dact",
        [place],
        [dquery, dkv, project],
        [(*own, F32), (frame_count, rim, features), (frame_count, rim, features)],
        [(frame_count, extended, features)],
        matmuls=3,
    )
    sent_piece = space_piece
    for step, time_step in zip(steps, steps[1:]):
        space_other = exchange(sent_piece, "space", step)
        time_other = exchange(time_piece, "space", time_step)
        space_other, to_near, to_far = lax.optimization_barrier((space_other, to_near, to_far))
        sent_piece = add_pair("add_space", space_piece, space_other)
        space_piece, time_other = lax.optimization_barrier((sent_piece, time_other))
        time_piece = add_pair("add_space_time", time_piece, time_other)
    space_other = exchange(sent_piece, "space", steps[-1])
    time_piece, to_near, to_far = lax.optimization_barrier((time_piece, to_near, to_far))
    from_far = swap_far(to_far, "space")
    from_near = exchange(to_near, "space", 1)
    (piece,) = call(
        both_kernel,
        "add_space_last",
        [],
        [space_piece, space_other, time_piece],
        [(chunk, LANES)],
        matmuls=64,
    )
    joined = over_tm([piece] * time_count)

    field_grad, mixed_field = call(
        field_kernel,
        "field_grad",
        [place],
        [wave, mixed_grad, dact, from_near, from_far, *rides],
        [own, own],
        matmuls=3,
    )
    field_grad, mixed_field, *joined = lax.optimization_barrier((field_grad, mixed_field, *joined))
    (own_half,) = call(join_kernel, "join_tm", [place], joined, [(grad_rows, LANES)])
    other_half = exchange(own_half, "space", 1)

    grads = ()
    for half in (own_half, other_half):

        def grads_body(*refs, mine=half is own_half):
            grads_kernel(time_count, mine, *refs)

        grads = call(
            grads_body,
            "weight_grads",
            [place],
            [half],
            [(2, features, 3 * features, F32), (2, features, features, F32)],
            [
                (2, features, 2 * features, F32),
                pltpu.SemaphoreType.DMA((4,)),
            ],
            hbm=grads,
            aliases={2: 0, 3: 1} if grads else None,
            out_spec=pl.BlockSpec(memory_space=pltpu.HBM),
        )
    project_grad, combine_grad = grads
    return (mixed_field, field_grad, project_grad, combine_grad)


def solution(mesh):
    in_specs = (P("tm", "space", None), P("tm", "space", None), P("tm", "space", None), P(), P())
    out_specs = (P("tm", "space", None), P("tm", "space", None), P(), P())
    return jax.shard_map(
        per_device, mesh=mesh, in_specs=in_specs, out_specs=out_specs, check_vma=False
    )
```

```python
import math

import jax
import jax.numpy as jnp
from jax import lax
from jax.experimental import pallas as pl
from jax.experimental.pallas import tpu as pltpu
from jax.sharding import PartitionSpec as P

HEADS = 8
BLOCK = 128
HREACH = 2
LANES = 128
GROUP_ROWS = 16
VMEM_BYTES = 24 * 1024 * 1024
BF16 = jnp.bfloat16
F32 = jnp.float32


epsilon = 1e-05


def cost(matmuls):
    flops = matmuls * 2 * 1024 * 256 * 512
    return pl.CostEstimate(flops=flops, bytes_accessed=flops // 256, transcendentals=flops // 1024)


def dot_nn(left, right):
    return lax.dot_general(left, right, (((1,), (0,)), ((), ())), preferred_element_type=F32)


def dot_nt(left, right):
    return lax.dot_general(left, right, (((1,), (1,)), ((), ())), preferred_element_type=F32)


def dot_tn(left, right):
    return lax.dot_general(left, right, (((0,), (0,)), ((), ())), preferred_element_type=F32)


def layer_norm(rows):
    widened = rows.astype(F32)
    centered = widened - jnp.mean(widened, axis=-1, keepdims=True)
    inverse = lax.rsqrt(jnp.mean(centered * centered, axis=-1, keepdims=True) + epsilon)
    return (centered * inverse, inverse)


def norm_backward(upstream, normed, inverse):
    mean_grad = jnp.mean(upstream, axis=-1, keepdims=True)
    mean_cross = jnp.mean(upstream * normed, axis=-1, keepdims=True)
    return inverse * (upstream - mean_grad - normed * mean_cross)


def flip(matrix):
    return matrix.astype(BF16).T


def pair_columns(rows_t, pair, width):
    count = rows_t.shape[1]
    base = (pair * 2 * width) // LANES * LANES
    parts = []
    for head in (2 * pair, 2 * pair + 1):
        start = head * width - base
        pieces = []
        if start:
            pieces.append(jnp.zeros((start, count), rows_t.dtype))
        pieces.append(rows_t[head * width : (head + 1) * width])
        if start + width < LANES:
            pieces.append(jnp.zeros((LANES - start - width, count), rows_t.dtype))
        parts.append(jnp.concatenate(pieces, axis=0))
    return jnp.concatenate(parts, axis=1)


def pair_group(matrix, pair, width):
    base = (pair * 2 * width) // LANES * LANES
    return matrix[:, base : base + LANES]


def pair_diagonal(product, width):
    count = product.shape[1] // 2
    return jnp.concatenate([product[:width, :count], product[width:, count:]], axis=0)


def head_rows(rows, width):
    column = lax.broadcasted_iota(jnp.int32, (1, rows.shape[1]), 1) // width
    return jnp.concatenate(
        [rows * (column == head).astype(F32).astype(BF16) for head in range(HEADS)], axis=0
    )


def head_spread(per_head, width):
    return jnp.concatenate(
        [
            jnp.broadcast_to(per_head[head : head + 1], (width, per_head.shape[1]))
            for head in range(HEADS)
        ],
        axis=0,
    )


def listed_blocks(lists_ref, frame, block):
    own = lists_ref[frame, block, 0]
    return [
        lists_ref[frame, block, entry] - own + (block + HREACH)
        for entry in range(lists_ref.shape[2])
    ]


def halo_start(core, rim, row_count, near):
    after = core == 0 if near else core != 0
    return pl.multiple_of(jnp.where(after, rim + row_count, 0), BLOCK)


def project_rows(
    frame, start, rows, project_ref, turned_ref, act_ref, kv_ref, keys_t_ref, values_t_ref
):
    features = rows.shape[1]
    normed, _ = layer_norm(rows)
    act = normed.astype(BF16)
    span = pl.ds(start, rows.shape[0])
    act_ref[frame, span] = act
    kv_ref[frame, span] = dot_nn(act, project_ref[0, :, features:]).astype(BF16)
    keys_t = dot_nt(turned_ref[0, features : 2 * features], act).astype(BF16)
    values_t = dot_nt(turned_ref[0, 2 * features :], act).astype(BF16)
    for block in range(rows.shape[0] // BLOCK):
        lanes = slice(block * BLOCK, (block + 1) * BLOCK)
        keys_t_ref[frame, start // BLOCK + block] = keys_t[:, lanes]
        values_t_ref[frame, start // BLOCK + block] = values_t[:, lanes]
    return act


def prepare_kernel(
    place_ref,
    near_ref,
    wave_hbm,
    cot_hbm,
    project_hbm,
    combine_hbm,
    wave_ref,
    project_ref,
    turned_ref,
    combine_ref,
    cot_ref,
    query_ref,
    query_t_ref,
    act_ref,
    kv_ref,
    keys_t_ref,
    values_t_ref,
    sems,
):
    moves = [
        pltpu.make_async_copy(source, target, sems.at[index])
        for index, (source, target) in enumerate(
            (
                (project_hbm, project_ref),
                (wave_hbm, wave_ref),
                (combine_hbm, combine_ref),
                (cot_hbm, cot_ref),
            )
        )
    ]
    for move in moves:
        move.start()
    frame_count, row_count, features = wave_ref.shape
    rim = near_ref.shape[1]
    core = place_ref[1] % 2
    moves[0].wait()
    turned_ref[0] = flip(project_ref[0])
    for frame in range(frame_count):
        project_rows(
            frame,
            halo_start(core, rim, row_count, True),
            near_ref[frame],
            project_ref,
            turned_ref,
            act_ref,
            kv_ref,
            keys_t_ref,
            values_t_ref,
        )
    moves[1].wait()
    for frame in range(frame_count):
        act = project_rows(
            frame, rim, wave_ref[frame], project_ref, turned_ref, act_ref, kv_ref, keys_t_ref, values_t_ref
        )
        query_ref[frame] = dot_nn(act, project_ref[0, :, :features]).astype(BF16)
        query_t_ref[frame] = dot_nt(turned_ref[0, :features], act).astype(BF16)
    turned_ref[1] = flip(project_ref[1])
    moves[2].wait()
    moves[3].wait()


def space_forward_kernel(
    lists_ref,
    place_ref,
    far_ref,
    wave_ref,
    cot_ref,
    project_ref,
    turned_ref,
    combine_ref,
    query_t_ref,
    act_in,
    kv_in,
    keys_t_in,
    values_t_in,
    act_ref,
    kv_ref,
    keys_t_ref,
    values_t_ref,
    probs_ref,
    inverse_sum_ref,
    attended_ref,
    *rest,
):
    del act_in, kv_in, keys_t_in, values_t_in
    *sent_refs, mixed_s = rest
    me = place_ref[0]
    core = place_ref[1] % 2
    frame_count, row_count, features = wave_ref.shape
    rim = far_ref.shape[1]
    width = features // HEADS
    block_count = row_count // BLOCK
    exponent_scale = math.log2(math.e) / math.sqrt(width)
    for frame in range(frame_count):
        project_rows(
            frame,
            halo_start(core, rim, row_count, False),
            far_ref[frame],
            project_ref,
            turned_ref,
            act_ref,
            kv_ref,
            keys_t_ref,
            values_t_ref,
        )
    blocks = [(frame, block) for frame in range(frame_count) for block in range(block_count)]
    loaded = {}

    def load(index):
        frame, block = blocks[index]
        places = listed_blocks(lists_ref, frame, block)
        keys = jnp.concatenate(
            [kv_ref[frame, pl.ds(place * BLOCK, BLOCK), :features] for place in places], axis=0
        )
        loaded[index] = (keys, query_t_ref[frame, :, block * BLOCK : (block + 1) * BLOCK], places)

    def pair_scores(step):
        index, pair = divmod(step, HEADS // 2)
        if index not in loaded:
            load(index)
        keys, query_t, _ = loaded[index]
        return dot_nn(pair_group(keys, pair, width), pair_columns(query_t, pair, width))

    steps = len(blocks) * HEADS // 2
    scores, ahead = pair_scores(0), pair_scores(1)
    outs = []
    for step in range(steps):
        following = pair_scores(step + 2) if step + 2 < steps else None
        index, pair = divmod(step, HEADS // 2)
        frame, block = blocks[index]
        if pair == 0:
            block_values_t = jnp.concatenate(
                [values_t_ref[frame, place] for place in loaded[index][2]], axis=1
            )
            outs = []
        top = jnp.max(scores, axis=0, keepdims=True)
        exp_scores = jnp.exp2((scores - top) * exponent_scale)
        inverse_sum = 1.0 / jnp.sum(exp_scores, axis=0, keepdims=True)
        probs = exp_scores.astype(BF16)
        probs_ref[frame, block, :, pair * 2 * BLOCK : (pair + 1) * 2 * BLOCK] = probs
        inverse_sum_ref[frame, block, 2 * pair : 2 * pair + 1] = inverse_sum[:, :BLOCK]
        inverse_sum_ref[frame, block, 2 * pair + 1 : 2 * pair + 2] = inverse_sum[:, BLOCK:]
        out = dot_nn(block_values_t[pair * 2 * width : (pair + 1) * 2 * width], probs)
        outs.append(pair_diagonal(out * inverse_sum, width))
        scores, ahead = ahead, following
        if pair == HEADS // 2 - 1:
            attended_t = jnp.concatenate(outs, axis=0)
            span = slice(block * BLOCK, (block + 1) * BLOCK)
            attended_ref[frame, :, span] = attended_t.astype(BF16)
            mixed_s[frame, span] = (
                wave_ref[frame, span].astype(F32) + dot_nn(flip(attended_t), combine_ref[0])
            ).astype(BF16)
    for distance, ref in enumerate(sent_refs):
        rows = ref.shape[1]
        span = pl.ds(pl.multiple_of((me ^ distance) * rows, GROUP_ROWS), rows)
        ref[:, :, :features] = mixed_s[:, span]
        ref[:, :, features:] = cot_ref[:, span]


def time_kernel(
    scale,
    count_in,
    *refs,
):
    arrived_refs = refs[:count_in]
    project_ref, turned_ref, combine_ref = refs[count_in : count_in + 3]
    grad_refs = refs[count_in + 3 : 2 * count_in + 3]
    act_ref, dproj_ref, attended_t_ref, cot_ref, mixed_ref = refs[2 * count_in + 3 :]
    part_frames, row_count, features = grad_refs[0].shape
    width = features // HEADS
    count = part_frames * count_in * GROUP_ROWS
    groups = row_count // GROUP_ROWS
    exponent_scale = scale * math.log2(math.e)

    def grouped(lanes):
        return jnp.concatenate(
            [
                ref[:, group * GROUP_ROWS : (group + 1) * GROUP_ROWS, lanes].reshape(
                    part_frames * GROUP_ROWS, features
                )
                for group in range(groups)
                for ref in arrived_refs
            ],
            axis=0,
        )

    rows = grouped(slice(0, features))
    cot = grouped(slice(features, 2 * features))
    cot_ref[...] = cot
    normed, inverse = layer_norm(rows)
    act = normed.astype(BF16)
    act_ref[...] = act
    projected = dot_nn(act, project_ref[1]).astype(BF16)
    projected_t = dot_nt(turned_ref[1], act).astype(BF16)
    all_dattn = dot_nt(cot, combine_ref[1]).astype(BF16)
    all_dattn_t = dot_nt(combine_ref[1], cot).astype(BF16)
    all_count = HEADS * count
    key_row = lax.broadcasted_iota(jnp.int32, (count, all_count), 0) % GROUP_ROWS
    query_row = lax.broadcasted_iota(jnp.int32, (count, all_count), 1) % GROUP_ROWS
    same_row = key_row == query_row
    attended_groups, dquery_groups, dkey_groups, dvalue_groups = [], [], [], []
    pairs = range(HEADS // 2)

    def products(group):
        span = slice(group * count, (group + 1) * count)
        return tuple(
            jnp.concatenate(
                [
                    dot_nn(pair_group(left, pair, width), pair_columns(right, pair, width))
                    for pair in pairs
                ],
                axis=1,
            )
            for left, right in (
                (projected[span, features : 2 * features], projected_t[:features, span]),
                (projected[span, 2 * features :], all_dattn_t[:, span]),
            )
        )

    def by_heads(left_t, right):
        return jnp.concatenate(
            [
                pair_diagonal(
                    dot_nn(
                        left_t[pair * 2 * width : (pair + 1) * 2 * width],
                        right[:, pair * 2 * count : (pair + 1) * 2 * count],
                    ),
                    width,
                )
                for pair in pairs
            ],
            axis=0,
        )

    scores, dprobs = products(0)
    for group in range(groups):
        following = products(group + 1) if group + 1 < groups else (None, None)
        span = slice(group * count, (group + 1) * count)
        scores = jnp.where(same_row, scores, -3e38)
        top = jnp.max(scores, axis=0, keepdims=True)
        exp_scores = jnp.exp2((scores - top) * exponent_scale)
        probs = (exp_scores * (1.0 / jnp.sum(exp_scores, axis=0, keepdims=True))).astype(BF16)
        probs_wide = probs.astype(F32)
        delta = jnp.sum(probs_wide * dprobs, axis=0, keepdims=True)
        dscores = (probs_wide * (dprobs - delta) * scale).astype(BF16)
        attended_groups.append(by_heads(projected_t[2 * features :, span], probs).astype(BF16))
        dquery_groups.append(flip(by_heads(projected_t[features : 2 * features, span], dscores)))
        dkey_groups.append(
            dot_nn(dscores, head_rows(projected[span, :features], width)).astype(BF16)
        )
        dvalue_groups.append(dot_nn(probs, head_rows(all_dattn[span], width)).astype(BF16))
        scores, dprobs = following
    attended = jnp.concatenate([flip(attended_t) for attended_t in attended_groups], axis=0)
    mixed_ref[...] = (rows.astype(F32) + dot_nn(attended, combine_ref[1])).astype(BF16)
    attended_t_ref[...] = jnp.concatenate(attended_groups, axis=1)
    dproj = jnp.concatenate(
        [jnp.concatenate(parts, axis=0) for parts in (dquery_groups, dkey_groups, dvalue_groups)],
        axis=1,
    )
    dproj_ref[...] = dproj
    dact = dot_nt(dproj, project_ref[1])
    mixed_grad = (cot.astype(F32) + norm_backward(dact, normed, inverse)).astype(BF16)
    for part, ref in enumerate(grad_refs):
        for group in range(groups):
            span = slice(group * GROUP_ROWS, (group + 1) * GROUP_ROWS)
            for frame in range(part_frames):
                start = ((group * count_in + part) * part_frames + frame) * GROUP_ROWS
                ref[frame, span] = mixed_grad[start : start + GROUP_ROWS]


def time_grads_kernel(
    factor, part_frames, row_count, place_ref, act_ref, dproj_ref, attended_t_ref, cot_ref, mixed_ref, *refs
):
    *ride_refs, stacked_s = refs
    count_in = len(ride_refs)
    features = act_ref.shape[1]
    groups = row_count // GROUP_ROWS
    stack_grads(
        [dot_tn(act_ref[...], dproj_ref[...]), dot_nn(attended_t_ref[...], cot_ref[...])],
        factor,
        stacked_s,
    )
    chunk = stacked_s.shape[0] // count_in
    part_rows = part_frames * row_count
    for part, ref in enumerate(ride_refs):
        for group in range(groups):
            for frame in range(part_frames):
                start = ((group * count_in + part) * part_frames + frame) * GROUP_ROWS
                for lane_group in range(features // LANES):
                    row = chunk + lane_group * part_rows + frame * row_count + group * GROUP_ROWS
                    ref[row : row + GROUP_ROWS] = mixed_ref[
                        start : start + GROUP_ROWS, lane_group * LANES : (lane_group + 1) * LANES
                    ]
        half = chunk // 2
        for core in range(2):
            start = pl.multiple_of((core * count_in + (place_ref[0] ^ part)) * half, GROUP_ROWS)
            ref[core * half : (core + 1) * half] = stacked_s[pl.ds(start, half)]


def space_backward_kernel(
    scale,
    factor,
    count_in,
    lists_ref,
    place_ref,
    *refs,
):
    returned_refs = refs[:count_in]
    (
        act_ref,
        kv_ref,
        keys_t_ref,
        query_ref,
        probs_ref,
        inverse_sum_ref,
        attended_ref,
        combine_ref,
        mixed_grad_ref,
        dquery_ref,
        dkv_ref,
        kept_ref,
        sent_ref,
        dscores_s,
        dkv_s,
        stacked_s,
    ) = refs[count_in:]
    me = place_ref[0]
    frame_count, row_count, features = mixed_grad_ref.shape
    width = features // HEADS
    block_count = row_count // BLOCK
    rim = HREACH * BLOCK
    for distance, ref in enumerate(returned_refs):
        rows = ref.shape[1]
        span = pl.ds(pl.multiple_of((me ^ distance) * rows, GROUP_ROWS), rows)
        mixed_grad_ref[:, span] = ref[...]
    blocks = [(frame, block) for frame in range(frame_count) for block in range(block_count)]
    all_dattn_t = [
        dot_nt(combine_ref[0], mixed_grad_ref[frame]).astype(BF16) for frame in range(frame_count)
    ]
    loaded = {}

    def load(index):
        frame, block = blocks[index]
        places = listed_blocks(lists_ref, frame, block)
        values = jnp.concatenate(
            [kv_ref[frame, pl.ds(place * BLOCK, BLOCK), features:] for place in places], axis=0
        )
        loaded[index] = (
            values,
            all_dattn_t[frame][:, block * BLOCK : (block + 1) * BLOCK],
            places,
        )

    def pair_products(step):
        index, pair = divmod(step, HEADS // 2)
        if index not in loaded:
            load(index)
        values, dattn_t, _ = loaded[index]
        return dot_nn(pair_group(values, pair, width), pair_columns(dattn_t, pair, width))

    def add_listed(index, lanes, parts):
        frame = blocks[index][0]
        for entry, place in enumerate(loaded[index][2]):
            rows = pl.ds(place * BLOCK, BLOCK)
            dkv_s[frame, rows, lanes] += parts[entry * BLOCK : (entry + 1) * BLOCK]

    def add_keys(index):
        frame, block = blocks[index]
        queries = head_rows(query_ref[frame, block * BLOCK : (block + 1) * BLOCK], width)
        add_listed(index, slice(0, features), dot_nn(dscores_s[frame, block], queries))

    dkv_s[...] = jnp.zeros(dkv_s.shape, F32)
    steps = len(blocks) * HEADS // 2
    dprobs, ahead = pair_products(0), pair_products(1)
    dquery_parts = []
    for step in range(steps):
        following = pair_products(step + 2) if step + 2 < steps else None
        index, pair = divmod(step, HEADS // 2)
        frame, block = blocks[index]
        _, dattn_t, places = loaded[index]
        if pair == 0:
            span = slice(block * BLOCK, (block + 1) * BLOCK)
            block_keys_t = jnp.concatenate([keys_t_ref[frame, place] for place in places], axis=1)
            dattn_wide = dattn_t.astype(F32)
            inverse_sum = inverse_sum_ref[frame, block]
            delta = jnp.sum(
                (dattn_wide * attended_ref[frame, :, span].astype(F32)).reshape(
                    HEADS, width, BLOCK
                ),
                axis=1,
            )
            row_scale = inverse_sum * scale
            dquery_parts = []
        if pair == 1:
            scaled_dattn = flip(dattn_wide * head_spread(inverse_sum, width))
            add_listed(
                index,
                slice(features, 2 * features),
                dot_nn(probs_ref[frame, block], head_rows(scaled_dattn, width)),
            )
        if pair == 2 and index:
            add_keys(index - 1)
        heads = slice(pair * 2 * width, (pair + 1) * 2 * width)
        columns = slice(pair * 2 * BLOCK, (pair + 1) * 2 * BLOCK)
        pair_delta, pair_scale = (
            jnp.concatenate([rows[2 * pair : 2 * pair + 1], rows[2 * pair + 1 : 2 * pair + 2]], axis=1)
            for rows in (delta, row_scale)
        )
        probs = probs_ref[frame, block, :, columns].astype(F32)
        dscores = (probs * ((dprobs - pair_delta) * pair_scale)).astype(BF16)
        dscores_s[frame, block, :, columns] = dscores
        dquery_parts.append(pair_diagonal(dot_nn(block_keys_t[heads], dscores), width))
        dprobs, ahead = ahead, following
        if pair == HEADS // 2 - 1:
            dquery_ref[frame, span] = flip(jnp.concatenate(dquery_parts, axis=0))
    add_keys(len(blocks) - 1)
    dkv_ref[...] = dkv_s[...].astype(BF16)
    extended = dkv_ref.shape[1]
    act = act_ref[...]
    own_act = act[:, rim : rim + row_count].reshape(frame_count * row_count, features)
    stack_grads(
        [
            dot_tn(own_act, dquery_ref[...].reshape(frame_count * row_count, features)),
            dot_tn(
                act.reshape(frame_count * extended, features),
                dkv_ref[...].reshape(frame_count * extended, 2 * features),
            ),
            sum(
                dot_nn(attended_ref[frame], mixed_grad_ref[frame]) for frame in range(frame_count)
            ),
        ],
        factor,
        stacked_s,
    )
    halve(place_ref[1] % 2, stacked_s, kept_ref, sent_ref)


def dact_kernel(place_ref, dquery_ref, dkv_ref, project_ref, dact_ref, near_ref, far_ref, dact_s):
    frame_count, row_count, features = dquery_ref.shape
    rim = near_ref.shape[1]
    core = place_ref[1] % 2
    for frame in range(frame_count):
        dact = dot_nt(dkv_ref[frame], project_ref[0, :, features:])
        dact_s[frame] = dact.astype(BF16)
        dact_ref[frame] = dact[rim : rim + row_count] + dot_nt(
            dquery_ref[frame], project_ref[0, :, :features]
        )
    near_ref[...] = dact_s[:, pl.ds(halo_start(core, rim, row_count, True), rim)]
    far_ref[...] = dact_s[:, pl.ds(halo_start(core, rim, row_count, False), rim)]


def field_kernel(place_ref, wave_ref, mixed_grad_ref, dact_ref, near_ref, far_ref, *refs):
    *ride_refs, field_ref, mixed_ref = refs
    frame_count, row_count, features = wave_ref.shape
    rows = row_count // len(ride_refs)
    lane_groups = features // LANES
    part_rows = frame_count * rows
    for frame in range(frame_count):
        normed, inverse = layer_norm(wave_ref[frame])
        dact = dact_ref[frame] + near_ref[frame].astype(F32) + far_ref[frame].astype(F32)
        field_ref[frame] = (
            mixed_grad_ref[frame].astype(F32) + norm_backward(dact, normed, inverse)
        ).astype(BF16)
        for distance, ref in enumerate(ride_refs):
            span = pl.ds(pl.multiple_of((place_ref[0] ^ distance) * rows, GROUP_ROWS), rows)
            for lane_group in range(lane_groups):
                start = ref.shape[0] - (lane_groups - lane_group) * part_rows + frame * rows
                mixed_ref[frame, span, lane_group * LANES : (lane_group + 1) * LANES] = ref[
                    start : start + rows
                ]


def ordered_sum(me, refs, parts_s):
    rows = parts_s.shape[1]
    for distance, ref in enumerate(refs):
        parts_s[me ^ distance] = ref[:rows]
    total = parts_s[0].astype(F32)
    for part in range(1, len(refs)):
        total = total + parts_s[part].astype(F32)
    return total.astype(BF16)


def halve(core, whole_s, kept_ref, sent_ref):
    half = kept_ref.shape[0]
    kept_ref[...] = whole_s[pl.ds(pl.multiple_of(core * half, GROUP_ROWS), half)]
    sent_ref[...] = whole_s[pl.ds(pl.multiple_of((1 - core) * half, GROUP_ROWS), half)]


def cores_kernel(place_ref, *refs):
    *ride_refs, kept_ref, sent_ref, parts_s, time_s = refs
    time_s[...] = ordered_sum(place_ref[0], ride_refs, parts_s)
    halve(place_ref[1] % 2, time_s, kept_ref, sent_ref)


def split_kernel(place_ref, kept_ref, arrived_ref, *refs):
    *part_refs, sum_s = refs
    sum_s[...] = add_rounded(kept_ref, arrived_ref)
    rows = part_refs[0].shape[0]
    for distance, ref in enumerate(part_refs):
        ref[...] = sum_s[pl.ds(pl.multiple_of((place_ref[0] ^ distance) * rows, GROUP_ROWS), rows)]


def tm_sum_kernel(place_ref, *refs):
    *part_refs, time_ref, time_other_ref, space_out_ref, time_out_ref, parts_s = refs
    space_out_ref[...] = ordered_sum(place_ref[0], part_refs, parts_s)
    time_out_ref[...] = add_rounded(time_ref, time_other_ref)


def add_rounded(left_ref, right_ref):
    return (left_ref[...].astype(F32) + right_ref[...].astype(F32)).astype(BF16)


def pairs_kernel(*refs):
    out_refs = refs[2 * len(refs) // 3 :]
    for index, ref in enumerate(out_refs):
        ref[...] = add_rounded(refs[2 * index], refs[2 * index + 1])


def both_kernel(space_ref, space_other_ref, time_ref, total_ref):
    rows = space_ref.shape[0]
    total_ref[:rows] = add_rounded(space_ref, space_other_ref)
    total_ref[rows:] = time_ref[...]


def join_kernel(place_ref, *refs):
    *part_refs, joined_ref = refs
    for distance, ref in enumerate(part_refs):
        rows = ref.shape[0]
        joined_ref[pl.ds(pl.multiple_of((place_ref[0] ^ distance) * rows, GROUP_ROWS), rows)] = ref[
            ...
        ]


def grads_kernel(time_count, own, place_ref, half_ref, *refs):
    project_hbm, combine_hbm, wide_s, sems = refs[-4:]
    features = combine_hbm.shape[1]
    core = place_ref[1] % 2
    rows = half_ref.shape[0] // time_count // 2
    for part in range(time_count):
        group, inner = divmod(part * rows, features)
        for layer in range(2):
            wide_s[layer, inner : inner + rows, group * LANES : (group + 1) * LANES] = half_ref[
                (2 * part + layer) * rows : (2 * part + layer + 1) * rows
            ].astype(F32)

    def write(half):
        moves = []
        for layer in range(2):
            if half:
                pieces = [
                    (slice(0, features), project_hbm.at[layer, :, 2 * features :]),
                    (slice(features, 2 * features), combine_hbm.at[layer]),
                ]
            else:
                pieces = [(slice(0, 2 * features), project_hbm.at[layer, :, : 2 * features])]
            for lanes, target in pieces:
                moves.append(
                    pltpu.make_async_copy(
                        wide_s.at[layer, :, lanes], target, sems.at[len(moves)]
                    )
                )
        for move in moves:
            move.start()
        for move in moves:
            move.wait()

    for half in range(2):

        @pl.when((core if own else 1 - core) == half)
        def _():
            write(half)


def stack_grads(grads, factor, stacked_ref):
    row = 0
    for grad in grads:
        for lane in range(0, grad.shape[1], LANES):
            stacked_ref[row : row + grad.shape[0]] = (
                grad[:, lane : lane + LANES] * factor
            ).astype(BF16)
            row += grad.shape[0]


def in_hbm(cells):
    return pltpu.with_memory_space_constraint(cells, pltpu.HBM)


def swap_far(cells, axis):
    pairs = [(i, i + 1) for i in range(1, lax.axis_size(axis) - 1, 2)]
    return lax.ppermute(cells, axis, pairs + [(j, i) for i, j in pairs])


def exchange(cells, axis, distance):
    return lax.ppermute(cells, axis, [(i, i ^ distance) for i in range(lax.axis_size(axis))])


def per_device(wave_field, cotangent, block_lists, project_weights, combine_weights):
    frame_count, row_count, features = wave_field.shape
    width = features // HEADS
    scale = 1.0 / math.sqrt(width)
    block_count = row_count // BLOCK
    list_length = block_lists.shape[-1]
    rim = HREACH * BLOCK
    extended = row_count + 2 * rim
    keys_count = list_length * BLOCK
    time_count = lax.axis_size("tm")
    all_frames = frame_count * time_count
    sent_rows = row_count // time_count
    factor = 1.0 / math.sqrt(frame_count * row_count * time_count * lax.axis_size("space"))
    space_count = lax.axis_size("space") // 2
    grad_rows = 4 * features // LANES * features
    chunk = grad_rows // time_count
    ride_rows = chunk + frame_count * sent_rows * features // LANES
    tokens = all_frames * sent_rows
    places = block_count + 2 * HREACH
    smem_spec = pl.BlockSpec(memory_space=pltpu.SMEM)
    vmem_spec = pl.BlockSpec(memory_space=pltpu.VMEM)
    hbm_spec = pl.BlockSpec(memory_space=pl.ANY)

    def call(
        body, name, scalars, operands, outs, scratch=(), matmuls=1, hbm=(), aliases=None, out_spec=None
    ):
        def typed(shape):
            return (shape[:-1], shape[-1]) if not isinstance(shape[-1], int) else (shape, BF16)

        return pl.pallas_call(
            body,
            in_specs=[smem_spec] * len(scalars)
            + [vmem_spec] * len(operands)
            + [hbm_spec] * len(hbm),
            out_specs=[out_spec or vmem_spec] * len(outs),
            out_shape=[jax.ShapeDtypeStruct(*typed(shape)) for shape in outs],
            scratch_shapes=[
                pltpu.VMEM(*typed(shape)) if isinstance(shape, tuple) else shape
                for shape in scratch
            ],
            compiler_params=pltpu.CompilerParams(vmem_limit_bytes=VMEM_BYTES),
            cost_estimate=cost(matmuls),
            input_output_aliases=aliases or {},
            name=name,
        )(*scalars, *operands, *hbm)

    def over_tm(pieces):
        return [pieces[0]] + [exchange(pieces[d], "tm", d) for d in range(1, time_count)]

    own = (frame_count, row_count, features)
    part = (frame_count, sent_rows, features)
    far = swap_far(wave_field, "space")
    near = exchange(wave_field, "space", 1)
    place = jnp.stack([lax.axis_index("tm"), lax.axis_index("space")]).astype(jnp.int32)
    extended_shapes = [
        (frame_count, extended, features),
        (frame_count, extended, 2 * features),
        (frame_count, places, features, BLOCK),
        (frame_count, places, features, BLOCK),
    ]
    wave, project, turned, combine, cot, queries, queries_t, *projected = call(
        prepare_kernel,
        "prepare",
        [place],
        [near],
        [
            own,
            (2, features, 3 * features),
            (2, 3 * features, features),
            (2, features, features),
            own,
            own,
            (frame_count, features, row_count),
            *extended_shapes,
        ],
        [pltpu.SemaphoreType.DMA((4,))],
        matmuls=12,
        hbm=[in_hbm(cells) for cells in (wave_field, cotangent, project_weights, combine_weights)],
    )
    block_lists = in_hbm(block_lists)
    act, keys_values, keys_t, _, probs, inverse_sum, attended, *parts = call(
        space_forward_kernel,
        "space_forward",
        [block_lists, place],
        [far, wave, cot, project, turned, combine, queries_t, *projected],
        [
            *extended_shapes,
            (frame_count, block_count, keys_count, HEADS * BLOCK),
            (frame_count, block_count, HEADS, BLOCK, F32),
            (frame_count, features, row_count),
            *[(frame_count, sent_rows, 2 * features)] * time_count,
        ],
        [own],
        matmuls=40,
        aliases={9 + index: index for index in range(4)},
    )
    kept_space = [act, keys_values, keys_t, queries, probs, inverse_sum, attended]
    arrived = over_tm(parts)

    def time_body(*refs):
        time_kernel(scale, time_count, *refs)

    outs = call(
        time_body,
        "time_pair",
        [],
        [*arrived, project, turned, combine],
        [
            *[part] * time_count,
            (tokens, features),
            (tokens, 3 * features),
            (features, tokens),
            (tokens, features),
            (tokens, features),
        ],
        matmuls=36,
    )
    parts, kept_time = outs[:time_count], outs[time_count:]

    def time_grads_body(*refs):
        time_grads_kernel(factor, frame_count, sent_rows, *refs)

    rides = call(
        time_grads_body,
        "time_grads",
        [place],
        kept_time,
        [(ride_rows, LANES)] * time_count,
        [(grad_rows, LANES)],
        matmuls=6,
    )
    returned = over_tm(parts)
    rides = over_tm(rides)
    returned[1], rides[0] = lax.optimization_barrier((returned[1], rides[0]))

    def backward_body(*refs):
        space_backward_kernel(scale, factor, time_count, *refs)

    mixed_grad, dquery, dkv, space_kept, space_sent = call(
        backward_body,
        "space_backward",
        [block_lists, place],
        [*returned, *kept_space, combine],
        [own, own, (frame_count, extended, 2 * features), *[(grad_rows // 2, LANES)] * 2],
        [
            (frame_count, block_count, keys_count, HEADS * BLOCK),
            (frame_count, extended, 2 * features, F32),
            (grad_rows, LANES),
        ],
        matmuls=44,
    )

    def add_pair(name, piece, other):
        (total,) = call(pairs_kernel, name, [], [piece, other], [(chunk // 2, LANES)])
        return total

    space_other = exchange(space_sent, "space", 1)
    time_kept, time_sent = call(
        cores_kernel,
        "add_tm_time",
        [place],
        rides,
        [(chunk // 2, LANES)] * 2,
        [(time_count, chunk, LANES), (chunk, LANES)],
        matmuls=24,
    )
    time_other = exchange(time_sent, "space", 1)
    space_other, time_kept = lax.optimization_barrier((space_other, time_kept))
    space_pieces = call(
        split_kernel,
        "add_cores",
        [place],
        [space_kept, space_other],
        [(chunk // 2, LANES)] * time_count,
        [(grad_rows // 2, LANES)],
    )
    space_pieces = over_tm(space_pieces)
    time_piece = add_pair("add_cores_time", time_kept, time_other)
    steps = [2 << bit for bit in range((space_count - 1).bit_length())]
    time_other = exchange(time_piece, "space", steps[0])
    space_piece, time_piece = call(
        tm_sum_kernel,
        "add_tm_space",
        [place],
        [*space_pieces, time_piece, time_other],
        [(chunk // 2, LANES)] * 2,
        [(time_count, chunk // 2, LANES)],
    )

    space_piece, dquery = lax.optimization_barrier((space_piece, dquery))
    dact, to_near, to_far = call(
        dact_kernel,
        "space_dact",
        [place],
        [dquery, dkv, project],
        [(*own, F32), (frame_count, rim, features), (frame_count, rim, features)],
        [(frame_count, extended, features)],
        matmuls=3,
    )
    sent_piece = space_piece
    for step, time_step in zip(steps, steps[1:]):
        space_other = exchange(sent_piece, "space", step)
        time_other = exchange(time_piece, "space", time_step)
        space_other, to_near, to_far = lax.optimization_barrier((space_other, to_near, to_far))
        sent_piece = add_pair("add_space", space_piece, space_other)
        space_piece, time_other = lax.optimization_barrier((sent_piece, time_other))
        time_piece = add_pair("add_space_time", time_piece, time_other)
    space_other = exchange(sent_piece, "space", steps[-1])
    time_piece, to_near, to_far = lax.optimization_barrier((time_piece, to_near, to_far))
    from_far = swap_far(to_far, "space")
    from_near = exchange(to_near, "space", 1)
    (piece,) = call(
        both_kernel,
        "add_space_last",
        [],
        [space_piece, space_other, time_piece],
        [(chunk, LANES)],
        matmuls=64,
    )
    joined = over_tm([piece] * time_count)

    field_grad, mixed_field = call(
        field_kernel,
        "field_grad",
        [place],
        [wave, mixed_grad, dact, from_near, from_far, *rides],
        [own, own],
        matmuls=3,
    )
    field_grad, mixed_field, *joined = lax.optimization_barrier((field_grad, mixed_field, *joined))
    (own_half,) = call(join_kernel, "join_tm", [place], joined, [(grad_rows, LANES)])
    other_half = exchange(own_half, "space", 1)

    grads = ()
    for half in (own_half, other_half):

        def grads_body(*refs, mine=half is own_half):
            grads_kernel(time_count, mine, *refs)

        grads = call(
            grads_body,
            "weight_grads",
            [place],
            [half],
            [(2, features, 3 * features, F32), (2, features, features, F32)],
            [
                (2, features, 2 * features, F32),
                pltpu.SemaphoreType.DMA((4,)),
            ],
            hbm=grads,
            aliases={2: 0, 3: 1} if grads else None,
            out_spec=pl.BlockSpec(memory_space=pltpu.HBM),
        )
    project_grad, combine_grad = grads
    return (mixed_field, field_grad, project_grad, combine_grad)


def solution(mesh):
    in_specs = (P("tm", "space", None), P("tm", "space", None), P("tm", "space", None), P(), P())
    out_specs = (P("tm", "space", None), P("tm", "space", None), P(), P())
    return jax.shard_map(
        per_device, mesh=mesh, in_specs=in_specs, out_specs=out_specs, check_vma=False
    )
```
